128 devices in a mesh: gx: 32 (over x, y_lo, z), gy: 4 (over y_hi, core).
Axes of the slice: x: 4, y: 4 (y_hi: 2, y_lo: 2; y = y_hi * 2 + y_lo), z: 4, core: 2. Of those that a mesh axis runs over, the one named last changes fastest.
Arguments:
- pressure: float32 [512, 128, 512], P('gx', 'gy'), may hold values from -2.5 to 2.5
- velocity: float32 [3, 512, 128, 512], P(None, 'gx', 'gy'), may hold values from -2.5 to 2.5
- stretch: float32 [131072, 256], P(('gx', 'gy')), may hold values from 0.8 to 1.25
- rest_radius: float32 [131072, 256], P(('gx', 'gy')), may hold values from 1 to 3
- wall_speed: float32 [131072, 256], P(('gx', 'gy')), may hold values from -2.5 to 2.5
- block_cells: int32 [131072], P(('gx', 'gy')), may hold values from -1 to 1023, as said below
- depart_slot: int32 [4, 32, 4, 8], P(None, 'gx', 'gy'), may hold values from -1 to 1023, as said below
- depart_way: int32 [4, 32, 4, 8], P(None, 'gx', 'gy'), may hold values from 0 to 3, as said below
Outputs:
- pressure_out: float32 [512, 128, 512], P('gx', 'gy')
- velocity_out: float32 [3, 512, 128, 512], P(None, 'gx', 'gy')
- radius_out: float32 [131072, 256], P(('gx', 'gy'))
- speed_out: float32 [131072, 256], P(('gx', 'gy'))
- cells_out: int32 [131072], P(('gx', 'gy'))
The draws below stay inside these ranges and needn't reach their ends.
Inputs may be any that keep to these rules, and one draw needn't show every extreme that they name: `block_cells`: each tile has at most 896 occupied slots at the start and at least 896 // 3 (a third of it, rounded down); some tile has exactly 896. `depart_slot`: A used entry names a slot occupied at the start whose block has not left before; each slot is named by at most one entry in the whole window. Every tile has room for its arrivals. `depart_way`: tiles at the ends of the second tile index never send past them.
All inputs are finite; a program needn't handle non-finite values.
Results may differ from the reference program's by a relative error of at most 0.0003.
Values sent between devices are 32-bit elements; how exact they have to be, the bound alone decides.
A program may use at most 128 MiB of HBM per device.

```python
import math
import jax
import jax.numpy as jnp
from jax import lax

CX = 16
CY = 32
NZ = 512
SLOTS = 1024
BLOCK = 256
STEPS = 4
DEP = 8
TILES_X = 32
TILES_Y = 4
NX = 512
NY = 128
NCOL = 1024
ALL_SLOTS = 131072
LIVE_MAX = 896
N_GX = 32
N_GY = 4


def layout(key):
    tiles = TILES_X * TILES_Y
    keys = jax.random.split(jax.random.fold_in(key, 11), 8)
    counts = jax.random.randint(keys[0], (tiles,), LIVE_MAX // 3, LIVE_MAX + 1, dtype=jnp.int32)
    counts = counts.at[jax.random.randint(keys[1], (), 0, tiles, dtype=jnp.int32)].set(LIVE_MAX)
    orders = jax.vmap(lambda sub: jax.random.permutation(sub, SLOTS))(jax.random.split(keys[2], tiles)).astype(jnp.int32)
    ranks = jnp.argsort(orders, axis=1).astype(jnp.int32)
    columns = jax.random.randint(keys[3], (tiles, SLOTS), 0, NCOL, dtype=jnp.int32)
    cells = jnp.where(ranks < counts[:, None], columns, -1).astype(jnp.int32)
    leaving = orders[:, :STEPS * DEP].reshape(tiles, STEPS, DEP).transpose(1, 0, 2)
    kept = jax.random.randint(keys[4], leaving.shape, 0, 4, dtype=jnp.int32) > 0
    leaving = jnp.where(kept, leaving, -1).astype(jnp.int32)
    heading = jax.random.randint(keys[5], leaving.shape, 0, 4, dtype=jnp.int32)
    second = jnp.arange(tiles, dtype=jnp.int32) % TILES_Y
    heading = jnp.where((second == 0)[None, :, None] & (heading == 2), 3, heading)
    heading = jnp.where((second == TILES_Y - 1)[None, :, None] & (heading == 3), 2, heading)
    target_x = jax.random.randint(keys[6], (), 0, TILES_X, dtype=jnp.int32)
    target_y = jax.random.randint(keys[7], (), 1, TILES_Y - 1, dtype=jnp.int32)
    senders = (((target_x - 1) % TILES_X * TILES_Y + target_y, 1), ((target_x + 1) % TILES_X * TILES_Y + target_y, 0), (target_x * TILES_Y + target_y - 1, 3), (target_x * TILES_Y + target_y + 1, 2))
    for sender, toward in senders:
        leaving = leaving.at[0, sender].set(orders[sender, :DEP])
        heading = heading.at[0, sender].set(toward)
    shape = (STEPS, TILES_X, TILES_Y, DEP)
    return (cells.reshape(tiles * SLOTS), leaving.reshape(shape).astype(jnp.int32), heading.reshape(shape).astype(jnp.int32))


def draw_block_cells(key, part):
    return layout(key)[0]


def draw_depart_slot(key, part):
    return layout(key)[1]


def draw_depart_way(key, part):
    return layout(key)[2]


def levels(key, extent, shards, low, top_value):
    gain, own = 1.0, jax.random.fold_in(key, 6)
    for axis_at, blocks in shards:
        heights = jnp.exp(jax.random.uniform(jax.random.fold_in(own, axis_at), (blocks,), jnp.float32, low / len(shards), top_value / len(shards)))
        gain = gain * jnp.repeat(heights, extent[axis_at] // blocks).reshape([-1 if axis == axis_at else 1 for axis in range(len(extent))])
    return gain


def centred(rng, shape, scale, most, cuts=(), held_as=jnp.bfloat16):
    level = levels(rng, shape, cuts, -0.22, 0.18) if cuts else 1.0
    values = jax.random.normal(rng, shape, jnp.float32) * scale * level
    return jnp.minimum(jnp.maximum(values, -most), most).astype(held_as)


def setup_inputs(seed: int = 0) -> dict:
    key_of = jax.random.split(jax.random.key(seed), 9)
    pressure = centred(key_of[0], (NX, NY, NZ), 0.5, 2.5, ((0, 32), (1, 4)), jnp.float32)
    velocity = centred(key_of[1], (3, NX, NY, NZ), 0.5, 2.5, ((1, 32), (2, 4)), jnp.float32)
    stretch = jnp.clip(jnp.exp(math.log(1.25) - 0.4462871 * jax.random.uniform(key_of[2], (ALL_SLOTS, BLOCK), jnp.float32) ** levels(key_of[2], (ALL_SLOTS, BLOCK), ((0, 128),), -0.2, 0.2)), 0.8, 1.25)
    rest_radius = jnp.clip(jnp.exp(math.log(3.0) - 1.0986123 * jax.random.uniform(key_of[3], (ALL_SLOTS, BLOCK), jnp.float32) ** levels(key_of[3], (ALL_SLOTS, BLOCK), ((0, 128),), -0.2, 0.2)), 1.0, 3.0)
    wall_speed = centred(key_of[4], (ALL_SLOTS, BLOCK), 0.5, 2.5, ((0, 128),), jnp.float32)
    block_cells = draw_block_cells(jax.random.fold_in(key_of[8], 71), 0)
    depart_slot = draw_depart_slot(jax.random.fold_in(key_of[8], 71), 0)
    depart_way = draw_depart_way(jax.random.fold_in(key_of[8], 71), 0)
    return {"pressure": pressure, "velocity": velocity, "stretch": stretch, "rest_radius": rest_radius, "wall_speed": wall_speed, "block_cells": block_cells, "depart_slot": depart_slot, "depart_way": depart_way}


time_step = 0.04
flow_gain = 0.4
bulk_gain = 0.4
source_gain = 0.01
ambient = 1.0
tension = 0.1
viscosity = 0.02
liquid_speed = 20.0
polytropic = 1.4
four_pi = 12.566370614359172


def wall_update(radius, speed_now, rest, local_pressure, occupied):
    safe_radius = jnp.where(occupied, radius, 1.0)
    safe_rest = jnp.where(occupied, rest, 1.0)
    safe_speed = jnp.where(occupied, speed_now, 0.0)
    mach_number = safe_speed / liquid_speed
    wall_pressure = (ambient + 2.0 * tension / safe_rest) * jnp.exp(3.0 * polytropic * jnp.log(safe_rest / safe_radius)) - 2.0 * tension / safe_radius - 4.0 * viscosity * safe_speed / safe_radius
    driving = (1.0 + mach_number) * (wall_pressure - ambient - local_pressure) - 1.5 * (1.0 - mach_number / 3.0) * safe_speed * safe_speed
    acceleration = driving / ((1.0 - mach_number) * safe_radius)
    new_speed = safe_speed + time_step * acceleration
    new_radius = safe_radius + time_step * new_speed
    new_speed = jnp.where(occupied, new_speed, 0.0)
    new_radius = jnp.where(occupied, new_radius, 0.0)
    volume_rate = four_pi * new_radius * new_radius * new_speed
    return new_radius, new_speed, volume_rate


def slope_x(field):
    return (jnp.roll(field, -1, 0) - jnp.roll(field, 1, 0)) * 0.5


def slope_y(field):
    padded = jnp.pad(field, ((0, 0), (1, 1), (0, 0)))
    return (padded[:, 2:] - padded[:, :-2]) * 0.5


def slope_z(field):
    padded = jnp.pad(field, ((0, 0), (0, 0), (1, 1)))
    return (padded[:, :, 2:] - padded[:, :, :-2]) * 0.5


def field_step(pressure, velocity, source):
    new_x = velocity[0] - flow_gain * slope_x(pressure)
    new_y = velocity[1] - flow_gain * slope_y(pressure)
    new_z = velocity[2] - flow_gain * slope_z(pressure)
    divergence = slope_x(new_x) + slope_y(new_y) + slope_z(new_z)
    new_pressure = pressure - bulk_gain * divergence + (bulk_gain * source_gain) * source
    return new_pressure, jnp.stack([new_x, new_y, new_z])


def tile_view(field):
    return field.reshape(N_GX, CX, N_GY, CY, NZ).transpose(0, 2, 1, 3, 4).reshape(N_GX, N_GY, NCOL, BLOCK)


def grid_view(tiles):
    return tiles.reshape(N_GX, N_GY, CX, CY, NZ).transpose(0, 2, 1, 3, 4).reshape(NX, NY, NZ)


def settle(states, labels, arrivals, arrival_labels):
    present = arrival_labels > 0
    arrival_rank = jnp.cumsum(present.astype(jnp.int32), axis=-1).astype(jnp.int32) - 1
    vacant = labels == 0
    vacant_rank = jnp.cumsum(vacant.astype(jnp.int32), axis=-1).astype(jnp.int32) - 1
    pairing = present[..., :, None] & vacant[..., None, :] & (arrival_rank[..., :, None] == vacant_rank[..., None, :])
    flat = arrivals.reshape(arrivals.shape[:-2] + (-1,))
    placed = jnp.einsum('...as,...af->...sf', pairing.astype(jnp.float32), flat.astype(jnp.float32), precision=lax.Precision.HIGHEST)
    states = states + placed.reshape(states.shape)
    labels = labels + jnp.sum(jnp.where(pairing, arrival_labels[..., :, None], 0), axis=-2).astype(jnp.int32)
    return states, labels


def from_lower_x(field):
    return jnp.roll(field, 1, 0)


def from_upper_x(field):
    return jnp.roll(field, -1, 0)


def from_lower_y(field):
    return jnp.concatenate([jnp.zeros_like(field[:, :1]), field[:, :-1]], axis=1)


def from_upper_y(field):
    return jnp.concatenate([field[:, 1:], jnp.zeros_like(field[:, :1])], axis=1)


def migrate(states, labels, leave_slot, leave_way):
    picker = jax.vmap(jax.vmap(lambda table, index: jnp.take(table, index, axis=0)))
    leaving_ok = leave_slot >= 0
    safe_slot = jnp.maximum(leave_slot, 0).astype(jnp.int32)
    leaving = picker(states, safe_slot)
    leaving_labels = jnp.where(leaving_ok, picker(labels, safe_slot), 0).astype(jnp.int32)
    slot_ids = jnp.arange(SLOTS, dtype=jnp.int32)
    departed = jnp.any((safe_slot[..., :, None] == slot_ids) & leaving_ok[..., :, None], axis=-2)
    states = jnp.where(departed[..., None, None], 0.0, states)
    labels = jnp.where(departed, 0, labels).astype(jnp.int32)
    moved_rows = []
    moved_labels = []
    for mover, heading in ((from_lower_x, 1), (from_upper_x, 0), (from_lower_y, 3), (from_upper_y, 2)):
        chosen = leaving_ok & (leave_way == heading)
        moved_rows.append(mover(jnp.where(chosen[..., None, None], leaving, 0.0)))
        moved_labels.append(mover(jnp.where(chosen, leaving_labels, 0).astype(jnp.int32)))
    arrivals = jnp.concatenate(moved_rows, axis=2)
    arrival_labels = jnp.concatenate(moved_labels, axis=2)
    return settle(states, labels, arrivals, arrival_labels)


def reference(pressure, velocity, stretch, rest_radius, wall_speed, block_cells, depart_slot, depart_way):
    labels = (block_cells + 1).astype(jnp.int32).reshape(N_GX, N_GY, SLOTS)
    occupied = (labels > 0)[..., None]
    rest = jnp.where(occupied, rest_radius.reshape(N_GX, N_GY, SLOTS, BLOCK), 0.0)
    speeds = jnp.where(occupied, wall_speed.reshape(N_GX, N_GY, SLOTS, BLOCK), 0.0)
    states = jnp.stack([rest * stretch.reshape(N_GX, N_GY, SLOTS, BLOCK), speeds, rest], axis=-2)
    picker = jax.vmap(jax.vmap(lambda table, index: jnp.take(table, index, axis=0)))
    summer = jax.vmap(jax.vmap(lambda rates, index: jax.ops.segment_sum(rates, index, num_segments=NCOL)))
    for section in range(STEPS):
        cell_index = labels - 1
        occupied = (cell_index >= 0)[..., None]
        safe_index = jnp.maximum(cell_index, 0).astype(jnp.int32)
        local_pressure = picker(tile_view(pressure), safe_index)
        new_radius, new_speed, volume_rate = wall_update(states[..., 0, :], states[..., 1, :], states[..., 2, :], local_pressure, occupied)
        states = jnp.stack([new_radius, new_speed, states[..., 2, :]], axis=-2)
        source = grid_view(summer(volume_rate, safe_index))
        pressure, velocity = field_step(pressure, velocity, source)
        states, labels = migrate(states, labels, depart_slot[section], depart_way[section])
    radius_out = states[..., 0, :].reshape(ALL_SLOTS, BLOCK)
    speed_out = states[..., 1, :].reshape(ALL_SLOTS, BLOCK)
    cells_out = (labels - 1).astype(jnp.int32).reshape(ALL_SLOTS)
    return pressure, velocity, radius_out, speed_out, cells_out
```

```python
import functools
import math

import jax
import jax.numpy as jnp
from jax import lax
from jax.experimental import pallas as pl
from jax.experimental.pallas import tpu as pltpu
from jax.sharding import PartitionSpec as P

MESH = pl.DeviceIdType.MESH
f32 = jnp.float32
bf16 = jnp.bfloat16

STEPS = 4
DEP = 8
SLOTS = 1024
BLOCK = 256
LANES = 128
ARRIVE = STEPS * 4 * DEP
ROWS = SLOTS + ARRIVE
SLOT_BLOCKS = SLOTS // LANES
WAY_OF = (1, 0, 3, 2)

time_step = 0.04
half_gain = 0.2
source_scale = 0.004 * 12.566370614359172
exponent = 4.2
inv_ln2 = 1.0 / math.log(2.0)


def split(value):
    high = value.astype(bf16)
    return high, (value - high.astype(f32)).astype(bf16)


def wall_update(radius, speed, level, pressure):
    one_less = 1.0 - 0.05 * speed
    inverse = 1.0 / (one_less * radius)
    inv_radius = inverse * one_less
    wall = jnp.exp2(level - (exponent * inv_ln2) * jnp.log(radius))
    excess = wall - (0.2 + 0.08 * speed) * inv_radius - (1.0 + pressure)
    driving = (2.0 - one_less) * excess - (1.0 + 0.5 * one_less) * (speed * speed)
    speed = speed + time_step * (driving * inverse)
    radius = radius + time_step * speed
    return radius, speed, source_scale * (radius * radius) * speed


def kernel(
    cells_s, slot_s, way_s, cells_v, press, vel, stretch, rest, speed0,
    p_out, v_out, r_out, s_out, c_out,
    PR, VX, VY, VZ, R, S, A, AR, SB, OH, OHT, PH, PL, PG, VH, VL, SRC, YS, YR, VYS, VYR,
    MT, MR, MSK, AMSK, LT, LR, PLACE, CAT,
    in_sem, out_sem, meta_s, meta_r, xs, xr, vs, vr, ds_, dr,
):
    _, cx, cy, nz = vel.shape
    nq = nz // LANES
    half = cx * cy
    ncol = 2 * half
    jbs = cy // 16
    gx, gy = lax.axis_index("gx"), lax.axis_index("gy")
    ngx, ngy = lax.axis_size("gx"), lax.axis_size("gy")
    has_lo, has_hi = gy > 0, gy < ngy - 1
    targets = (
        (lax.rem(gx + 1, ngx), gy),
        (lax.rem(gx + ngx - 1, ngx), gy),
        (gx, lax.rem(gy + 1, ngy)),
        (gx, lax.rem(gy + ngy - 1, ngy)),
    )
    sends = (None, None, has_hi, has_lo)
    takes = (None, None, has_lo, has_hi)

    def under(flag, action):
        if flag is None:
            action()
        else:
            pl.when(flag)(action)

    barrier = pltpu.get_barrier_semaphore()
    for d in range(4):
        under(
            sends[d],
            lambda d=d: pl.semaphore_signal(
                barrier, inc=1, device_id=targets[d], device_id_type=MESH
            ),
        )

    inputs = []
    for q in range(nq):
        inputs.append((press.at[:, :, pl.ds(q * LANES, LANES)], PR.at[0, q, pl.ds(2, cx), pl.ds(8, cy), :]))
    inputs.append((rest, A))
    inputs.append((stretch, R))
    inputs.append((speed0, S))
    for comp in range(3):
        for q in range(nq):
            dst = (
                VX.at[q, pl.ds(1, cx), :, :],
                VY.at[q, :, pl.ds(8, cy), :],
                VZ.at[q],
            )[comp]
            inputs.append((vel.at[comp, :, :, pl.ds(q * LANES, LANES)], dst))
    loads = [pltpu.make_async_copy(a, b, in_sem.at[k]) for k, (a, b) in enumerate(inputs)]
    for load in loads:
        load.start()

    lane8 = lax.broadcasted_iota(jnp.int32, (8, LANES), 1)
    sub8 = lax.broadcasted_iota(jnp.int32, (8, LANES), 0)
    slot_id = sub8 * LANES + lane8
    label = cells_v[...] + 1
    leave_at = jnp.where(label > 0, STEPS, -1)
    entry_of = (lane8 // 32) * DEP + lane8 % DEP
    wanted = (lane8 // DEP) % 4
    wanted = jnp.where(wanted < 2, 1 - wanted, 5 - wanted)
    meta = jnp.zeros((8, LANES), jnp.int32)
    for e in range(STEPS * DEP):
        slot = slot_s[e]
        moved = jnp.where(slot >= 0, cells_s[jnp.maximum(slot, 0)] + 1, 0)
        meta = jnp.where((entry_of == e) & (wanted == way_s[e]), moved, meta)
        leave_at = jnp.where(slot_id == slot, e // DEP, leave_at)
    MT[...] = meta.astype(f32)

    @pl.when(jnp.logical_not(has_lo))
    def _():
        MR[2] = jnp.zeros((8, LANES), f32)
        YR[:, 0] = jnp.zeros(YR.shape[:1] + YR.shape[2:], f32)
        VYR[0] = jnp.zeros(VYR.shape[1:], f32)

    @pl.when(jnp.logical_not(has_hi))
    def _():
        MR[3] = jnp.zeros((8, LANES), f32)
        YR[:, 1] = jnp.zeros(YR.shape[:1] + YR.shape[2:], f32)
        VYR[1] = jnp.zeros(VYR.shape[1:], f32)

    pl.semaphore_wait(barrier, 2 + has_lo.astype(jnp.int32) + has_hi.astype(jnp.int32))

    def remote(src, dst, send_sem, recv_sem, d):
        return pltpu.make_async_remote_copy(
            src_ref=src, dst_ref=dst, send_sem=send_sem, recv_sem=recv_sem,
            device_id=targets[d], device_id_type=MESH,
        )

    def meta_copy(d):
        return remote(MT, MR.at[d], meta_s.at[d], meta_r.at[d], d)

    def p_copy(t, par, d):
        if d < 2:
            src = PR.at[par, :, pl.ds((cx, 2)[d], 2), pl.ds(8, cy), :]
            dst = PR.at[par, :, pl.ds((0, cx + 2)[d], 2), pl.ds(8, cy), :]
        else:
            src, dst = YS.at[t, 3 - d], YR.at[t, d - 2]
        return remote(src, dst, xs.at[t, d], xr.at[t, d], d)

    def v_copy(d):
        if d < 2:
            src = VX.at[:, pl.ds((cx, 1)[d], 1), :, :]
            dst = VX.at[:, pl.ds((0, cx + 1)[d], 1), :, :]
        else:
            src, dst = VYS.at[3 - d], VYR.at[d - 2]
        return remote(src, dst, vs.at[d], vr.at[d], d)

    def dep_copy(t, d):
        return remote(
            SB.at[t], AR.at[:, pl.ds(t * 32 + d * DEP, DEP), :], ds_.at[t, d], dr.at[t, d], d
        )

    def start(make):
        for d in range(4):
            under(sends[d], lambda d=d: make(d).start())

    def wait_sent(make):
        for d in range(4):
            under(sends[d], lambda d=d: make(d).wait_send())

    def wait_taken(make):
        for d in range(4):
            under(takes[d], lambda d=d: make(d).wait_recv())

    start(meta_copy)

    def pack_rows(t, par):
        def body(i, carry):
            for q in range(nq):
                YS[t, 0, q, i] = PR[par, q, i + 2, 8:10, :]
                YS[t, 1, q, i] = PR[par, q, i + 2, 6 + cy : 8 + cy, :]
            return carry

        lax.fori_loop(0, cx, body, 0)

    def keep_parts(i, jb, q, value):
        high, low = split(value)
        row = pl.multiple_of((q // 2) * half + i * cy + jb * 16, 16)
        col = (q % 2) * LANES
        PH[pl.ds(row, 16), col : col + LANES] = high
        PL[pl.ds(row, 16), col : col + LANES] = low

    for k in range(nq):
        loads[k].wait()
    pack_rows(0, 0)
    start(lambda d: p_copy(0, 0, d))

    def first_split(n, carry):
        i, jb = n // jbs, n % jbs
        for q in range(nq):
            keep_parts(i, jb, q, PR[0, q, i + 2, pl.ds(pl.multiple_of(8 + jb * 16, 8), 16), :])
        return carry

    lax.fori_loop(0, cx * jbs, first_split, 0)

    for k in range(nq, nq + 3):
        loads[k].wait()

    def first_state(n, carry):
        rows = pl.ds(pl.multiple_of(n * 16, 16), 16)
        rest_now = A[rows, :]
        R[rows, :] = R[rows, :] * rest_now
        A[rows, :] = inv_ln2 * (jnp.log(1.0 + 0.2 / rest_now) + exponent * jnp.log(rest_now))
        return carry

    lax.fori_loop(0, SLOTS // 16, first_state, 0, unroll=2)
    VH[pl.ds(SLOTS, ARRIVE), :] = jnp.zeros((ARRIVE, BLOCK), bf16)
    VL[pl.ds(SLOTS, ARRIVE), :] = jnp.zeros((ARRIVE, BLOCK), bf16)

    for k in range(nq + 3, nq + 3 + 3 * nq):
        loads[k].wait()

    def pack_flow(i, carry):
        for q in range(nq):
            VYS[0, q, i] = VY[q, i, 8:9, :]
            VYS[1, q, i] = VY[q, i, 7 + cy : 8 + cy, :]
        return carry

    lax.fori_loop(0, cx, pack_flow, 0)
    start(v_copy)

    wait_taken(meta_copy)
    came = (lane8 // DEP) % 4
    alab = jnp.where(
        came == 0, MR[0], jnp.where(came == 1, MR[1], jnp.where(came == 2, MR[2], MR[3]))
    )
    present = alab > 0.0
    lrow = lax.broadcasted_iota(jnp.int32, (LANES, LANES), 0)
    lcol = lax.broadcasted_iota(jnp.int32, (LANES, LANES), 1)
    upper = jnp.where(lrow <= lcol, 1.0, 0.0)
    upper_block = jnp.where(lrow // 32 == lcol // 32, upper, 0.0).astype(bf16)
    upper = upper.astype(bf16)
    ones = jnp.ones((LANES, LANES), bf16)
    present_f = jnp.where(present, 1.0, 0.0)
    arank = jnp.dot(present_f.astype(bf16), upper_block, preferred_element_type=f32) - 1.0
    arank = jnp.where(present, arank, -5.0)
    vacant = label == 0
    ranks = []
    for t in range(STEPS):
        vacant = vacant | (leave_at == t)
        flag = jnp.where(vacant, 1.0, 0.0).astype(bf16)
        rank = jnp.dot(flag, upper, preferred_element_type=f32) - 1.0
        total = jnp.dot(flag, ones, preferred_element_type=f32)
        for r in range(SLOT_BLOCKS - 1):
            rank = rank + jnp.where(sub8 > r, total[r : r + 1, :], 0.0)
        ranks.append(jnp.where(vacant, rank, -1.0))
        count = jnp.sum(jnp.where(lane8 // 32 == t, present_f, 0.0), axis=1, keepdims=True)
        vacant = vacant & (rank >= count)

    def code_of(lab):
        cell = lab - 1
        return jnp.where(lab > 0, (cell & 1) * half + (cell >> 1), -1).astype(f32)

    code = code_of(label)
    acode = code_of(alab.astype(jnp.int32))
    stack = [code, leave_at.astype(f32)] + ranks + [acode, alab]
    stack = stack + [jnp.zeros((8, LANES), f32)] * (16 - len(stack))
    LT[...] = jnp.concatenate(stack, axis=0).T
    LR[0:8, :] = code
    LR[8:16, :] = acode

    wide = lax.broadcasted_iota(jnp.int32, (16, ncol), 1).astype(f32)
    for r in range(SLOT_BLOCKS + 1):
        at = r if r < SLOT_BLOCKS else 48

        def one_hot_rows(m, carry, r=r, at=at):
            rows = pl.ds(pl.multiple_of(m * 16, 16), 16)
            column = LT[rows, at : at + 1]
            hot = jnp.where(column == wide, 1.0, 0.0).astype(bf16)
            OH[pl.ds(pl.multiple_of(r * LANES + m * 16, 16), 16), :] = hot
            return carry

        lax.fori_loop(0, LANES // 16, one_hot_rows, 0)

    tall = lax.broadcasted_iota(jnp.int32, (LANES, LANES), 0)

    def one_hot_columns(m, carry):
        ident = (tall + m * LANES).astype(f32)
        rows = pl.ds(pl.multiple_of(m * LANES, LANES), LANES)
        for r in range(SLOT_BLOCKS + 1):
            hot = jnp.where(ident == LR[r : r + 1, :], 1.0, 0.0).astype(bf16)
            OHT[rows, r * LANES : (r + 1) * LANES] = hot
        return carry

    lax.fori_loop(0, ncol // LANES, one_hot_columns, 0)

    group = lcol // 32
    for r in range(SLOT_BLOCKS):
        MSK[r * LANES : (r + 1) * LANES, :] = jnp.broadcast_to(
            LT[:, 8 + r : 9 + r], (LANES, LANES)
        )
        mine = jnp.broadcast_to(LT[:, 16 + r : 17 + r], (LANES, LANES))
        for t in range(1, STEPS):
            mine = jnp.where(group == t, LT[:, 16 + 8 * t + r : 17 + 8 * t + r], mine)
        hot = jnp.where(mine == arank[0:1, :], 1.0, 0.0).astype(bf16)
        PLACE[r * LANES : (r + 1) * LANES, 0:LANES] = hot
        PLACE[r * LANES : (r + 1) * LANES, LANES : 2 * LANES] = hot
    AMSK[...] = jnp.broadcast_to(LT[:, 56:57], (LANES, LANES))

    alab_high, alab_low = split(alab)
    final = jnp.where(leave_at == STEPS, label, 0).astype(f32)
    for r in range(SLOT_BLOCKS):
        hot = PLACE[r * LANES : (r + 1) * LANES, 0:LANES]
        nt = (((1,), (1,)), ((), ()))
        placed = lax.dot_general(alab_high, hot, nt, preferred_element_type=f32)
        placed = placed + lax.dot_general(alab_low, hot, nt, preferred_element_type=f32)
        final = final + jnp.where(sub8 == r, placed, 0.0)
    c_out[...] = final.astype(jnp.int32) - 1

    lane16 = lax.broadcasted_iota(jnp.int32, (16, LANES), 1)
    first_lane, last_lane = lane16 == 0, lane16 == LANES - 1

    def slope_z(tiles):
        zero = jnp.zeros((16, LANES), f32)
        ahead = [pltpu.roll(v, LANES - 1, 1) for v in tiles] + [zero]
        behind = [zero] + [pltpu.roll(v, 1, 1) for v in tiles]
        return [
            jnp.where(last_lane, ahead[q + 1], ahead[q])
            - jnp.where(first_lane, behind[q], behind[q + 1])
            for q in range(nq)
        ]

    low_gate = jnp.where(has_lo, 1.0, 0.0).astype(f32)
    high_gate = jnp.where(has_hi, 1.0, 0.0).astype(f32)
    chunk = 384

    def step(t, carry):
        par = lax.rem(t, 2)
        new = 1 - par

        def gather(m, carry):
            rows = pl.ds(pl.multiple_of(m * chunk, chunk), chunk)
            hot = OH[rows, :]
            PG[rows, :] = jnp.dot(hot, PH[...], preferred_element_type=f32) + jnp.dot(
                hot, PL[...], preferred_element_type=f32
            )
            return carry

        lax.fori_loop(0, ROWS // chunk, gather, 0)

        @pl.when(t > 0)
        def _():
            wait_taken(lambda d: dep_copy(t - 1, d))

        limit = t.astype(f32)

        def bubbles(n, carry):
            rows = pl.ds(pl.multiple_of(n * 16, 16), 16)
            radius, speed, rate = wall_update(R[rows, :], S[rows, :], A[rows, :], PG[rows, :])
            R[rows, :] = radius
            S[rows, :] = speed
            keep = MSK[rows, :]
            keep = jnp.concatenate([keep, keep], axis=1) >= limit
            high, low = split(jnp.where(keep, rate, 0.0))
            VH[rows, :] = high
            VL[rows, :] = low
            return carry

        lax.fori_loop(0, SLOTS // 16, bubbles, 0, unroll=2)

        for k in range(DEP):
            row = pl.ds(jnp.maximum(slot_s[t * DEP + k], 0), 1)
            SB[t, 0, k : k + 1, :] = R[row, :]
            SB[t, 1, k : k + 1, :] = S[row, :]
            SB[t, 2, k : k + 1, :] = A[row, :]
        start(lambda d: dep_copy(t, d))

        def arrived(n, carry):
            rows = pl.ds(pl.multiple_of(n * 16, 16), 16)
            low_rows = pl.ds(pl.multiple_of(SLOTS + n * 16, 16), 16)
            radius, speed, rate = wall_update(
                AR[0, rows, :], AR[1, rows, :], AR[2, rows, :], PG[low_rows, :]
            )
            AR[0, rows, :] = radius
            AR[1, rows, :] = speed
            keep = AMSK[rows, :]
            keep = jnp.concatenate([keep, keep], axis=1) > 0.0
            high, low = split(jnp.where(keep, rate, 0.0))
            VH[low_rows, :] = high
            VL[low_rows, :] = low
            return carry

        lax.fori_loop(0, 2 * t, arrived, 0)

        def scatter(m, carry):
            rows = pl.ds(pl.multiple_of(m * LANES, LANES), LANES)
            hot = OHT[rows, :]
            SRC[rows, :] = jnp.dot(hot, VH[...], preferred_element_type=f32) + jnp.dot(
                hot, VL[...], preferred_element_type=f32
            )
            return carry

        lax.fori_loop(0, ncol // LANES, scatter, 0)

        wait_taken(lambda d: p_copy(t, par, d))
        wait_sent(lambda d: p_copy(t, par, d))

        @pl.when(t == 0)
        def _():
            wait_taken(v_copy)
            wait_sent(v_copy)

            def unpack(i, carry):
                for q in range(nq):
                    VY[q, i, 7:8, :] = VYR[0, q, i]
                    VY[q, i, 8 + cy : 9 + cy, :] = VYR[1, q, i]
                return carry

            lax.fori_loop(0, cx, unpack, 0)

        def flow_x(n, carry):
            i, jb = n // jbs, n % jbs
            rows = pl.ds(pl.multiple_of(jb * 16, 16), 16)
            at = pl.ds(pl.multiple_of(8 + jb * 16, 8), 16)
            for q in range(nq):
                VX[q, i, rows, :] = VX[q, i, rows, :] - half_gain * (
                    PR[par, q, i + 2, at, :] - PR[par, q, i, at, :]
                )
            return carry

        lax.fori_loop(0, (cx + 2) * jbs, flow_x, 0, unroll=2)

        def side_rows(i, carry):
            for q in range(nq):
                PR[par, q, i + 2, 6:8, :] = YR[t, 0, q, i]
                PR[par, q, i + 2, 8 + cy : 10 + cy, :] = YR[t, 1, q, i]
                VY[q, i, 7:8, :] = low_gate * (
                    VY[q, i, 7:8, :]
                    - half_gain * (PR[par, q, i + 2, 8:9, :] - YR[t, 0, q, i, 0:1, :])
                )
                VY[q, i, 8 + cy : 9 + cy, :] = high_gate * (
                    VY[q, i, 8 + cy : 9 + cy, :]
                    - half_gain * (YR[t, 1, q, i, 1:2, :] - PR[par, q, i + 2, 7 + cy : 8 + cy, :])
                )
            return carry

        lax.fori_loop(0, cx, side_rows, 0)

        def flow_yz(n, carry):
            i, jb = n // jbs, n % jbs
            rows = pl.ds(pl.multiple_of(jb * 16, 16), 16)
            at = pl.ds(pl.multiple_of(8 + jb * 16, 8), 16)
            after, before = pl.ds(9 + jb * 16, 16), pl.ds(7 + jb * 16, 16)
            slopes = slope_z([PR[par, q, i + 2, at, :] for q in range(nq)])
            for q in range(nq):
                VZ[q, i, rows, :] = VZ[q, i, rows, :] - half_gain * slopes[q]
                VY[q, i, at, :] = VY[q, i, at, :] - half_gain * (
                    PR[par, q, i + 2, after, :] - PR[par, q, i + 2, before, :]
                )
            return carry

        lax.fori_loop(0, cx * jbs, flow_yz, 0, unroll=2)

        def pressure(n, carry):
            i, jb = n // jbs, n % jbs
            rows = pl.ds(pl.multiple_of(jb * 16, 16), 16)
            at = pl.ds(pl.multiple_of(8 + jb * 16, 8), 16)
            after, before = pl.ds(9 + jb * 16, 16), pl.ds(7 + jb * 16, 16)
            slopes = slope_z([VZ[q, i, rows, :] for q in range(nq)])
            for q in range(nq):
                rise = (
                    (VX[q, i + 2, rows, :] - VX[q, i, rows, :])
                    + (VY[q, i, after, :] - VY[q, i, before, :])
                    + slopes[q]
                )
                row = pl.multiple_of((q // 2) * half + i * cy + jb * 16, 16)
                col = (q % 2) * LANES
                value = (
                    PR[par, q, i + 2, at, :]
                    - half_gain * rise
                    + SRC[pl.ds(row, 16), col : col + LANES]
                )
                PR[new, q, i + 2, at, :] = value
                keep_parts(i, jb, q, value)
            return carry

        lax.fori_loop(0, cx * jbs, pressure, 0, unroll=2)

        @pl.when(t < STEPS - 1)
        def _():
            pack_rows(t + 1, new)
            start(lambda d: p_copy(t + 1, new, d))

        return carry

    lax.fori_loop(0, STEPS, step, 0)

    last = STEPS % 2
    results = []
    for q in range(nq):
        results.append((PR.at[last, q, pl.ds(2, cx), pl.ds(8, cy), :], p_out.at[:, :, pl.ds(q * LANES, LANES)]))
        for comp in range(3):
            src = (
                VX.at[q, pl.ds(1, cx), :, :],
                VY.at[q, :, pl.ds(8, cy), :],
                VZ.at[q],
            )[comp]
            results.append((src, v_out.at[comp, :, :, pl.ds(q * LANES, LANES)]))
    results.append((R, r_out))
    results.append((S, s_out))
    stores = [pltpu.make_async_copy(a, b, out_sem.at[k]) for k, (a, b) in enumerate(results)]
    for store in stores[: 4 * nq]:
        store.start()

    wait_taken(lambda d: dep_copy(STEPS - 1, d))
    keep = AMSK[...] > 0.0
    for k in range(2):
        for w in range(2):
            col = slice(w * LANES, (w + 1) * LANES)
            high, low = split(jnp.where(keep, AR[k, :, col], 0.0))
            to = slice(k * BLOCK + w * LANES, k * BLOCK + (w + 1) * LANES)
            CAT[0:ARRIVE, to] = high
            CAT[ARRIVE : 2 * ARRIVE, to] = low

    def finish(m, carry):
        rows = pl.ds(pl.multiple_of(m * LANES, LANES), LANES)
        placed = jnp.dot(PLACE[rows, :], CAT[...], preferred_element_type=f32)
        keep = MSK[rows, :]
        keep = jnp.concatenate([keep, keep], axis=1) >= float(STEPS)
        R[rows, :] = jnp.where(keep, R[rows, :], 0.0) + placed[:, :BLOCK]
        S[rows, :] = jnp.where(keep, S[rows, :], 0.0) + placed[:, BLOCK:]
        return carry

    lax.fori_loop(0, SLOT_BLOCKS, finish, 0)
    for store in stores[4 * nq :]:
        store.start()
    wait_sent(meta_copy)
    for t in range(STEPS):
        wait_sent(lambda d, t=t: dep_copy(t, d))
    for store in stores:
        store.wait()


def on_device(
    pressure, velocity, stretch, rest_radius, wall_speed, block_cells, depart_slot, depart_way
):
    cx, cy, nz = pressure.shape
    nq = nz // LANES
    ncol = 2 * cx * cy
    smem = pl.BlockSpec(memory_space=pltpu.SMEM)
    vmem = pl.BlockSpec(memory_space=pltpu.VMEM)
    hbm = pl.BlockSpec(memory_space=pl.ANY)
    dma = pltpu.SemaphoreType.DMA
    p, v, r, s, c = pl.pallas_call(
        kernel,
        out_shape=(
            jax.ShapeDtypeStruct(pressure.shape, f32),
            jax.ShapeDtypeStruct(velocity.shape, f32),
            jax.ShapeDtypeStruct(stretch.shape, f32),
            jax.ShapeDtypeStruct(stretch.shape, f32),
            jax.ShapeDtypeStruct((SLOT_BLOCKS, LANES), jnp.int32),
        ),
        in_specs=[smem, smem, smem, vmem, hbm, hbm, hbm, hbm, hbm],
        out_specs=(hbm, hbm, hbm, hbm, vmem),
        scratch_shapes=[
            pltpu.VMEM((2, nq, cx + 4, cy + 16, LANES), f32),
            pltpu.VMEM((nq, cx + 2, cy, LANES), f32),
            pltpu.VMEM((nq, cx, cy + 16, LANES), f32),
            pltpu.VMEM((nq, cx, cy, LANES), f32),
            pltpu.VMEM((SLOTS, BLOCK), f32),
            pltpu.VMEM((SLOTS, BLOCK), f32),
            pltpu.VMEM((SLOTS, BLOCK), f32),
            pltpu.VMEM((3, ARRIVE, BLOCK), f32),
            pltpu.VMEM((STEPS, 3, DEP, BLOCK), f32),
            pltpu.VMEM((ROWS, ncol), bf16),
            pltpu.VMEM((ncol, ROWS), bf16),
            pltpu.VMEM((ncol, BLOCK), bf16),
            pltpu.VMEM((ncol, BLOCK), bf16),
            pltpu.VMEM((ROWS, BLOCK), f32),
            pltpu.VMEM((ROWS, BLOCK), bf16),
            pltpu.VMEM((ROWS, BLOCK), bf16),
            pltpu.VMEM((ncol, BLOCK), f32),
            pltpu.VMEM((STEPS, 2, nq, cx, 2, LANES), f32),
            pltpu.VMEM((STEPS, 2, nq, cx, 2, LANES), f32),
            pltpu.VMEM((2, nq, cx, 1, LANES), f32),
            pltpu.VMEM((2, nq, cx, 1, LANES), f32),
            pltpu.VMEM((8, LANES), f32),
            pltpu.VMEM((4, 8, LANES), f32),
            pltpu.VMEM((SLOTS, LANES), f32),
            pltpu.VMEM((ARRIVE, LANES), f32),
            pltpu.VMEM((LANES, LANES), f32),
            pltpu.VMEM((16, LANES), f32),
            pltpu.VMEM((SLOTS, 2 * ARRIVE), bf16),
            pltpu.VMEM((2 * ARRIVE, 2 * BLOCK), bf16),
            dma((4 * nq + 3,)),
            dma((4 * nq + 2,)),
            dma((4,)),
            dma((4,)),
            dma((STEPS, 4)),
            dma((STEPS, 4)),
            dma((4,)),
            dma((4,)),
            dma((STEPS, 4)),
            dma((STEPS, 4)),
        ],
        compiler_params=pltpu.CompilerParams(
            collective_id=0, has_side_effects=True, vmem_limit_bytes=50 * 2**20
        ),
        cost_estimate=pl.CostEstimate(
            flops=10 * 2**30, bytes_accessed=13 * 2**20, transcendentals=2**22
        ),
    )(
        block_cells,
        depart_slot.reshape(-1),
        depart_way.reshape(-1),
        block_cells.reshape(SLOT_BLOCKS, LANES),
        pressure,
        velocity,
        stretch,
        rest_radius,
        wall_speed,
    )
    return p, v, r, s, c.reshape(-1)


def solution(mesh):
    placed = (
        P("gx", "gy", None),
        P(None, "gx", "gy", None),
        P(("gx", "gy"), None),
        P(("gx", "gy"), None),
        P(("gx", "gy"), None),
        P(("gx", "gy")),
        P(None, "gx", "gy", None),
        P(None, "gx", "gy", None),
    )
    return jax.shard_map(
        on_device,
        mesh=mesh,
        in_specs=placed,
        out_specs=(
            P("gx", "gy", None),
            P(None, "gx", "gy", None),
            P(("gx", "gy"), None),
            P(("gx", "gy"), None),
            P(("gx", "gy")),
        ),
        check_vma=False,
    )
```

```python
import functools
import math

import jax
import jax.numpy as jnp
from jax import lax
from jax.experimental import pallas as pl
from jax.experimental.pallas import tpu as pltpu
from jax.sharding import PartitionSpec as P

MESH = pl.DeviceIdType.MESH
f32 = jnp.float32
bf16 = jnp.bfloat16

STEPS = 4
DEP = 8
SLOTS = 1024
BLOCK = 256
LANES = 128
ARRIVE = STEPS * 4 * DEP
ROWS = SLOTS + ARRIVE
SLOT_BLOCKS = SLOTS // LANES
WAY_OF = (1, 0, 3, 2)

time_step = 0.04
half_gain = 0.2
source_scale = 0.004 * 12.566370614359172
exponent = 4.2
inv_ln2 = 1.0 / math.log(2.0)


def split(value):
    high = value.astype(bf16)
    return high, (value - high.astype(f32)).astype(bf16)


def wall_update(radius, speed, level, pressure):
    one_less = 1.0 - 0.05 * speed
    divisor = one_less * radius
    inverse = pl.reciprocal(divisor, approx=True)
    inverse = inverse * (2.0 - divisor * inverse)
    inv_radius = inverse * one_less
    wall = jnp.exp2(level - (exponent * inv_ln2) * jnp.log(radius))
    excess = wall - (0.2 + 0.08 * speed) * inv_radius - (1.0 + pressure)
    driving = (2.0 - one_less) * excess - (1.0 + 0.5 * one_less) * (speed * speed)
    speed = speed + time_step * (driving * inverse)
    radius = radius + time_step * speed
    return radius, speed, source_scale * (radius * radius) * speed


def kernel(
    cells_h, slot_h, way_h, cells_b, press, vel, stretch, rest, speed0,
    p_out, VX, VY, VZ, R, S, c_out,
    PR, A, AR, SB, OH, OHT, PHL, PG, VHL, SRC, YS, YR, VYS, VYR,
    MT, MR, MSK, AMSK, LT, LR, PLACE, CAT, cells_s, slot_s, way_s, cells_v,
    in_sem, meta_s, meta_r, xs, xr, vs, vr, ds_, dr,
):
    _, cx, cy, nz = vel.shape
    nq = nz // LANES
    half = cx * cy
    ncol = 2 * half
    jbs = cy // 16
    gx, gy = lax.axis_index("gx"), lax.axis_index("gy")
    ngx, ngy = lax.axis_size("gx"), lax.axis_size("gy")
    has_lo, has_hi = gy > 0, gy < ngy - 1
    targets = (
        (lax.rem(gx + 1, ngx), gy),
        (lax.rem(gx + ngx - 1, ngx), gy),
        (gx, lax.rem(gy + 1, ngy)),
        (gx, lax.rem(gy + ngy - 1, ngy)),
    )
    sends = (None, None, has_hi, has_lo)
    takes = (None, None, has_lo, has_hi)

    def under(flag, action):
        if flag is None:
            action()
        else:
            pl.when(flag)(action)

    barrier = pltpu.get_barrier_semaphore()
    for d in range(4):
        under(
            sends[d],
            lambda d=d: pl.semaphore_signal(
                barrier, inc=1, device_id=targets[d], device_id_type=MESH
            ),
        )

    inputs = [(cells_h, cells_s), (slot_h, slot_s), (way_h, way_s), (cells_b, cells_v)]
    for q in range(nq):
        inputs.append((press.at[:, :, pl.ds(q * LANES, LANES)], PR.at[0, q, pl.ds(2, cx), pl.ds(8, cy), :]))
    inputs.append((rest, A))
    inputs.append((stretch, R))
    inputs.append((speed0, S))
    for comp in range(3):
        for q in range(nq):
            dst = (
                VX.at[q, pl.ds(1, cx), :, :],
                VY.at[q, :, pl.ds(8, cy), :],
                VZ.at[q],
            )[comp]
            inputs.append((vel.at[comp, :, :, pl.ds(q * LANES, LANES)], dst))
    loads = [pltpu.make_async_copy(a, b, in_sem.at[k]) for k, (a, b) in enumerate(inputs)]
    for load in loads:
        load.start()

    for load in loads[:4]:
        load.wait()
    loads = loads[4:]

    lane8 = lax.broadcasted_iota(jnp.int32, (8, LANES), 1)
    sub8 = lax.broadcasted_iota(jnp.int32, (8, LANES), 0)
    slot_id = sub8 * LANES + lane8
    label = cells_v[...] + 1
    leave_at = jnp.where(label > 0, STEPS, -1)
    entry_of = (lane8 // 32) * DEP + lane8 % DEP
    wanted = (lane8 // DEP) % 4
    wanted = jnp.where(wanted < 2, 1 - wanted, 5 - wanted)
    meta = jnp.zeros((8, LANES), jnp.int32)
    for e in range(STEPS * DEP):
        slot = slot_s[e // DEP, 0, 0, e % DEP]
        moved = jnp.where(slot >= 0, cells_s[jnp.maximum(slot, 0)] + 1, 0)
        meta = jnp.where((entry_of == e) & (wanted == way_s[e // DEP, 0, 0, e % DEP]), moved, meta)
        leave_at = jnp.where(slot_id == slot, e // DEP, leave_at)
    MT[...] = meta.astype(f32)

    @pl.when(jnp.logical_not(has_lo))
    def _():
        MR[2] = jnp.zeros((8, LANES), f32)
        YR[:, 0] = jnp.zeros(YR.shape[:1] + YR.shape[2:], f32)
        VYR[0] = jnp.zeros(VYR.shape[1:], f32)

    @pl.when(jnp.logical_not(has_hi))
    def _():
        MR[3] = jnp.zeros((8, LANES), f32)
        YR[:, 1] = jnp.zeros(YR.shape[:1] + YR.shape[2:], f32)
        VYR[1] = jnp.zeros(VYR.shape[1:], f32)

    pl.semaphore_wait(barrier, 2 + has_lo.astype(jnp.int32) + has_hi.astype(jnp.int32))

    def remote(src, dst, send_sem, recv_sem, d):
        return pltpu.make_async_remote_copy(
            src_ref=src, dst_ref=dst, send_sem=send_sem, recv_sem=recv_sem,
            device_id=targets[d], device_id_type=MESH,
        )

    def meta_copy(d):
        return remote(MT, MR.at[d], meta_s.at[d], meta_r.at[d], d)

    def p_copy(t, par, d):
        if d < 2:
            src = PR.at[par, :, pl.ds((cx, 2)[d], 2), pl.ds(8, cy), :]
            dst = PR.at[par, :, pl.ds((0, cx + 2)[d], 2), pl.ds(8, cy), :]
        else:
            src, dst = YS.at[t, 3 - d], YR.at[t, d - 2]
        return remote(src, dst, xs.at[t, d], xr.at[t, d], d)

    def v_copy(d):
        if d < 2:
            src = VX.at[:, pl.ds((cx, 1)[d], 1), :, :]
            dst = VX.at[:, pl.ds((0, cx + 1)[d], 1), :, :]
        else:
            src, dst = VYS.at[3 - d], VYR.at[d - 2]
        return remote(src, dst, vs.at[d], vr.at[d], d)

    def dep_copy(t, d):
        return remote(
            SB.at[t], AR.at[:, pl.ds(t * 32 + d * DEP, DEP), :], ds_.at[t, d], dr.at[t, d], d
        )

    def start(make):
        for d in range(4):
            under(sends[d], lambda d=d: make(d).start())

    def wait_sent(make):
        for d in range(4):
            under(sends[d], lambda d=d: make(d).wait_send())

    def wait_taken(make):
        for d in range(4):
            under(takes[d], lambda d=d: make(d).wait_recv())

    start(meta_copy)

    def pack_rows(t, par):
        def body(i, carry):
            for q in range(nq):
                YS[t, 0, q, i] = PR[par, q, i + 2, 8:10, :]
                YS[t, 1, q, i] = PR[par, q, i + 2, 6 + cy : 8 + cy, :]
            return carry

        lax.fori_loop(0, cx, body, 0, unroll=4)

    def keep_parts(i, jb, q, value):
        high, low = split(value)
        row = pl.multiple_of((q // 2) * half + i * cy + jb * 16, 16)
        col = (q % 2) * LANES
        PHL[pl.ds(row, 16), col : col + LANES] = high
        PHL[pl.ds(pl.multiple_of(row + ncol, 16), 16), col : col + LANES] = low

    for k in range(nq):
        loads[k].wait()
    pack_rows(0, 0)
    start(lambda d: p_copy(0, 0, d))

    def first_split(n, carry):
        i, jb = n // jbs, n % jbs
        for q in range(nq):
            keep_parts(i, jb, q, PR[0, q, i + 2, pl.ds(pl.multiple_of(8 + jb * 16, 8), 16), :])
        return carry

    lax.fori_loop(0, cx * jbs, first_split, 0, unroll=4)

    for k in range(nq, nq + 3):
        loads[k].wait()

    def first_state(n, carry):
        rows = pl.ds(pl.multiple_of(n * 16, 16), 16)
        rest_now = A[rows, :]
        R[rows, :] = R[rows, :] * rest_now
        A[rows, :] = inv_ln2 * (jnp.log(1.0 + 0.2 / rest_now) + exponent * jnp.log(rest_now))
        return carry

    lax.fori_loop(0, SLOTS // 16, first_state, 0, unroll=4)
    VHL[pl.ds(SLOTS, ARRIVE), :] = jnp.zeros((ARRIVE, BLOCK), bf16)
    VHL[pl.ds(ROWS + SLOTS, ARRIVE), :] = jnp.zeros((ARRIVE, BLOCK), bf16)

    for k in range(nq + 3, nq + 3 + 3 * nq):
        loads[k].wait()

    def pack_flow(i, carry):
        for q in range(nq):
            VYS[0, q, i] = VY[q, i, 8:9, :]
            VYS[1, q, i] = VY[q, i, 7 + cy : 8 + cy, :]
        return carry

    lax.fori_loop(0, cx, pack_flow, 0, unroll=4)
    start(v_copy)

    wait_taken(meta_copy)
    came = (lane8 // DEP) % 4
    alab = jnp.where(
        came == 0, MR[0], jnp.where(came == 1, MR[1], jnp.where(came == 2, MR[2], MR[3]))
    )
    present = alab > 0.0
    lrow = lax.broadcasted_iota(jnp.int32, (LANES, LANES), 0)
    lcol = lax.broadcasted_iota(jnp.int32, (LANES, LANES), 1)
    upper = jnp.where(lrow <= lcol, 1.0, 0.0)
    upper_block = jnp.where(lrow // 32 == lcol // 32, upper, 0.0).astype(bf16)
    upper = upper.astype(bf16)
    ones = jnp.ones((LANES, LANES), bf16)
    present_f = jnp.where(present, 1.0, 0.0)
    arank = jnp.dot(present_f.astype(bf16), upper_block, preferred_element_type=f32) - 1.0
    arank = jnp.where(present, arank, -5.0)
    vacant = label == 0
    ranks = []
    for t in range(STEPS):
        vacant = vacant | (leave_at == t)
        flag = jnp.where(vacant, 1.0, 0.0).astype(bf16)
        rank = jnp.dot(flag, upper, preferred_element_type=f32) - 1.0
        total = jnp.dot(flag, ones, preferred_element_type=f32)
        for r in range(SLOT_BLOCKS - 1):
            rank = rank + jnp.where(sub8 > r, total[r : r + 1, :], 0.0)
        ranks.append(jnp.where(vacant, rank, -1.0))
        count = jnp.sum(jnp.where(lane8 // 32 == t, present_f, 0.0), axis=1, keepdims=True)
        vacant = vacant & (rank >= count)

    def code_of(lab):
        cell = lab - 1
        return jnp.where(lab > 0, (cell & 1) * half + (cell >> 1), -1).astype(f32)

    code = code_of(label)
    acode = code_of(alab.astype(jnp.int32))
    stack = [code, leave_at.astype(f32)] + ranks + [acode, alab]
    stack = stack + [jnp.zeros((8, LANES), f32)] * (16 - len(stack))
    LT[...] = jnp.concatenate(stack, axis=0).T
    LR[0:8, :] = code
    LR[8:16, :] = acode

    wide = lax.broadcasted_iota(jnp.int32, (16, ncol), 1).astype(f32)
    for r in range(SLOT_BLOCKS + 1):
        at = r if r < SLOT_BLOCKS else 48

        def one_hot_rows(m, carry, r=r, at=at):
            rows = pl.ds(pl.multiple_of(m * 16, 16), 16)
            column = LT[rows, at : at + 1]
            hot = jnp.where(column == wide, 1.0, 0.0).astype(bf16)
            OH[pl.ds(pl.multiple_of(r * LANES + m * 16, 16), 16), :] = hot
            return carry

        lax.fori_loop(0, LANES // 16, one_hot_rows, 0, unroll=2)

    tall = lax.broadcasted_iota(jnp.int32, (LANES, LANES), 0)

    def one_hot_columns(m, carry):
        ident = (tall + m * LANES).astype(f32)
        rows = pl.ds(pl.multiple_of(m * LANES, LANES), LANES)
        for r in range(SLOT_BLOCKS + 1):
            hot = jnp.where(ident == LR[r : r + 1, :], 1.0, 0.0).astype(bf16)
            OHT[rows, r * LANES : (r + 1) * LANES] = hot
        return carry

    lax.fori_loop(0, ncol // LANES, one_hot_columns, 0)

    group = lcol // 32
    for r in range(SLOT_BLOCKS):
        MSK[r * LANES : (r + 1) * LANES, :] = jnp.broadcast_to(
            LT[:, 8 + r : 9 + r], (LANES, LANES)
        )
        mine = jnp.broadcast_to(LT[:, 16 + r : 17 + r], (LANES, LANES))
        for t in range(1, STEPS):
            mine = jnp.where(group == t, LT[:, 16 + 8 * t + r : 17 + 8 * t + r], mine)
        hot = jnp.where(mine == arank[0:1, :], 1.0, 0.0).astype(bf16)
        PLACE[r * LANES : (r + 1) * LANES, 0:LANES] = hot
        PLACE[r * LANES : (r + 1) * LANES, LANES : 2 * LANES] = hot
    AMSK[...] = jnp.broadcast_to(LT[:, 56:57], (LANES, LANES))

    alab_high, alab_low = split(alab)
    final = jnp.where(leave_at == STEPS, label, 0).astype(f32)
    for r in range(SLOT_BLOCKS):
        hot = PLACE[r * LANES : (r + 1) * LANES, 0:LANES]
        nt = (((1,), (1,)), ((), ()))
        placed = lax.dot_general(alab_high, hot, nt, preferred_element_type=f32)
        placed = placed + lax.dot_general(alab_low, hot, nt, preferred_element_type=f32)
        final = final + jnp.where(sub8 == r, placed, 0.0)
    c_out[...] = final.astype(jnp.int32) - 1

    lane16 = lax.broadcasted_iota(jnp.int32, (16, LANES), 1)
    first_lane, last_lane = lane16 == 0, lane16 == LANES - 1

    def slope_z(tiles):
        zero = jnp.zeros((16, LANES), f32)
        ahead = [pltpu.roll(v, LANES - 1, 1) for v in tiles] + [zero]
        behind = [zero] + [pltpu.roll(v, 1, 1) for v in tiles]
        return [
            jnp.where(last_lane, ahead[q + 1], ahead[q])
            - jnp.where(first_lane, behind[q], behind[q + 1])
            for q in range(nq)
        ]

    low_gate = jnp.where(has_lo, 1.0, 0.0).astype(f32)
    high_gate = jnp.where(has_hi, 1.0, 0.0).astype(f32)
    chunk = 384
    part = min(256, ncol)

    def step(t, carry):
        par = lax.rem(t, 2)
        new = 1 - par

        def gather(m, carry):
            rows = pl.ds(pl.multiple_of(m * chunk, chunk), chunk)
            hot = OH[rows, :]
            hot = jnp.concatenate([hot, hot], axis=1)
            PG[rows, :] = jnp.dot(hot, PHL[...], preferred_element_type=f32)
            return carry

        lax.fori_loop(0, ROWS // chunk, gather, 0)

        @pl.when(t > 0)
        def _():
            wait_taken(lambda d: dep_copy(t - 1, d))

        limit = t.astype(f32)

        def bubbles(n, carry):
            rows = pl.ds(pl.multiple_of(n * 16, 16), 16)
            radius, speed, rate = wall_update(R[rows, :], S[rows, :], A[rows, :], PG[rows, :])
            R[rows, :] = radius
            S[rows, :] = speed
            keep = MSK[rows, :]
            keep = jnp.concatenate([keep, keep], axis=1) >= limit
            high, low = split(jnp.where(keep, rate, 0.0))
            VHL[rows, :] = high
            VHL[pl.ds(pl.multiple_of(ROWS + n * 16, 16), 16), :] = low
            return carry

        lax.fori_loop(0, SLOTS // 16, bubbles, 0, unroll=4)

        for k in range(DEP):
            row = pl.ds(jnp.maximum(slot_s[t, 0, 0, k], 0), 1)
            SB[t, 0, k : k + 1, :] = R[row, :]
            SB[t, 1, k : k + 1, :] = S[row, :]
            SB[t, 2, k : k + 1, :] = A[row, :]
        start(lambda d: dep_copy(t, d))

        def arrived(n, carry):
            rows = pl.ds(pl.multiple_of(n * 16, 16), 16)
            low_rows = pl.ds(pl.multiple_of(SLOTS + n * 16, 16), 16)
            radius, speed, rate = wall_update(
                AR[0, rows, :], AR[1, rows, :], AR[2, rows, :], PG[low_rows, :]
            )
            AR[0, rows, :] = radius
            AR[1, rows, :] = speed
            keep = AMSK[rows, :]
            keep = jnp.concatenate([keep, keep], axis=1) > 0.0
            high, low = split(jnp.where(keep, rate, 0.0))
            VHL[low_rows, :] = high
            VHL[pl.ds(pl.multiple_of(ROWS + SLOTS + n * 16, 16), 16), :] = low
            return carry

        lax.fori_loop(0, 2 * t, arrived, 0)

        def scatter(m, carry):
            rows = pl.ds(pl.multiple_of(m * part, part), part)
            hot = OHT[rows, :]
            hot = jnp.concatenate([hot, hot], axis=1)
            SRC[rows, :] = jnp.dot(hot, VHL[...], preferred_element_type=f32)
            return carry

        lax.fori_loop(0, ncol // part, scatter, 0)

        wait_taken(lambda d: p_copy(t, par, d))
        wait_sent(lambda d: p_copy(t, par, d))

        @pl.when(t == 0)
        def _():
            wait_taken(v_copy)
            wait_sent(v_copy)

            def unpack(i, carry):
                for q in range(nq):
                    VY[q, i, 7:8, :] = VYR[0, q, i]
                    VY[q, i, 8 + cy : 9 + cy, :] = VYR[1, q, i]
                return carry

            lax.fori_loop(0, cx, unpack, 0)

        def flow_x(n, carry):
            i, jb = n // jbs, n % jbs
            rows = pl.ds(pl.multiple_of(jb * 16, 16), 16)
            at = pl.ds(pl.multiple_of(8 + jb * 16, 8), 16)
            for q in range(nq):
                VX[q, i, rows, :] = VX[q, i, rows, :] - half_gain * (
                    PR[par, q, i + 2, at, :] - PR[par, q, i, at, :]
                )
            return carry

        lax.fori_loop(0, (cx + 2) * jbs, flow_x, 0, unroll=4)

        def side_rows(i, carry):
            for q in range(nq):
                PR[par, q, i + 2, 6:8, :] = YR[t, 0, q, i]
                PR[par, q, i + 2, 8 + cy : 10 + cy, :] = YR[t, 1, q, i]
                VY[q, i, 7:8, :] = low_gate * (
                    VY[q, i, 7:8, :]
                    - half_gain * (PR[par, q, i + 2, 8:9, :] - YR[t, 0, q, i, 0:1, :])
                )
                VY[q, i, 8 + cy : 9 + cy, :] = high_gate * (
                    VY[q, i, 8 + cy : 9 + cy, :]
                    - half_gain * (YR[t, 1, q, i, 1:2, :] - PR[par, q, i + 2, 7 + cy : 8 + cy, :])
                )
            return carry

        lax.fori_loop(0, cx, side_rows, 0, unroll=4)

        def flow_yz(n, carry):
            i, jb = n // jbs, n % jbs
            rows = pl.ds(pl.multiple_of(jb * 16, 16), 16)
            at = pl.ds(pl.multiple_of(8 + jb * 16, 8), 16)
            after, before = pl.ds(9 + jb * 16, 16), pl.ds(7 + jb * 16, 16)
            slopes = slope_z([PR[par, q, i + 2, at, :] for q in range(nq)])
            for q in range(nq):
                VZ[q, i, rows, :] = VZ[q, i, rows, :] - half_gain * slopes[q]
                VY[q, i, at, :] = VY[q, i, at, :] - half_gain * (
                    PR[par, q, i + 2, after, :] - PR[par, q, i + 2, before, :]
                )
            return carry

        lax.fori_loop(0, cx * jbs, flow_yz, 0, unroll=4)

        def pressure(final, n, carry):
            i, jb = n // jbs, n % jbs
            rows = pl.ds(pl.multiple_of(jb * 16, 16), 16)
            at = pl.ds(pl.multiple_of(8 + jb * 16, 8), 16)
            after, before = pl.ds(9 + jb * 16, 16), pl.ds(7 + jb * 16, 16)
            slopes = slope_z([VZ[q, i, rows, :] for q in range(nq)])
            for q in range(nq):
                rise = (
                    (VX[q, i + 2, rows, :] - VX[q, i, rows, :])
                    + (VY[q, i, after, :] - VY[q, i, before, :])
                    + slopes[q]
                )
                row = pl.multiple_of((q // 2) * half + i * cy + jb * 16, 16)
                col = (q % 2) * LANES
                value = (
                    PR[par, q, i + 2, at, :]
                    - half_gain * rise
                    + SRC[pl.ds(row, 16), col : col + LANES]
                )
                if final:
                    p_out[i, rows, q * LANES : (q + 1) * LANES] = value
                else:
                    PR[new, q, i + 2, at, :] = value
                    keep_parts(i, jb, q, value)
            return carry

        @pl.when(t == STEPS - 1)
        def _():
            lax.fori_loop(0, cx * jbs, functools.partial(pressure, True), 0, unroll=4)

        @pl.when(t < STEPS - 1)
        def _():
            lax.fori_loop(0, cx * jbs, functools.partial(pressure, False), 0, unroll=4)

        @pl.when(t < STEPS - 1)
        def _():
            pack_rows(t + 1, new)
            start(lambda d: p_copy(t + 1, new, d))

        return carry

    lax.fori_loop(0, STEPS, step, 0)

    wait_taken(lambda d: dep_copy(STEPS - 1, d))
    keep = AMSK[...] > 0.0
    for k in range(2):
        for w in range(2):
            col = slice(w * LANES, (w + 1) * LANES)
            high, low = split(jnp.where(keep, AR[k, :, col], 0.0))
            to = slice(k * BLOCK + w * LANES, k * BLOCK + (w + 1) * LANES)
            CAT[0:ARRIVE, to] = high
            CAT[ARRIVE : 2 * ARRIVE, to] = low

    def finish(m, carry):
        rows = pl.ds(pl.multiple_of(m * LANES, LANES), LANES)
        placed = jnp.dot(PLACE[rows, :], CAT[...], preferred_element_type=f32)
        keep = MSK[rows, :]
        keep = jnp.concatenate([keep, keep], axis=1) >= float(STEPS)
        R[rows, :] = jnp.where(keep, R[rows, :], 0.0) + placed[:, :BLOCK]
        S[rows, :] = jnp.where(keep, S[rows, :], 0.0) + placed[:, BLOCK:]
        return carry

    lax.fori_loop(0, SLOT_BLOCKS, finish, 0)
    wait_sent(meta_copy)
    for t in range(STEPS):
        wait_sent(lambda d, t=t: dep_copy(t, d))


def write_out(p, vx, vy, vz, r, s, c, p_out, v_out, r_out, s_out, c_out, sems):
    _, cx, cy, nz = v_out.shape
    pairs = [(p, p_out), (r, r_out), (s, s_out), (c, c_out)]
    for q in range(nz // LANES):
        lanes = pl.ds(q * LANES, LANES)
        pairs.append((vx.at[q, pl.ds(1, cx), :, :], v_out.at[0, :, :, lanes]))
        pairs.append((vy.at[q, :, pl.ds(8, cy), :], v_out.at[1, :, :, lanes]))
        pairs.append((vz.at[q], v_out.at[2, :, :, lanes]))
    copies = [pltpu.make_async_copy(a, b, sems.at[k]) for k, (a, b) in enumerate(pairs)]
    for copy in copies:
        copy.start()
    for copy in copies:
        copy.wait()


def on_device(
    pressure, velocity, stretch, rest_radius, wall_speed, block_cells, depart_slot, depart_way
):
    cx, cy, nz = pressure.shape
    nq = nz // LANES
    ncol = 2 * cx * cy
    vmem = pl.BlockSpec(memory_space=pltpu.VMEM)
    hbm = pl.BlockSpec(memory_space=pl.ANY)
    dma = pltpu.SemaphoreType.DMA
    vmem_out = pltpu.VMEM
    parts = pl.pallas_call(
        kernel,
        out_shape=(
            vmem_out(pressure.shape, f32),
            vmem_out((nq, cx + 2, cy, LANES), f32),
            vmem_out((nq, cx, cy + 16, LANES), f32),
            vmem_out((nq, cx, cy, LANES), f32),
            vmem_out((SLOTS, BLOCK), f32),
            vmem_out((SLOTS, BLOCK), f32),
            vmem_out((SLOT_BLOCKS, LANES), jnp.int32),
        ),
        in_specs=[pl.BlockSpec(memory_space=pltpu.HBM)] * 9,
        out_specs=(vmem,) * 7,
        scratch_shapes=[
            pltpu.VMEM((2, nq, cx + 4, cy + 16, LANES), f32),
            pltpu.VMEM((SLOTS, BLOCK), f32),
            pltpu.VMEM((3, ARRIVE, BLOCK), f32),
            pltpu.VMEM((STEPS, 3, DEP, BLOCK), f32),
            pltpu.VMEM((ROWS, ncol), bf16),
            pltpu.VMEM((ncol, ROWS), bf16),
            pltpu.VMEM((2 * ncol, BLOCK), bf16),
            pltpu.VMEM((ROWS, BLOCK), f32),
            pltpu.VMEM((2 * ROWS, BLOCK), bf16),
            pltpu.VMEM((ncol, BLOCK), f32),
            pltpu.VMEM((STEPS, 2, nq, cx, 2, LANES), f32),
            pltpu.VMEM((STEPS, 2, nq, cx, 2, LANES), f32),
            pltpu.VMEM((2, nq, cx, 1, LANES), f32),
            pltpu.VMEM((2, nq, cx, 1, LANES), f32),
            pltpu.VMEM((8, LANES), f32),
            pltpu.VMEM((4, 8, LANES), f32),
            pltpu.VMEM((SLOTS, LANES), f32),
            pltpu.VMEM((ARRIVE, LANES), f32),
            pltpu.VMEM((LANES, LANES), f32),
            pltpu.VMEM((16, LANES), f32),
            pltpu.VMEM((SLOTS, 2 * ARRIVE), bf16),
            pltpu.VMEM((2 * ARRIVE, 2 * BLOCK), bf16),
            pltpu.SMEM((SLOTS,), jnp.int32),
            pltpu.SMEM((STEPS, 1, 1, DEP), jnp.int32),
            pltpu.SMEM((STEPS, 1, 1, DEP), jnp.int32),
            pltpu.VMEM((SLOT_BLOCKS, LANES), jnp.int32),
            dma((4 * nq + 7,)),
            dma((4,)),
            dma((4,)),
            dma((STEPS, 4)),
            dma((STEPS, 4)),
            dma((4,)),
            dma((4,)),
            dma((STEPS, 4)),
            dma((STEPS, 4)),
        ],
        compiler_params=pltpu.CompilerParams(
            collective_id=0, has_side_effects=True, vmem_limit_bytes=36 * 2**20
        ),
        cost_estimate=pl.CostEstimate(
            flops=10 * 2**30, bytes_accessed=13 * 2**20, transcendentals=2**22
        ),
    )(
        *(
            pltpu.with_memory_space_constraint(value, pltpu.HBM)
            for value in (
                block_cells,
                depart_slot,
                depart_way,
                block_cells.reshape(SLOT_BLOCKS, LANES),
                pressure,
                velocity,
                stretch,
                rest_radius,
                wall_speed,
            )
        )
    )
    parts = [pltpu.with_memory_space_constraint(part, pltpu.VMEM) for part in parts]
    p, v, r, s, c = pl.pallas_call(
        write_out,
        out_shape=(
            jax.ShapeDtypeStruct(pressure.shape, f32),
            jax.ShapeDtypeStruct(velocity.shape, f32),
            jax.ShapeDtypeStruct(stretch.shape, f32),
            jax.ShapeDtypeStruct(stretch.shape, f32),
            jax.ShapeDtypeStruct((SLOT_BLOCKS, LANES), jnp.int32),
        ),
        in_specs=[vmem] * 7,
        out_specs=(hbm,) * 5,
        scratch_shapes=[dma((3 * nq + 4,))],
        compiler_params=pltpu.CompilerParams(vmem_limit_bytes=4 * 2**20),
        cost_estimate=pl.CostEstimate(flops=0, bytes_accessed=13 * 2**20, transcendentals=0),
    )(*parts)
    return p, v, r, s, c.reshape(-1)


def solution(mesh):
    placed = (
        P("gx", "gy", None),
        P(None, "gx", "gy", None),
        P(("gx", "gy"), None),
        P(("gx", "gy"), None),
        P(("gx", "gy"), None),
        P(("gx", "gy")),
        P(None, "gx", "gy", None),
        P(None, "gx", "gy", None),
    )
    return jax.shard_map(
        on_device,
        mesh=mesh,
        in_specs=placed,
        out_specs=(
            P("gx", "gy", None),
            P(None, "gx", "gy", None),
            P(("gx", "gy"), None),
            P(("gx", "gy"), None),
            P(("gx", "gy")),
        ),
        check_vma=False,
    )
```

```python
import functools
import math

import jax
import jax.numpy as jnp
from jax import lax
from jax.experimental import pallas as pl
from jax.experimental.pallas import tpu as pltpu
from jax.sharding import PartitionSpec as P

MESH = pl.DeviceIdType.MESH
f32 = jnp.float32
bf16 = jnp.bfloat16

STEPS = 4
DEP = 8
SLOTS = 1024
BLOCK = 256
LANES = 128
ARRIVE = STEPS * 4 * DEP
ROWS = SLOTS + ARRIVE
SLOT_BLOCKS = SLOTS // LANES
WAY_OF = (1, 0, 3, 2)

time_step = 0.04
half_gain = 0.2
source_scale = 0.004 * 12.566370614359172
exponent = 4.2
inv_ln2 = 1.0 / math.log(2.0)


def split(value):
    high = value.astype(bf16)
    return high, (value - high.astype(f32)).astype(bf16)


def wall_update(radius, speed, level, pressure):
    one_less = 1.0 - 0.05 * speed
    divisor = one_less * radius
    inverse = pl.reciprocal(divisor, approx=True)
    inverse = inverse * (2.0 - divisor * inverse)
    inv_radius = inverse * one_less
    wall = jnp.exp2(level - (exponent * inv_ln2) * jnp.log(radius))
    excess = wall - (0.2 + 0.08 * speed) * inv_radius - (1.0 + pressure)
    driving = (2.0 - one_less) * excess - (1.0 + 0.5 * one_less) * (speed * speed)
    speed = speed + time_step * (driving * inverse)
    radius = radius + time_step * speed
    return radius, speed, source_scale * (radius * radius) * speed


def kernel(
    cells_h, slot_h, way_h, cells_b, press, vel, stretch, rest, speed0,
    PR, VX, VY, VZ, R, S, c_out,
    A, AR, SB, OH, OHT, PHL, PG, VHL, SRC, XR, YS, YR, VYS, VYR,
    MT, MR, MSK, AMSK, LT, LR, PLACE, CAT, cells_s, slot_s, way_s, cells_v,
    in_sem, meta_s, meta_r, xs, xr, vs, vr, ds_, dr,
):
    _, cx, cy, nz = vel.shape
    nq = nz // LANES
    half = cx * cy
    ncol = 2 * half
    jbs = cy // 16
    part = min(256, ncol)
    planes = part // (2 * cy)
    groups = cx // planes
    shift = (planes * cy).bit_length() - 1
    zero_row = lax.axis_index("gx") // 4096
    gx, gy = lax.axis_index("gx"), lax.axis_index("gy")
    ngx, ngy = lax.axis_size("gx"), lax.axis_size("gy")
    has_lo, has_hi = gy > 0, gy < ngy - 1
    targets = (
        (lax.rem(gx + 1, ngx), gy),
        (lax.rem(gx + ngx - 1, ngx), gy),
        (gx, lax.rem(gy + 1, ngy)),
        (gx, lax.rem(gy + ngy - 1, ngy)),
    )
    sends = (None, None, has_hi, has_lo)
    takes = (None, None, has_lo, has_hi)

    def under(flag, action):
        if flag is None:
            action()
        else:
            pl.when(flag)(action)

    barrier = pltpu.get_barrier_semaphore()
    for d in range(4):
        under(
            sends[d],
            lambda d=d: pl.semaphore_signal(
                barrier, inc=1, device_id=targets[d], device_id_type=MESH
            ),
        )

    inputs = [(cells_h, cells_s), (slot_h, slot_s), (way_h, way_s), (cells_b, cells_v)]
    for q in range(nq):
        inputs.append((press.at[:, :, pl.ds(q * LANES, LANES)], PR.at[q, :, pl.ds(8, cy), :]))
    inputs.append((rest, A))
    inputs.append((stretch, R))
    inputs.append((speed0, S))
    for comp in range(3):
        for q in range(nq):
            dst = (
                VX.at[q, pl.ds(1, cx), :, :],
                VY.at[q, :, pl.ds(8, cy), :],
                VZ.at[q],
            )[comp]
            inputs.append((vel.at[comp, :, :, pl.ds(q * LANES, LANES)], dst))
    loads = [pltpu.make_async_copy(a, b, in_sem.at[k]) for k, (a, b) in enumerate(inputs)]
    for load in loads:
        load.start()

    for load in loads[:4]:
        load.wait()
    loads = loads[4:]

    lane8 = lax.broadcasted_iota(jnp.int32, (8, LANES), 1)
    sub8 = lax.broadcasted_iota(jnp.int32, (8, LANES), 0)
    slot_id = sub8 * LANES + lane8
    label = cells_v[...] + 1
    leave_at = jnp.where(label > 0, STEPS, -1)
    entry_of = (lane8 // 32) * DEP + lane8 % DEP
    wanted = (lane8 // DEP) % 4
    wanted = jnp.where(wanted < 2, 1 - wanted, 5 - wanted)
    meta = jnp.zeros((8, LANES), jnp.int32)
    for e in range(STEPS * DEP):
        slot = slot_s[e // DEP, 0, 0, e % DEP]
        moved = jnp.where(slot >= 0, cells_s[jnp.maximum(slot, 0)] + 1, 0)
        meta = jnp.where((entry_of == e) & (wanted == way_s[e // DEP, 0, 0, e % DEP]), moved, meta)
        leave_at = jnp.where(slot_id == slot, e // DEP, leave_at)
    MT[...] = meta.astype(f32)

    @pl.when(jnp.logical_not(has_lo))
    def _():
        MR[2] = jnp.zeros((8, LANES), f32)
        YR[:, 0] = jnp.zeros(YR.shape[:1] + YR.shape[2:], f32)
        VYR[0] = jnp.zeros(VYR.shape[1:], f32)

    @pl.when(jnp.logical_not(has_hi))
    def _():
        MR[3] = jnp.zeros((8, LANES), f32)
        YR[:, 1] = jnp.zeros(YR.shape[:1] + YR.shape[2:], f32)
        VYR[1] = jnp.zeros(VYR.shape[1:], f32)

    pl.semaphore_wait(barrier, 2 + has_lo.astype(jnp.int32) + has_hi.astype(jnp.int32))

    def remote(src, dst, send_sem, recv_sem, d):
        return pltpu.make_async_remote_copy(
            src_ref=src, dst_ref=dst, send_sem=send_sem, recv_sem=recv_sem,
            device_id=targets[d], device_id_type=MESH,
        )

    def meta_copy(d):
        return remote(MT, MR.at[d], meta_s.at[d], meta_r.at[d], d)

    def p_copy(t, d):
        if d < 2:
            src = PR.at[:, pl.ds((cx - 2, 0)[d], 2), pl.ds(8, cy), :]
            return remote(src, XR.at[t, d], xs.at[t, d], xr.at[t, d], d)
        return remote(YS.at[t, 3 - d], YR.at[t, d - 2], xs.at[t, d], xr.at[t, d], d)

    def v_copy(d):
        if d < 2:
            src = VX.at[:, pl.ds((cx, 1)[d], 1), :, :]
            dst = VX.at[:, pl.ds((0, cx + 1)[d], 1), :, :]
        else:
            src, dst = VYS.at[3 - d], VYR.at[d - 2]
        return remote(src, dst, vs.at[d], vr.at[d], d)

    def dep_copy(t, d):
        return remote(
            SB.at[t], AR.at[:, pl.ds(t * 32 + d * DEP, DEP), :], ds_.at[t, d], dr.at[t, d], d
        )

    def start(make):
        for d in range(4):
            under(sends[d], lambda d=d: make(d).start())

    def wait_sent(make):
        for d in range(4):
            under(sends[d], lambda d=d: make(d).wait_send())

    def wait_taken(make):
        for d in range(4):
            under(takes[d], lambda d=d: make(d).wait_recv())

    start(meta_copy)

    def pack_rows(t):
        for i in range(cx):
            for q in range(nq):
                YS[t, 0, q, i] = PR[q, i, 8:10, :]
                YS[t, 1, q, i] = PR[q, i, 6 + cy : 8 + cy, :]

    def column_row(i, h, jb):
        return (i // planes) * part + (h * planes + i % planes) * cy + jb * 16

    def keep_parts(i, jb, q, value):
        high, low = split(value)
        row = column_row(i, q // 2, jb)
        col = (q % 2) * LANES
        PHL[row : row + 16, col : col + LANES] = high
        PHL[row + ncol : row + ncol + 16, col : col + LANES] = low

    def rows_of(jb):
        return slice(jb * 16, jb * 16 + 16), slice(8 + jb * 16, 24 + jb * 16)

    for k in range(nq):
        loads[k].wait()
    pack_rows(0)
    start(lambda d: p_copy(0, d))
    for i in range(cx):
        for jb in range(jbs):
            for q in range(nq):
                keep_parts(i, jb, q, PR[q, i, rows_of(jb)[1], :])

    for k in range(nq + 3, nq + 3 + 3 * nq):
        loads[k].wait()

    def pack_flow(i, carry):
        for q in range(nq):
            VYS[0, q, i] = VY[q, i, 8:9, :]
            VYS[1, q, i] = VY[q, i, 7 + cy : 8 + cy, :]
        return carry

    lax.fori_loop(0, cx, pack_flow, 0, unroll=4)
    start(v_copy)

    for k in range(nq, nq + 3):
        loads[k].wait()

    def first_state(n, carry):
        rows = pl.ds(pl.multiple_of(n * 16, 16), 16)
        rest_now = A[rows, :]
        R[rows, :] = R[rows, :] * rest_now
        A[rows, :] = inv_ln2 * (jnp.log(1.0 + 0.2 / rest_now) + exponent * jnp.log(rest_now))
        return carry

    lax.fori_loop(0, SLOTS // 16, first_state, 0, unroll=4)
    VHL[pl.ds(SLOTS, ARRIVE), :] = jnp.zeros((ARRIVE, BLOCK), bf16)
    VHL[pl.ds(ROWS + SLOTS, ARRIVE), :] = jnp.zeros((ARRIVE, BLOCK), bf16)

    wait_taken(meta_copy)
    came = (lane8 // DEP) % 4
    alab = jnp.where(
        came == 0, MR[0], jnp.where(came == 1, MR[1], jnp.where(came == 2, MR[2], MR[3]))
    )
    present = alab > 0.0
    lrow = lax.broadcasted_iota(jnp.int32, (LANES, LANES), 0)
    lcol = lax.broadcasted_iota(jnp.int32, (LANES, LANES), 1)
    upper = jnp.where(lrow <= lcol, 1.0, 0.0)
    upper_block = jnp.where(lrow // 32 == lcol // 32, upper, 0.0).astype(bf16)
    upper = upper.astype(bf16)
    ones = jnp.ones((LANES, LANES), bf16)
    present_f = jnp.where(present, 1.0, 0.0)
    arank = jnp.dot(present_f.astype(bf16), upper_block, preferred_element_type=f32) - 1.0
    arank = jnp.where(present, arank, -5.0)
    vacant = label == 0
    ranks = []
    for t in range(STEPS):
        vacant = vacant | (leave_at == t)
        flag = jnp.where(vacant, 1.0, 0.0).astype(bf16)
        rank = jnp.dot(flag, upper, preferred_element_type=f32) - 1.0
        total = jnp.dot(flag, ones, preferred_element_type=f32)
        for r in range(SLOT_BLOCKS - 1):
            rank = rank + jnp.where(sub8 > r, total[r : r + 1, :], 0.0)
        ranks.append(jnp.where(vacant, rank, -1.0))
        count = jnp.sum(jnp.where(lane8 // 32 == t, present_f, 0.0), axis=1, keepdims=True)
        vacant = vacant & (rank >= count)

    def code_of(lab):
        cell = lab - 1
        place = cell >> 1
        row = (place >> shift) * part + (cell & 1) * (planes * cy)
        return jnp.where(lab > 0, row + (place & (planes * cy - 1)), -1).astype(f32)

    code = code_of(label)
    acode = code_of(alab.astype(jnp.int32))
    stack = [code, leave_at.astype(f32)] + ranks + [acode, alab]
    stack = stack + [jnp.zeros((8, LANES), f32)] * (16 - len(stack))
    LT[...] = jnp.concatenate(stack, axis=0).T
    LR[0:8, :] = code
    LR[8:16, :] = acode

    wide = lax.broadcasted_iota(jnp.int32, (16, ncol), 1).astype(f32)
    for r in range(SLOT_BLOCKS + 1):
        at = r if r < SLOT_BLOCKS else 48

        def one_hot_rows(m, carry, r=r, at=at):
            rows = pl.ds(pl.multiple_of(m * 16, 16), 16)
            column = LT[rows, at : at + 1]
            hot = jnp.where(column == wide, 1.0, 0.0).astype(bf16)
            OH[pl.ds(pl.multiple_of(r * LANES + m * 16, 16), 16), :] = hot
            return carry

        lax.fori_loop(0, LANES // 16, one_hot_rows, 0, unroll=2)

    tall = lax.broadcasted_iota(jnp.int32, (LANES, LANES), 0)

    def one_hot_columns(m, carry):
        ident = (tall + m * LANES).astype(f32)
        rows = pl.ds(pl.multiple_of(m * LANES, LANES), LANES)
        for r in range(SLOT_BLOCKS + 1):
            hot = jnp.where(ident == LR[r : r + 1, :], 1.0, 0.0).astype(bf16)
            OHT[rows, r * LANES : (r + 1) * LANES] = hot
        return carry

    lax.fori_loop(0, ncol // LANES, one_hot_columns, 0)

    group = lcol // 32
    for r in range(SLOT_BLOCKS):
        MSK[r * LANES : (r + 1) * LANES, :] = jnp.broadcast_to(
            LT[:, 8 + r : 9 + r], (LANES, LANES)
        )
        mine = jnp.broadcast_to(LT[:, 16 + r : 17 + r], (LANES, LANES))
        for t in range(1, STEPS):
            mine = jnp.where(group == t, LT[:, 16 + 8 * t + r : 17 + 8 * t + r], mine)
        hot = jnp.where(mine == arank[0:1, :], 1.0, 0.0).astype(bf16)
        PLACE[r * LANES : (r + 1) * LANES, 0:LANES] = hot
        PLACE[r * LANES : (r + 1) * LANES, LANES : 2 * LANES] = hot
    AMSK[...] = jnp.broadcast_to(LT[:, 56:57], (LANES, LANES))

    alab_high, alab_low = split(alab)
    final = jnp.where(leave_at == STEPS, label, 0).astype(f32)
    for r in range(SLOT_BLOCKS):
        hot = PLACE[r * LANES : (r + 1) * LANES, 0:LANES]
        nt = (((1,), (1,)), ((), ()))
        placed = lax.dot_general(alab_high, hot, nt, preferred_element_type=f32)
        placed = placed + lax.dot_general(alab_low, hot, nt, preferred_element_type=f32)
        final = final + jnp.where(sub8 == r, placed, 0.0)
    c_out[...] = final.astype(jnp.int32) - 1

    lane16 = lax.broadcasted_iota(jnp.int32, (16, LANES), 1)
    first_lane, last_lane = lane16 == 0, lane16 == LANES - 1

    def slope_z(tiles):
        zero = jnp.zeros((16, LANES), f32)
        ahead = [pltpu.roll(v, LANES - 1, 1) for v in tiles] + [zero]
        behind = [zero] + [pltpu.roll(v, 1, 1) for v in tiles]
        return [
            jnp.where(last_lane, ahead[q + 1], ahead[q])
            - jnp.where(first_lane, behind[q], behind[q + 1])
            for q in range(nq)
        ]

    low_gate = jnp.where(has_lo, 1.0, 0.0).astype(f32)
    high_gate = jnp.where(has_hi, 1.0, 0.0).astype(f32)
    chunk = 256

    def gather(low_row, count):
        hot = OH[low_row : low_row + count, :]
        hot = jnp.concatenate([hot, hot], axis=1)
        PG[low_row : low_row + count, :] = jnp.dot(hot, PHL[...], preferred_element_type=f32)

    def scatter(m):
        hot = OHT[m * part : (m + 1) * part, :]
        hot = jnp.concatenate([hot, hot], axis=1)
        SRC[m * part : (m + 1) * part, :] = jnp.dot(hot, VHL[...], preferred_element_type=f32)

    def step(t, carry):
        limit = t.astype(f32)

        def bubbles(first):
            rows = slice(first, first + 16)
            radius, speed, rate = wall_update(R[rows, :], S[rows, :], A[rows, :], PG[rows, :])
            R[rows, :] = radius
            S[rows, :] = speed
            keep = MSK[rows, :]
            keep = jnp.concatenate([keep, keep], axis=1) >= limit
            high, low = split(jnp.where(keep, rate, 0.0))
            VHL[rows, :] = high
            VHL[ROWS + first : ROWS + first + 16, :] = low

        gather(0, chunk)
        for m in range(SLOTS // chunk):
            if m + 1 < SLOTS // chunk:
                gather((m + 1) * chunk, chunk)
            else:
                gather(SLOTS, ARRIVE)
            for b in range(chunk // 16):
                bubbles(m * chunk + b * 16)

        for k in range(DEP):
            row = pl.ds(jnp.maximum(slot_s[t, 0, 0, k], 0), 1)
            SB[t, 0, k : k + 1, :] = R[row, :]
            SB[t, 1, k : k + 1, :] = S[row, :]
            SB[t, 2, k : k + 1, :] = A[row, :]
        start(lambda d: dep_copy(t, d))

        @pl.when(t > 0)
        def _():
            wait_taken(lambda d: dep_copy(t - 1, d))

        def arrived(n, carry):
            for b in range(2):
                first = n * 32 + b * 16
                rows = pl.ds(pl.multiple_of(first, 16), 16)
                low_rows = pl.ds(pl.multiple_of(SLOTS + first, 16), 16)
                radius, speed, rate = wall_update(
                    AR[0, rows, :], AR[1, rows, :], AR[2, rows, :], PG[low_rows, :]
                )
                AR[0, rows, :] = radius
                AR[1, rows, :] = speed
                keep = AMSK[rows, :]
                keep = jnp.concatenate([keep, keep], axis=1) > 0.0
                high, low = split(jnp.where(keep, rate, 0.0))
                VHL[low_rows, :] = high
                VHL[pl.ds(pl.multiple_of(ROWS + SLOTS + first, 16), 16), :] = low
            return carry

        lax.fori_loop(0, t, arrived, 0)

        def flow_x(i, after, before):
            for q in range(nq):
                for jb in range(jbs):
                    rows, at = rows_of(jb)
                    ahead = PR[q, i + 1, at, :] if after is None else XR[t, 1, q, after, rows, :]
                    back = PR[q, i - 1, at, :] if before is None else XR[t, 0, q, before, rows, :]
                    VX[q, i + 1, rows, :] = VX[q, i + 1, rows, :] - half_gain * (ahead - back)

        def flow_z(i, jb):
            rows, at = rows_of(jb)
            slopes = slope_z([PR[q, i, at, :] for q in range(nq)])
            for q in range(nq):
                VZ[q, i, rows, :] = VZ[q, i, rows, :] - half_gain * slopes[q]

        def flow_y(i, jb):
            _, at = rows_of(jb)
            for q in range(nq):
                VY[q, i, at, :] = VY[q, i, at, :] - half_gain * (
                    PR[q, i, pl.ds(9 + jb * 16 + zero_row, 16), :]
                    - PR[q, i, pl.ds(7 + jb * 16 + zero_row, 16), :]
                )

        def side_rows(i):
            for q in range(nq):
                below, above = YR[t, 0, q, i], YR[t, 1, q, i]
                PR[q, i, 6:8, :] = below
                PR[q, i, 8 + cy : 10 + cy, :] = above
                VY[q, i, 7:8, :] = low_gate * (
                    VY[q, i, 7:8, :] - half_gain * (PR[q, i, 8:9, :] - below[0:1, :])
                )
                VY[q, i, 8 + cy : 9 + cy, :] = high_gate * (
                    VY[q, i, 8 + cy : 9 + cy, :]
                    - half_gain * (above[1:2, :] - PR[q, i, 7 + cy : 8 + cy, :])
                )

        def pressure(i, jb):
            rows, at = rows_of(jb)
            slopes = slope_z([VZ[q, i, rows, :] for q in range(nq)])
            for q in range(nq):
                rise = (
                    (VX[q, i + 2, rows, :] - VX[q, i, rows, :])
                    + (
                        VY[q, i, pl.ds(9 + jb * 16 + zero_row, 16), :]
                        - VY[q, i, pl.ds(7 + jb * 16 + zero_row, 16), :]
                    )
                    + slopes[q]
                )
                row = column_row(i, q // 2, jb)
                col = (q % 2) * LANES
                value = PR[q, i, at, :] - half_gain * rise + SRC[row : row + 16, col : col + LANES]
                PR[q, i, at, :] = value
                keep_parts(i, jb, q, value)

        early = max(1, groups // 2)
        for m in range(early):
            scatter(m)
            for i in range(m * cx // early, (m + 1) * cx // early):
                if 0 < i < cx - 1:
                    flow_x(i, None, None)
                for jb in range(jbs):
                    flow_z(i, jb)

        wait_taken(lambda d: p_copy(t, d))
        wait_sent(lambda d: p_copy(t, d))

        @pl.when(t == 0)
        def _():
            wait_taken(v_copy)
            wait_sent(v_copy)
            for i in range(cx):
                for q in range(nq):
                    VY[q, i, 7:8, :] = VYR[0, q, i]
                    VY[q, i, 8 + cy : 9 + cy, :] = VYR[1, q, i]

        if early < groups:
            scatter(early)
        flow_x(-1, None, 0)
        flow_x(0, None, 1)
        flow_x(cx - 1, 0, None)
        flow_x(cx, 1, None)
        for i in range(cx):
            side_rows(i)
            for jb in range(jbs):
                flow_y(i, jb)
        for m in range(groups):
            if early < m + 1 < groups:
                scatter(m + 1)
            for i in range(m * planes, (m + 1) * planes):
                for jb in range(jbs):
                    pressure(i, jb)

        @pl.when(t < STEPS - 1)
        def _():
            pack_rows(t + 1)
            start(lambda d: p_copy(t + 1, d))

        return carry

    lax.fori_loop(0, STEPS, step, 0)

    wait_taken(lambda d: dep_copy(STEPS - 1, d))
    keep = AMSK[...] > 0.0
    for k in range(2):
        for w in range(2):
            col = slice(w * LANES, (w + 1) * LANES)
            high, low = split(jnp.where(keep, AR[k, :, col], 0.0))
            to = slice(k * BLOCK + w * LANES, k * BLOCK + (w + 1) * LANES)
            CAT[0:ARRIVE, to] = high
            CAT[ARRIVE : 2 * ARRIVE, to] = low

    def finish(m, carry):
        rows = pl.ds(pl.multiple_of(m * LANES, LANES), LANES)
        placed = jnp.dot(PLACE[rows, :], CAT[...], preferred_element_type=f32)
        keep = MSK[rows, :]
        keep = jnp.concatenate([keep, keep], axis=1) >= float(STEPS)
        R[rows, :] = jnp.where(keep, R[rows, :], 0.0) + placed[:, :BLOCK]
        S[rows, :] = jnp.where(keep, S[rows, :], 0.0) + placed[:, BLOCK:]
        return carry

    lax.fori_loop(0, SLOT_BLOCKS, finish, 0)
    wait_sent(meta_copy)
    for t in range(STEPS):
        wait_sent(lambda d, t=t: dep_copy(t, d))


def write_out(p, vx, vy, vz, r, s, c, p_out, v_out, r_out, s_out, c_out, sems):
    _, cx, cy, nz = v_out.shape
    pairs = [(r, r_out), (s, s_out), (c, c_out)]
    for q in range(nz // LANES):
        lanes = pl.ds(q * LANES, LANES)
        pairs.append((vx.at[q, pl.ds(1, cx), :, :], v_out.at[0, :, :, lanes]))
        pairs.append((vy.at[q, :, pl.ds(8, cy), :], v_out.at[1, :, :, lanes]))
        pairs.append((vz.at[q], v_out.at[2, :, :, lanes]))
        pairs.append((p.at[q, :, pl.ds(8, cy), :], p_out.at[:, :, lanes]))
    copies = [pltpu.make_async_copy(a, b, sems.at[k]) for k, (a, b) in enumerate(pairs)]
    for copy in copies:
        copy.start()
    for copy in copies:
        copy.wait()


def on_device(
    pressure, velocity, stretch, rest_radius, wall_speed, block_cells, depart_slot, depart_way
):
    cx, cy, nz = pressure.shape
    nq = nz // LANES
    ncol = 2 * cx * cy
    vmem = pl.BlockSpec(memory_space=pltpu.VMEM)
    hbm = pl.BlockSpec(memory_space=pl.ANY)
    dma = pltpu.SemaphoreType.DMA
    vmem_out = pltpu.VMEM
    parts = pl.pallas_call(
        kernel,
        out_shape=(
            vmem_out((nq, cx, cy + 16, LANES), f32),
            vmem_out((nq, cx + 2, cy, LANES), f32),
            vmem_out((nq, cx, cy + 16, LANES), f32),
            vmem_out((nq, cx, cy, LANES), f32),
            vmem_out((SLOTS, BLOCK), f32),
            vmem_out((SLOTS, BLOCK), f32),
            vmem_out((SLOT_BLOCKS, LANES), jnp.int32),
        ),
        in_specs=[pl.BlockSpec(memory_space=pltpu.HBM)] * 9,
        out_specs=(vmem,) * 7,
        scratch_shapes=[
            pltpu.VMEM((SLOTS, BLOCK), f32),
            pltpu.VMEM((3, ARRIVE, BLOCK), f32),
            pltpu.VMEM((STEPS, 3, DEP, BLOCK), f32),
            pltpu.VMEM((ROWS, ncol), bf16),
            pltpu.VMEM((ncol, ROWS), bf16),
            pltpu.VMEM((2 * ncol, BLOCK), bf16),
            pltpu.VMEM((ROWS, BLOCK), f32),
            pltpu.VMEM((2 * ROWS, BLOCK), bf16),
            pltpu.VMEM((ncol, BLOCK), f32),
            pltpu.VMEM((STEPS, 2, nq, 2, cy, LANES), f32),
            pltpu.VMEM((STEPS, 2, nq, cx, 2, LANES), f32),
            pltpu.VMEM((STEPS, 2, nq, cx, 2, LANES), f32),
            pltpu.VMEM((2, nq, cx, 1, LANES), f32),
            pltpu.VMEM((2, nq, cx, 1, LANES), f32),
            pltpu.VMEM((8, LANES), f32),
            pltpu.VMEM((4, 8, LANES), f32),
            pltpu.VMEM((SLOTS, LANES), f32),
            pltpu.VMEM((ARRIVE, LANES), f32),
            pltpu.VMEM((LANES, LANES), f32),
            pltpu.VMEM((16, LANES), f32),
            pltpu.VMEM((SLOTS, 2 * ARRIVE), bf16),
            pltpu.VMEM((2 * ARRIVE, 2 * BLOCK), bf16),
            pltpu.SMEM((SLOTS,), jnp.int32),
            pltpu.SMEM((STEPS, 1, 1, DEP), jnp.int32),
            pltpu.SMEM((STEPS, 1, 1, DEP), jnp.int32),
            pltpu.VMEM((SLOT_BLOCKS, LANES), jnp.int32),
            dma((4 * nq + 7,)),
            dma((4,)),
            dma((4,)),
            dma((STEPS, 4)),
            dma((STEPS, 4)),
            dma((4,)),
            dma((4,)),
            dma((STEPS, 4)),
            dma((STEPS, 4)),
        ],
        compiler_params=pltpu.CompilerParams(
            collective_id=0, has_side_effects=True, vmem_limit_bytes=36 * 2**20
        ),
        cost_estimate=pl.CostEstimate(
            flops=10 * 2**30, bytes_accessed=13 * 2**20, transcendentals=2**22
        ),
    )(
        *(
            pltpu.with_memory_space_constraint(value, pltpu.HBM)
            for value in (
                block_cells,
                depart_slot,
                depart_way,
                block_cells.reshape(SLOT_BLOCKS, LANES),
                pressure,
                velocity,
                stretch,
                rest_radius,
                wall_speed,
            )
        )
    )
    parts = [pltpu.with_memory_space_constraint(part, pltpu.VMEM) for part in parts]
    p, v, r, s, c = pl.pallas_call(
        write_out,
        out_shape=(
            jax.ShapeDtypeStruct(pressure.shape, f32),
            jax.ShapeDtypeStruct(velocity.shape, f32),
            jax.ShapeDtypeStruct(stretch.shape, f32),
            jax.ShapeDtypeStruct(stretch.shape, f32),
            jax.ShapeDtypeStruct((SLOT_BLOCKS, LANES), jnp.int32),
        ),
        in_specs=[vmem] * 7,
        out_specs=(hbm,) * 5,
        scratch_shapes=[dma((4 * nq + 3,))],
        compiler_params=pltpu.CompilerParams(vmem_limit_bytes=4 * 2**20),
        cost_estimate=pl.CostEstimate(flops=0, bytes_accessed=13 * 2**20, transcendentals=0),
    )(*parts)
    return p, v, r, s, c.reshape(-1)


def solution(mesh):
    placed = (
        P("gx", "gy", None),
        P(None, "gx", "gy", None),
        P(("gx", "gy"), None),
        P(("gx", "gy"), None),
        P(("gx", "gy"), None),
        P(("gx", "gy")),
        P(None, "gx", "gy", None),
        P(None, "gx", "gy", None),
    )
    return jax.shard_map(
        on_device,
        mesh=mesh,
        in_specs=placed,
        out_specs=(
            P("gx", "gy", None),
            P(None, "gx", "gy", None),
            P(("gx", "gy"), None),
            P(("gx", "gy"), None),
            P(("gx", "gy")),
        ),
        check_vma=False,
    )
```

```python
import functools
import math

import jax
import jax.numpy as jnp
from jax import lax
from jax.experimental import pallas as pl
from jax.experimental.pallas import tpu as pltpu
from jax.sharding import PartitionSpec as P

MESH = pl.DeviceIdType.MESH
f32 = jnp.float32
bf16 = jnp.bfloat16

STEPS = 4
DEP = 8
SLOTS = 1024
BLOCK = 256
LANES = 128
ARRIVE = STEPS * 4 * DEP
ROWS = SLOTS + ARRIVE
SLOT_BLOCKS = SLOTS // LANES
WAY_OF = (1, 0, 3, 2)

time_step = 0.04
half_gain = 0.2
source_scale = 0.004 * 12.566370614359172
exponent = 4.2
inv_ln2 = 1.0 / math.log(2.0)


def split(value):
    high = value.astype(bf16)
    return high, (value - high.astype(f32)).astype(bf16)


def wall_update(radius, speed, level, pressure):
    one_less = 1.0 - 0.05 * speed
    divisor = one_less * radius
    inverse = pl.reciprocal(divisor, approx=True)
    inverse = inverse * (2.0 - divisor * inverse)
    inv_radius = inverse * one_less
    wall = jnp.exp2(level - (exponent * inv_ln2) * jnp.log(radius))
    excess = wall - (0.2 + 0.08 * speed) * inv_radius - (1.0 + pressure)
    driving = (2.0 - one_less) * excess - (1.0 + 0.5 * one_less) * (speed * speed)
    speed = speed + time_step * (driving * inverse)
    radius = radius + time_step * speed
    return radius, speed, source_scale * (radius * radius) * speed


def kernel(
    cells_h, slot_h, way_h, cells_b, press, vel, stretch, rest, speed0,
    PR, VX, VY, VZ, R, S, c_out,
    A, AR, SB, OH, OHT, PHL, PG, VHL, SRC, XR, YS, YR, VYS, VYR,
    MT, MR, MSK, AMSK, LT, LR, PLACE, CAT, cells_s, slot_s, way_s, cells_v,
    in_sem, meta_s, meta_r, xs, xr, vs, vr, ds_, dr, fs, fr,
):
    _, cx, cy, nz = vel.shape
    nq = nz // LANES
    half = cx * cy
    ncol = 2 * half
    jbs = cy // 16
    part = min(256, ncol)
    planes = part // (2 * cy)
    groups = cx // planes
    shift = (planes * cy).bit_length() - 1
    zero_row = lax.axis_index("gx") // 4096
    gx, gy = lax.axis_index("gx"), lax.axis_index("gy")
    ngx, ngy = lax.axis_size("gx"), lax.axis_size("gy")
    has_lo, has_hi = gy > 0, gy < ngy - 1
    targets = (
        (lax.rem(gx + 1, ngx), gy),
        (lax.rem(gx + ngx - 1, ngx), gy),
        (gx, lax.rem(gy + 1, ngy)),
        (gx, lax.rem(gy + ngy - 1, ngy)),
    )
    sends = (None, None, has_hi, has_lo)
    takes = (None, None, has_lo, has_hi)

    def under(flag, action):
        if flag is None:
            action()
        else:
            pl.when(flag)(action)

    barrier = pltpu.get_barrier_semaphore()
    for d in range(4):
        under(
            sends[d],
            lambda d=d: pl.semaphore_signal(
                barrier, inc=1, device_id=targets[d], device_id_type=MESH
            ),
        )

    inputs = [(cells_h, cells_s), (slot_h, slot_s), (way_h, way_s), (cells_b, cells_v)]
    for q in range(nq):
        inputs.append((press.at[:, :, pl.ds(q * LANES, LANES)], PR.at[q, :, pl.ds(8, cy), :]))
    inputs.append((rest, A))
    inputs.append((stretch, R))
    inputs.append((speed0, S))
    for comp in range(3):
        for q in range(nq):
            dst = (
                VX.at[q, pl.ds(1, cx), :, :],
                VY.at[q, :, pl.ds(8, cy), :],
                VZ.at[q],
            )[comp]
            inputs.append((vel.at[comp, :, :, pl.ds(q * LANES, LANES)], dst))
    loads = [pltpu.make_async_copy(a, b, in_sem.at[k]) for k, (a, b) in enumerate(inputs)]
    for load in loads:
        load.start()

    for load in loads[:4]:
        load.wait()
    loads = loads[4:]

    lane8 = lax.broadcasted_iota(jnp.int32, (8, LANES), 1)
    sub8 = lax.broadcasted_iota(jnp.int32, (8, LANES), 0)
    slot_id = sub8 * LANES + lane8
    label = cells_v[...] + 1
    leave_at = jnp.where(label > 0, STEPS, -1)
    entry_of = (lane8 // 32) * DEP + lane8 % DEP
    wanted = (lane8 // DEP) % 4
    wanted = jnp.where(wanted < 2, 1 - wanted, 5 - wanted)
    meta = jnp.zeros((8, LANES), jnp.int32)
    for e in range(STEPS * DEP):
        slot = slot_s[e // DEP, 0, 0, e % DEP]
        moved = jnp.where(slot >= 0, cells_s[jnp.maximum(slot, 0)] + 1, 0)
        meta = jnp.where((entry_of == e) & (wanted == way_s[e // DEP, 0, 0, e % DEP]), moved, meta)
        leave_at = jnp.where(slot_id == slot, e // DEP, leave_at)
    MT[...] = meta.astype(f32)

    @pl.when(jnp.logical_not(has_lo))
    def _():
        MR[2] = jnp.zeros((8, LANES), f32)
        YR[:, 0] = jnp.zeros(YR.shape[:1] + YR.shape[2:], f32)
        VYR[0] = jnp.zeros(VYR.shape[1:], f32)

    @pl.when(jnp.logical_not(has_hi))
    def _():
        MR[3] = jnp.zeros((8, LANES), f32)
        YR[:, 1] = jnp.zeros(YR.shape[:1] + YR.shape[2:], f32)
        VYR[1] = jnp.zeros(VYR.shape[1:], f32)

    edge_rows = jnp.zeros((nq, cx, 8, LANES), f32)
    PR[:, :, 0:8, :] = edge_rows
    PR[:, :, 8 + cy : 16 + cy, :] = edge_rows
    pl.semaphore_wait(barrier, 2 + has_lo.astype(jnp.int32) + has_hi.astype(jnp.int32))

    def remote(src, dst, send_sem, recv_sem, d):
        return pltpu.make_async_remote_copy(
            src_ref=src, dst_ref=dst, send_sem=send_sem, recv_sem=recv_sem,
            device_id=targets[d], device_id_type=MESH,
        )

    def meta_copy(d):
        return remote(MT, MR.at[d], meta_s.at[d], meta_r.at[d], d)

    def p_copy(t, d):
        if d < 2:
            src = PR.at[:, pl.ds((cx - 2, 0)[d], 2), pl.ds(8, cy), :]
            return remote(src, XR.at[t, d], xs.at[t, d], xr.at[t, d], d)
        return remote(YS.at[t, 3 - d], YR.at[t, d - 2], xs.at[t, d], xr.at[t, d], d)

    def first_copies(d):
        side = (cx - 2, 0)[d]
        for q in range(nq):
            lanes = pl.ds(q * LANES, LANES)
            yield remote(
                press.at[pl.ds(side, 2), :, lanes], XR.at[0, d, q], fs.at[0, d, q], fr.at[0, d, q], d
            )
        for q in range(nq):
            lanes = pl.ds(q * LANES, LANES)
            yield remote(
                vel.at[0, pl.ds((cx - 1, 0)[d], 1), :, lanes],
                VX.at[q, pl.ds((0, cx + 1)[d], 1), :, :],
                fs.at[1, d, q],
                fr.at[1, d, q],
                d,
            )

    def v_copy(d):
        return remote(VYS.at[3 - d], VYR.at[d - 2], vs.at[d], vr.at[d], d)

    def dep_copy(t, d):
        return remote(
            SB.at[t], AR.at[:, pl.ds(t * 32 + d * DEP, DEP), :], ds_.at[t, d], dr.at[t, d], d
        )

    def start(make, ways=(0, 1, 2, 3)):
        for d in ways:
            under(sends[d], lambda d=d: make(d).start())

    def wait_sent(make, ways=(0, 1, 2, 3)):
        for d in ways:
            under(sends[d], lambda d=d: make(d).wait_send())

    def wait_taken(make, ways=(0, 1, 2, 3)):
        for d in ways:
            under(takes[d], lambda d=d: make(d).wait_recv())

    start(meta_copy)
    for d in range(2):
        for copy in first_copies(d):
            copy.start()

    def pack_rows(t):
        for i in range(cx):
            for q in range(nq):
                YS[t, 0, q, i] = PR[q, i, 8:10, :]
                YS[t, 1, q, i] = PR[q, i, 6 + cy : 8 + cy, :]

    def column_row(i, h, jb):
        return (i // planes) * part + (h * planes + i % planes) * cy + jb * 16

    def keep_parts(i, jb, q, value):
        high, low = split(value)
        row = column_row(i, q // 2, jb)
        col = (q % 2) * LANES
        PHL[row : row + 16, col : col + LANES] = high
        PHL[row + ncol : row + ncol + 16, col : col + LANES] = low

    def rows_of(jb):
        return slice(jb * 16, jb * 16 + 16), slice(8 + jb * 16, 24 + jb * 16)

    for k in range(nq):
        loads[k].wait()
    pack_rows(0)
    start(lambda d: p_copy(0, d), (2, 3))
    for i in range(cx):
        for jb in range(jbs):
            for q in range(nq):
                keep_parts(i, jb, q, PR[q, i, rows_of(jb)[1], :])

    for k in range(nq + 3, nq + 3 + 3 * nq):
        loads[k].wait()

    def pack_flow(i, carry):
        for q in range(nq):
            VYS[0, q, i] = VY[q, i, 8:9, :]
            VYS[1, q, i] = VY[q, i, 7 + cy : 8 + cy, :]
        return carry

    lax.fori_loop(0, cx, pack_flow, 0, unroll=4)
    start(v_copy, (2, 3))

    for k in range(nq, nq + 3):
        loads[k].wait()

    def first_state(n, carry):
        rows = pl.ds(pl.multiple_of(n * 16, 16), 16)
        rest_now = A[rows, :]
        R[rows, :] = R[rows, :] * rest_now
        A[rows, :] = inv_ln2 * (jnp.log(1.0 + 0.2 / rest_now) + exponent * jnp.log(rest_now))
        return carry

    lax.fori_loop(0, SLOTS // 16, first_state, 0, unroll=4)
    VHL[pl.ds(SLOTS, ARRIVE), :] = jnp.zeros((ARRIVE, BLOCK), bf16)
    VHL[pl.ds(ROWS + SLOTS, ARRIVE), :] = jnp.zeros((ARRIVE, BLOCK), bf16)

    wait_taken(meta_copy)
    came = (lane8 // DEP) % 4
    alab = jnp.where(
        came == 0, MR[0], jnp.where(came == 1, MR[1], jnp.where(came == 2, MR[2], MR[3]))
    )
    present = alab > 0.0
    lrow = lax.broadcasted_iota(jnp.int32, (LANES, LANES), 0)
    lcol = lax.broadcasted_iota(jnp.int32, (LANES, LANES), 1)
    upper = jnp.where(lrow <= lcol, 1.0, 0.0)
    upper_block = jnp.where(lrow // 32 == lcol // 32, upper, 0.0).astype(bf16)
    upper = upper.astype(bf16)
    ones = jnp.ones((LANES, LANES), bf16)
    present_f = jnp.where(present, 1.0, 0.0)
    arank = jnp.dot(present_f.astype(bf16), upper_block, preferred_element_type=f32) - 1.0
    arank = jnp.where(present, arank, -5.0)
    vacant = label == 0
    ranks = []
    for t in range(STEPS):
        vacant = vacant | (leave_at == t)
        flag = jnp.where(vacant, 1.0, 0.0).astype(bf16)
        rank = jnp.dot(flag, upper, preferred_element_type=f32) - 1.0
        total = jnp.dot(flag, ones, preferred_element_type=f32)
        for r in range(SLOT_BLOCKS - 1):
            rank = rank + jnp.where(sub8 > r, total[r : r + 1, :], 0.0)
        ranks.append(jnp.where(vacant, rank, -1.0))
        count = jnp.sum(jnp.where(lane8 // 32 == t, present_f, 0.0), axis=1, keepdims=True)
        vacant = vacant & (rank >= count)

    def code_of(lab):
        cell = lab - 1
        place = cell >> 1
        row = (place >> shift) * part + (cell & 1) * (planes * cy)
        return jnp.where(lab > 0, row + (place & (planes * cy - 1)), -1).astype(f32)

    code = code_of(label)
    acode = code_of(alab.astype(jnp.int32))
    stack = [code, leave_at.astype(f32)] + ranks + [acode, alab]
    stack = stack + [jnp.zeros((8, LANES), f32)] * (16 - len(stack))
    LT[...] = jnp.concatenate(stack, axis=0).T
    LR[0:8, :] = code
    LR[8:16, :] = acode

    wide = lax.broadcasted_iota(jnp.int32, (16, ncol), 1).astype(f32)
    for r in range(SLOT_BLOCKS + 1):
        at = r if r < SLOT_BLOCKS else 48

        def one_hot_rows(m, carry, r=r, at=at):
            rows = pl.ds(pl.multiple_of(m * 16, 16), 16)
            column = LT[rows, at : at + 1]
            hot = jnp.where(column == wide, 1.0, 0.0).astype(bf16)
            OH[pl.ds(pl.multiple_of(r * LANES + m * 16, 16), 16), :] = hot
            return carry

        lax.fori_loop(0, LANES // 16, one_hot_rows, 0, unroll=2)

    tall = lax.broadcasted_iota(jnp.int32, (LANES, LANES), 0)

    def one_hot_columns(m, carry):
        ident = (tall + m * LANES).astype(f32)
        rows = pl.ds(pl.multiple_of(m * LANES, LANES), LANES)
        for r in range(SLOT_BLOCKS + 1):
            hot = jnp.where(ident == LR[r : r + 1, :], 1.0, 0.0).astype(bf16)
            OHT[rows, r * LANES : (r + 1) * LANES] = hot
        return carry

    lax.fori_loop(0, ncol // LANES, one_hot_columns, 0)

    group = lcol // 32
    for r in range(SLOT_BLOCKS):
        MSK[r * LANES : (r + 1) * LANES, :] = jnp.broadcast_to(
            LT[:, 8 + r : 9 + r], (LANES, LANES)
        )
        mine = jnp.broadcast_to(LT[:, 16 + r : 17 + r], (LANES, LANES))
        for t in range(1, STEPS):
            mine = jnp.where(group == t, LT[:, 16 + 8 * t + r : 17 + 8 * t + r], mine)
        hot = jnp.where(mine == arank[0:1, :], 1.0, 0.0).astype(bf16)
        PLACE[r * LANES : (r + 1) * LANES, 0:LANES] = hot
        PLACE[r * LANES : (r + 1) * LANES, LANES : 2 * LANES] = hot
    AMSK[...] = jnp.broadcast_to(LT[:, 56:57], (LANES, LANES))

    alab_high, alab_low = split(alab)
    final = jnp.where(leave_at == STEPS, label, 0).astype(f32)
    for r in range(SLOT_BLOCKS):
        hot = PLACE[r * LANES : (r + 1) * LANES, 0:LANES]
        nt = (((1,), (1,)), ((), ()))
        placed = lax.dot_general(alab_high, hot, nt, preferred_element_type=f32)
        placed = placed + lax.dot_general(alab_low, hot, nt, preferred_element_type=f32)
        final = final + jnp.where(sub8 == r, placed, 0.0)
    c_out[...] = final.astype(jnp.int32) - 1

    lane16 = lax.broadcasted_iota(jnp.int32, (16, LANES), 1)
    first_lane, last_lane = lane16 == 0, lane16 == LANES - 1

    def slope_z(tiles):
        zero = jnp.zeros((16, LANES), f32)
        ahead = [pltpu.roll(v, LANES - 1, 1) for v in tiles] + [zero]
        behind = [zero] + [pltpu.roll(v, 1, 1) for v in tiles]
        return [
            jnp.where(last_lane, ahead[q + 1], ahead[q])
            - jnp.where(first_lane, behind[q], behind[q + 1])
            for q in range(nq)
        ]

    low_gate = jnp.where(has_lo, 1.0, 0.0).astype(f32)
    high_gate = jnp.where(has_hi, 1.0, 0.0).astype(f32)
    chunk = 256

    def gather(low_row, count):
        hot = OH[low_row : low_row + count, :]
        hot = jnp.concatenate([hot, hot], axis=1)
        PG[low_row : low_row + count, :] = jnp.dot(hot, PHL[...], preferred_element_type=f32)

    def scatter(m):
        hot = OHT[m * part : (m + 1) * part, :]
        hot = jnp.concatenate([hot, hot], axis=1)
        SRC[m * part : (m + 1) * part, :] = jnp.dot(hot, VHL[...], preferred_element_type=f32)

    def step(t, carry):
        limit = t.astype(f32)

        def bubbles(first):
            rows = slice(first, first + 16)
            radius, speed, rate = wall_update(R[rows, :], S[rows, :], A[rows, :], PG[rows, :])
            R[rows, :] = radius
            S[rows, :] = speed
            keep = MSK[rows, :]
            keep = jnp.concatenate([keep, keep], axis=1) >= limit
            high, low = split(jnp.where(keep, rate, 0.0))
            VHL[rows, :] = high
            VHL[ROWS + first : ROWS + first + 16, :] = low

        gather(0, chunk)
        for m in range(SLOTS // chunk):
            if m + 1 < SLOTS // chunk:
                gather((m + 1) * chunk, chunk)
            else:
                gather(SLOTS, ARRIVE)
            for b in range(chunk // 16):
                bubbles(m * chunk + b * 16)

        for k in range(DEP):
            row = pl.ds(jnp.maximum(slot_s[t, 0, 0, k], 0), 1)
            SB[t, 0, k : k + 1, :] = R[row, :]
            SB[t, 1, k : k + 1, :] = S[row, :]
            SB[t, 2, k : k + 1, :] = A[row, :]
        start(lambda d: dep_copy(t, d))

        @pl.when(t > 0)
        def _():
            wait_taken(lambda d: dep_copy(t - 1, d))

        def arrived(n, carry):
            for b in range(2):
                first = n * 32 + b * 16
                rows = pl.ds(pl.multiple_of(first, 16), 16)
                low_rows = pl.ds(pl.multiple_of(SLOTS + first, 16), 16)
                radius, speed, rate = wall_update(
                    AR[0, rows, :], AR[1, rows, :], AR[2, rows, :], PG[low_rows, :]
                )
                AR[0, rows, :] = radius
                AR[1, rows, :] = speed
                keep = AMSK[rows, :]
                keep = jnp.concatenate([keep, keep], axis=1) > 0.0
                high, low = split(jnp.where(keep, rate, 0.0))
                VHL[low_rows, :] = high
                VHL[pl.ds(pl.multiple_of(ROWS + SLOTS + first, 16), 16), :] = low
            return carry

        lax.fori_loop(0, t, arrived, 0)

        def flow_x(i, after, before):
            for q in range(nq):
                for jb in range(jbs):
                    rows, at = rows_of(jb)
                    ahead = PR[q, i + 1, at, :] if after is None else XR[t, 1, q, after, rows, :]
                    back = PR[q, i - 1, at, :] if before is None else XR[t, 0, q, before, rows, :]
                    VX[q, i + 1, rows, :] = VX[q, i + 1, rows, :] - half_gain * (ahead - back)

        def flow_z(i, jb):
            rows, at = rows_of(jb)
            slopes = slope_z([PR[q, i, at, :] for q in range(nq)])
            for q in range(nq):
                VZ[q, i, rows, :] = VZ[q, i, rows, :] - half_gain * slopes[q]

        def flow_y(i, jb):
            _, at = rows_of(jb)
            for q in range(nq):
                VY[q, i, at, :] = VY[q, i, at, :] - half_gain * (
                    PR[q, i, pl.ds(9 + jb * 16 + zero_row, 16), :]
                    - PR[q, i, pl.ds(7 + jb * 16 + zero_row, 16), :]
                )

        def side_rows(i):
            for q in range(nq):
                below, above = YR[t, 0, q, i], YR[t, 1, q, i]
                VY[q, i, 8:9, :] = VY[q, i, 8:9, :] + half_gain * below[1:2, :]
                VY[q, i, 7 + cy : 8 + cy, :] = (
                    VY[q, i, 7 + cy : 8 + cy, :] - half_gain * above[0:1, :]
                )
                VY[q, i, 7:8, :] = low_gate * (
                    VY[q, i, 7:8, :] - half_gain * (PR[q, i, 8:9, :] - below[0:1, :])
                )
                VY[q, i, 8 + cy : 9 + cy, :] = high_gate * (
                    VY[q, i, 8 + cy : 9 + cy, :]
                    - half_gain * (above[1:2, :] - PR[q, i, 7 + cy : 8 + cy, :])
                )

        def pressure(i, jb):
            rows, at = rows_of(jb)
            slopes = slope_z([VZ[q, i, rows, :] for q in range(nq)])
            for q in range(nq):
                rise = (
                    (VX[q, i + 2, rows, :] - VX[q, i, rows, :])
                    + (
                        VY[q, i, pl.ds(9 + jb * 16 + zero_row, 16), :]
                        - VY[q, i, pl.ds(7 + jb * 16 + zero_row, 16), :]
                    )
                    + slopes[q]
                )
                row = column_row(i, q // 2, jb)
                col = (q % 2) * LANES
                value = PR[q, i, at, :] - half_gain * rise + SRC[row : row + 16, col : col + LANES]
                PR[q, i, at, :] = value
                keep_parts(i, jb, q, value)

        order = [0, groups - 1] + list(range(1, groups - 1)) if groups > 1 else [0]
        early = order[:2]
        for k, m in enumerate(early):
            scatter(m)
            for i in range(k * cx // len(early), (k + 1) * cx // len(early)):
                if 0 < i < cx - 1:
                    flow_x(i, None, None)
                for jb in range(jbs):
                    flow_z(i, jb)
                    flow_y(i, jb)

        wait_taken(lambda d: p_copy(t, d), (2, 3))
        wait_sent(lambda d: p_copy(t, d), (2, 3))

        @pl.when(t > 0)
        def _():
            wait_taken(lambda d: p_copy(t, d), (0, 1))
            wait_sent(lambda d: p_copy(t, d), (0, 1))

        @pl.when(t == 0)
        def _():
            for d in range(2):
                for copy in first_copies(d):
                    copy.wait_recv()
                    copy.wait_send()
            wait_taken(v_copy, (2, 3))
            wait_sent(v_copy, (2, 3))
            for i in range(cx):
                for q in range(nq):
                    VY[q, i, 7:8, :] = VYR[0, q, i]
                    VY[q, i, 8 + cy : 9 + cy, :] = VYR[1, q, i]

        flow_x(-1, None, 0)
        flow_x(0, None, 1)
        flow_x(cx - 1, 0, None)
        flow_x(cx, 1, None)
        late = order[2:]
        ends = [0, 1, cx - 2, cx - 1]
        for m in late[:1]:
            scatter(m)
        for i in ends:
            side_rows(i)
            for jb in range(jbs):
                pressure(i, jb)

        @pl.when(t < STEPS - 1)
        def _():
            start(lambda d: p_copy(t + 1, d), (0, 1))

        for m in late[1:]:
            scatter(m)
        for m in order:
            for i in range(m * planes, (m + 1) * planes):
                if i not in ends:
                    side_rows(i)
                    for jb in range(jbs):
                        pressure(i, jb)

        @pl.when(t < STEPS - 1)
        def _():
            pack_rows(t + 1)
            start(lambda d: p_copy(t + 1, d), (2, 3))

        return carry

    lax.fori_loop(0, STEPS, step, 0)

    wait_taken(lambda d: dep_copy(STEPS - 1, d))
    keep = AMSK[...] > 0.0
    for k in range(2):
        for w in range(2):
            col = slice(w * LANES, (w + 1) * LANES)
            high, low = split(jnp.where(keep, AR[k, :, col], 0.0))
            to = slice(k * BLOCK + w * LANES, k * BLOCK + (w + 1) * LANES)
            CAT[0:ARRIVE, to] = high
            CAT[ARRIVE : 2 * ARRIVE, to] = low

    def finish(m, carry):
        rows = pl.ds(pl.multiple_of(m * LANES, LANES), LANES)
        placed = jnp.dot(PLACE[rows, :], CAT[...], preferred_element_type=f32)
        keep = MSK[rows, :]
        keep = jnp.concatenate([keep, keep], axis=1) >= float(STEPS)
        R[rows, :] = jnp.where(keep, R[rows, :], 0.0) + placed[:, :BLOCK]
        S[rows, :] = jnp.where(keep, S[rows, :], 0.0) + placed[:, BLOCK:]
        return carry

    lax.fori_loop(0, SLOT_BLOCKS, finish, 0)
    wait_sent(meta_copy)
    for t in range(STEPS):
        wait_sent(lambda d, t=t: dep_copy(t, d))


def write_out(p, vx, vy, vz, r, s, c, p_out, v_out, r_out, s_out, c_out, sems):
    _, cx, cy, nz = v_out.shape
    pairs = [(r, r_out), (s, s_out), (c, c_out)]
    for q in range(nz // LANES):
        lanes = pl.ds(q * LANES, LANES)
        pairs.append((vx.at[q, pl.ds(1, cx), :, :], v_out.at[0, :, :, lanes]))
        pairs.append((vy.at[q, :, pl.ds(8, cy), :], v_out.at[1, :, :, lanes]))
        pairs.append((vz.at[q], v_out.at[2, :, :, lanes]))
        pairs.append((p.at[q, :, pl.ds(8, cy), :], p_out.at[:, :, lanes]))
    copies = [pltpu.make_async_copy(a, b, sems.at[k]) for k, (a, b) in enumerate(pairs)]
    for copy in copies:
        copy.start()
    for copy in copies:
        copy.wait()


def on_device(
    pressure, velocity, stretch, rest_radius, wall_speed, block_cells, depart_slot, depart_way
):
    cx, cy, nz = pressure.shape
    nq = nz // LANES
    ncol = 2 * cx * cy
    vmem = pl.BlockSpec(memory_space=pltpu.VMEM)
    hbm = pl.BlockSpec(memory_space=pl.ANY)
    dma = pltpu.SemaphoreType.DMA
    vmem_out = pltpu.VMEM
    parts = pl.pallas_call(
        kernel,
        out_shape=(
            vmem_out((nq, cx, cy + 16, LANES), f32),
            vmem_out((nq, cx + 2, cy, LANES), f32),
            vmem_out((nq, cx, cy + 16, LANES), f32),
            vmem_out((nq, cx, cy, LANES), f32),
            vmem_out((SLOTS, BLOCK), f32),
            vmem_out((SLOTS, BLOCK), f32),
            vmem_out((SLOT_BLOCKS, LANES), jnp.int32),
        ),
        in_specs=[pl.BlockSpec(memory_space=pltpu.HBM)] * 9,
        out_specs=(vmem,) * 7,
        scratch_shapes=[
            pltpu.VMEM((SLOTS, BLOCK), f32),
            pltpu.VMEM((3, ARRIVE, BLOCK), f32),
            pltpu.VMEM((STEPS, 3, DEP, BLOCK), f32),
            pltpu.VMEM((ROWS, ncol), bf16),
            pltpu.VMEM((ncol, ROWS), bf16),
            pltpu.VMEM((2 * ncol, BLOCK), bf16),
            pltpu.VMEM((ROWS, BLOCK), f32),
            pltpu.VMEM((2 * ROWS, BLOCK), bf16),
            pltpu.VMEM((ncol, BLOCK), f32),
            pltpu.VMEM((STEPS, 2, nq, 2, cy, LANES), f32),
            pltpu.VMEM((STEPS, 2, nq, cx, 2, LANES), f32),
            pltpu.VMEM((STEPS, 2, nq, cx, 2, LANES), f32),
            pltpu.VMEM((2, nq, cx, 1, LANES), f32),
            pltpu.VMEM((2, nq, cx, 1, LANES), f32),
            pltpu.VMEM((8, LANES), f32),
            pltpu.VMEM((4, 8, LANES), f32),
            pltpu.VMEM((SLOTS, LANES), f32),
            pltpu.VMEM((ARRIVE, LANES), f32),
            pltpu.VMEM((LANES, LANES), f32),
            pltpu.VMEM((16, LANES), f32),
            pltpu.VMEM((SLOTS, 2 * ARRIVE), bf16),
            pltpu.VMEM((2 * ARRIVE, 2 * BLOCK), bf16),
            pltpu.SMEM((SLOTS,), jnp.int32),
            pltpu.SMEM((STEPS, 1, 1, DEP), jnp.int32),
            pltpu.SMEM((STEPS, 1, 1, DEP), jnp.int32),
            pltpu.VMEM((SLOT_BLOCKS, LANES), jnp.int32),
            dma((4 * nq + 7,)),
            dma((4,)),
            dma((4,)),
            dma((STEPS, 4)),
            dma((STEPS, 4)),
            dma((4,)),
            dma((4,)),
            dma((STEPS, 4)),
            dma((STEPS, 4)),
            dma((2, 2, nq)),
            dma((2, 2, nq)),
        ],
        compiler_params=pltpu.CompilerParams(
            collective_id=0, has_side_effects=True, vmem_limit_bytes=36 * 2**20
        ),
        cost_estimate=pl.CostEstimate(
            flops=10 * 2**30, bytes_accessed=13 * 2**20, transcendentals=2**22
        ),
    )(
        *(
            pltpu.with_memory_space_constraint(value, pltpu.HBM)
            for value in (
                block_cells,
                depart_slot,
                depart_way,
                block_cells.reshape(SLOT_BLOCKS, LANES),
                pressure,
                velocity,
                stretch,
                rest_radius,
                wall_speed,
            )
        )
    )
    parts = [pltpu.with_memory_space_constraint(part, pltpu.VMEM) for part in parts]
    p, v, r, s, c = pl.pallas_call(
        write_out,
        out_shape=(
            jax.ShapeDtypeStruct(pressure.shape, f32),
            jax.ShapeDtypeStruct(velocity.shape, f32),
            jax.ShapeDtypeStruct(stretch.shape, f32),
            jax.ShapeDtypeStruct(stretch.shape, f32),
            jax.ShapeDtypeStruct((SLOT_BLOCKS, LANES), jnp.int32),
        ),
        in_specs=[vmem] * 7,
        out_specs=(hbm,) * 5,
        scratch_shapes=[dma((4 * nq + 3,))],
        compiler_params=pltpu.CompilerParams(vmem_limit_bytes=4 * 2**20),
        cost_estimate=pl.CostEstimate(flops=0, bytes_accessed=13 * 2**20, transcendentals=0),
    )(*parts)
    return p, v, r, s, c.reshape(-1)


def solution(mesh):
    placed = (
        P("gx", "gy", None),
        P(None, "gx", "gy", None),
        P(("gx", "gy"), None),
        P(("gx", "gy"), None),
        P(("gx", "gy"), None),
        P(("gx", "gy")),
        P(None, "gx", "gy", None),
        P(None, "gx", "gy", None),
    )
    return jax.shard_map(
        on_device,
        mesh=mesh,
        in_specs=placed,
        out_specs=(
            P("gx", "gy", None),
            P(None, "gx", "gy", None),
            P(("gx", "gy"), None),
            P(("gx", "gy"), None),
            P(("gx", "gy")),
        ),
        check_vma=False,
    )
```

```python
import functools
import math

import jax
import jax.numpy as jnp
from jax import lax
from jax.experimental import pallas as pl
from jax.experimental.pallas import tpu as pltpu
from jax.sharding import PartitionSpec as P

MESH = pl.DeviceIdType.MESH
f32 = jnp.float32
bf16 = jnp.bfloat16

STEPS = 4
DEP = 8
SLOTS = 1024
BLOCK = 256
LANES = 128
ARRIVE = STEPS * 4 * DEP
ROWS = SLOTS + ARRIVE
SLOT_BLOCKS = SLOTS // LANES
WAY_OF = (1, 0, 3, 2)

time_step = 0.04
half_gain = 0.2
source_scale = 0.004 * 12.566370614359172
exponent = 4.2
inv_ln2 = 1.0 / math.log(2.0)


def split(value):
    high = value.astype(bf16)
    return high, (value - high.astype(f32)).astype(bf16)


def wall_update(radius, shift, level, pressure):
    mach = (0.05 / time_step) * shift
    one_less = 1.0 - mach
    divisor = one_less * radius
    inverse = pl.reciprocal(divisor, approx=True)
    inverse = inverse * (2.0 - divisor * inverse)
    inv_radius = inverse * one_less
    wall = jnp.exp2(level - (exponent * inv_ln2) * jnp.log(radius))
    squared = time_step * time_step
    excess = (
        wall
        - (0.2 * squared + (0.08 * time_step) * shift) * inv_radius
        - (squared + squared * pressure)
    )
    driving = (1.0 + mach) * excess - (1.5 - 0.5 * mach) * (shift * shift)
    shift = shift + driving * inverse
    radius = radius + shift
    return radius, shift, (source_scale / time_step) * (radius * radius) * shift


def kernel(
    cells_h, slot_h, way_h, cells_b, press, vel, stretch, rest, speed0,
    PR, VX, VY, VZ, R, S, c_out,
    A, AR, SB, OH, OHT, PHL, PG, VHL, SRC, XR, YS, YR, VYS, VYR,
    MT, MR, MSK, AMSK, LT, LR, PLACE, CAT, cells_s, slot_s, way_s, cells_v,
    in_sem, meta_s, meta_r, xs, xr, vs, vr, ds_, dr, fs, fr,
):
    _, cx, cy, nz = vel.shape
    nq = nz // LANES
    half = cx * cy
    ncol = 2 * half
    jbs = cy // 16
    part = min(256, ncol)
    planes = part // (2 * cy)
    groups = cx // planes
    shift = (planes * cy).bit_length() - 1
    zero_row = lax.axis_index("gx") // 4096
    gx, gy = lax.axis_index("gx"), lax.axis_index("gy")
    ngx, ngy = lax.axis_size("gx"), lax.axis_size("gy")
    has_lo, has_hi = gy > 0, gy < ngy - 1
    targets = (
        (lax.rem(gx + 1, ngx), gy),
        (lax.rem(gx + ngx - 1, ngx), gy),
        (gx, lax.rem(gy + 1, ngy)),
        (gx, lax.rem(gy + ngy - 1, ngy)),
    )
    sends = (None, None, has_hi, has_lo)
    takes = (None, None, has_lo, has_hi)

    def under(flag, action):
        if flag is None:
            action()
        else:
            pl.when(flag)(action)

    barrier = pltpu.get_barrier_semaphore()
    for d in range(4):
        under(
            sends[d],
            lambda d=d: pl.semaphore_signal(
                barrier, inc=1, device_id=targets[d], device_id_type=MESH
            ),
        )

    inputs = [(cells_h, cells_s), (slot_h, slot_s), (way_h, way_s), (cells_b, cells_v)]
    for q in range(nq):
        inputs.append((press.at[:, :, pl.ds(q * LANES, LANES)], PR.at[q, :, pl.ds(8, cy), :]))
    inputs.append((rest, A))
    inputs.append((stretch, R))
    inputs.append((speed0, S))
    for comp in range(3):
        for q in range(nq):
            dst = (
                VX.at[q, pl.ds(1, cx), :, :],
                VY.at[q, :, pl.ds(8, cy), :],
                VZ.at[q],
            )[comp]
            inputs.append((vel.at[comp, :, :, pl.ds(q * LANES, LANES)], dst))
    loads = [pltpu.make_async_copy(a, b, in_sem.at[k]) for k, (a, b) in enumerate(inputs)]
    for load in loads:
        load.start()
    small_loads, loads = loads[:4], loads[4:]

    @pl.when(jnp.logical_not(has_lo))
    def _():
        MR[2] = jnp.zeros((8, LANES), f32)
        YR[:, 0] = jnp.zeros(YR.shape[:1] + YR.shape[2:], f32)
        VYR[0] = jnp.zeros(VYR.shape[1:], f32)

    @pl.when(jnp.logical_not(has_hi))
    def _():
        MR[3] = jnp.zeros((8, LANES), f32)
        YR[:, 1] = jnp.zeros(YR.shape[:1] + YR.shape[2:], f32)
        VYR[1] = jnp.zeros(VYR.shape[1:], f32)

    edge_rows = jnp.zeros((nq, cx, 8, LANES), f32)
    PR[:, :, 0:8, :] = edge_rows
    PR[:, :, 8 + cy : 16 + cy, :] = edge_rows
    VHL[pl.ds(SLOTS, ARRIVE), :] = jnp.zeros((ARRIVE, BLOCK), bf16)
    VHL[pl.ds(ROWS + SLOTS, ARRIVE), :] = jnp.zeros((ARRIVE, BLOCK), bf16)
    OHT[:, SLOTS:ROWS] = jnp.zeros((ncol, ARRIVE), bf16)
    OH[SLOTS:ROWS, :] = jnp.zeros((ARRIVE, ncol), bf16)
    pl.semaphore_wait(barrier, 2 + has_lo.astype(jnp.int32) + has_hi.astype(jnp.int32))

    def remote(src, dst, send_sem, recv_sem, d):
        return pltpu.make_async_remote_copy(
            src_ref=src, dst_ref=dst, send_sem=send_sem, recv_sem=recv_sem,
            device_id=targets[d], device_id_type=MESH,
        )

    def meta_copy(d):
        return remote(MT, MR.at[d], meta_s.at[d], meta_r.at[d], d)

    def p_copy(t, d):
        if d < 2:
            src = PR.at[:, pl.ds((cx - 2, 0)[d], 2), pl.ds(8, cy), :]
            return remote(src, XR.at[t, d], xs.at[t, d], xr.at[t, d], d)
        return remote(YS.at[t, 3 - d], YR.at[t, d - 2], xs.at[t, d], xr.at[t, d], d)

    def first_copies(d):
        side = (cx - 2, 0)[d]
        for q in range(nq):
            lanes = pl.ds(q * LANES, LANES)
            yield remote(
                press.at[pl.ds(side, 2), :, lanes], XR.at[0, d, q], fs.at[0, d, q], fr.at[0, d, q], d
            )
        for q in range(nq):
            lanes = pl.ds(q * LANES, LANES)
            yield remote(
                vel.at[0, pl.ds((cx - 1, 0)[d], 1), :, lanes],
                VX.at[q, pl.ds((0, cx + 1)[d], 1), :, :],
                fs.at[1, d, q],
                fr.at[1, d, q],
                d,
            )

    def v_copy(d):
        return remote(VYS.at[3 - d], VYR.at[d - 2], vs.at[d], vr.at[d], d)

    def dep_copy(t, d):
        return remote(
            SB.at[t], AR.at[:, pl.ds(t * 32 + d * DEP, DEP), :], ds_.at[t, d], dr.at[t, d], d
        )

    def start(make, ways=(0, 1, 2, 3)):
        for d in ways:
            under(sends[d], lambda d=d: make(d).start())

    def wait_sent(make, ways=(0, 1, 2, 3)):
        for d in ways:
            under(sends[d], lambda d=d: make(d).wait_send())

    def wait_taken(make, ways=(0, 1, 2, 3)):
        for d in ways:
            under(takes[d], lambda d=d: make(d).wait_recv())

    for d in range(2):
        for copy in first_copies(d):
            copy.start()
    for load in small_loads:
        load.wait()

    lane8 = lax.broadcasted_iota(jnp.int32, (8, LANES), 1)
    sub8 = lax.broadcasted_iota(jnp.int32, (8, LANES), 0)
    slot_id = sub8 * LANES + lane8
    label = cells_v[...] + 1
    leave_at = jnp.where(label > 0, STEPS, -1)
    entry_of = (lane8 // 32) * DEP + lane8 % DEP
    wanted = (lane8 // DEP) % 4
    wanted = jnp.where(wanted < 2, 1 - wanted, 5 - wanted)
    meta = jnp.zeros((8, LANES), jnp.int32)
    for e in range(STEPS * DEP):
        slot = slot_s[e // DEP, 0, 0, e % DEP]
        moved = jnp.where(slot >= 0, cells_s[jnp.maximum(slot, 0)] + 1, 0)
        meta = jnp.where((entry_of == e) & (wanted == way_s[e // DEP, 0, 0, e % DEP]), moved, meta)
        leave_at = jnp.where(slot_id == slot, e // DEP, leave_at)
    MT[...] = meta.astype(f32)

    start(meta_copy)

    def pack_rows(t):
        for i in range(cx):
            for q in range(nq):
                YS[t, 0, q, i] = PR[q, i, 8:10, :]
                YS[t, 1, q, i] = PR[q, i, 6 + cy : 8 + cy, :]

    def column_row(i, h, jb):
        return (i // planes) * part + (h * planes + i % planes) * cy + jb * 16

    def keep_parts(i, jb, q, value):
        high, low = split(value)
        row = column_row(i, q // 2, jb)
        col = (q % 2) * LANES
        PHL[row : row + 16, col : col + LANES] = high
        PHL[row + ncol : row + ncol + 16, col : col + LANES] = low

    def rows_of(jb):
        return slice(jb * 16, jb * 16 + 16), slice(8 + jb * 16, 24 + jb * 16)

    def split_all():
        for i in range(cx):
            for jb in range(jbs):
                for q in range(nq):
                    keep_parts(i, jb, q, PR[q, i, rows_of(jb)[1], :])

    for k in range(nq):
        loads[k].wait()
    pack_rows(0)
    start(lambda d: p_copy(0, d), (2, 3))
    split_all()

    lrow = lax.broadcasted_iota(jnp.int32, (LANES, LANES), 0)
    lcol = lax.broadcasted_iota(jnp.int32, (LANES, LANES), 1)
    wide = lax.broadcasted_iota(jnp.int32, (16, ncol), 1).astype(f32)

    def code_of(lab):
        cell = lab - 1
        place = cell >> 1
        row = (place >> shift) * part + (cell & 1) * (planes * cy)
        return jnp.where(lab > 0, row + (place & (planes * cy - 1)), -1).astype(f32)

    def turn(stack):
        stack = stack + [jnp.zeros((8, LANES), f32)] * (16 - len(stack))
        LT[...] = jnp.concatenate(stack, axis=0).T

    def hot_rows(r, at):
        def body(m, carry):
            rows = pl.ds(pl.multiple_of(m * 16, 16), 16)
            hot = jnp.where(LT[rows, at : at + 1] == wide, 1.0, 0.0).astype(bf16)
            OH[pl.ds(pl.multiple_of(r * LANES + m * 16, 16), 16), :] = hot
            return carry

        lax.fori_loop(0, LANES // 16, body, 0, unroll=4)

    def hot_columns(first, last):
        def body(m, carry):
            ident = (lrow + m * LANES).astype(f32)
            rows = pl.ds(pl.multiple_of(m * LANES, LANES), LANES)
            for r in range(first, last):
                hot = jnp.where(ident == LR[r : r + 1, :], 1.0, 0.0).astype(bf16)
                OHT[rows, r * LANES : (r + 1) * LANES] = hot
            return carry

        lax.fori_loop(0, ncol // LANES, body, 0)

    code = code_of(label)
    turn([code, leave_at.astype(f32)])
    LR[0:8, :] = code
    for r in range(SLOT_BLOCKS):
        hot_rows(r, r)
    for r in range(SLOT_BLOCKS):
        MSK[r * LANES : (r + 1) * LANES, :] = jnp.broadcast_to(
            LT[:, 8 + r : 9 + r], (LANES, LANES)
        )
    hot_columns(0, SLOT_BLOCKS)

    for k in range(nq + 3, nq + 3 + 3 * nq):
        loads[k].wait()

    def pack_flow(i, carry):
        for q in range(nq):
            VYS[0, q, i] = VY[q, i, 8:9, :]
            VYS[1, q, i] = VY[q, i, 7 + cy : 8 + cy, :]
        return carry

    lax.fori_loop(0, cx, pack_flow, 0, unroll=4)
    start(v_copy, (2, 3))

    for k in range(nq, nq + 3):
        loads[k].wait()

    def first_state(n, carry):
        rows = pl.ds(pl.multiple_of(n * 16, 16), 16)
        rest_now = A[rows, :]
        R[rows, :] = R[rows, :] * rest_now
        S[rows, :] = time_step * S[rows, :]
        A[rows, :] = inv_ln2 * (
            jnp.log((time_step * time_step) * (1.0 + 0.2 / rest_now))
            + exponent * jnp.log(rest_now)
        )
        return carry

    lax.fori_loop(0, SLOTS // 16, first_state, 0, unroll=4)
    def plan():
        wait_taken(meta_copy)
        came = (lane8 // DEP) % 4
        alab = jnp.where(
            came == 0, MR[0], jnp.where(came == 1, MR[1], jnp.where(came == 2, MR[2], MR[3]))
        )
        present = alab > 0.0
        upper = jnp.where(lrow <= lcol, 1.0, 0.0)
        upper_block = jnp.where(lrow // 32 == lcol // 32, upper, 0.0).astype(bf16)
        upper = upper.astype(bf16)
        ones = jnp.ones((LANES, LANES), bf16)
        present_f = jnp.where(present, 1.0, 0.0)
        arank = jnp.dot(present_f.astype(bf16), upper_block, preferred_element_type=f32) - 1.0
        arank = jnp.where(present, arank, -5.0)
        vacant = label == 0
        ranks = []
        for t in range(STEPS):
            vacant = vacant | (leave_at == t)
            flag = jnp.where(vacant, 1.0, 0.0).astype(bf16)
            rank = jnp.dot(flag, upper, preferred_element_type=f32) - 1.0
            total = jnp.dot(flag, ones, preferred_element_type=f32)
            for r in range(SLOT_BLOCKS - 1):
                rank = rank + jnp.where(sub8 > r, total[r : r + 1, :], 0.0)
            ranks.append(jnp.where(vacant, rank, -1.0))
            count = jnp.sum(jnp.where(lane8 // 32 == t, present_f, 0.0), axis=1, keepdims=True)
            vacant = vacant & (rank >= count)

        acode = code_of(alab.astype(jnp.int32))
        turn(ranks + [acode, alab])
        LR[8:16, :] = acode
        hot_rows(SLOT_BLOCKS, 32)
        hot_columns(SLOT_BLOCKS, SLOT_BLOCKS + 1)
        AMSK[...] = jnp.broadcast_to(LT[:, 40:41], (LANES, LANES))

        group = lcol // 32
        alab_high, alab_low = split(alab)
        final = jnp.where(leave_at == STEPS, label, 0).astype(f32)
        nt = (((1,), (1,)), ((), ()))
        for r in range(SLOT_BLOCKS):
            mine = jnp.broadcast_to(LT[:, r : r + 1], (LANES, LANES))
            for t in range(1, STEPS):
                mine = jnp.where(group == t, LT[:, 8 * t + r : 8 * t + r + 1], mine)
            hot = jnp.where(mine == arank[0:1, :], 1.0, 0.0).astype(bf16)
            PLACE[r * LANES : (r + 1) * LANES, 0:LANES] = hot
            PLACE[r * LANES : (r + 1) * LANES, LANES : 2 * LANES] = hot
            placed = lax.dot_general(alab_high, hot, nt, preferred_element_type=f32)
            placed = placed + lax.dot_general(alab_low, hot, nt, preferred_element_type=f32)
            final = final + jnp.where(sub8 == r, placed, 0.0)
        c_out[...] = final.astype(jnp.int32) - 1

    def slope_z(tiles):
        height = tiles[0].shape[0]
        lane = lax.broadcasted_iota(jnp.int32, (height, LANES), 1)
        zero = jnp.zeros((height, LANES), f32)
        ahead = [pltpu.roll(v, LANES - 1, 1) for v in tiles] + [zero]
        behind = [zero] + [pltpu.roll(v, 1, 1) for v in tiles]
        return [
            jnp.where(lane == LANES - 1, ahead[q + 1], ahead[q])
            - jnp.where(lane == 0, behind[q], behind[q + 1])
            for q in range(nq)
        ]

    low_gate = jnp.where(has_lo, 1.0, 0.0).astype(f32)
    high_gate = jnp.where(has_hi, 1.0, 0.0).astype(f32)
    chunk = 256

    def gather(low_row, count):
        hot = OH[low_row : low_row + count, :]
        hot = jnp.concatenate([hot, hot], axis=1)
        PG[low_row : low_row + count, :] = jnp.dot(hot, PHL[...], preferred_element_type=f32)

    def scatter(m):
        hot = OHT[m * part : (m + 1) * part, :]
        hot = jnp.concatenate([hot, hot], axis=1)
        SRC[m * part : (m + 1) * part, :] = jnp.dot(hot, VHL[...], preferred_element_type=f32)

    def step(t, carry):
        limit = t.astype(f32)

        def bubbles(first):
            rows = slice(first, first + 16)
            radius, speed, rate = wall_update(R[rows, :], S[rows, :], A[rows, :], PG[rows, :])
            R[rows, :] = radius
            S[rows, :] = speed
            keep = MSK[rows, :]
            keep = jnp.concatenate([keep, keep], axis=1) >= limit
            high, low = split(jnp.where(keep, rate, 0.0))
            VHL[rows, :] = high
            VHL[ROWS + first : ROWS + first + 16, :] = low

        gather(0, chunk)
        for m in range(SLOTS // chunk):
            if m + 1 < SLOTS // chunk:
                gather((m + 1) * chunk, chunk)
            else:
                gather(SLOTS, ARRIVE)
            for b in range(chunk // 16):
                bubbles(m * chunk + b * 16)

        for k in range(DEP):
            row = pl.ds(jnp.maximum(slot_s[t, 0, 0, k], 0), 1)
            SB[t, 0, k : k + 1, :] = R[row, :]
            SB[t, 1, k : k + 1, :] = S[row, :]
            SB[t, 2, k : k + 1, :] = A[row, :]
        start(lambda d: dep_copy(t, d))

        @pl.when(t > 0)
        def _():
            wait_taken(lambda d: dep_copy(t - 1, d))

        def arrived(n, carry):
            for b in range(2):
                first = n * 32 + b * 16
                rows = pl.ds(pl.multiple_of(first, 16), 16)
                low_rows = pl.ds(pl.multiple_of(SLOTS + first, 16), 16)
                radius, speed, rate = wall_update(
                    AR[0, rows, :], AR[1, rows, :], AR[2, rows, :], PG[low_rows, :]
                )
                AR[0, rows, :] = radius
                AR[1, rows, :] = speed
                keep = AMSK[rows, :]
                keep = jnp.concatenate([keep, keep], axis=1) > 0.0
                high, low = split(jnp.where(keep, rate, 0.0))
                VHL[low_rows, :] = high
                VHL[pl.ds(pl.multiple_of(ROWS + SLOTS + first, 16), 16), :] = low
            return carry

        lax.fori_loop(0, t, arrived, 0)

        def flow_x(i, after, before):
            for q in range(nq):
                for jb in range(jbs):
                    rows, at = rows_of(jb)
                    ahead = PR[q, i + 1, at, :] if after is None else XR[t, 1, q, after, rows, :]
                    back = PR[q, i - 1, at, :] if before is None else XR[t, 0, q, before, rows, :]
                    VX[q, i + 1, rows, :] = VX[q, i + 1, rows, :] - half_gain * (ahead - back)

        def flow_z(i, jb):
            rows, at = rows_of(jb)
            slopes = slope_z([PR[q, i, at, :] for q in range(nq)])
            for q in range(nq):
                VZ[q, i, rows, :] = VZ[q, i, rows, :] - half_gain * slopes[q]

        def flow_y(i, jb):
            _, at = rows_of(jb)
            for q in range(nq):
                VY[q, i, at, :] = VY[q, i, at, :] - half_gain * (
                    PR[q, i, pl.ds(9 + jb * 16 + zero_row, 16), :]
                    - PR[q, i, pl.ds(7 + jb * 16 + zero_row, 16), :]
                )

        def side_rows(i):
            for q in range(nq):
                below, above = YR[t, 0, q, i], YR[t, 1, q, i]
                VY[q, i, 8:9, :] = VY[q, i, 8:9, :] + half_gain * below[1:2, :]
                VY[q, i, 7 + cy : 8 + cy, :] = (
                    VY[q, i, 7 + cy : 8 + cy, :] - half_gain * above[0:1, :]
                )
                VY[q, i, 7:8, :] = low_gate * (
                    VY[q, i, 7:8, :] - half_gain * (PR[q, i, 8:9, :] - below[0:1, :])
                )
                VY[q, i, 8 + cy : 9 + cy, :] = high_gate * (
                    VY[q, i, 8 + cy : 9 + cy, :]
                    - half_gain * (above[1:2, :] - PR[q, i, 7 + cy : 8 + cy, :])
                )


        def pressure(i, first):
            rows, at = slice(first, first + 8), slice(8 + first, 16 + first)
            slopes = slope_z([VZ[q, i, rows, :] for q in range(nq)])
            for q in range(nq):
                rise = (
                    (VX[q, i + 2, rows, :] - VX[q, i, rows, :])
                    + (
                        VY[q, i, pl.ds(9 + first + zero_row, 8), :]
                        - VY[q, i, pl.ds(7 + first + zero_row, 8), :]
                    )
                    + slopes[q]
                )
                row = column_row(i, q // 2, 0) + first
                col = (q % 2) * LANES
                PR[q, i, at, :] = (
                    PR[q, i, at, :] - half_gain * rise + SRC[row : row + 8, col : col + LANES]
                )

        order = [0, groups - 1] + list(range(1, groups - 1)) if groups > 1 else [0]
        early = order[:2]
        for k, m in enumerate(early):
            scatter(m)
            for i in range(k * cx // len(early), (k + 1) * cx // len(early)):
                if 0 < i < cx - 1:
                    flow_x(i, None, None)
                for jb in range(jbs):
                    flow_z(i, jb)
                    flow_y(i, jb)

        pl.when(t == 0)(plan)
        wait_taken(lambda d: p_copy(t, d), (2, 3))
        wait_sent(lambda d: p_copy(t, d), (2, 3))

        @pl.when(t > 0)
        def _():
            wait_taken(lambda d: p_copy(t, d), (0, 1))
            wait_sent(lambda d: p_copy(t, d), (0, 1))

        @pl.when(t == 0)
        def _():
            for d in range(2):
                for copy in first_copies(d):
                    copy.wait_recv()
                    copy.wait_send()
            wait_taken(v_copy, (2, 3))
            wait_sent(v_copy, (2, 3))
            for i in range(cx):
                for q in range(nq):
                    VY[q, i, 7:8, :] = VYR[0, q, i]
                    VY[q, i, 8 + cy : 9 + cy, :] = VYR[1, q, i]

        flow_x(-1, None, 0)
        flow_x(0, None, 1)
        flow_x(cx - 1, 0, None)
        flow_x(cx, 1, None)
        late = order[2:]
        ends = [0, 1, cx - 2, cx - 1]
        for m in late[:1]:
            scatter(m)
        for i in ends:
            side_rows(i)
            for first in range(0, cy, 8):
                pressure(i, first)

        @pl.when(t < STEPS - 1)
        def _():
            start(lambda d: p_copy(t + 1, d), (0, 1))

        for m in late[1:]:
            scatter(m)
        inner = [i for m in order for i in range(m * planes, (m + 1) * planes) if i not in ends]
        for i in inner:
            side_rows(i)
            for first in sorted({0, cy - 8}):
                pressure(i, first)

        @pl.when(t < STEPS - 1)
        def _():
            pack_rows(t + 1)
            start(lambda d: p_copy(t + 1, d), (2, 3))

        for i in inner:
            for first in range(8, cy - 8, 8):
                pressure(i, first)

        @pl.when(t < STEPS - 1)
        def _():
            split_all()

        return carry

    lax.fori_loop(0, STEPS, step, 0)

    wait_taken(lambda d: dep_copy(STEPS - 1, d))
    keep = AMSK[...] > 0.0
    for k in range(2):
        for w in range(2):
            col = slice(w * LANES, (w + 1) * LANES)
            high, low = split(jnp.where(keep, AR[k, :, col], 0.0))
            to = slice(k * BLOCK + w * LANES, k * BLOCK + (w + 1) * LANES)
            CAT[0:ARRIVE, to] = high
            CAT[ARRIVE : 2 * ARRIVE, to] = low

    def finish(m, carry):
        rows = pl.ds(pl.multiple_of(m * LANES, LANES), LANES)
        placed = jnp.dot(PLACE[rows, :], CAT[...], preferred_element_type=f32)
        keep = MSK[rows, :]
        keep = jnp.concatenate([keep, keep], axis=1) >= float(STEPS)
        R[rows, :] = jnp.where(keep, R[rows, :], 0.0) + placed[:, :BLOCK]
        S[rows, :] = (1.0 / time_step) * (jnp.where(keep, S[rows, :], 0.0) + placed[:, BLOCK:])
        return carry

    lax.fori_loop(0, SLOT_BLOCKS, finish, 0)
    wait_sent(meta_copy)
    for t in range(STEPS):
        wait_sent(lambda d, t=t: dep_copy(t, d))


def write_out(p, vx, vy, vz, r, s, c, p_out, v_out, r_out, s_out, c_out, sems):
    _, cx, cy, nz = v_out.shape
    pairs = [(r, r_out), (s, s_out), (c, c_out)]
    for q in range(nz // LANES):
        lanes = pl.ds(q * LANES, LANES)
        pairs.append((vx.at[q, pl.ds(1, cx), :, :], v_out.at[0, :, :, lanes]))
        pairs.append((vy.at[q, :, pl.ds(8, cy), :], v_out.at[1, :, :, lanes]))
        pairs.append((vz.at[q], v_out.at[2, :, :, lanes]))
        pairs.append((p.at[q, :, pl.ds(8, cy), :], p_out.at[:, :, lanes]))
    copies = [pltpu.make_async_copy(a, b, sems.at[k]) for k, (a, b) in enumerate(pairs)]
    for copy in copies:
        copy.start()
    for copy in copies:
        copy.wait()


def on_device(
    pressure, velocity, stretch, rest_radius, wall_speed, block_cells, depart_slot, depart_way
):
    cx, cy, nz = pressure.shape
    nq = nz // LANES
    ncol = 2 * cx * cy
    vmem = pl.BlockSpec(memory_space=pltpu.VMEM)
    hbm = pl.BlockSpec(memory_space=pl.ANY)
    dma = pltpu.SemaphoreType.DMA
    vmem_out = pltpu.VMEM
    parts = pl.pallas_call(
        kernel,
        out_shape=(
            vmem_out((nq, cx, cy + 16, LANES), f32),
            vmem_out((nq, cx + 2, cy, LANES), f32),
            vmem_out((nq, cx, cy + 16, LANES), f32),
            vmem_out((nq, cx, cy, LANES), f32),
            vmem_out((SLOTS, BLOCK), f32),
            vmem_out((SLOTS, BLOCK), f32),
            vmem_out((SLOT_BLOCKS, LANES), jnp.int32),
        ),
        in_specs=[pl.BlockSpec(memory_space=pltpu.HBM)] * 9,
        out_specs=(vmem,) * 7,
        scratch_shapes=[
            pltpu.VMEM((SLOTS, BLOCK), f32),
            pltpu.VMEM((3, ARRIVE, BLOCK), f32),
            pltpu.VMEM((STEPS, 3, DEP, BLOCK), f32),
            pltpu.VMEM((ROWS, ncol), bf16),
            pltpu.VMEM((ncol, ROWS), bf16),
            pltpu.VMEM((2 * ncol, BLOCK), bf16),
            pltpu.VMEM((ROWS, BLOCK), f32),
            pltpu.VMEM((2 * ROWS, BLOCK), bf16),
            pltpu.VMEM((ncol, BLOCK), f32),
            pltpu.VMEM((STEPS, 2, nq, 2, cy, LANES), f32),
            pltpu.VMEM((STEPS, 2, nq, cx, 2, LANES), f32),
            pltpu.VMEM((STEPS, 2, nq, cx, 2, LANES), f32),
            pltpu.VMEM((2, nq, cx, 1, LANES), f32),
            pltpu.VMEM((2, nq, cx, 1, LANES), f32),
            pltpu.VMEM((8, LANES), f32),
            pltpu.VMEM((4, 8, LANES), f32),
            pltpu.VMEM((SLOTS, LANES), f32),
            pltpu.VMEM((ARRIVE, LANES), f32),
            pltpu.VMEM((LANES, LANES), f32),
            pltpu.VMEM((16, LANES), f32),
            pltpu.VMEM((SLOTS, 2 * ARRIVE), bf16),
            pltpu.VMEM((2 * ARRIVE, 2 * BLOCK), bf16),
            pltpu.SMEM((SLOTS,), jnp.int32),
            pltpu.SMEM((STEPS, 1, 1, DEP), jnp.int32),
            pltpu.SMEM((STEPS, 1, 1, DEP), jnp.int32),
            pltpu.VMEM((SLOT_BLOCKS, LANES), jnp.int32),
            dma((4 * nq + 7,)),
            dma((4,)),
            dma((4,)),
            dma((STEPS, 4)),
            dma((STEPS, 4)),
            dma((4,)),
            dma((4,)),
            dma((STEPS, 4)),
            dma((STEPS, 4)),
            dma((2, 2, nq)),
            dma((2, 2, nq)),
        ],
        compiler_params=pltpu.CompilerParams(
            collective_id=0, has_side_effects=True, vmem_limit_bytes=36 * 2**20
        ),
        cost_estimate=pl.CostEstimate(
            flops=10 * 2**30, bytes_accessed=13 * 2**20, transcendentals=2**22
        ),
    )(
        *(
            pltpu.with_memory_space_constraint(value, pltpu.HBM)
            for value in (
                block_cells,
                depart_slot,
                depart_way,
                block_cells.reshape(SLOT_BLOCKS, LANES),
                pressure,
                velocity,
                stretch,
                rest_radius,
                wall_speed,
            )
        )
    )
    parts = [pltpu.with_memory_space_constraint(part, pltpu.VMEM) for part in parts]
    p, v, r, s, c = pl.pallas_call(
        write_out,
        out_shape=(
            jax.ShapeDtypeStruct(pressure.shape, f32),
            jax.ShapeDtypeStruct(velocity.shape, f32),
            jax.ShapeDtypeStruct(stretch.shape, f32),
            jax.ShapeDtypeStruct(stretch.shape, f32),
            jax.ShapeDtypeStruct((SLOT_BLOCKS, LANES), jnp.int32),
        ),
        in_specs=[vmem] * 7,
        out_specs=(hbm,) * 5,
        scratch_shapes=[dma((4 * nq + 3,))],
        compiler_params=pltpu.CompilerParams(vmem_limit_bytes=4 * 2**20),
        cost_estimate=pl.CostEstimate(flops=0, bytes_accessed=13 * 2**20, transcendentals=0),
    )(*parts)
    return p, v, r, s, c.reshape(-1)


def solution(mesh):
    placed = (
        P("gx", "gy", None),
        P(None, "gx", "gy", None),
        P(("gx", "gy"), None),
        P(("gx", "gy"), None),
        P(("gx", "gy"), None),
        P(("gx", "gy")),
        P(None, "gx", "gy", None),
        P(None, "gx", "gy", None),
    )
    return jax.shard_map(
        on_device,
        mesh=mesh,
        in_specs=placed,
        out_specs=(
            P("gx", "gy", None),
            P(None, "gx", "gy", None),
            P(("gx", "gy"), None),
            P(("gx", "gy"), None),
            P(("gx", "gy")),
        ),
        check_vma=False,
    )
```

```python
import functools
import math

import jax
import jax.numpy as jnp
from jax import lax
from jax.experimental import pallas as pl
from jax.experimental.pallas import tpu as pltpu
from jax.sharding import PartitionSpec as P

MESH = pl.DeviceIdType.MESH
f32 = jnp.float32
bf16 = jnp.bfloat16

STEPS = 4
DEP = 8
SLOTS = 1024
BLOCK = 256
LANES = 128
ARRIVE = STEPS * 4 * DEP
ROWS = SLOTS + ARRIVE
SLOT_BLOCKS = SLOTS // LANES
WAY_OF = (1, 0, 3, 2)

time_step = 0.04
half_gain = 0.2
source_scale = 0.004 * 12.566370614359172
exponent = 4.2
inv_ln2 = 1.0 / math.log(2.0)


def split(value):
    high = value.astype(bf16)
    return high, (value - high.astype(f32)).astype(bf16)


def wall_update(radius, shift, level, pressure):
    mach = (0.05 / time_step) * shift
    one_less = 1.0 - mach
    divisor = one_less * radius
    inverse = pl.reciprocal(divisor, approx=True)
    inverse = inverse * (2.0 - divisor * inverse)
    inv_radius = inverse * one_less
    wall = jnp.exp2(level - (exponent * inv_ln2) * jnp.log(radius))
    squared = time_step * time_step
    excess = (
        wall
        - (0.2 * squared + (0.08 * time_step) * shift) * inv_radius
        - (squared + squared * pressure)
    )
    driving = (1.0 + mach) * excess - (1.5 - 0.5 * mach) * (shift * shift)
    shift = shift + driving * inverse
    radius = radius + shift
    return radius, shift, (source_scale / time_step) * (radius * radius) * shift


def kernel(
    cells_h, slot_h, way_h, cells_b, press, vel, stretch, rest, speed0,
    PR, VX, VY, VZ, r_out, s_out, c_out,
    R, S, A, AR, SB, DB, OH, OHT, PHL, PG, VHL, SRC, XR, YS, YR, VYS, VYR,
    MT, MR, MSK, AMSK, LT, LR, PLACE, CAT, cells_s, slot_s, way_s, cells_v,
    in_sem, meta_s, meta_r, xs, xr, vs, vr, ds_, dr, fs, fr,
):
    _, cx, cy, nz = vel.shape
    nq = nz // LANES
    half = cx * cy
    ncol = 2 * half
    jbs = cy // 16
    part = min(256, ncol)
    planes = part // (2 * cy)
    groups = cx // planes
    shift = (planes * cy).bit_length() - 1
    zero_row = lax.axis_index("gx") // 4096
    gx, gy = lax.axis_index("gx"), lax.axis_index("gy")
    ngx, ngy = lax.axis_size("gx"), lax.axis_size("gy")
    has_lo, has_hi = gy > 0, gy < ngy - 1
    targets = (
        (lax.rem(gx + 1, ngx), gy),
        (lax.rem(gx + ngx - 1, ngx), gy),
        (gx, lax.rem(gy + 1, ngy)),
        (gx, lax.rem(gy + ngy - 1, ngy)),
    )
    sends = (None, None, has_hi, has_lo)
    takes = (None, None, has_lo, has_hi)

    def under(flag, action):
        if flag is None:
            action()
        else:
            pl.when(flag)(action)

    barrier = pltpu.get_barrier_semaphore()
    for d in range(4):
        under(
            sends[d],
            lambda d=d: pl.semaphore_signal(
                barrier, inc=1, device_id=targets[d], device_id_type=MESH
            ),
        )

    inputs = [(cells_h, cells_s), (slot_h, slot_s), (way_h, way_s), (cells_b, cells_v)]
    for q in range(nq):
        inputs.append((press.at[:, :, pl.ds(q * LANES, LANES)], PR.at[q, :, pl.ds(8, cy), :]))
    own = pl.ds(0, SLOTS)
    inputs.append((rest, A.at[own, :]))
    inputs.append((stretch, R.at[own, :]))
    inputs.append((speed0, S.at[own, :]))
    for comp in range(3):
        for q in range(nq):
            dst = (
                VX.at[q, pl.ds(1, cx), :, :],
                VY.at[q, :, pl.ds(8, cy), :],
                VZ.at[q],
            )[comp]
            inputs.append((vel.at[comp, :, :, pl.ds(q * LANES, LANES)], dst))
    loads = [pltpu.make_async_copy(a, b, in_sem.at[k]) for k, (a, b) in enumerate(inputs)]
    for load in loads:
        load.start()
    small_loads, loads = loads[:4], loads[4:]

    @pl.when(jnp.logical_not(has_lo))
    def _():
        MR[2] = jnp.zeros((8, LANES), f32)
        YR[:, 0] = jnp.zeros(YR.shape[:1] + YR.shape[2:], f32)
        VYR[0] = jnp.zeros(VYR.shape[1:], f32)

    @pl.when(jnp.logical_not(has_hi))
    def _():
        MR[3] = jnp.zeros((8, LANES), f32)
        YR[:, 1] = jnp.zeros(YR.shape[:1] + YR.shape[2:], f32)
        VYR[1] = jnp.zeros(VYR.shape[1:], f32)

    edge_rows = jnp.zeros((nq, cx, 8, LANES), f32)
    PR[:, :, 0:8, :] = edge_rows
    PR[:, :, 8 + cy : 16 + cy, :] = edge_rows
    empty = jnp.zeros((ARRIVE, BLOCK), f32)
    R[SLOTS:ROWS, :] = empty + 1.0
    S[SLOTS:ROWS, :] = empty
    A[SLOTS:ROWS, :] = empty
    MSK[SLOTS:ROWS, :] = jnp.full((ARRIVE, LANES), -1.0, f32)
    OHT[:, SLOTS:ROWS] = jnp.zeros((ncol, ARRIVE), bf16)
    OH[SLOTS:ROWS, :] = jnp.zeros((ARRIVE, ncol), bf16)
    pl.semaphore_wait(barrier, 2 + has_lo.astype(jnp.int32) + has_hi.astype(jnp.int32))

    def remote(src, dst, send_sem, recv_sem, d):
        return pltpu.make_async_remote_copy(
            src_ref=src, dst_ref=dst, send_sem=send_sem, recv_sem=recv_sem,
            device_id=targets[d], device_id_type=MESH,
        )

    def meta_copy(d):
        return remote(MT, MR.at[d], meta_s.at[d], meta_r.at[d], d)

    def p_copy(t, d):
        if d < 2:
            src = PR.at[:, pl.ds((cx - 2, 0)[d], 2), pl.ds(8, cy), :]
            return remote(src, XR.at[t, d], xs.at[t, d], xr.at[t, d], d)
        return remote(YS.at[t, 3 - d], YR.at[t, d - 2], xs.at[t, d], xr.at[t, d], d)

    def first_copies(d):
        side = (cx - 2, 0)[d]
        for q in range(nq):
            lanes = pl.ds(q * LANES, LANES)
            yield remote(
                press.at[pl.ds(side, 2), :, lanes], XR.at[0, d, q], fs.at[0, d, q], fr.at[0, d, q], d
            )
        for q in range(nq):
            lanes = pl.ds(q * LANES, LANES)
            yield remote(
                vel.at[0, pl.ds((cx - 1, 0)[d], 1), :, lanes],
                VX.at[q, pl.ds((0, cx + 1)[d], 1), :, :],
                fs.at[1, d, q],
                fr.at[1, d, q],
                d,
            )

    def v_copy(d):
        return remote(VYS.at[3 - d], VYR.at[d - 2], vs.at[d], vr.at[d], d)

    def dep_copy(t, d):
        return remote(
            SB.at[t], AR.at[:, pl.ds(t * 32 + d * DEP, DEP), :], ds_.at[t, d], dr.at[t, d], d
        )

    def start(make, ways=(0, 1, 2, 3)):
        for d in ways:
            under(sends[d], lambda d=d: make(d).start())

    def wait_sent(make, ways=(0, 1, 2, 3)):
        for d in ways:
            under(sends[d], lambda d=d: make(d).wait_send())

    def wait_taken(make, ways=(0, 1, 2, 3)):
        for d in ways:
            under(takes[d], lambda d=d: make(d).wait_recv())

    for d in range(2):
        for copy in first_copies(d):
            copy.start()
    for load in small_loads:
        load.wait()

    lane8 = lax.broadcasted_iota(jnp.int32, (8, LANES), 1)
    sub8 = lax.broadcasted_iota(jnp.int32, (8, LANES), 0)
    slot_id = sub8 * LANES + lane8
    label = cells_v[...] + 1
    leave_at = jnp.where(label > 0, STEPS, -1)
    entry_of = (lane8 // 32) * DEP + lane8 % DEP
    wanted = (lane8 // DEP) % 4
    wanted = jnp.where(wanted < 2, 1 - wanted, 5 - wanted)
    meta = jnp.zeros((8, LANES), jnp.int32)
    for e in range(STEPS * DEP):
        slot = slot_s[e // DEP, 0, 0, e % DEP]
        moved = jnp.where(slot >= 0, cells_s[jnp.maximum(slot, 0)] + 1, 0)
        meta = jnp.where((entry_of == e) & (wanted == way_s[e // DEP, 0, 0, e % DEP]), moved, meta)
        leave_at = jnp.where(slot_id == slot, e // DEP, leave_at)
    MT[...] = meta.astype(f32)

    start(meta_copy)

    def pack_rows(t):
        for i in range(cx):
            for q in range(nq):
                YS[t, 0, q, i] = PR[q, i, 8:10, :]
                YS[t, 1, q, i] = PR[q, i, 6 + cy : 8 + cy, :]

    def column_row(i, h, jb):
        return (i // planes) * part + (h * planes + i % planes) * cy + jb * 16

    def keep_parts(i, jb, q, value):
        high, low = split(value)
        row = column_row(i, q // 2, jb)
        col = (q % 2) * 2 * LANES
        PHL[row : row + 16, col : col + LANES] = high
        PHL[row : row + 16, col + LANES : col + 2 * LANES] = low

    def rows_of(jb):
        return slice(jb * 16, jb * 16 + 16), slice(8 + jb * 16, 24 + jb * 16)

    def split_all():
        for i in range(cx):
            for jb in range(jbs):
                for q in range(nq):
                    keep_parts(i, jb, q, PR[q, i, rows_of(jb)[1], :])

    for k in range(nq):
        loads[k].wait()
    pack_rows(0)
    start(lambda d: p_copy(0, d), (2, 3))
    split_all()

    lrow = lax.broadcasted_iota(jnp.int32, (LANES, LANES), 0)
    lcol = lax.broadcasted_iota(jnp.int32, (LANES, LANES), 1)
    wide = lax.broadcasted_iota(jnp.int32, (16, ncol), 1).astype(f32)

    def code_of(lab):
        cell = lab - 1
        place = cell >> 1
        row = (place >> shift) * part + (cell & 1) * (planes * cy)
        return jnp.where(lab > 0, row + (place & (planes * cy - 1)), -1).astype(f32)

    def turn(stack):
        stack = stack + [jnp.zeros((8, LANES), f32)] * (16 - len(stack))
        LT[...] = jnp.concatenate(stack, axis=0).T

    def hot_rows(r, at):
        def body(m, carry):
            rows = pl.ds(pl.multiple_of(m * 16, 16), 16)
            hot = jnp.where(LT[rows, at : at + 1] == wide, 1.0, 0.0).astype(bf16)
            OH[pl.ds(pl.multiple_of(r * LANES + m * 16, 16), 16), :] = hot
            return carry

        lax.fori_loop(0, LANES // 16, body, 0, unroll=4)

    def hot_columns(first, last):
        def body(m, carry):
            ident = (lrow + m * LANES).astype(f32)
            rows = pl.ds(pl.multiple_of(m * LANES, LANES), LANES)
            for r in range(first, last):
                hot = jnp.where(ident == LR[r : r + 1, :], 1.0, 0.0).astype(bf16)
                OHT[rows, r * LANES : (r + 1) * LANES] = hot
            return carry

        lax.fori_loop(0, ncol // LANES, body, 0)

    code = code_of(label)
    turn([code, leave_at.astype(f32)])
    LR[0:8, :] = code
    for r in range(SLOT_BLOCKS):
        hot_rows(r, r)
    for r in range(SLOT_BLOCKS):
        MSK[r * LANES : (r + 1) * LANES, :] = jnp.broadcast_to(
            LT[:, 8 + r : 9 + r], (LANES, LANES)
        )
    hot_columns(0, SLOT_BLOCKS)

    for k in range(nq + 3, nq + 3 + 3 * nq):
        loads[k].wait()

    def pack_flow(i, carry):
        for q in range(nq):
            VYS[0, q, i] = VY[q, i, 8:9, :]
            VYS[1, q, i] = VY[q, i, 7 + cy : 8 + cy, :]
        return carry

    lax.fori_loop(0, cx, pack_flow, 0, unroll=4)
    start(v_copy, (2, 3))

    for k in range(nq, nq + 3):
        loads[k].wait()

    def first_state(n, carry):
        rows = pl.ds(pl.multiple_of(n * 16, 16), 16)
        rest_now = A[rows, :]
        R[rows, :] = R[rows, :] * rest_now
        S[rows, :] = time_step * S[rows, :]
        A[rows, :] = inv_ln2 * (
            jnp.log((time_step * time_step) * (1.0 + 0.2 / rest_now))
            + exponent * jnp.log(rest_now)
        )
        return carry

    lax.fori_loop(0, SLOTS // 16, first_state, 0, unroll=4)
    def plan():
        wait_taken(meta_copy)
        came = (lane8 // DEP) % 4
        alab = jnp.where(
            came == 0, MR[0], jnp.where(came == 1, MR[1], jnp.where(came == 2, MR[2], MR[3]))
        )
        present = alab > 0.0
        upper = jnp.where(lrow <= lcol, 1.0, 0.0)
        upper_block = jnp.where(lrow // 32 == lcol // 32, upper, 0.0).astype(bf16)
        upper = upper.astype(bf16)
        ones = jnp.ones((LANES, LANES), bf16)
        present_f = jnp.where(present, 1.0, 0.0)
        arank = jnp.dot(present_f.astype(bf16), upper_block, preferred_element_type=f32) - 1.0
        arank = jnp.where(present, arank, -5.0)
        vacant = label == 0
        ranks = []
        for t in range(STEPS):
            vacant = vacant | (leave_at == t)
            flag = jnp.where(vacant, 1.0, 0.0).astype(bf16)
            rank = jnp.dot(flag, upper, preferred_element_type=f32) - 1.0
            total = jnp.dot(flag, ones, preferred_element_type=f32)
            for r in range(SLOT_BLOCKS - 1):
                rank = rank + jnp.where(sub8 > r, total[r : r + 1, :], 0.0)
            ranks.append(jnp.where(vacant, rank, -1.0))
            count = jnp.sum(jnp.where(lane8 // 32 == t, present_f, 0.0), axis=1, keepdims=True)
            vacant = vacant & (rank >= count)

        acode = code_of(alab.astype(jnp.int32))
        turn(ranks + [acode, alab])
        LR[8:16, :] = acode
        hot_rows(SLOT_BLOCKS, 32)
        hot_columns(SLOT_BLOCKS, SLOT_BLOCKS + 1)
        AMSK[...] = jnp.broadcast_to(LT[:, 40:41], (LANES, LANES))

        group = lcol // 32
        alab_high, alab_low = split(alab)
        final = jnp.where(leave_at == STEPS, label, 0).astype(f32)
        nt = (((1,), (1,)), ((), ()))
        for r in range(SLOT_BLOCKS):
            mine = jnp.broadcast_to(LT[:, r : r + 1], (LANES, LANES))
            for t in range(1, STEPS):
                mine = jnp.where(group == t, LT[:, 8 * t + r : 8 * t + r + 1], mine)
            hot = jnp.where(mine == arank[0:1, :], 1.0, 0.0).astype(bf16)
            PLACE[r * LANES : (r + 1) * LANES, 0:LANES] = hot
            PLACE[r * LANES : (r + 1) * LANES, LANES : 2 * LANES] = hot
            placed = lax.dot_general(alab_high, hot, nt, preferred_element_type=f32)
            placed = placed + lax.dot_general(alab_low, hot, nt, preferred_element_type=f32)
            final = final + jnp.where(sub8 == r, placed, 0.0)
        c_out[...] = final.astype(jnp.int32) - 1

    def slope_z(tiles):
        height = tiles[0].shape[0]
        lane = lax.broadcasted_iota(jnp.int32, (height, LANES), 1)
        zero = jnp.zeros((height, LANES), f32)
        ahead = [pltpu.roll(v, LANES - 1, 1) for v in tiles] + [zero]
        behind = [zero] + [pltpu.roll(v, 1, 1) for v in tiles]
        return [
            jnp.where(lane == LANES - 1, ahead[q + 1], ahead[q])
            - jnp.where(lane == 0, behind[q], behind[q + 1])
            for q in range(nq)
        ]

    low_gate = jnp.where(has_lo, 1.0, 0.0).astype(f32)
    high_gate = jnp.where(has_hi, 1.0, 0.0).astype(f32)

    def halves(w):
        return slice(w * LANES, (w + 1) * LANES), slice(2 * w * LANES, 2 * (w + 1) * LANES)

    def gather(w):
        narrow, pair = halves(w)
        both = jnp.dot(OH[...], PHL[:, pair], preferred_element_type=f32)
        PG[:, narrow] = both[:, :LANES] + both[:, LANES:]

    def scatter(w):
        narrow, pair = halves(w)
        both = jnp.dot(OHT[...], VHL[:, pair], preferred_element_type=f32)
        SRC[:, narrow] = both[:, :LANES] + both[:, LANES:]

    def take_arrivals(t):
        wait_taken(lambda d: dep_copy(t, d))
        rows = pl.ds(pl.multiple_of(t * 32, 32), 32)
        to = pl.ds(pl.multiple_of(SLOTS + t * 32, 32), 32)
        R[to, :] = AR[0, rows, :]
        S[to, :] = AR[1, rows, :]
        A[to, :] = AR[2, rows, :]
        MSK[to, :] = jnp.where(AMSK[rows, :] > 0.0, 2.0 * STEPS, -1.0)

    def step(t, carry):
        limit = t.astype(f32)

        def bubbles(first, w):
            rows = slice(first, first + 16)
            col = halves(w)[0]
            radius, speed, rate = wall_update(R[rows, col], S[rows, col], A[rows, col], PG[rows, col])
            R[rows, col] = radius
            S[rows, col] = speed
            high, low = split(jnp.where(MSK[rows, :] >= limit, rate, 0.0))
            VHL[rows, 2 * w * LANES : (2 * w + 1) * LANES] = high
            VHL[rows, (2 * w + 1) * LANES : (2 * w + 2) * LANES] = low

        for k in range(DEP):
            slot = jnp.maximum(slot_s[t, 0, 0, k], 0)
            cell = jnp.maximum(cells_s[slot], 0)
            place = cell >> 1
            row = pl.ds(slot, 1)
            DB[0, k : k + 1, :] = R[row, :]
            DB[1, k : k + 1, :] = S[row, :]
            DB[2, k : k + 1, :] = A[row, :]
            for w in range(2):
                DB[3, k : k + 1, halves(w)[0]] = PR[
                    2 * (cell & 1) + w,
                    place >> (cy.bit_length() - 1),
                    pl.ds(8 + (place & (cy - 1)), 1),
                    :,
                ]
        radius, speed, _ = wall_update(DB[0], DB[1], DB[2], DB[3])
        SB[t, 0] = radius
        SB[t, 1] = speed
        SB[t, 2] = DB[2]
        start(lambda d: dep_copy(t, d))

        @pl.when(t > 0)
        def _():
            take_arrivals(t - 1)

        gather(0)
        gather(1)
        for first in range(0, ROWS, 16):
            bubbles(first, 0)
        scatter(0)
        for first in range(0, ROWS, 16):
            bubbles(first, 1)
        scatter(1)

        def flow_x(i, after, before):
            for q in range(nq):
                for jb in range(jbs):
                    rows, at = rows_of(jb)
                    ahead = PR[q, i + 1, at, :] if after is None else XR[t, 1, q, after, rows, :]
                    back = PR[q, i - 1, at, :] if before is None else XR[t, 0, q, before, rows, :]
                    VX[q, i + 1, rows, :] = VX[q, i + 1, rows, :] - half_gain * (ahead - back)

        def flow_z(i, jb):
            rows, at = rows_of(jb)
            slopes = slope_z([PR[q, i, at, :] for q in range(nq)])
            for q in range(nq):
                VZ[q, i, rows, :] = VZ[q, i, rows, :] - half_gain * slopes[q]

        def flow_y(i, jb):
            _, at = rows_of(jb)
            for q in range(nq):
                VY[q, i, at, :] = VY[q, i, at, :] - half_gain * (
                    PR[q, i, pl.ds(9 + jb * 16 + zero_row, 16), :]
                    - PR[q, i, pl.ds(7 + jb * 16 + zero_row, 16), :]
                )

        def side_rows(i):
            for q in range(nq):
                below, above = YR[t, 0, q, i], YR[t, 1, q, i]
                VY[q, i, 8:9, :] = VY[q, i, 8:9, :] + half_gain * below[1:2, :]
                VY[q, i, 7 + cy : 8 + cy, :] = (
                    VY[q, i, 7 + cy : 8 + cy, :] - half_gain * above[0:1, :]
                )
                VY[q, i, 7:8, :] = low_gate * (
                    VY[q, i, 7:8, :] - half_gain * (PR[q, i, 8:9, :] - below[0:1, :])
                )
                VY[q, i, 8 + cy : 9 + cy, :] = high_gate * (
                    VY[q, i, 8 + cy : 9 + cy, :]
                    - half_gain * (above[1:2, :] - PR[q, i, 7 + cy : 8 + cy, :])
                )


        def pressure(i, first):
            rows, at = slice(first, first + 8), slice(8 + first, 16 + first)
            slopes = slope_z([VZ[q, i, rows, :] for q in range(nq)])
            for q in range(nq):
                rise = (
                    (VX[q, i + 2, rows, :] - VX[q, i, rows, :])
                    + (
                        VY[q, i, pl.ds(9 + first + zero_row, 8), :]
                        - VY[q, i, pl.ds(7 + first + zero_row, 8), :]
                    )
                    + slopes[q]
                )
                row = column_row(i, q // 2, 0) + first
                col = (q % 2) * LANES
                PR[q, i, at, :] = (
                    PR[q, i, at, :] - half_gain * rise + SRC[row : row + 8, col : col + LANES]
                )

        for i in range(cx):
            if 0 < i < cx - 1:
                flow_x(i, None, None)
            for jb in range(jbs):
                flow_z(i, jb)
                flow_y(i, jb)

        pl.when(t == 0)(plan)
        wait_taken(lambda d: p_copy(t, d), (2, 3))
        wait_sent(lambda d: p_copy(t, d), (2, 3))

        @pl.when(t > 0)
        def _():
            wait_taken(lambda d: p_copy(t, d), (0, 1))
            wait_sent(lambda d: p_copy(t, d), (0, 1))

        @pl.when(t == 0)
        def _():
            for d in range(2):
                for copy in first_copies(d):
                    copy.wait_recv()
                    copy.wait_send()
            wait_taken(v_copy, (2, 3))
            wait_sent(v_copy, (2, 3))
            for i in range(cx):
                for q in range(nq):
                    VY[q, i, 7:8, :] = VYR[0, q, i]
                    VY[q, i, 8 + cy : 9 + cy, :] = VYR[1, q, i]

        flow_x(-1, None, 0)
        flow_x(0, None, 1)
        flow_x(cx - 1, 0, None)
        flow_x(cx, 1, None)
        ends = [0, 1, cx - 2, cx - 1]
        for i in ends:
            side_rows(i)
            for first in range(0, cy, 8):
                pressure(i, first)

        @pl.when(t < STEPS - 1)
        def _():
            start(lambda d: p_copy(t + 1, d), (0, 1))

        inner = range(2, cx - 2)
        for i in inner:
            side_rows(i)
            for first in sorted({0, cy - 8}):
                pressure(i, first)

        @pl.when(t < STEPS - 1)
        def _():
            pack_rows(t + 1)
            start(lambda d: p_copy(t + 1, d), (2, 3))

        for i in inner:
            for first in range(8, cy - 8, 8):
                pressure(i, first)

        @pl.when(t < STEPS - 1)
        def _():
            split_all()

        return carry

    lax.fori_loop(0, STEPS, step, 0)

    take_arrivals(STEPS - 1)
    keep = AMSK[...] > 0.0
    for k, state in enumerate((R, S)):
        for w in range(2):
            high, low = split(jnp.where(keep, state[SLOTS:ROWS, halves(w)[0]], 0.0))
            to = slice(k * BLOCK + w * LANES, k * BLOCK + (w + 1) * LANES)
            CAT[0:ARRIVE, to] = high
            CAT[ARRIVE : 2 * ARRIVE, to] = low

    def finish(m, carry):
        rows = pl.ds(pl.multiple_of(m * LANES, LANES), LANES)
        placed = jnp.dot(PLACE[rows, :], CAT[...], preferred_element_type=f32)
        keep = MSK[rows, :]
        keep = jnp.concatenate([keep, keep], axis=1) >= float(STEPS)
        r_out[rows, :] = jnp.where(keep, R[rows, :], 0.0) + placed[:, :BLOCK]
        s_out[rows, :] = (1.0 / time_step) * (jnp.where(keep, S[rows, :], 0.0) + placed[:, BLOCK:])
        return carry

    lax.fori_loop(0, SLOT_BLOCKS, finish, 0)
    wait_sent(meta_copy)
    for t in range(STEPS):
        wait_sent(lambda d, t=t: dep_copy(t, d))


def write_out(p, vx, vy, vz, r, s, c, p_out, v_out, r_out, s_out, c_out, sems):
    _, cx, cy, nz = v_out.shape
    pairs = [(r, r_out), (s, s_out), (c, c_out)]
    for q in range(nz // LANES):
        lanes = pl.ds(q * LANES, LANES)
        pairs.append((vx.at[q, pl.ds(1, cx), :, :], v_out.at[0, :, :, lanes]))
        pairs.append((vy.at[q, :, pl.ds(8, cy), :], v_out.at[1, :, :, lanes]))
        pairs.append((vz.at[q], v_out.at[2, :, :, lanes]))
        pairs.append((p.at[q, :, pl.ds(8, cy), :], p_out.at[:, :, lanes]))
    copies = [pltpu.make_async_copy(a, b, sems.at[k]) for k, (a, b) in enumerate(pairs)]
    for copy in copies:
        copy.start()
    for copy in copies:
        copy.wait()


def on_device(
    pressure, velocity, stretch, rest_radius, wall_speed, block_cells, depart_slot, depart_way
):
    cx, cy, nz = pressure.shape
    nq = nz // LANES
    ncol = 2 * cx * cy
    vmem = pl.BlockSpec(memory_space=pltpu.VMEM)
    hbm = pl.BlockSpec(memory_space=pl.ANY)
    dma = pltpu.SemaphoreType.DMA
    vmem_out = pltpu.VMEM
    parts = pl.pallas_call(
        kernel,
        out_shape=(
            vmem_out((nq, cx, cy + 16, LANES), f32),
            vmem_out((nq, cx + 2, cy, LANES), f32),
            vmem_out((nq, cx, cy + 16, LANES), f32),
            vmem_out((nq, cx, cy, LANES), f32),
            vmem_out((SLOTS, BLOCK), f32),
            vmem_out((SLOTS, BLOCK), f32),
            vmem_out((SLOT_BLOCKS, LANES), jnp.int32),
        ),
        in_specs=[pl.BlockSpec(memory_space=pltpu.HBM)] * 9,
        out_specs=(vmem,) * 7,
        scratch_shapes=[
            pltpu.VMEM((ROWS, BLOCK), f32),
            pltpu.VMEM((ROWS, BLOCK), f32),
            pltpu.VMEM((ROWS, BLOCK), f32),
            pltpu.VMEM((3, ARRIVE, BLOCK), f32),
            pltpu.VMEM((STEPS, 3, DEP, BLOCK), f32),
            pltpu.VMEM((4, DEP, BLOCK), f32),
            pltpu.VMEM((ROWS, ncol), bf16),
            pltpu.VMEM((ncol, ROWS), bf16),
            pltpu.VMEM((ncol, 2 * BLOCK), bf16),
            pltpu.VMEM((ROWS, BLOCK), f32),
            pltpu.VMEM((ROWS, 2 * BLOCK), bf16),
            pltpu.VMEM((ncol, BLOCK), f32),
            pltpu.VMEM((STEPS, 2, nq, 2, cy, LANES), f32),
            pltpu.VMEM((STEPS, 2, nq, cx, 2, LANES), f32),
            pltpu.VMEM((STEPS, 2, nq, cx, 2, LANES), f32),
            pltpu.VMEM((2, nq, cx, 1, LANES), f32),
            pltpu.VMEM((2, nq, cx, 1, LANES), f32),
            pltpu.VMEM((8, LANES), f32),
            pltpu.VMEM((4, 8, LANES), f32),
            pltpu.VMEM((ROWS, LANES), f32),
            pltpu.VMEM((ARRIVE, LANES), f32),
            pltpu.VMEM((LANES, LANES), f32),
            pltpu.VMEM((16, LANES), f32),
            pltpu.VMEM((SLOTS, 2 * ARRIVE), bf16),
            pltpu.VMEM((2 * ARRIVE, 2 * BLOCK), bf16),
            pltpu.SMEM((SLOTS,), jnp.int32),
            pltpu.SMEM((STEPS, 1, 1, DEP), jnp.int32),
            pltpu.SMEM((STEPS, 1, 1, DEP), jnp.int32),
            pltpu.VMEM((SLOT_BLOCKS, LANES), jnp.int32),
            dma((4 * nq + 7,)),
            dma((4,)),
            dma((4,)),
            dma((STEPS, 4)),
            dma((STEPS, 4)),
            dma((4,)),
            dma((4,)),
            dma((STEPS, 4)),
            dma((STEPS, 4)),
            dma((2, 2, nq)),
            dma((2, 2, nq)),
        ],
        compiler_params=pltpu.CompilerParams(
            collective_id=0, has_side_effects=True, vmem_limit_bytes=36 * 2**20
        ),
        cost_estimate=pl.CostEstimate(
            flops=10 * 2**30, bytes_accessed=13 * 2**20, transcendentals=2**22
        ),
    )(
        *(
            pltpu.with_memory_space_constraint(value, pltpu.HBM)
            for value in (
                block_cells,
                depart_slot,
                depart_way,
                block_cells.reshape(SLOT_BLOCKS, LANES),
                pressure,
                velocity,
                stretch,
                rest_radius,
                wall_speed,
            )
        )
    )
    parts = [pltpu.with_memory_space_constraint(part, pltpu.VMEM) for part in parts]
    p, v, r, s, c = pl.pallas_call(
        write_out,
        out_shape=(
            jax.ShapeDtypeStruct(pressure.shape, f32),
            jax.ShapeDtypeStruct(velocity.shape, f32),
            jax.ShapeDtypeStruct(stretch.shape, f32),
            jax.ShapeDtypeStruct(stretch.shape, f32),
            jax.ShapeDtypeStruct((SLOT_BLOCKS, LANES), jnp.int32),
        ),
        in_specs=[vmem] * 7,
        out_specs=(hbm,) * 5,
        scratch_shapes=[dma((4 * nq + 3,))],
        compiler_params=pltpu.CompilerParams(vmem_limit_bytes=4 * 2**20),
        cost_estimate=pl.CostEstimate(flops=0, bytes_accessed=13 * 2**20, transcendentals=0),
    )(*parts)
    return p, v, r, s, c.reshape(-1)


def solution(mesh):
    placed = (
        P("gx", "gy", None),
        P(None, "gx", "gy", None),
        P(("gx", "gy"), None),
        P(("gx", "gy"), None),
        P(("gx", "gy"), None),
        P(("gx", "gy")),
        P(None, "gx", "gy", None),
        P(None, "gx", "gy", None),
    )
    return jax.shard_map(
        on_device,
        mesh=mesh,
        in_specs=placed,
        out_specs=(
            P("gx", "gy", None),
            P(None, "gx", "gy", None),
            P(("gx", "gy"), None),
            P(("gx", "gy"), None),
            P(("gx", "gy")),
        ),
        check_vma=False,
    )
```

```python
import functools
import math

import jax
import jax.numpy as jnp
from jax import lax
from jax.experimental import pallas as pl
from jax.experimental.pallas import tpu as pltpu
from jax.sharding import PartitionSpec as P

MESH = pl.DeviceIdType.MESH
f32 = jnp.float32
bf16 = jnp.bfloat16

STEPS = 4
DEP = 8
SLOTS = 1024
BLOCK = 256
LANES = 128
ARRIVE = STEPS * 4 * DEP
ROWS = SLOTS + ARRIVE
SLOT_BLOCKS = SLOTS // LANES
WAY_OF = (1, 0, 3, 2)

time_step = 0.04
half_gain = 0.2
source_scale = 0.004 * 12.566370614359172
exponent = 4.2
inv_ln2 = 1.0 / math.log(2.0)


def split(value):
    high = value.astype(bf16)
    return high, (value - high.astype(f32)).astype(bf16)


def wall_update(radius, shift, level, pressure):
    mach = (0.05 / time_step) * shift
    one_less = 1.0 - mach
    divisor = one_less * radius
    inverse = pl.reciprocal(divisor, approx=True)
    inverse = inverse * (2.0 - divisor * inverse)
    inv_radius = inverse * one_less
    wall = jnp.exp2(level - (exponent * inv_ln2) * jnp.log(radius))
    squared = time_step * time_step
    excess = (
        wall
        - (0.2 * squared + (0.08 * time_step) * shift) * inv_radius
        - (squared + squared * pressure)
    )
    driving = (1.0 + mach) * excess - (1.5 - 0.5 * mach) * (shift * shift)
    shift = shift + driving * inverse
    radius = radius + shift
    return radius, shift, (source_scale / time_step) * (radius * radius) * shift


def kernel(
    cells_h, slot_h, way_h, cells_b, press, vel, stretch, rest, speed0,
    PR, VX, VY, VZ, r_out, s_out, c_out,
    R, S, A, AR, SB, DB, OH, OHT, PHL, PG, VHL, SRC, XS, XR, YS, YR, VYS, VYR,
    MT, MR, MSK, AMSK, LT, LR, PLACE, CAT, cells_s, slot_s, way_s, cells_v,
    in_sem, meta_s, meta_r, xs, xr, vs, vr, ds_, dr, fs, fr,
):
    _, cx, cy, nz = vel.shape
    nq = nz // LANES
    half = cx * cy
    ncol = 2 * half
    jbs = cy // 16
    part = min(256, ncol)
    planes = part // (2 * cy)
    groups = cx // planes
    shift = (planes * cy).bit_length() - 1
    zero_row = lax.axis_index("gx") // 4096
    gx, gy = lax.axis_index("gx"), lax.axis_index("gy")
    ngx, ngy = lax.axis_size("gx"), lax.axis_size("gy")
    has_lo, has_hi = gy > 0, gy < ngy - 1
    targets = (
        (lax.rem(gx + 1, ngx), gy),
        (lax.rem(gx + ngx - 1, ngx), gy),
        (gx, lax.rem(gy + 1, ngy)),
        (gx, lax.rem(gy + ngy - 1, ngy)),
    )
    sends = (None, None, has_hi, has_lo)
    takes = (None, None, has_lo, has_hi)

    def under(flag, action):
        if flag is None:
            action()
        else:
            pl.when(flag)(action)

    barrier = pltpu.get_barrier_semaphore()
    for d in range(4):
        under(
            sends[d],
            lambda d=d: pl.semaphore_signal(
                barrier, inc=1, device_id=targets[d], device_id_type=MESH
            ),
        )

    inputs = [(cells_h, cells_s), (slot_h, slot_s), (way_h, way_s), (cells_b, cells_v)]
    for q in range(nq):
        inputs.append((press.at[:, :, pl.ds(q * LANES, LANES)], PR.at[q, :, pl.ds(8, cy), :]))
    for q in range(nq):
        lanes = pl.ds(q * LANES, LANES)
        inputs.append((vel.at[1, :, :, lanes], VY.at[q, :, pl.ds(8, cy), :]))
    own = pl.ds(0, SLOTS)
    inputs.append((rest, A.at[own, :]))
    inputs.append((stretch, R.at[own, :]))
    inputs.append((speed0, S.at[own, :]))
    for q in range(nq):
        lanes = pl.ds(q * LANES, LANES)
        inputs.append((vel.at[0, :, :, lanes], VX.at[q, pl.ds(1, cx), :, :]))
        inputs.append((vel.at[2, :, :, lanes], VZ.at[q]))
    loads = [pltpu.make_async_copy(a, b, in_sem.at[k]) for k, (a, b) in enumerate(inputs)]
    for load in loads:
        load.start()
    small_loads, loads = loads[:4], loads[4:]

    @pl.when(jnp.logical_not(has_lo))
    def _():
        MR[2] = jnp.zeros((8, LANES), f32)
        YR[:, 0] = jnp.zeros(YR.shape[:1] + YR.shape[2:], f32)
        VYR[0] = jnp.zeros(VYR.shape[1:], f32)

    @pl.when(jnp.logical_not(has_hi))
    def _():
        MR[3] = jnp.zeros((8, LANES), f32)
        YR[:, 1] = jnp.zeros(YR.shape[:1] + YR.shape[2:], f32)
        VYR[1] = jnp.zeros(VYR.shape[1:], f32)

    edge_rows = jnp.zeros((nq, cx, 8, LANES), f32)
    PR[:, :, 0:8, :] = edge_rows
    PR[:, :, 8 + cy : 16 + cy, :] = edge_rows
    VY[:, :, 0:8, :] = edge_rows
    VY[:, :, 8 + cy : 16 + cy, :] = edge_rows
    empty = jnp.zeros((ARRIVE, BLOCK), f32)
    R[SLOTS:ROWS, :] = empty + 1.0
    S[SLOTS:ROWS, :] = empty
    A[SLOTS:ROWS, :] = empty
    MSK[SLOTS:ROWS, :] = jnp.full((ARRIVE, LANES), -1.0, f32)
    OHT[:, SLOTS:ROWS] = jnp.zeros((ncol, ARRIVE), bf16)
    OH[SLOTS:ROWS, :] = jnp.zeros((ARRIVE, ncol), bf16)
    pl.semaphore_wait(barrier, 2 + has_lo.astype(jnp.int32) + has_hi.astype(jnp.int32))

    def remote(src, dst, send_sem, recv_sem, d):
        return pltpu.make_async_remote_copy(
            src_ref=src, dst_ref=dst, send_sem=send_sem, recv_sem=recv_sem,
            device_id=targets[d], device_id_type=MESH,
        )

    def meta_copy(d):
        return remote(MT, MR.at[d], meta_s.at[d], meta_r.at[d], d)

    def p_copy(t, d):
        if d < 2:
            return remote(XS.at[t, 1 - d], XR.at[t, d], xs.at[t, d], xr.at[t, d], d)
        return remote(YS.at[t, 3 - d], YR.at[t, d - 2], xs.at[t, d], xr.at[t, d], d)

    def first_copies(d):
        side = (cx - 2, 0)[d]
        for q in range(nq):
            lanes = pl.ds(q * LANES, LANES)
            yield remote(
                press.at[pl.ds(side, 2), :, lanes], XR.at[0, d, q], fs.at[0, d, q], fr.at[0, d, q], d
            )
        for q in range(nq):
            lanes = pl.ds(q * LANES, LANES)
            yield remote(
                vel.at[0, pl.ds((cx - 1, 0)[d], 1), :, lanes],
                VX.at[q, pl.ds((0, cx + 1)[d], 1), :, :],
                fs.at[1, d, q],
                fr.at[1, d, q],
                d,
            )

    def v_copy(d):
        return remote(VYS.at[3 - d], VYR.at[d - 2], vs.at[d], vr.at[d], d)

    def dep_copy(t, d):
        return remote(
            SB.at[t], AR.at[:, pl.ds(t * 32 + d * DEP, DEP), :], ds_.at[t, d], dr.at[t, d], d
        )

    def start(make, ways=(0, 1, 2, 3)):
        for d in ways:
            under(sends[d], lambda d=d: make(d).start())

    def wait_sent(make, ways=(0, 1, 2, 3)):
        for d in ways:
            under(sends[d], lambda d=d: make(d).wait_send())

    def wait_taken(make, ways=(0, 1, 2, 3)):
        for d in ways:
            under(takes[d], lambda d=d: make(d).wait_recv())

    for d in range(2):
        for copy in first_copies(d):
            copy.start()
    edges = ((0, 1), (cy - 2, cy - 1))

    def one(row):
        return pl.ds(row + zero_row, 1)

    def pack_rows(t):
        for side in range(2):
            for r in range(2):
                for q in range(nq):
                    for i in range(cx):
                        YS[t, side, r, q, one(i), :] = PR[q, i, one(8 + edges[side][r]), :]

    def unpack_rows(t, planes_now):
        for side in range(2):
            for r in range(2):
                for q in range(nq):
                    for i in planes_now:
                        PR[q, i, one(8 + edges[side][r]), :] = YS[t, side, r, q, one(i), :]

    def column_row(i, h, jb):
        return (i // planes) * part + (h * planes + i % planes) * cy + jb * 16

    def keep_parts(i, jb, q, value):
        high, low = split(value)
        row = column_row(i, q // 2, jb)
        col = (q % 2) * 2 * LANES
        PHL[row : row + 16, col : col + LANES] = high
        PHL[row : row + 16, col + LANES : col + 2 * LANES] = low

    def rows_of(jb):
        return slice(jb * 16, jb * 16 + 16), slice(8 + jb * 16, 24 + jb * 16)

    def split_all():
        for i in range(cx):
            for jb in range(jbs):
                for q in range(nq):
                    keep_parts(i, jb, q, PR[q, i, rows_of(jb)[1], :])

    for k in range(nq):
        loads[k].wait()
    pack_rows(0)
    start(lambda d: p_copy(0, d), (2, 3))
    for q in range(nq):
        for r in range(2):
            XS[0, 0, q, r] = PR[q, r, 8 : 8 + cy, :]
            XS[0, 1, q, r] = PR[q, cx - 2 + r, 8 : 8 + cy, :]
    for k in range(nq, 2 * nq):
        loads[k].wait()
    for q in range(nq):
        for i in range(cx):
            VYS[0, q, one(i), :] = VY[q, i, one(8), :]
            VYS[1, q, one(i), :] = VY[q, i, one(7 + cy), :]
    start(v_copy, (2, 3))

    for load in small_loads:
        load.wait()

    lane8 = lax.broadcasted_iota(jnp.int32, (8, LANES), 1)
    sub8 = lax.broadcasted_iota(jnp.int32, (8, LANES), 0)
    slot_id = sub8 * LANES + lane8
    label = cells_v[...] + 1
    leave_at = jnp.where(label > 0, STEPS, -1)
    entry_of = (lane8 // 32) * DEP + lane8 % DEP
    wanted = (lane8 // DEP) % 4
    wanted = jnp.where(wanted < 2, 1 - wanted, 5 - wanted)
    meta = jnp.zeros((8, LANES), jnp.int32)
    for e in range(STEPS * DEP):
        slot = slot_s[e // DEP, 0, 0, e % DEP]
        moved = jnp.where(slot >= 0, cells_s[jnp.maximum(slot, 0)] + 1, 0)
        meta = jnp.where((entry_of == e) & (wanted == way_s[e // DEP, 0, 0, e % DEP]), moved, meta)
        leave_at = jnp.where(slot_id == slot, e // DEP, leave_at)
    MT[...] = meta.astype(f32)

    start(meta_copy)

    split_all()

    lrow = lax.broadcasted_iota(jnp.int32, (LANES, LANES), 0)
    lcol = lax.broadcasted_iota(jnp.int32, (LANES, LANES), 1)
    wide = lax.broadcasted_iota(jnp.int32, (16, ncol), 1).astype(f32)

    def code_of(lab):
        cell = lab - 1
        place = cell >> 1
        row = (place >> shift) * part + (cell & 1) * (planes * cy)
        return jnp.where(lab > 0, row + (place & (planes * cy - 1)), -1).astype(f32)

    def turn(stack):
        stack = stack + [jnp.zeros((8, LANES), f32)] * (16 - len(stack))
        LT[...] = jnp.concatenate(stack, axis=0).T

    def hot_rows(r, at):
        def body(m, carry):
            rows = pl.ds(pl.multiple_of(m * 16, 16), 16)
            hot = jnp.where(LT[rows, at : at + 1] == wide, 1.0, 0.0).astype(bf16)
            OH[pl.ds(pl.multiple_of(r * LANES + m * 16, 16), 16), :] = hot
            return carry

        lax.fori_loop(0, LANES // 16, body, 0, unroll=4)

    def hot_columns(first, last):
        def body(m, carry):
            ident = (lrow + m * LANES).astype(f32)
            rows = pl.ds(pl.multiple_of(m * LANES, LANES), LANES)
            for r in range(first, last):
                hot = jnp.where(ident == LR[r : r + 1, :], 1.0, 0.0).astype(bf16)
                OHT[rows, r * LANES : (r + 1) * LANES] = hot
            return carry

        lax.fori_loop(0, ncol // LANES, body, 0)

    code = code_of(label)
    turn([code, leave_at.astype(f32)])
    LR[0:8, :] = code
    for r in range(SLOT_BLOCKS):
        hot_rows(r, r)
    for r in range(SLOT_BLOCKS):
        MSK[r * LANES : (r + 1) * LANES, :] = jnp.broadcast_to(
            LT[:, 8 + r : 9 + r], (LANES, LANES)
        )
    hot_columns(0, SLOT_BLOCKS)

    for k in range(2 * nq, 2 * nq + 3):
        loads[k].wait()

    def first_state(n, carry):
        rows = pl.ds(pl.multiple_of(n * 16, 16), 16)
        rest_now = A[rows, :]
        R[rows, :] = R[rows, :] * rest_now
        S[rows, :] = time_step * S[rows, :]
        A[rows, :] = inv_ln2 * (
            jnp.log((time_step * time_step) * (1.0 + 0.2 / rest_now))
            + exponent * jnp.log(rest_now)
        )
        return carry

    lax.fori_loop(0, SLOTS // 16, first_state, 0, unroll=4)
    for k in range(2 * nq + 3, 4 * nq + 3):
        loads[k].wait()

    def plan():
        wait_taken(meta_copy)
        came = (lane8 // DEP) % 4
        alab = jnp.where(
            came == 0, MR[0], jnp.where(came == 1, MR[1], jnp.where(came == 2, MR[2], MR[3]))
        )
        present = alab > 0.0
        upper = jnp.where(lrow <= lcol, 1.0, 0.0)
        upper_block = jnp.where(lrow // 32 == lcol // 32, upper, 0.0).astype(bf16)
        upper = upper.astype(bf16)
        ones = jnp.ones((LANES, LANES), bf16)
        present_f = jnp.where(present, 1.0, 0.0)
        arank = jnp.dot(present_f.astype(bf16), upper_block, preferred_element_type=f32) - 1.0
        arank = jnp.where(present, arank, -5.0)
        vacant = label == 0
        ranks = []
        for t in range(STEPS):
            vacant = vacant | (leave_at == t)
            flag = jnp.where(vacant, 1.0, 0.0).astype(bf16)
            rank = jnp.dot(flag, upper, preferred_element_type=f32) - 1.0
            total = jnp.dot(flag, ones, preferred_element_type=f32)
            for r in range(SLOT_BLOCKS - 1):
                rank = rank + jnp.where(sub8 > r, total[r : r + 1, :], 0.0)
            ranks.append(jnp.where(vacant, rank, -1.0))
            count = jnp.sum(jnp.where(lane8 // 32 == t, present_f, 0.0), axis=1, keepdims=True)
            vacant = vacant & (rank >= count)

        acode = code_of(alab.astype(jnp.int32))
        turn(ranks + [acode, alab])
        LR[8:16, :] = acode
        hot_rows(SLOT_BLOCKS, 32)
        hot_columns(SLOT_BLOCKS, SLOT_BLOCKS + 1)
        AMSK[...] = jnp.broadcast_to(LT[:, 40:41], (LANES, LANES))

        group = lcol // 32
        alab_high, alab_low = split(alab)
        final = jnp.where(leave_at == STEPS, label, 0).astype(f32)
        nt = (((1,), (1,)), ((), ()))
        for r in range(SLOT_BLOCKS):
            mine = jnp.broadcast_to(LT[:, r : r + 1], (LANES, LANES))
            for t in range(1, STEPS):
                mine = jnp.where(group == t, LT[:, 8 * t + r : 8 * t + r + 1], mine)
            hot = jnp.where(mine == arank[0:1, :], 1.0, 0.0).astype(bf16)
            PLACE[r * LANES : (r + 1) * LANES, 0:LANES] = hot
            PLACE[r * LANES : (r + 1) * LANES, LANES : 2 * LANES] = hot
            placed = lax.dot_general(alab_high, hot, nt, preferred_element_type=f32)
            placed = placed + lax.dot_general(alab_low, hot, nt, preferred_element_type=f32)
            final = final + jnp.where(sub8 == r, placed, 0.0)
        c_out[...] = final.astype(jnp.int32) - 1

    def slope_z(tiles):
        height = tiles[0].shape[0]
        lane = lax.broadcasted_iota(jnp.int32, (height, LANES), 1)
        zero = jnp.zeros((height, LANES), f32)
        ahead = [pltpu.roll(v, LANES - 1, 1) for v in tiles] + [zero]
        behind = [zero] + [pltpu.roll(v, 1, 1) for v in tiles]
        return [
            jnp.where(lane == LANES - 1, ahead[q + 1], ahead[q])
            - jnp.where(lane == 0, behind[q], behind[q + 1])
            for q in range(nq)
        ]

    low_gate = jnp.where(has_lo, 1.0, 0.0).astype(f32)
    high_gate = jnp.where(has_hi, 1.0, 0.0).astype(f32)

    def halves(w):
        return slice(w * LANES, (w + 1) * LANES), slice(2 * w * LANES, 2 * (w + 1) * LANES)

    def gather(w):
        narrow, pair = halves(w)
        both = jnp.dot(OH[...], PHL[:, pair], preferred_element_type=f32)
        PG[:, narrow] = both[:, :LANES] + both[:, LANES:]

    def scatter(w):
        narrow, pair = halves(w)
        both = jnp.dot(OHT[...], VHL[:, pair], preferred_element_type=f32)
        SRC[:, narrow] = both[:, :LANES] + both[:, LANES:]

    def take_arrivals(t):
        wait_taken(lambda d: dep_copy(t, d))
        rows = pl.ds(pl.multiple_of(t * 32, 32), 32)
        to = pl.ds(pl.multiple_of(SLOTS + t * 32, 32), 32)
        R[to, :] = AR[0, rows, :]
        S[to, :] = AR[1, rows, :]
        A[to, :] = AR[2, rows, :]
        MSK[to, :] = jnp.where(AMSK[rows, :] > 0.0, 2.0 * STEPS, -1.0)

    def step(t, carry):
        limit = t.astype(f32)

        def bubbles(first, w):
            rows = slice(first, first + 16)
            col = halves(w)[0]
            radius, speed, rate = wall_update(R[rows, col], S[rows, col], A[rows, col], PG[rows, col])
            R[rows, col] = radius
            S[rows, col] = speed
            high, low = split(jnp.where(MSK[rows, :] >= limit, rate, 0.0))
            VHL[rows, 2 * w * LANES : (2 * w + 1) * LANES] = high
            VHL[rows, (2 * w + 1) * LANES : (2 * w + 2) * LANES] = low

        for k in range(DEP):
            slot = jnp.maximum(slot_s[t, 0, 0, k], 0)
            cell = jnp.maximum(cells_s[slot], 0)
            place = cell >> 1
            row = pl.ds(slot, 1)
            DB[0, k : k + 1, :] = R[row, :]
            DB[1, k : k + 1, :] = S[row, :]
            DB[2, k : k + 1, :] = A[row, :]
            for w in range(2):
                DB[3, k : k + 1, halves(w)[0]] = PR[
                    2 * (cell & 1) + w,
                    place >> (cy.bit_length() - 1),
                    pl.ds(8 + (place & (cy - 1)), 1),
                    :,
                ]
        radius, speed, _ = wall_update(DB[0], DB[1], DB[2], DB[3])
        SB[t, 0] = radius
        SB[t, 1] = speed
        SB[t, 2] = DB[2]
        start(lambda d: dep_copy(t, d))

        @pl.when(t > 0)
        def _():
            take_arrivals(t - 1)

        gather(0)
        gather(1)
        for first in range(0, ROWS, 16):
            bubbles(first, 0)
        scatter(0)
        for first in range(0, ROWS, 16):
            bubbles(first, 1)
        scatter(1)

        def flow_x(i):
            for q in range(nq):
                for jb in range(jbs):
                    rows, at = rows_of(jb)
                    flow = VX[q, i + 1, rows, :]
                    if i == 0:
                        flow = flow - half_gain * PR[q, 1, at, :]
                    elif i == cx - 1:
                        flow = flow + half_gain * PR[q, cx - 2, at, :]
                    else:
                        flow = flow - half_gain * (PR[q, i + 1, at, :] - PR[q, i - 1, at, :])
                    VX[q, i + 1, rows, :] = flow

        def flow_z(i, jb):
            rows, at = rows_of(jb)
            slopes = slope_z([PR[q, i, at, :] for q in range(nq)])
            for q in range(nq):
                VZ[q, i, rows, :] = VZ[q, i, rows, :] - half_gain * slopes[q]

        def flow_y(i, jb):
            _, at = rows_of(jb)
            for q in range(nq):
                VY[q, i, at, :] = VY[q, i, at, :] - half_gain * (
                    PR[q, i, pl.ds(9 + jb * 16 + zero_row, 16), :]
                    - PR[q, i, pl.ds(7 + jb * 16 + zero_row, 16), :]
                )

        def pressure(i, jb):
            rows, at = rows_of(jb)
            slopes = slope_z([VZ[q, i, rows, :] for q in range(nq)])
            for q in range(nq):
                rise = slopes[q] + (
                    VY[q, i, pl.ds(9 + jb * 16 + zero_row, 16), :]
                    - VY[q, i, pl.ds(7 + jb * 16 + zero_row, 16), :]
                )
                if i + 1 < cx:
                    rise = rise + VX[q, i + 2, rows, :]
                if i > 0:
                    rise = rise - VX[q, i, rows, :]
                row = column_row(i, q // 2, jb)
                col = (q % 2) * LANES
                PR[q, i, at, :] = (
                    PR[q, i, at, :] - half_gain * rise + SRC[row : row + 16, col : col + LANES]
                )

        for i in range(cx):
            flow_x(i)
            for jb in range(jbs):
                flow_z(i, jb)
                flow_y(i, jb)
        for i in range(cx):
            for jb in range(jbs):
                pressure(i, jb)
        pack_rows(t + 1)

        pl.when(t == 0)(plan)
        wait_taken(lambda d: p_copy(t, d), (2, 3))

        @pl.when(t > 0)
        def _():
            wait_taken(lambda d: p_copy(t, d), (0, 1))

        @pl.when(t == 0)
        def _():
            for d in range(2):
                for copy in first_copies(d):
                    copy.wait_recv()
            wait_taken(v_copy, (2, 3))

        below, above = VYR[0], VYR[1]
        below = low_gate * (below - half_gain * (YS[t, 0, 0] - YR[t, 0, 0]))
        above = high_gate * (above - half_gain * (YR[t, 1, 1] - YS[t, 1, 1]))
        VYR[0] = below
        VYR[1] = above
        both_gains = half_gain * half_gain
        YS[t + 1, 0, 0] = YS[t + 1, 0, 0] + half_gain * below
        YS[t + 1, 0, 1] = YS[t + 1, 0, 1] + both_gains * YR[t, 0, 1]
        YS[t + 1, 1, 0] = YS[t + 1, 1, 0] + both_gains * YR[t, 1, 0]
        YS[t + 1, 1, 1] = YS[t + 1, 1, 1] - half_gain * above
        for q in range(nq):
            for jb in range(jbs):
                rows, at = rows_of(jb)
                far, near = XR[t, 0, q, 0, rows, :], XR[t, 0, q, 1, rows, :]
                beside = VX[q, 0, rows, :] - half_gain * (XS[t, 0, q, 0, rows, :] - far)
                VX[q, 0, rows, :] = beside
                VX[q, 1, rows, :] = VX[q, 1, rows, :] + half_gain * near
                first = PR[q, 0, at, :] + half_gain * beside
                second = PR[q, 1, at, :] + both_gains * near
                PR[q, 0, at, :] = first
                PR[q, 1, at, :] = second
                XS[t + 1, 0, q, 0, rows, :] = first
                XS[t + 1, 0, q, 1, rows, :] = second
                near, far = XR[t, 1, q, 0, rows, :], XR[t, 1, q, 1, rows, :]
                beside = VX[q, cx + 1, rows, :] - half_gain * (far - XS[t, 1, q, 1, rows, :])
                VX[q, cx + 1, rows, :] = beside
                VX[q, cx, rows, :] = VX[q, cx, rows, :] - half_gain * near
                first = PR[q, cx - 2, at, :] + both_gains * near
                second = PR[q, cx - 1, at, :] - half_gain * beside
                PR[q, cx - 2, at, :] = first
                PR[q, cx - 1, at, :] = second
                XS[t + 1, 1, q, 0, rows, :] = first
                XS[t + 1, 1, q, 1, rows, :] = second
        ends = ((0, 0, 0), (1, 0, 1), (cx - 2, 1, 0), (cx - 1, 1, 1))
        for i, x_side, x_row in ends:
            for side in range(2):
                for r in range(2):
                    for q in range(nq):
                        row = one(edges[side][r])
                        if i == 0:
                            part_x = half_gain * VX[q, 0, row, :]
                        elif i == 1:
                            part_x = both_gains * XR[t, 0, q, 1, row, :]
                        elif i == cx - 2:
                            part_x = both_gains * XR[t, 1, q, 0, row, :]
                        else:
                            part_x = -half_gain * VX[q, cx + 1, row, :]
                        value = YS[t + 1, side, r, q, one(i), :] + part_x
                        YS[t + 1, side, r, q, one(i), :] = value
                        XS[t + 1, x_side, q, x_row, row, :] = value

        @pl.when(t < STEPS - 1)
        def _():
            start(lambda d: p_copy(t + 1, d), (2, 3))
            start(lambda d: p_copy(t + 1, d), (0, 1))

        unpack_rows(t + 1, range(cx))
        for q in range(nq):
            for i in range(cx):
                low, high = one(8), one(7 + cy)
                VY[q, i, low, :] = VY[q, i, low, :] + half_gain * YR[t, 0, 1, q, one(i), :]
                VY[q, i, high, :] = VY[q, i, high, :] - half_gain * YR[t, 1, 0, q, one(i), :]

        @pl.when(t < STEPS - 1)
        def _():
            split_all()

        return carry

    lax.fori_loop(0, STEPS, step, 0)

    take_arrivals(STEPS - 1)
    keep = AMSK[...] > 0.0
    for k, state in enumerate((R, S)):
        for w in range(2):
            high, low = split(jnp.where(keep, state[SLOTS:ROWS, halves(w)[0]], 0.0))
            to = slice(k * BLOCK + w * LANES, k * BLOCK + (w + 1) * LANES)
            CAT[0:ARRIVE, to] = high
            CAT[ARRIVE : 2 * ARRIVE, to] = low

    def finish(m, carry):
        rows = pl.ds(pl.multiple_of(m * LANES, LANES), LANES)
        placed = jnp.dot(PLACE[rows, :], CAT[...], preferred_element_type=f32)
        keep = MSK[rows, :]
        keep = jnp.concatenate([keep, keep], axis=1) >= float(STEPS)
        r_out[rows, :] = jnp.where(keep, R[rows, :], 0.0) + placed[:, :BLOCK]
        s_out[rows, :] = (1.0 / time_step) * (jnp.where(keep, S[rows, :], 0.0) + placed[:, BLOCK:])
        return carry

    lax.fori_loop(0, SLOT_BLOCKS, finish, 0)
    wait_sent(meta_copy)
    for t in range(STEPS):
        wait_sent(lambda d, t=t: dep_copy(t, d))
        wait_sent(lambda d, t=t: p_copy(t, d), (2, 3) if t == 0 else (0, 1, 2, 3))
    wait_sent(v_copy, (2, 3))
    for d in range(2):
        for copy in first_copies(d):
            copy.wait_send()


def write_out(p, vx, vy, vz, r, s, c, p_out, v_out, r_out, s_out, c_out, sems):
    _, cx, cy, nz = v_out.shape
    pairs = [(r, r_out), (s, s_out), (c, c_out)]
    for q in range(nz // LANES):
        lanes = pl.ds(q * LANES, LANES)
        pairs.append((vx.at[q, pl.ds(1, cx), :, :], v_out.at[0, :, :, lanes]))
        pairs.append((vy.at[q, :, pl.ds(8, cy), :], v_out.at[1, :, :, lanes]))
        pairs.append((vz.at[q], v_out.at[2, :, :, lanes]))
        pairs.append((p.at[q, :, pl.ds(8, cy), :], p_out.at[:, :, lanes]))
    copies = [pltpu.make_async_copy(a, b, sems.at[k]) for k, (a, b) in enumerate(pairs)]
    for copy in copies:
        copy.start()
    for copy in copies:
        copy.wait()


def on_device(
    pressure, velocity, stretch, rest_radius, wall_speed, block_cells, depart_slot, depart_way
):
    cx, cy, nz = pressure.shape
    nq = nz // LANES
    ncol = 2 * cx * cy
    vmem = pl.BlockSpec(memory_space=pltpu.VMEM)
    hbm = pl.BlockSpec(memory_space=pl.ANY)
    dma = pltpu.SemaphoreType.DMA
    vmem_out = pltpu.VMEM
    parts = pl.pallas_call(
        kernel,
        out_shape=(
            vmem_out((nq, cx, cy + 16, LANES), f32),
            vmem_out((nq, cx + 2, cy, LANES), f32),
            vmem_out((nq, cx, cy + 16, LANES), f32),
            vmem_out((nq, cx, cy, LANES), f32),
            vmem_out((SLOTS, BLOCK), f32),
            vmem_out((SLOTS, BLOCK), f32),
            vmem_out((SLOT_BLOCKS, LANES), jnp.int32),
        ),
        in_specs=[pl.BlockSpec(memory_space=pltpu.HBM)] * 9,
        out_specs=(vmem,) * 7,
        scratch_shapes=[
            pltpu.VMEM((ROWS, BLOCK), f32),
            pltpu.VMEM((ROWS, BLOCK), f32),
            pltpu.VMEM((ROWS, BLOCK), f32),
            pltpu.VMEM((3, ARRIVE, BLOCK), f32),
            pltpu.VMEM((STEPS, 3, DEP, BLOCK), f32),
            pltpu.VMEM((4, DEP, BLOCK), f32),
            pltpu.VMEM((ROWS, ncol), bf16),
            pltpu.VMEM((ncol, ROWS), bf16),
            pltpu.VMEM((ncol, 2 * BLOCK), bf16),
            pltpu.VMEM((ROWS, BLOCK), f32),
            pltpu.VMEM((ROWS, 2 * BLOCK), bf16),
            pltpu.VMEM((ncol, BLOCK), f32),
            pltpu.VMEM((STEPS + 1, 2, nq, 2, cy, LANES), f32),
            pltpu.VMEM((STEPS, 2, nq, 2, cy, LANES), f32),
            pltpu.VMEM((STEPS + 1, 2, 2, nq, cx, LANES), f32),
            pltpu.VMEM((STEPS, 2, 2, nq, cx, LANES), f32),
            pltpu.VMEM((2, nq, cx, LANES), f32),
            pltpu.VMEM((2, nq, cx, LANES), f32),
            pltpu.VMEM((8, LANES), f32),
            pltpu.VMEM((4, 8, LANES), f32),
            pltpu.VMEM((ROWS, LANES), f32),
            pltpu.VMEM((ARRIVE, LANES), f32),
            pltpu.VMEM((LANES, LANES), f32),
            pltpu.VMEM((16, LANES), f32),
            pltpu.VMEM((SLOTS, 2 * ARRIVE), bf16),
            pltpu.VMEM((2 * ARRIVE, 2 * BLOCK), bf16),
            pltpu.SMEM((SLOTS,), jnp.int32),
            pltpu.SMEM((STEPS, 1, 1, DEP), jnp.int32),
            pltpu.SMEM((STEPS, 1, 1, DEP), jnp.int32),
            pltpu.VMEM((SLOT_BLOCKS, LANES), jnp.int32),
            dma((4 * nq + 7,)),
            dma((4,)),
            dma((4,)),
            dma((STEPS, 4)),
            dma((STEPS, 4)),
            dma((4,)),
            dma((4,)),
            dma((STEPS, 4)),
            dma((STEPS, 4)),
            dma((2, 2, nq)),
            dma((2, 2, nq)),
        ],
        compiler_params=pltpu.CompilerParams(
            collective_id=0, has_side_effects=True, vmem_limit_bytes=36 * 2**20
        ),
        cost_estimate=pl.CostEstimate(
            flops=10 * 2**30, bytes_accessed=13 * 2**20, transcendentals=2**22
        ),
    )(
        *(
            pltpu.with_memory_space_constraint(value, pltpu.HBM)
            for value in (
                block_cells,
                depart_slot,
                depart_way,
                block_cells.reshape(SLOT_BLOCKS, LANES),
                pressure,
                velocity,
                stretch,
                rest_radius,
                wall_speed,
            )
        )
    )
    parts = [pltpu.with_memory_space_constraint(part, pltpu.VMEM) for part in parts]
    p, v, r, s, c = pl.pallas_call(
        write_out,
        out_shape=(
            jax.ShapeDtypeStruct(pressure.shape, f32),
            jax.ShapeDtypeStruct(velocity.shape, f32),
            jax.ShapeDtypeStruct(stretch.shape, f32),
            jax.ShapeDtypeStruct(stretch.shape, f32),
            jax.ShapeDtypeStruct((SLOT_BLOCKS, LANES), jnp.int32),
        ),
        in_specs=[vmem] * 7,
        out_specs=(hbm,) * 5,
        scratch_shapes=[dma((4 * nq + 3,))],
        compiler_params=pltpu.CompilerParams(vmem_limit_bytes=4 * 2**20),
        cost_estimate=pl.CostEstimate(flops=0, bytes_accessed=13 * 2**20, transcendentals=0),
    )(*parts)
    return p, v, r, s, c.reshape(-1)


def solution(mesh):
    placed = (
        P("gx", "gy", None),
        P(None, "gx", "gy", None),
        P(("gx", "gy"), None),
        P(("gx", "gy"), None),
        P(("gx", "gy"), None),
        P(("gx", "gy")),
        P(None, "gx", "gy", None),
        P(None, "gx", "gy", None),
    )
    return jax.shard_map(
        on_device,
        mesh=mesh,
        in_specs=placed,
        out_specs=(
            P("gx", "gy", None),
            P(None, "gx", "gy", None),
            P(("gx", "gy"), None),
            P(("gx", "gy"), None),
            P(("gx", "gy")),
        ),
        check_vma=False,
    )
```

```python
import functools
import math

import jax
import jax.numpy as jnp
from jax import lax
from jax.experimental import pallas as pl
from jax.experimental.pallas import tpu as pltpu
from jax.sharding import PartitionSpec as P

MESH = pl.DeviceIdType.MESH
f32 = jnp.float32
bf16 = jnp.bfloat16

STEPS = 4
DEP = 8
SLOTS = 1024
BLOCK = 256
LANES = 128
ARRIVE = STEPS * 4 * DEP
ROWS = SLOTS + ARRIVE
SLOT_BLOCKS = SLOTS // LANES
WAY_OF = (1, 0, 3, 2)

time_step = 0.04
half_gain = 0.2
source_scale = 0.004 * 12.566370614359172
exponent = 4.2
inv_ln2 = 1.0 / math.log(2.0)


def split(value):
    high = value.astype(bf16)
    return high, (value - high.astype(f32)).astype(bf16)


def wall_update(radius, shift, level, pressure):
    mach = (0.05 / time_step) * shift
    one_less = 1.0 - mach
    divisor = one_less * radius
    inverse = pl.reciprocal(divisor, approx=True)
    inverse = inverse * (2.0 - divisor * inverse)
    inv_radius = inverse * one_less
    wall = jnp.exp2(level - (exponent * inv_ln2) * jnp.log(radius))
    squared = time_step * time_step
    excess = (
        wall
        - (0.2 * squared + (0.08 * time_step) * shift) * inv_radius
        - (squared + squared * pressure)
    )
    driving = (1.0 + mach) * excess - (1.5 - 0.5 * mach) * (shift * shift)
    shift = shift + driving * inverse
    radius = radius + shift
    return radius, shift, (source_scale / time_step) * (radius * radius) * shift


def kernel(
    cells_h, slot_h, way_h, cells_b, press, vel, stretch, rest, speed0,
    PR, VX, VY, VZ, R, S, MSK, PLACE, CAT, c_out,
    A, AR, SB, DB, OH, OHT, PHL, PG, VHL, SRC, XS, XR, YS, YR, VYS, VYR,
    MT, MR, AMSK, LT, LR, cells_s, slot_s, way_s, cells_v,
    in_sem, meta_s, meta_r, xs, xr, vs, vr, ds_, dr, fs, fr,
):
    _, cx, cy, nz = vel.shape
    nq = nz // LANES
    half = cx * cy
    ncol = 2 * half
    jbs = cy // 16
    part = min(256, ncol)
    planes = part // (2 * cy)
    groups = cx // planes
    shift = (planes * cy).bit_length() - 1
    zero_row = lax.axis_index("gx") // 4096
    gx, gy = lax.axis_index("gx"), lax.axis_index("gy")
    ngx, ngy = lax.axis_size("gx"), lax.axis_size("gy")
    has_lo, has_hi = gy > 0, gy < ngy - 1
    targets = (
        (lax.rem(gx + 1, ngx), gy),
        (lax.rem(gx + ngx - 1, ngx), gy),
        (gx, lax.rem(gy + 1, ngy)),
        (gx, lax.rem(gy + ngy - 1, ngy)),
    )
    sends = (None, None, has_hi, has_lo)
    takes = (None, None, has_lo, has_hi)

    def under(flag, action):
        if flag is None:
            action()
        else:
            pl.when(flag)(action)

    barrier = pltpu.get_barrier_semaphore()
    for d in range(4):
        under(
            sends[d],
            lambda d=d: pl.semaphore_signal(
                barrier, inc=1, device_id=targets[d], device_id_type=MESH
            ),
        )

    inputs = [(cells_h, cells_s), (slot_h, slot_s), (way_h, way_s), (cells_b, cells_v)]
    for q in range(nq):
        inputs.append((press.at[:, :, pl.ds(q * LANES, LANES)], PR.at[q, :, pl.ds(8, cy), :]))
    for q in range(nq):
        lanes = pl.ds(q * LANES, LANES)
        inputs.append((vel.at[1, :, :, lanes], VY.at[q, :, pl.ds(8, cy), :]))
    own = pl.ds(0, SLOTS)
    inputs.append((rest, A.at[own, :]))
    inputs.append((stretch, R.at[own, :]))
    inputs.append((speed0, S.at[own, :]))
    for q in range(nq):
        lanes = pl.ds(q * LANES, LANES)
        inputs.append((vel.at[0, :, :, lanes], VX.at[q, pl.ds(1, cx), :, :]))
        inputs.append((vel.at[2, :, :, lanes], VZ.at[q]))
    loads = [pltpu.make_async_copy(a, b, in_sem.at[k]) for k, (a, b) in enumerate(inputs)]
    for load in loads:
        load.start()
    small_loads, loads = loads[:4], loads[4:]

    @pl.when(jnp.logical_not(has_lo))
    def _():
        MR[2] = jnp.zeros((8, LANES), f32)
        YR[:, 0] = jnp.zeros(YR.shape[:1] + YR.shape[2:], f32)
        VYR[0] = jnp.zeros(VYR.shape[1:], f32)

    @pl.when(jnp.logical_not(has_hi))
    def _():
        MR[3] = jnp.zeros((8, LANES), f32)
        YR[:, 1] = jnp.zeros(YR.shape[:1] + YR.shape[2:], f32)
        VYR[1] = jnp.zeros(VYR.shape[1:], f32)

    edge_rows = jnp.zeros((nq, cx, 8, LANES), f32)
    PR[:, :, 0:8, :] = edge_rows
    PR[:, :, 8 + cy : 16 + cy, :] = edge_rows
    VY[:, :, 0:8, :] = edge_rows
    VY[:, :, 8 + cy : 16 + cy, :] = edge_rows
    empty = jnp.zeros((ARRIVE, BLOCK), f32)
    R[SLOTS:ROWS, :] = empty + 1.0
    S[SLOTS:ROWS, :] = empty
    A[SLOTS:ROWS, :] = empty
    MSK[SLOTS:ROWS, :] = jnp.full((ARRIVE, LANES), -1.0, f32)
    OHT[:, SLOTS:ROWS] = jnp.zeros((ncol, ARRIVE), bf16)
    OH[SLOTS:ROWS, :] = jnp.zeros((ARRIVE, ncol), bf16)
    pl.semaphore_wait(barrier, 2 + has_lo.astype(jnp.int32) + has_hi.astype(jnp.int32))

    def remote(src, dst, send_sem, recv_sem, d):
        return pltpu.make_async_remote_copy(
            src_ref=src, dst_ref=dst, send_sem=send_sem, recv_sem=recv_sem,
            device_id=targets[d], device_id_type=MESH,
        )

    def meta_copy(d):
        return remote(MT, MR.at[d], meta_s.at[d], meta_r.at[d], d)

    def p_copy(t, d):
        if d < 2:
            return remote(XS.at[t, 1 - d], XR.at[t, d], xs.at[t, d], xr.at[t, d], d)
        return remote(YS.at[t, 3 - d], YR.at[t, d - 2], xs.at[t, d], xr.at[t, d], d)

    def first_copies(d):
        side = (cx - 2, 0)[d]
        for q in range(nq):
            lanes = pl.ds(q * LANES, LANES)
            yield remote(
                press.at[pl.ds(side, 2), :, lanes], XR.at[0, d, q], fs.at[0, d, q], fr.at[0, d, q], d
            )
        for q in range(nq):
            lanes = pl.ds(q * LANES, LANES)
            yield remote(
                vel.at[0, pl.ds((cx - 1, 0)[d], 1), :, lanes],
                VX.at[q, pl.ds((0, cx + 1)[d], 1), :, :],
                fs.at[1, d, q],
                fr.at[1, d, q],
                d,
            )

    def v_copy(d):
        return remote(VYS.at[3 - d], VYR.at[d - 2], vs.at[d], vr.at[d], d)

    def dep_copy(t, d):
        return remote(
            SB.at[t], AR.at[:, pl.ds(t * 32 + d * DEP, DEP), :], ds_.at[t, d], dr.at[t, d], d
        )

    odd = lax.rem(gy, 2) == 1
    even = jnp.logical_not(odd)
    far_hi, near_hi = has_hi & odd, has_hi & even
    far_lo, near_lo = has_lo & even, has_lo & odd

    def start(make, ways=(0, 1, 2, 3)):
        order = ((far_hi, 2), (far_lo, 3), (None, 0), (None, 1), (near_hi, 2), (near_lo, 3))
        for flag, d in order:
            if d in ways:
                under(flag, lambda d=d: make(d).start())

    def wait_sent(make, ways=(0, 1, 2, 3)):
        for d in ways:
            under(sends[d], lambda d=d: make(d).wait_send())

    def wait_taken(make, ways=(0, 1, 2, 3)):
        for d in ways:
            under(takes[d], lambda d=d: make(d).wait_recv())

    for d in range(2):
        for copy in first_copies(d):
            copy.start()
    edges = ((0, 1), (cy - 2, cy - 1))

    def one(row):
        return pl.ds(row + zero_row, 1)

    def pack_rows(t):
        for side in range(2):
            for r in range(2):
                for q in range(nq):
                    for i in range(cx):
                        YS[t, side, r, q, one(i), :] = PR[q, i, one(8 + edges[side][r]), :]

    def unpack_rows(t, planes_now):
        for side in range(2):
            for r in range(2):
                for q in range(nq):
                    for i in planes_now:
                        PR[q, i, one(8 + edges[side][r]), :] = YS[t, side, r, q, one(i), :]

    def column_row(i, h, jb):
        return (i // planes) * part + (h * planes + i % planes) * cy + jb * 16

    def keep_parts(i, jb, q, value):
        high, low = split(value)
        row = column_row(i, q // 2, jb)
        col = (q % 2) * 2 * LANES
        PHL[row : row + 16, col : col + LANES] = high
        PHL[row : row + 16, col + LANES : col + 2 * LANES] = low

    def rows_of(jb):
        return slice(jb * 16, jb * 16 + 16), slice(8 + jb * 16, 24 + jb * 16)

    def split_all():
        for i in range(cx):
            for jb in range(jbs):
                for q in range(nq):
                    keep_parts(i, jb, q, PR[q, i, rows_of(jb)[1], :])

    for k in range(nq):
        loads[k].wait()
    pack_rows(0)
    start(lambda d: p_copy(0, d), (2, 3))
    for q in range(nq):
        for r in range(2):
            XS[0, 0, q, r] = PR[q, r, 8 : 8 + cy, :]
            XS[0, 1, q, r] = PR[q, cx - 2 + r, 8 : 8 + cy, :]
    for k in range(nq, 2 * nq):
        loads[k].wait()
    for q in range(nq):
        for i in range(cx):
            VYS[0, q, one(i), :] = VY[q, i, one(8), :]
            VYS[1, q, one(i), :] = VY[q, i, one(7 + cy), :]
    start(v_copy, (2, 3))

    for load in small_loads:
        load.wait()

    lane8 = lax.broadcasted_iota(jnp.int32, (8, LANES), 1)
    sub8 = lax.broadcasted_iota(jnp.int32, (8, LANES), 0)
    slot_id = sub8 * LANES + lane8
    label = cells_v[...] + 1
    leave_at = jnp.where(label > 0, STEPS, -1)
    entry_of = (lane8 // 32) * DEP + lane8 % DEP
    wanted = (lane8 // DEP) % 4
    wanted = jnp.where(wanted < 2, 1 - wanted, 5 - wanted)
    meta = jnp.zeros((8, LANES), jnp.int32)
    for e in range(STEPS * DEP):
        slot = slot_s[e // DEP, 0, 0, e % DEP]
        moved = jnp.where(slot >= 0, cells_s[jnp.maximum(slot, 0)] + 1, 0)
        meta = jnp.where((entry_of == e) & (wanted == way_s[e // DEP, 0, 0, e % DEP]), moved, meta)
        leave_at = jnp.where(slot_id == slot, e // DEP, leave_at)
    MT[...] = meta.astype(f32)

    start(meta_copy)

    split_all()

    lrow = lax.broadcasted_iota(jnp.int32, (LANES, LANES), 0)
    lcol = lax.broadcasted_iota(jnp.int32, (LANES, LANES), 1)
    wide = lax.broadcasted_iota(jnp.int32, (16, ncol), 1).astype(f32)

    def code_of(lab):
        cell = lab - 1
        place = cell >> 1
        row = (place >> shift) * part + (cell & 1) * (planes * cy)
        return jnp.where(lab > 0, row + (place & (planes * cy - 1)), -1).astype(f32)

    def turn(stack):
        stack = stack + [jnp.zeros((8, LANES), f32)] * (16 - len(stack))
        LT[...] = jnp.concatenate(stack, axis=0).T

    def hot_rows(r, at):
        def body(m, carry):
            rows = pl.ds(pl.multiple_of(m * 16, 16), 16)
            hot = jnp.where(LT[rows, at : at + 1] == wide, 1.0, 0.0).astype(bf16)
            OH[pl.ds(pl.multiple_of(r * LANES + m * 16, 16), 16), :] = hot
            return carry

        lax.fori_loop(0, LANES // 16, body, 0, unroll=4)

    def hot_columns(first, last):
        def body(m, carry):
            ident = (lrow + m * LANES).astype(f32)
            rows = pl.ds(pl.multiple_of(m * LANES, LANES), LANES)
            for r in range(first, last):
                hot = jnp.where(ident == LR[r : r + 1, :], 1.0, 0.0).astype(bf16)
                OHT[rows, r * LANES : (r + 1) * LANES] = hot
            return carry

        lax.fori_loop(0, ncol // LANES, body, 0)

    code = code_of(label)
    turn([code, leave_at.astype(f32)])
    LR[0:8, :] = code
    for r in range(SLOT_BLOCKS):
        hot_rows(r, r)
    for r in range(SLOT_BLOCKS):
        MSK[r * LANES : (r + 1) * LANES, :] = jnp.broadcast_to(
            LT[:, 8 + r : 9 + r], (LANES, LANES)
        )
    hot_columns(0, SLOT_BLOCKS)

    for k in range(2 * nq, 2 * nq + 3):
        loads[k].wait()

    def first_state(n, carry):
        rows = pl.ds(pl.multiple_of(n * 16, 16), 16)
        rest_now = A[rows, :]
        R[rows, :] = R[rows, :] * rest_now
        S[rows, :] = time_step * S[rows, :]
        A[rows, :] = inv_ln2 * (
            jnp.log((time_step * time_step) * (1.0 + 0.2 / rest_now))
            + exponent * jnp.log(rest_now)
        )
        return carry

    lax.fori_loop(0, SLOTS // 16, first_state, 0, unroll=4)
    for k in range(2 * nq + 3, 4 * nq + 3):
        loads[k].wait()

    def plan():
        wait_taken(meta_copy)
        came = (lane8 // DEP) % 4
        alab = jnp.where(
            came == 0, MR[0], jnp.where(came == 1, MR[1], jnp.where(came == 2, MR[2], MR[3]))
        )
        present = alab > 0.0
        upper = jnp.where(lrow <= lcol, 1.0, 0.0)
        upper_block = jnp.where(lrow // 32 == lcol // 32, upper, 0.0).astype(bf16)
        upper = upper.astype(bf16)
        ones = jnp.ones((LANES, LANES), bf16)
        present_f = jnp.where(present, 1.0, 0.0)
        arank = jnp.dot(present_f.astype(bf16), upper_block, preferred_element_type=f32) - 1.0
        arank = jnp.where(present, arank, -5.0)
        vacant = label == 0
        ranks = []
        for t in range(STEPS):
            vacant = vacant | (leave_at == t)
            flag = jnp.where(vacant, 1.0, 0.0).astype(bf16)
            rank = jnp.dot(flag, upper, preferred_element_type=f32) - 1.0
            total = jnp.dot(flag, ones, preferred_element_type=f32)
            for r in range(SLOT_BLOCKS - 1):
                rank = rank + jnp.where(sub8 > r, total[r : r + 1, :], 0.0)
            ranks.append(jnp.where(vacant, rank, -1.0))
            count = jnp.sum(jnp.where(lane8 // 32 == t, present_f, 0.0), axis=1, keepdims=True)
            vacant = vacant & (rank >= count)

        acode = code_of(alab.astype(jnp.int32))
        turn(ranks + [acode, alab])
        LR[8:16, :] = acode
        hot_rows(SLOT_BLOCKS, 32)
        hot_columns(SLOT_BLOCKS, SLOT_BLOCKS + 1)
        AMSK[...] = jnp.broadcast_to(LT[:, 40:41], (LANES, LANES))

        group = lcol // 32
        alab_high, alab_low = split(alab)
        final = jnp.where(leave_at == STEPS, label, 0).astype(f32)
        nt = (((1,), (1,)), ((), ()))
        for r in range(SLOT_BLOCKS):
            mine = jnp.broadcast_to(LT[:, r : r + 1], (LANES, LANES))
            for t in range(1, STEPS):
                mine = jnp.where(group == t, LT[:, 8 * t + r : 8 * t + r + 1], mine)
            hot = jnp.where(mine == arank[0:1, :], 1.0, 0.0).astype(bf16)
            PLACE[r * LANES : (r + 1) * LANES, 0:LANES] = hot
            PLACE[r * LANES : (r + 1) * LANES, LANES : 2 * LANES] = hot
            placed = lax.dot_general(alab_high, hot, nt, preferred_element_type=f32)
            placed = placed + lax.dot_general(alab_low, hot, nt, preferred_element_type=f32)
            final = final + jnp.where(sub8 == r, placed, 0.0)
        c_out[...] = final.astype(jnp.int32) - 1

    def slope_z(tiles):
        height = tiles[0].shape[0]
        lane = lax.broadcasted_iota(jnp.int32, (height, LANES), 1)
        zero = jnp.zeros((height, LANES), f32)
        ahead = [pltpu.roll(v, LANES - 1, 1) for v in tiles] + [zero]
        behind = [zero] + [pltpu.roll(v, 1, 1) for v in tiles]
        return [
            jnp.where(lane == LANES - 1, ahead[q + 1], ahead[q])
            - jnp.where(lane == 0, behind[q], behind[q + 1])
            for q in range(nq)
        ]

    low_gate = jnp.where(has_lo, 1.0, 0.0).astype(f32)
    high_gate = jnp.where(has_hi, 1.0, 0.0).astype(f32)

    def halves(w):
        return slice(w * LANES, (w + 1) * LANES), slice(2 * w * LANES, 2 * (w + 1) * LANES)

    def gather(w):
        narrow, pair = halves(w)
        both = jnp.dot(OH[...], PHL[:, pair], preferred_element_type=f32)
        PG[:, narrow] = both[:, :LANES] + both[:, LANES:]

    def scatter(w):
        narrow, pair = halves(w)
        both = jnp.dot(OHT[...], VHL[:, pair], preferred_element_type=f32)
        SRC[:, narrow] = both[:, :LANES] + both[:, LANES:]

    def take_arrivals(t):
        wait_taken(lambda d: dep_copy(t, d))
        rows = pl.ds(pl.multiple_of(t * 32, 32), 32)
        to = pl.ds(pl.multiple_of(SLOTS + t * 32, 32), 32)
        R[to, :] = AR[0, rows, :]
        S[to, :] = AR[1, rows, :]
        A[to, :] = AR[2, rows, :]
        MSK[to, :] = jnp.where(AMSK[rows, :] > 0.0, 2.0 * STEPS, -1.0)

    def step(t, carry):
        limit = t.astype(f32)

        def bubbles(first, w):
            rows = slice(first, first + 16)
            col = halves(w)[0]
            radius, speed, rate = wall_update(R[rows, col], S[rows, col], A[rows, col], PG[rows, col])
            R[rows, col] = radius
            S[rows, col] = speed
            high, low = split(jnp.where(MSK[rows, :] >= limit, rate, 0.0))
            VHL[rows, 2 * w * LANES : (2 * w + 1) * LANES] = high
            VHL[rows, (2 * w + 1) * LANES : (2 * w + 2) * LANES] = low

        for k in range(DEP):
            slot = jnp.maximum(slot_s[t, 0, 0, k], 0)
            cell = jnp.maximum(cells_s[slot], 0)
            place = cell >> 1
            row = pl.ds(slot, 1)
            DB[0, k : k + 1, :] = R[row, :]
            DB[1, k : k + 1, :] = S[row, :]
            DB[2, k : k + 1, :] = A[row, :]
            for w in range(2):
                DB[3, k : k + 1, halves(w)[0]] = PR[
                    2 * (cell & 1) + w,
                    place >> (cy.bit_length() - 1),
                    pl.ds(8 + (place & (cy - 1)), 1),
                    :,
                ]
        radius, speed, _ = wall_update(DB[0], DB[1], DB[2], DB[3])
        SB[t, 0] = radius
        SB[t, 1] = speed
        SB[t, 2] = DB[2]
        start(lambda d: dep_copy(t, d))

        @pl.when(t > 0)
        def _():
            take_arrivals(t - 1)

        gather(0)
        gather(1)
        for first in range(0, ROWS, 16):
            bubbles(first, 0)
        scatter(0)
        for first in range(0, ROWS, 16):
            bubbles(first, 1)
        scatter(1)

        def flow_x(i):
            for q in range(nq):
                for jb in range(jbs):
                    rows, at = rows_of(jb)
                    flow = VX[q, i + 1, rows, :]
                    if i == 0:
                        flow = flow - half_gain * PR[q, 1, at, :]
                    elif i == cx - 1:
                        flow = flow + half_gain * PR[q, cx - 2, at, :]
                    else:
                        flow = flow - half_gain * (PR[q, i + 1, at, :] - PR[q, i - 1, at, :])
                    VX[q, i + 1, rows, :] = flow

        def flow_z(i, jb):
            rows, at = rows_of(jb)
            slopes = slope_z([PR[q, i, at, :] for q in range(nq)])
            for q in range(nq):
                VZ[q, i, rows, :] = VZ[q, i, rows, :] - half_gain * slopes[q]

        def flow_y(i, jb):
            _, at = rows_of(jb)
            for q in range(nq):
                VY[q, i, at, :] = VY[q, i, at, :] - half_gain * (
                    PR[q, i, pl.ds(9 + jb * 16 + zero_row, 16), :]
                    - PR[q, i, pl.ds(7 + jb * 16 + zero_row, 16), :]
                )

        def pressure(i, jb):
            rows, at = rows_of(jb)
            slopes = slope_z([VZ[q, i, rows, :] for q in range(nq)])
            for q in range(nq):
                rise = slopes[q] + (
                    VY[q, i, pl.ds(9 + jb * 16 + zero_row, 16), :]
                    - VY[q, i, pl.ds(7 + jb * 16 + zero_row, 16), :]
                )
                if i + 1 < cx:
                    rise = rise + VX[q, i + 2, rows, :]
                if i > 0:
                    rise = rise - VX[q, i, rows, :]
                row = column_row(i, q // 2, jb)
                col = (q % 2) * LANES
                PR[q, i, at, :] = (
                    PR[q, i, at, :] - half_gain * rise + SRC[row : row + 16, col : col + LANES]
                )

        for i in range(cx):
            flow_x(i)
            for jb in range(jbs):
                flow_z(i, jb)
                flow_y(i, jb)
        for i in range(cx):
            for jb in range(jbs):
                pressure(i, jb)
        pack_rows(t + 1)

        pl.when(t == 0)(plan)
        wait_taken(lambda d: p_copy(t, d), (2, 3))

        @pl.when(t > 0)
        def _():
            wait_taken(lambda d: p_copy(t, d), (0, 1))

        @pl.when(t == 0)
        def _():
            for d in range(2):
                for copy in first_copies(d):
                    copy.wait_recv()
            wait_taken(v_copy, (2, 3))

        below, above = VYR[0], VYR[1]
        below = low_gate * (below - half_gain * (YS[t, 0, 0] - YR[t, 0, 0]))
        above = high_gate * (above - half_gain * (YR[t, 1, 1] - YS[t, 1, 1]))
        VYR[0] = below
        VYR[1] = above
        both_gains = half_gain * half_gain
        YS[t + 1, 0, 0] = YS[t + 1, 0, 0] + half_gain * below
        YS[t + 1, 0, 1] = YS[t + 1, 0, 1] + both_gains * YR[t, 0, 1]
        YS[t + 1, 1, 0] = YS[t + 1, 1, 0] + both_gains * YR[t, 1, 0]
        YS[t + 1, 1, 1] = YS[t + 1, 1, 1] - half_gain * above
        for q in range(nq):
            for jb in range(jbs):
                rows, at = rows_of(jb)
                far, near = XR[t, 0, q, 0, rows, :], XR[t, 0, q, 1, rows, :]
                beside = VX[q, 0, rows, :] - half_gain * (XS[t, 0, q, 0, rows, :] - far)
                VX[q, 0, rows, :] = beside
                VX[q, 1, rows, :] = VX[q, 1, rows, :] + half_gain * near
                first = PR[q, 0, at, :] + half_gain * beside
                second = PR[q, 1, at, :] + both_gains * near
                PR[q, 0, at, :] = first
                PR[q, 1, at, :] = second
                XS[t + 1, 0, q, 0, rows, :] = first
                XS[t + 1, 0, q, 1, rows, :] = second
                near, far = XR[t, 1, q, 0, rows, :], XR[t, 1, q, 1, rows, :]
                beside = VX[q, cx + 1, rows, :] - half_gain * (far - XS[t, 1, q, 1, rows, :])
                VX[q, cx + 1, rows, :] = beside
                VX[q, cx, rows, :] = VX[q, cx, rows, :] - half_gain * near
                first = PR[q, cx - 2, at, :] + both_gains * near
                second = PR[q, cx - 1, at, :] - half_gain * beside
                PR[q, cx - 2, at, :] = first
                PR[q, cx - 1, at, :] = second
                XS[t + 1, 1, q, 0, rows, :] = first
                XS[t + 1, 1, q, 1, rows, :] = second
        ends = ((0, 0, 0), (1, 0, 1), (cx - 2, 1, 0), (cx - 1, 1, 1))
        for i, x_side, x_row in ends:
            for side in range(2):
                for r in range(2):
                    for q in range(nq):
                        row = one(edges[side][r])
                        if i == 0:
                            part_x = half_gain * VX[q, 0, row, :]
                        elif i == 1:
                            part_x = both_gains * XR[t, 0, q, 1, row, :]
                        elif i == cx - 2:
                            part_x = both_gains * XR[t, 1, q, 0, row, :]
                        else:
                            part_x = -half_gain * VX[q, cx + 1, row, :]
                        value = YS[t + 1, side, r, q, one(i), :] + part_x
                        YS[t + 1, side, r, q, one(i), :] = value
                        XS[t + 1, x_side, q, x_row, row, :] = value

        @pl.when(t < STEPS - 1)
        def _():
            start(lambda d: p_copy(t + 1, d))

        unpack_rows(t + 1, range(cx))
        for q in range(nq):
            for i in range(cx):
                low, high = one(8), one(7 + cy)
                VY[q, i, low, :] = VY[q, i, low, :] + half_gain * YR[t, 0, 1, q, one(i), :]
                VY[q, i, high, :] = VY[q, i, high, :] - half_gain * YR[t, 1, 0, q, one(i), :]

        @pl.when(t < STEPS - 1)
        def _():
            split_all()

        return carry

    lax.fori_loop(0, STEPS, step, 0)

    take_arrivals(STEPS - 1)
    keep = AMSK[...] > 0.0
    for k, state in enumerate((R, S)):
        for w in range(2):
            high, low = split(jnp.where(keep, state[SLOTS:ROWS, halves(w)[0]], 0.0))
            to = slice(k * BLOCK + w * LANES, k * BLOCK + (w + 1) * LANES)
            CAT[0:ARRIVE, to] = high
            CAT[ARRIVE : 2 * ARRIVE, to] = low

    wait_sent(meta_copy)
    for t in range(STEPS):
        wait_sent(lambda d, t=t: dep_copy(t, d))
        wait_sent(lambda d, t=t: p_copy(t, d), (2, 3) if t == 0 else (0, 1, 2, 3))
    wait_sent(v_copy, (2, 3))
    for d in range(2):
        for copy in first_copies(d):
            copy.wait_send()


def write_out(
    p, vx, vy, vz, r, s, mask, place, cat, c, p_out, v_out, r_out, s_out, c_out, r_end, s_end, sems
):
    _, cx, cy, nz = v_out.shape
    pairs = []
    for q in range(nz // LANES):
        lanes = pl.ds(q * LANES, LANES)
        pairs.append((vx.at[q, pl.ds(1, cx), :, :], v_out.at[0, :, :, lanes]))
        pairs.append((vy.at[q, :, pl.ds(8, cy), :], v_out.at[1, :, :, lanes]))
        pairs.append((vz.at[q], v_out.at[2, :, :, lanes]))
        pairs.append((p.at[q, :, pl.ds(8, cy), :], p_out.at[:, :, lanes]))
    pairs.append((c, c_out))
    copies = [pltpu.make_async_copy(a, b, sems.at[k]) for k, (a, b) in enumerate(pairs)]
    for copy in copies:
        copy.start()
    count = 256
    for first in range(0, SLOTS, count):
        rows = slice(first, first + count)
        placed = jnp.dot(place[rows, :], cat[...], preferred_element_type=f32)
        keep = mask[rows, :]
        keep = jnp.concatenate([keep, keep], axis=1) >= float(STEPS)
        r_end[rows, :] = jnp.where(keep, r[rows, :], 0.0) + placed[:, :BLOCK]
        s_end[rows, :] = (1.0 / time_step) * (jnp.where(keep, s[rows, :], 0.0) + placed[:, BLOCK:])
        for a, b in ((r_end, r_out), (s_end, s_out)):
            rows_of = pl.ds(first, count)
            copy = pltpu.make_async_copy(a.at[rows_of, :], b.at[rows_of, :], sems.at[len(copies)])
            copy.start()
            copies.append(copy)
    for copy in copies:
        copy.wait()


def on_device(
    pressure, velocity, stretch, rest_radius, wall_speed, block_cells, depart_slot, depart_way
):
    cx, cy, nz = pressure.shape
    nq = nz // LANES
    ncol = 2 * cx * cy
    vmem = pl.BlockSpec(memory_space=pltpu.VMEM)
    hbm = pl.BlockSpec(memory_space=pl.ANY)
    dma = pltpu.SemaphoreType.DMA
    vmem_out = pltpu.VMEM
    parts = pl.pallas_call(
        kernel,
        out_shape=(
            vmem_out((nq, cx, cy + 16, LANES), f32),
            vmem_out((nq, cx + 2, cy, LANES), f32),
            vmem_out((nq, cx, cy + 16, LANES), f32),
            vmem_out((nq, cx, cy, LANES), f32),
            vmem_out((ROWS, BLOCK), f32),
            vmem_out((ROWS, BLOCK), f32),
            vmem_out((ROWS, LANES), f32),
            vmem_out((SLOTS, 2 * ARRIVE), bf16),
            vmem_out((2 * ARRIVE, 2 * BLOCK), bf16),
            vmem_out((SLOT_BLOCKS, LANES), jnp.int32),
        ),
        in_specs=[pl.BlockSpec(memory_space=pltpu.HBM)] * 9,
        out_specs=(vmem,) * 10,
        scratch_shapes=[
            pltpu.VMEM((ROWS, BLOCK), f32),
            pltpu.VMEM((3, ARRIVE, BLOCK), f32),
            pltpu.VMEM((STEPS, 3, DEP, BLOCK), f32),
            pltpu.VMEM((4, DEP, BLOCK), f32),
            pltpu.VMEM((ROWS, ncol), bf16),
            pltpu.VMEM((ncol, ROWS), bf16),
            pltpu.VMEM((ncol, 2 * BLOCK), bf16),
            pltpu.VMEM((ROWS, BLOCK), f32),
            pltpu.VMEM((ROWS, 2 * BLOCK), bf16),
            pltpu.VMEM((ncol, BLOCK), f32),
            pltpu.VMEM((STEPS + 1, 2, nq, 2, cy, LANES), f32),
            pltpu.VMEM((STEPS, 2, nq, 2, cy, LANES), f32),
            pltpu.VMEM((STEPS + 1, 2, 2, nq, cx, LANES), f32),
            pltpu.VMEM((STEPS, 2, 2, nq, cx, LANES), f32),
            pltpu.VMEM((2, nq, cx, LANES), f32),
            pltpu.VMEM((2, nq, cx, LANES), f32),
            pltpu.VMEM((8, LANES), f32),
            pltpu.VMEM((4, 8, LANES), f32),
            pltpu.VMEM((ARRIVE, LANES), f32),
            pltpu.VMEM((LANES, LANES), f32),
            pltpu.VMEM((16, LANES), f32),
            pltpu.SMEM((SLOTS,), jnp.int32),
            pltpu.SMEM((STEPS, 1, 1, DEP), jnp.int32),
            pltpu.SMEM((STEPS, 1, 1, DEP), jnp.int32),
            pltpu.VMEM((SLOT_BLOCKS, LANES), jnp.int32),
            dma((4 * nq + 7,)),
            dma((4,)),
            dma((4,)),
            dma((STEPS, 4)),
            dma((STEPS, 4)),
            dma((4,)),
            dma((4,)),
            dma((STEPS, 4)),
            dma((STEPS, 4)),
            dma((2, 2, nq)),
            dma((2, 2, nq)),
        ],
        compiler_params=pltpu.CompilerParams(
            collective_id=0, has_side_effects=True, vmem_limit_bytes=36 * 2**20
        ),
        cost_estimate=pl.CostEstimate(
            flops=10 * 2**30, bytes_accessed=13 * 2**20, transcendentals=2**22
        ),
    )(
        *(
            pltpu.with_memory_space_constraint(value, pltpu.HBM)
            for value in (
                block_cells,
                depart_slot,
                depart_way,
                block_cells.reshape(SLOT_BLOCKS, LANES),
                pressure,
                velocity,
                stretch,
                rest_radius,
                wall_speed,
            )
        )
    )
    parts = [pltpu.with_memory_space_constraint(part, pltpu.VMEM) for part in parts]
    p, v, r, s, c = pl.pallas_call(
        write_out,
        out_shape=(
            jax.ShapeDtypeStruct(pressure.shape, f32),
            jax.ShapeDtypeStruct(velocity.shape, f32),
            jax.ShapeDtypeStruct(stretch.shape, f32),
            jax.ShapeDtypeStruct(stretch.shape, f32),
            jax.ShapeDtypeStruct((SLOT_BLOCKS, LANES), jnp.int32),
        ),
        in_specs=[vmem] * 10,
        out_specs=(hbm,) * 5,
        scratch_shapes=[
            pltpu.VMEM((SLOTS, BLOCK), f32),
            pltpu.VMEM((SLOTS, BLOCK), f32),
            dma((4 * nq + 1 + 8,)),
        ],
        compiler_params=pltpu.CompilerParams(vmem_limit_bytes=8 * 2**20),
        cost_estimate=pl.CostEstimate(flops=0, bytes_accessed=13 * 2**20, transcendentals=0),
    )(*parts)
    return p, v, r, s, c.reshape(-1)


def solution(mesh):
    placed = (
        P("gx", "gy", None),
        P(None, "gx", "gy", None),
        P(("gx", "gy"), None),
        P(("gx", "gy"), None),
        P(("gx", "gy"), None),
        P(("gx", "gy")),
        P(None, "gx", "gy", None),
        P(None, "gx", "gy", None),
    )
    return jax.shard_map(
        on_device,
        mesh=mesh,
        in_specs=placed,
        out_specs=(
            P("gx", "gy", None),
            P(None, "gx", "gy", None),
            P(("gx", "gy"), None),
            P(("gx", "gy"), None),
            P(("gx", "gy")),
        ),
        check_vma=False,
    )
```

```python
import functools
import math

import jax
import jax.numpy as jnp
from jax import lax
from jax.experimental import pallas as pl
from jax.experimental.pallas import tpu as pltpu
from jax.sharding import PartitionSpec as P

MESH = pl.DeviceIdType.MESH
f32 = jnp.float32
bf16 = jnp.bfloat16

STEPS = 4
DEP = 8
SLOTS = 1024
BLOCK = 256
LANES = 128
ARRIVE = STEPS * 4 * DEP
ROWS = SLOTS + ARRIVE
SLOT_BLOCKS = SLOTS // LANES
WAY_OF = (1, 0, 3, 2)

time_step = 0.04
half_gain = 0.2
source_scale = 0.004 * 12.566370614359172
exponent = 4.2
inv_ln2 = 1.0 / math.log(2.0)


def split(value):
    high = value.astype(bf16)
    return high, (value - high.astype(f32)).astype(bf16)


def wall_update(radius, shift, level, pressure):
    mach = (0.05 / time_step) * shift
    one_less = 1.0 - mach
    divisor = one_less * radius
    inverse = pl.reciprocal(divisor, approx=True)
    inverse = inverse * (2.0 - divisor * inverse)
    inv_radius = inverse * one_less
    wall = jnp.exp2(level - (exponent * inv_ln2) * jnp.log(radius))
    squared = time_step * time_step
    excess = (
        wall
        - (0.2 * squared + (0.08 * time_step) * shift) * inv_radius
        - (squared + squared * pressure)
    )
    driving = (1.0 + mach) * excess - (1.5 - 0.5 * mach) * (shift * shift)
    shift = shift + driving * inverse
    radius = radius + shift
    return radius, shift, (source_scale / time_step) * (radius * radius) * shift


def kernel(
    cells_h, slot_h, way_h, cells_b, press, vel, stretch, rest, speed0,
    PR, VX, VY, VZ, R, S, MSK, PLACE, CAT, c_out,
    A, AR, SB, DB, OH, OHT, PHL, PG, VHL, SRC, XS, XR, YS, YR, VYS, VYR,
    MT, MR, AMSK, LT, LR, cells_s, slot_s, way_s, cells_v,
    in_sem, meta_s, meta_r, xs, xr, vs, vr, ds_, dr, fs, fr,
):
    _, cx, cy, nz = vel.shape
    nq = nz // LANES
    half = cx * cy
    ncol = 2 * half
    jbs = cy // 16
    part = min(256, ncol)
    planes = part // (2 * cy)
    groups = cx // planes
    shift = (planes * cy).bit_length() - 1
    zero_row = lax.axis_index("gx") // 4096
    gx, gy = lax.axis_index("gx"), lax.axis_index("gy")
    ngx, ngy = lax.axis_size("gx"), lax.axis_size("gy")
    has_lo, has_hi = gy > 0, gy < ngy - 1
    targets = (
        (lax.rem(gx + 1, ngx), gy),
        (lax.rem(gx + ngx - 1, ngx), gy),
        (gx, lax.rem(gy + 1, ngy)),
        (gx, lax.rem(gy + ngy - 1, ngy)),
    )
    sends = (None, None, has_hi, has_lo)
    takes = (None, None, has_lo, has_hi)

    def under(flag, action):
        if flag is None:
            action()
        else:
            pl.when(flag)(action)

    barrier = pltpu.get_barrier_semaphore()
    for d in range(4):
        under(
            sends[d],
            lambda d=d: pl.semaphore_signal(
                barrier, inc=1, device_id=targets[d], device_id_type=MESH
            ),
        )

    inputs = [(cells_h, cells_s), (slot_h, slot_s), (way_h, way_s), (cells_b, cells_v)]
    for q in range(nq):
        inputs.append((press.at[:, :, pl.ds(q * LANES, LANES)], PR.at[q, :, pl.ds(8, cy), :]))
    for q in range(nq):
        lanes = pl.ds(q * LANES, LANES)
        inputs.append((vel.at[1, :, :, lanes], VY.at[q, :, pl.ds(8, cy), :]))
    own = pl.ds(0, SLOTS)
    inputs.append((rest, A.at[own, :]))
    inputs.append((stretch, R.at[own, :]))
    inputs.append((speed0, S.at[own, :]))
    for q in range(nq):
        lanes = pl.ds(q * LANES, LANES)
        inputs.append((vel.at[0, :, :, lanes], VX.at[q, pl.ds(1, cx), :, :]))
        inputs.append((vel.at[2, :, :, lanes], VZ.at[q]))
    loads = [pltpu.make_async_copy(a, b, in_sem.at[k]) for k, (a, b) in enumerate(inputs)]
    for load in loads:
        load.start()
    small_loads, loads = loads[:4], loads[4:]

    @pl.when(jnp.logical_not(has_lo))
    def _():
        MR[2] = jnp.zeros((8, LANES), f32)
        YR[:, 0] = jnp.zeros(YR.shape[:1] + YR.shape[2:], f32)
        VYR[0] = jnp.zeros(VYR.shape[1:], f32)

    @pl.when(jnp.logical_not(has_hi))
    def _():
        MR[3] = jnp.zeros((8, LANES), f32)
        YR[:, 1] = jnp.zeros(YR.shape[:1] + YR.shape[2:], f32)
        VYR[1] = jnp.zeros(VYR.shape[1:], f32)

    edge_rows = jnp.zeros((nq, cx, 8, LANES), f32)
    PR[:, :, 0:8, :] = edge_rows
    PR[:, :, 8 + cy : 16 + cy, :] = edge_rows
    VY[:, :, 0:8, :] = edge_rows
    VY[:, :, 8 + cy : 16 + cy, :] = edge_rows
    empty = jnp.zeros((ARRIVE, BLOCK), f32)
    R[SLOTS:ROWS, :] = empty + 1.0
    S[SLOTS:ROWS, :] = empty
    A[SLOTS:ROWS, :] = empty
    MSK[SLOTS:ROWS, :] = jnp.full((ARRIVE, LANES), -1.0, f32)
    OHT[:, SLOTS:ROWS] = jnp.zeros((ncol, ARRIVE), bf16)
    OH[SLOTS:ROWS, :] = jnp.zeros((ARRIVE, ncol), bf16)
    pl.semaphore_wait(barrier, 2 + has_lo.astype(jnp.int32) + has_hi.astype(jnp.int32))

    def remote(src, dst, send_sem, recv_sem, d):
        return pltpu.make_async_remote_copy(
            src_ref=src, dst_ref=dst, send_sem=send_sem, recv_sem=recv_sem,
            device_id=targets[d], device_id_type=MESH,
        )

    def meta_copy(d):
        return [remote(MT, MR.at[d], meta_s.at[d], meta_r.at[d], d)]

    pieces = nq

    def p_copy(t, d):
        for k in range(pieces):
            sems = xs.at[t, d, k], xr.at[t, d, k]
            if d < 2:
                yield remote(XS.at[t, 1 - d, k], XR.at[t, d, k], *sems, d)
            else:
                yield remote(YS.at[t, 3 - d, :, k], YR.at[t, d - 2, :, k], *sems, d)

    def first_copies(d):
        side = (cx - 2, 0)[d]
        for q in range(nq):
            lanes = pl.ds(q * LANES, LANES)
            yield remote(
                press.at[pl.ds(side, 2), :, lanes], XR.at[0, d, q], fs.at[0, d, q], fr.at[0, d, q], d
            )
        for q in range(nq):
            lanes = pl.ds(q * LANES, LANES)
            yield remote(
                vel.at[0, pl.ds((cx - 1, 0)[d], 1), :, lanes],
                VX.at[q, pl.ds((0, cx + 1)[d], 1), :, :],
                fs.at[1, d, q],
                fr.at[1, d, q],
                d,
            )

    def v_copy(d):
        return [remote(VYS.at[3 - d], VYR.at[d - 2], vs.at[d], vr.at[d], d)]

    def dep_copy(t, d):
        to = AR.at[:, pl.ds(t * 32 + d * DEP, DEP), :]
        return [remote(SB.at[t], to, ds_.at[t, d], dr.at[t, d], d)]

    odd = lax.rem(gy, 2) == 1
    even = jnp.logical_not(odd)
    far_hi, near_hi = has_hi & odd, has_hi & even
    far_lo, near_lo = has_lo & even, has_lo & odd

    def start(make, ways=(0, 1, 2, 3)):
        order = ((far_hi, 2), (far_lo, 3), (None, 0), (None, 1), (near_hi, 2), (near_lo, 3))
        for flag, d in order:
            if d in ways:
                under(flag, lambda d=d: [copy.start() for copy in make(d)] and None)

    def wait_sent(make, ways=(0, 1, 2, 3)):
        for d in ways:
            under(sends[d], lambda d=d: [copy.wait_send() for copy in make(d)] and None)

    def wait_taken(make, ways=(0, 1, 2, 3)):
        for d in ways:
            under(takes[d], lambda d=d: [copy.wait_recv() for copy in make(d)] and None)

    for d in range(2):
        for copy in first_copies(d):
            copy.start()
    edges = ((0, 1), (cy - 2, cy - 1))

    def one(row):
        return pl.ds(row + zero_row, 1)

    pitch = cy + 16
    PR_rows = PR.reshape(nq * cx * pitch, LANES)
    VY_rows = VY.reshape(nq * cx * pitch, LANES)

    def across(q, row):
        return pl.ds(q * cx * pitch + 8 + row, cx, stride=pitch), slice(None)

    def pack_rows(t):
        for side in range(2):
            for r in range(2):
                for q in range(nq):
                    YS[t, side, r, q] = PR_rows[across(q, edges[side][r])]

    def unpack_rows(t):
        for side in range(2):
            for r in range(2):
                for q in range(nq):
                    PR_rows[across(q, edges[side][r])] = YS[t, side, r, q]

    def column_row(i, h, jb):
        return (i // planes) * part + (h * planes + i % planes) * cy + jb * 16

    def keep_parts(i, jb, q, value):
        high, low = split(value)
        row = column_row(i, q // 2, jb)
        col = (q % 2) * 2 * LANES
        PHL[row : row + 16, col : col + LANES] = high
        PHL[row : row + 16, col + LANES : col + 2 * LANES] = low

    def rows_of(jb):
        return slice(jb * 16, jb * 16 + 16), slice(8 + jb * 16, 24 + jb * 16)

    def split_all():
        for i in range(cx):
            for jb in range(jbs):
                for q in range(nq):
                    keep_parts(i, jb, q, PR[q, i, rows_of(jb)[1], :])

    for k in range(nq):
        loads[k].wait()
    pack_rows(0)
    start(lambda d: p_copy(0, d), (2, 3))
    for q in range(nq):
        for r in range(2):
            XS[0, 0, q, r] = PR[q, r, 8 : 8 + cy, :]
            XS[0, 1, q, r] = PR[q, cx - 2 + r, 8 : 8 + cy, :]
    for k in range(nq, 2 * nq):
        loads[k].wait()
    for q in range(nq):
        VYS[0, q] = VY_rows[across(q, 0)]
        VYS[1, q] = VY_rows[across(q, cy - 1)]
    start(v_copy, (2, 3))

    for load in small_loads:
        load.wait()

    lane8 = lax.broadcasted_iota(jnp.int32, (8, LANES), 1)
    sub8 = lax.broadcasted_iota(jnp.int32, (8, LANES), 0)
    slot_id = sub8 * LANES + lane8
    label = cells_v[...] + 1
    leave_at = jnp.where(label > 0, STEPS, -1)
    entry_of = (lane8 // 32) * DEP + lane8 % DEP
    wanted = (lane8 // DEP) % 4
    wanted = jnp.where(wanted < 2, 1 - wanted, 5 - wanted)
    meta = jnp.zeros((8, LANES), jnp.int32)
    for e in range(STEPS * DEP):
        slot = slot_s[e // DEP, 0, 0, e % DEP]
        moved = jnp.where(slot >= 0, cells_s[jnp.maximum(slot, 0)] + 1, 0)
        meta = jnp.where((entry_of == e) & (wanted == way_s[e // DEP, 0, 0, e % DEP]), moved, meta)
        leave_at = jnp.where(slot_id == slot, e // DEP, leave_at)
    MT[...] = meta.astype(f32)

    start(meta_copy)

    split_all()

    lrow = lax.broadcasted_iota(jnp.int32, (LANES, LANES), 0)
    lcol = lax.broadcasted_iota(jnp.int32, (LANES, LANES), 1)
    wide = lax.broadcasted_iota(jnp.int32, (16, ncol), 1).astype(f32)

    def code_of(lab):
        cell = lab - 1
        place = cell >> 1
        row = (place >> shift) * part + (cell & 1) * (planes * cy)
        return jnp.where(lab > 0, row + (place & (planes * cy - 1)), -1).astype(f32)

    def turn(stack):
        stack = stack + [jnp.zeros((8, LANES), f32)] * (16 - len(stack))
        LT[...] = jnp.concatenate(stack, axis=0).T

    def hot_rows(r, at):
        def body(m, carry):
            rows = pl.ds(pl.multiple_of(m * 16, 16), 16)
            hot = jnp.where(LT[rows, at : at + 1] == wide, 1.0, 0.0).astype(bf16)
            OH[pl.ds(pl.multiple_of(r * LANES + m * 16, 16), 16), :] = hot
            return carry

        lax.fori_loop(0, LANES // 16, body, 0, unroll=4)

    def hot_columns(first, last):
        def body(m, carry):
            ident = (lrow + m * LANES).astype(f32)
            rows = pl.ds(pl.multiple_of(m * LANES, LANES), LANES)
            for r in range(first, last):
                hot = jnp.where(ident == LR[r : r + 1, :], 1.0, 0.0).astype(bf16)
                OHT[rows, r * LANES : (r + 1) * LANES] = hot
            return carry

        lax.fori_loop(0, ncol // LANES, body, 0)

    code = code_of(label)
    turn([code, leave_at.astype(f32)])
    LR[0:8, :] = code
    for r in range(SLOT_BLOCKS):
        hot_rows(r, r)
    for r in range(SLOT_BLOCKS):
        MSK[r * LANES : (r + 1) * LANES, :] = jnp.broadcast_to(
            LT[:, 8 + r : 9 + r], (LANES, LANES)
        )
    hot_columns(0, SLOT_BLOCKS)

    for k in range(2 * nq, 2 * nq + 3):
        loads[k].wait()

    def first_state(n, carry):
        rows = pl.ds(pl.multiple_of(n * 16, 16), 16)
        rest_now = A[rows, :]
        R[rows, :] = R[rows, :] * rest_now
        S[rows, :] = time_step * S[rows, :]
        A[rows, :] = inv_ln2 * (
            jnp.log((time_step * time_step) * (1.0 + 0.2 / rest_now))
            + exponent * jnp.log(rest_now)
        )
        return carry

    lax.fori_loop(0, SLOTS // 16, first_state, 0, unroll=4)
    for k in range(2 * nq + 3, 4 * nq + 3):
        loads[k].wait()

    def plan():
        wait_taken(meta_copy)
        came = (lane8 // DEP) % 4
        alab = jnp.where(
            came == 0, MR[0], jnp.where(came == 1, MR[1], jnp.where(came == 2, MR[2], MR[3]))
        )
        present = alab > 0.0
        upper = jnp.where(lrow <= lcol, 1.0, 0.0)
        upper_block = jnp.where(lrow // 32 == lcol // 32, upper, 0.0).astype(bf16)
        upper = upper.astype(bf16)
        ones = jnp.ones((LANES, LANES), bf16)
        present_f = jnp.where(present, 1.0, 0.0)
        arank = jnp.dot(present_f.astype(bf16), upper_block, preferred_element_type=f32) - 1.0
        arank = jnp.where(present, arank, -5.0)
        vacant = label == 0
        ranks = []
        for t in range(STEPS):
            vacant = vacant | (leave_at == t)
            flag = jnp.where(vacant, 1.0, 0.0).astype(bf16)
            rank = jnp.dot(flag, upper, preferred_element_type=f32) - 1.0
            total = jnp.dot(flag, ones, preferred_element_type=f32)
            for r in range(SLOT_BLOCKS - 1):
                rank = rank + jnp.where(sub8 > r, total[r : r + 1, :], 0.0)
            ranks.append(jnp.where(vacant, rank, -1.0))
            count = jnp.sum(jnp.where(lane8 // 32 == t, present_f, 0.0), axis=1, keepdims=True)
            vacant = vacant & (rank >= count)

        acode = code_of(alab.astype(jnp.int32))
        turn(ranks + [acode, alab])
        LR[8:16, :] = acode
        hot_rows(SLOT_BLOCKS, 32)
        hot_columns(SLOT_BLOCKS, SLOT_BLOCKS + 1)
        AMSK[...] = jnp.broadcast_to(LT[:, 40:41], (LANES, LANES))

        group = lcol // 32
        alab_high, alab_low = split(alab)
        final = jnp.where(leave_at == STEPS, label, 0).astype(f32)
        nt = (((1,), (1,)), ((), ()))
        for r in range(SLOT_BLOCKS):
            mine = jnp.broadcast_to(LT[:, r : r + 1], (LANES, LANES))
            for t in range(1, STEPS):
                mine = jnp.where(group == t, LT[:, 8 * t + r : 8 * t + r + 1], mine)
            hot = jnp.where(mine == arank[0:1, :], 1.0, 0.0).astype(bf16)
            PLACE[r * LANES : (r + 1) * LANES, 0:LANES] = hot
            PLACE[r * LANES : (r + 1) * LANES, LANES : 2 * LANES] = hot
            placed = lax.dot_general(alab_high, hot, nt, preferred_element_type=f32)
            placed = placed + lax.dot_general(alab_low, hot, nt, preferred_element_type=f32)
            final = final + jnp.where(sub8 == r, placed, 0.0)
        c_out[...] = final.astype(jnp.int32) - 1

    def slope_z(tiles):
        height = tiles[0].shape[0]
        lane = lax.broadcasted_iota(jnp.int32, (height, LANES), 1)
        zero = jnp.zeros((height, LANES), f32)
        ahead = [pltpu.roll(v, LANES - 1, 1) for v in tiles] + [zero]
        behind = [zero] + [pltpu.roll(v, 1, 1) for v in tiles]
        return [
            jnp.where(lane == LANES - 1, ahead[q + 1], ahead[q])
            - jnp.where(lane == 0, behind[q], behind[q + 1])
            for q in range(nq)
        ]

    low_gate = jnp.where(has_lo, 1.0, 0.0).astype(f32)
    high_gate = jnp.where(has_hi, 1.0, 0.0).astype(f32)

    def halves(w):
        return slice(w * LANES, (w + 1) * LANES), slice(2 * w * LANES, 2 * (w + 1) * LANES)

    def gather(w):
        narrow, pair = halves(w)
        both = jnp.dot(OH[...], PHL[:, pair], preferred_element_type=f32)
        PG[:, narrow] = both[:, :LANES] + both[:, LANES:]

    def scatter(w):
        narrow, pair = halves(w)
        both = jnp.dot(OHT[...], VHL[:, pair], preferred_element_type=f32)
        SRC[:, narrow] = both[:, :LANES] + both[:, LANES:]

    def take_arrivals(t):
        wait_taken(lambda d: dep_copy(t, d))
        rows = pl.ds(pl.multiple_of(t * 32, 32), 32)
        to = pl.ds(pl.multiple_of(SLOTS + t * 32, 32), 32)
        R[to, :] = AR[0, rows, :]
        S[to, :] = AR[1, rows, :]
        A[to, :] = AR[2, rows, :]
        MSK[to, :] = jnp.where(AMSK[rows, :] > 0.0, 2.0 * STEPS, -1.0)

    def step(t, carry):
        limit = t.astype(f32)

        def bubbles(first, w):
            rows = slice(first, first + 16)
            col = halves(w)[0]
            radius, speed, rate = wall_update(R[rows, col], S[rows, col], A[rows, col], PG[rows, col])
            R[rows, col] = radius
            S[rows, col] = speed
            high, low = split(jnp.where(MSK[rows, :] >= limit, rate, 0.0))
            VHL[rows, 2 * w * LANES : (2 * w + 1) * LANES] = high
            VHL[rows, (2 * w + 1) * LANES : (2 * w + 2) * LANES] = low

        for k in range(DEP):
            slot = jnp.maximum(slot_s[t, 0, 0, k], 0)
            cell = jnp.maximum(cells_s[slot], 0)
            place = cell >> 1
            row = pl.ds(slot, 1)
            DB[0, k : k + 1, :] = R[row, :]
            DB[1, k : k + 1, :] = S[row, :]
            DB[2, k : k + 1, :] = A[row, :]
            for w in range(2):
                DB[3, k : k + 1, halves(w)[0]] = PR[
                    2 * (cell & 1) + w,
                    place >> (cy.bit_length() - 1),
                    pl.ds(8 + (place & (cy - 1)), 1),
                    :,
                ]
        radius, speed, _ = wall_update(DB[0], DB[1], DB[2], DB[3])
        SB[t, 0] = radius
        SB[t, 1] = speed
        SB[t, 2] = DB[2]
        start(lambda d: dep_copy(t, d))

        @pl.when(t > 0)
        def _():
            take_arrivals(t - 1)

        gather(0)
        gather(1)
        for first in range(0, ROWS, 16):
            bubbles(first, 0)
        scatter(0)
        for first in range(0, ROWS, 16):
            bubbles(first, 1)
        scatter(1)

        def flow_x(i):
            for q in range(nq):
                for jb in range(jbs):
                    rows, at = rows_of(jb)
                    flow = VX[q, i + 1, rows, :]
                    if i == 0:
                        flow = flow - half_gain * PR[q, 1, at, :]
                    elif i == cx - 1:
                        flow = flow + half_gain * PR[q, cx - 2, at, :]
                    else:
                        flow = flow - half_gain * (PR[q, i + 1, at, :] - PR[q, i - 1, at, :])
                    VX[q, i + 1, rows, :] = flow

        def flow_z(i, jb):
            rows, at = rows_of(jb)
            slopes = slope_z([PR[q, i, at, :] for q in range(nq)])
            for q in range(nq):
                VZ[q, i, rows, :] = VZ[q, i, rows, :] - half_gain * slopes[q]

        def flow_y(i, jb):
            _, at = rows_of(jb)
            for q in range(nq):
                VY[q, i, at, :] = VY[q, i, at, :] - half_gain * (
                    PR[q, i, pl.ds(9 + jb * 16 + zero_row, 16), :]
                    - PR[q, i, pl.ds(7 + jb * 16 + zero_row, 16), :]
                )

        def pressure(i, jb):
            rows, at = rows_of(jb)
            slopes = slope_z([VZ[q, i, rows, :] for q in range(nq)])
            for q in range(nq):
                rise = slopes[q] + (
                    VY[q, i, pl.ds(9 + jb * 16 + zero_row, 16), :]
                    - VY[q, i, pl.ds(7 + jb * 16 + zero_row, 16), :]
                )
                if i + 1 < cx:
                    rise = rise + VX[q, i + 2, rows, :]
                if i > 0:
                    rise = rise - VX[q, i, rows, :]
                row = column_row(i, q // 2, jb)
                col = (q % 2) * LANES
                PR[q, i, at, :] = (
                    PR[q, i, at, :] - half_gain * rise + SRC[row : row + 16, col : col + LANES]
                )

        for i in range(cx):
            flow_x(i)
            for jb in range(jbs):
                flow_z(i, jb)
                flow_y(i, jb)
        for i in range(cx):
            for jb in range(jbs):
                pressure(i, jb)
        pack_rows(t + 1)

        pl.when(t == 0)(plan)
        wait_taken(lambda d: p_copy(t, d), (2, 3))

        @pl.when(t > 0)
        def _():
            wait_taken(lambda d: p_copy(t, d), (0, 1))

        @pl.when(t == 0)
        def _():
            for d in range(2):
                for copy in first_copies(d):
                    copy.wait_recv()
            wait_taken(v_copy, (2, 3))

        below, above = VYR[0], VYR[1]
        below = low_gate * (below - half_gain * (YS[t, 0, 0] - YR[t, 0, 0]))
        above = high_gate * (above - half_gain * (YR[t, 1, 1] - YS[t, 1, 1]))
        VYR[0] = below
        VYR[1] = above
        both_gains = half_gain * half_gain
        YS[t + 1, 0, 0] = YS[t + 1, 0, 0] + half_gain * below
        YS[t + 1, 0, 1] = YS[t + 1, 0, 1] + both_gains * YR[t, 0, 1]
        YS[t + 1, 1, 0] = YS[t + 1, 1, 0] + both_gains * YR[t, 1, 0]
        YS[t + 1, 1, 1] = YS[t + 1, 1, 1] - half_gain * above
        for q in range(nq):
            for jb in range(jbs):
                rows, at = rows_of(jb)
                far, near = XR[t, 0, q, 0, rows, :], XR[t, 0, q, 1, rows, :]
                beside = VX[q, 0, rows, :] - half_gain * (XS[t, 0, q, 0, rows, :] - far)
                VX[q, 0, rows, :] = beside
                VX[q, 1, rows, :] = VX[q, 1, rows, :] + half_gain * near
                first = PR[q, 0, at, :] + half_gain * beside
                second = PR[q, 1, at, :] + both_gains * near
                PR[q, 0, at, :] = first
                PR[q, 1, at, :] = second
                XS[t + 1, 0, q, 0, rows, :] = first
                XS[t + 1, 0, q, 1, rows, :] = second
                near, far = XR[t, 1, q, 0, rows, :], XR[t, 1, q, 1, rows, :]
                beside = VX[q, cx + 1, rows, :] - half_gain * (far - XS[t, 1, q, 1, rows, :])
                VX[q, cx + 1, rows, :] = beside
                VX[q, cx, rows, :] = VX[q, cx, rows, :] - half_gain * near
                first = PR[q, cx - 2, at, :] + both_gains * near
                second = PR[q, cx - 1, at, :] - half_gain * beside
                PR[q, cx - 2, at, :] = first
                PR[q, cx - 1, at, :] = second
                XS[t + 1, 1, q, 0, rows, :] = first
                XS[t + 1, 1, q, 1, rows, :] = second
        ends = ((0, 0, 0), (1, 0, 1), (cx - 2, 1, 0), (cx - 1, 1, 1))
        for i, x_side, x_row in ends:
            for side in range(2):
                for r in range(2):
                    for q in range(nq):
                        row = one(edges[side][r])
                        if i == 0:
                            part_x = half_gain * VX[q, 0, row, :]
                        elif i == 1:
                            part_x = both_gains * XR[t, 0, q, 1, row, :]
                        elif i == cx - 2:
                            part_x = both_gains * XR[t, 1, q, 0, row, :]
                        else:
                            part_x = -half_gain * VX[q, cx + 1, row, :]
                        value = YS[t + 1, side, r, q, one(i), :] + part_x
                        YS[t + 1, side, r, q, one(i), :] = value
                        XS[t + 1, x_side, q, x_row, row, :] = value

        @pl.when(t < STEPS - 1)
        def _():
            start(lambda d: p_copy(t + 1, d))

        unpack_rows(t + 1)
        for q in range(nq):
            low, high = across(q, 0), across(q, cy - 1)
            VY_rows[low] = VY_rows[low] + half_gain * YR[t, 0, 1, q]
            VY_rows[high] = VY_rows[high] - half_gain * YR[t, 1, 0, q]

        @pl.when(t < STEPS - 1)
        def _():
            split_all()

        return carry

    lax.fori_loop(0, STEPS, step, 0)

    take_arrivals(STEPS - 1)
    keep = AMSK[...] > 0.0
    for k, state in enumerate((R, S)):
        for w in range(2):
            high, low = split(jnp.where(keep, state[SLOTS:ROWS, halves(w)[0]], 0.0))
            to = slice(k * BLOCK + w * LANES, k * BLOCK + (w + 1) * LANES)
            CAT[0:ARRIVE, to] = high
            CAT[ARRIVE : 2 * ARRIVE, to] = low

    wait_sent(meta_copy)
    for t in range(STEPS):
        wait_sent(lambda d, t=t: dep_copy(t, d))
        wait_sent(lambda d, t=t: p_copy(t, d), (2, 3) if t == 0 else (0, 1, 2, 3))
    wait_sent(v_copy, (2, 3))
    for d in range(2):
        for copy in first_copies(d):
            copy.wait_send()


def write_out(
    p, vx, vy, vz, r, s, mask, place, cat, c, p_out, v_out, r_out, s_out, c_out, r_end, s_end, sems
):
    _, cx, cy, nz = v_out.shape
    pairs = []
    for q in range(nz // LANES):
        lanes = pl.ds(q * LANES, LANES)
        pairs.append((vx.at[q, pl.ds(1, cx), :, :], v_out.at[0, :, :, lanes]))
        pairs.append((vy.at[q, :, pl.ds(8, cy), :], v_out.at[1, :, :, lanes]))
        pairs.append((vz.at[q], v_out.at[2, :, :, lanes]))
        pairs.append((p.at[q, :, pl.ds(8, cy), :], p_out.at[:, :, lanes]))
    pairs.append((c, c_out))
    copies = [pltpu.make_async_copy(a, b, sems.at[k]) for k, (a, b) in enumerate(pairs)]
    for copy in copies:
        copy.start()
    count = 256
    for first in range(0, SLOTS, count):
        rows = slice(first, first + count)
        placed = jnp.dot(place[rows, :], cat[...], preferred_element_type=f32)
        keep = mask[rows, :]
        keep = jnp.concatenate([keep, keep], axis=1) >= float(STEPS)
        r_end[rows, :] = jnp.where(keep, r[rows, :], 0.0) + placed[:, :BLOCK]
        s_end[rows, :] = (1.0 / time_step) * (jnp.where(keep, s[rows, :], 0.0) + placed[:, BLOCK:])
        for a, b in ((r_end, r_out), (s_end, s_out)):
            rows_of = pl.ds(first, count)
            copy = pltpu.make_async_copy(a.at[rows_of, :], b.at[rows_of, :], sems.at[len(copies)])
            copy.start()
            copies.append(copy)
    for copy in copies:
        copy.wait()


def on_device(
    pressure, velocity, stretch, rest_radius, wall_speed, block_cells, depart_slot, depart_way
):
    cx, cy, nz = pressure.shape
    nq = nz // LANES
    ncol = 2 * cx * cy
    vmem = pl.BlockSpec(memory_space=pltpu.VMEM)
    hbm = pl.BlockSpec(memory_space=pl.ANY)
    dma = pltpu.SemaphoreType.DMA
    vmem_out = pltpu.VMEM
    parts = pl.pallas_call(
        kernel,
        out_shape=(
            vmem_out((nq, cx, cy + 16, LANES), f32),
            vmem_out((nq, cx + 2, cy, LANES), f32),
            vmem_out((nq, cx, cy + 16, LANES), f32),
            vmem_out((nq, cx, cy, LANES), f32),
            vmem_out((ROWS, BLOCK), f32),
            vmem_out((ROWS, BLOCK), f32),
            vmem_out((ROWS, LANES), f32),
            vmem_out((SLOTS, 2 * ARRIVE), bf16),
            vmem_out((2 * ARRIVE, 2 * BLOCK), bf16),
            vmem_out((SLOT_BLOCKS, LANES), jnp.int32),
        ),
        in_specs=[pl.BlockSpec(memory_space=pltpu.HBM)] * 9,
        out_specs=(vmem,) * 10,
        scratch_shapes=[
            pltpu.VMEM((ROWS, BLOCK), f32),
            pltpu.VMEM((3, ARRIVE, BLOCK), f32),
            pltpu.VMEM((STEPS, 3, DEP, BLOCK), f32),
            pltpu.VMEM((4, DEP, BLOCK), f32),
            pltpu.VMEM((ROWS, ncol), bf16),
            pltpu.VMEM((ncol, ROWS), bf16),
            pltpu.VMEM((ncol, 2 * BLOCK), bf16),
            pltpu.VMEM((ROWS, BLOCK), f32),
            pltpu.VMEM((ROWS, 2 * BLOCK), bf16),
            pltpu.VMEM((ncol, BLOCK), f32),
            pltpu.VMEM((STEPS + 1, 2, nq, 2, cy, LANES), f32),
            pltpu.VMEM((STEPS, 2, nq, 2, cy, LANES), f32),
            pltpu.VMEM((STEPS + 1, 2, 2, nq, cx, LANES), f32),
            pltpu.VMEM((STEPS, 2, 2, nq, cx, LANES), f32),
            pltpu.VMEM((2, nq, cx, LANES), f32),
            pltpu.VMEM((2, nq, cx, LANES), f32),
            pltpu.VMEM((8, LANES), f32),
            pltpu.VMEM((4, 8, LANES), f32),
            pltpu.VMEM((ARRIVE, LANES), f32),
            pltpu.VMEM((LANES, LANES), f32),
            pltpu.VMEM((16, LANES), f32),
            pltpu.SMEM((SLOTS,), jnp.int32),
            pltpu.SMEM((STEPS, 1, 1, DEP), jnp.int32),
            pltpu.SMEM((STEPS, 1, 1, DEP), jnp.int32),
            pltpu.VMEM((SLOT_BLOCKS, LANES), jnp.int32),
            dma((4 * nq + 7,)),
            dma((4,)),
            dma((4,)),
            dma((STEPS, 4, nq)),
            dma((STEPS, 4, nq)),
            dma((4,)),
            dma((4,)),
            dma((STEPS, 4)),
            dma((STEPS, 4)),
            dma((2, 2, nq)),
            dma((2, 2, nq)),
        ],
        compiler_params=pltpu.CompilerParams(
            collective_id=0, has_side_effects=True, vmem_limit_bytes=36 * 2**20
        ),
        cost_estimate=pl.CostEstimate(
            flops=10 * 2**30, bytes_accessed=13 * 2**20, transcendentals=2**22
        ),
    )(
        *(
            pltpu.with_memory_space_constraint(value, pltpu.HBM)
            for value in (
                block_cells,
                depart_slot,
                depart_way,
                block_cells.reshape(SLOT_BLOCKS, LANES),
                pressure,
                velocity,
                stretch,
                rest_radius,
                wall_speed,
            )
        )
    )
    parts = [pltpu.with_memory_space_constraint(part, pltpu.VMEM) for part in parts]
    p, v, r, s, c = pl.pallas_call(
        write_out,
        out_shape=(
            jax.ShapeDtypeStruct(pressure.shape, f32),
            jax.ShapeDtypeStruct(velocity.shape, f32),
            jax.ShapeDtypeStruct(stretch.shape, f32),
            jax.ShapeDtypeStruct(stretch.shape, f32),
            jax.ShapeDtypeStruct((SLOT_BLOCKS, LANES), jnp.int32),
        ),
        in_specs=[vmem] * 10,
        out_specs=(hbm,) * 5,
        scratch_shapes=[
            pltpu.VMEM((SLOTS, BLOCK), f32),
            pltpu.VMEM((SLOTS, BLOCK), f32),
            dma((4 * nq + 1 + 8,)),
        ],
        compiler_params=pltpu.CompilerParams(vmem_limit_bytes=8 * 2**20),
        cost_estimate=pl.CostEstimate(flops=0, bytes_accessed=13 * 2**20, transcendentals=0),
    )(*parts)
    return p, v, r, s, c.reshape(-1)


def solution(mesh):
    placed = (
        P("gx", "gy", None),
        P(None, "gx", "gy", None),
        P(("gx", "gy"), None),
        P(("gx", "gy"), None),
        P(("gx", "gy"), None),
        P(("gx", "gy")),
        P(None, "gx", "gy", None),
        P(None, "gx", "gy", None),
    )
    return jax.shard_map(
        on_device,
        mesh=mesh,
        in_specs=placed,
        out_specs=(
            P("gx", "gy", None),
            P(None, "gx", "gy", None),
            P(("gx", "gy"), None),
            P(("gx", "gy"), None),
            P(("gx", "gy")),
        ),
        check_vma=False,
    )
```

```python
import functools
import math

import jax
import jax.numpy as jnp
from jax import lax
from jax.experimental import pallas as pl
from jax.experimental.pallas import tpu as pltpu
from jax.sharding import PartitionSpec as P

MESH = pl.DeviceIdType.MESH
f32 = jnp.float32
bf16 = jnp.bfloat16

STEPS = 4
DEP = 8
SLOTS = 1024
BLOCK = 256
LANES = 128
ARRIVE = STEPS * 4 * DEP
ROWS = SLOTS + ARRIVE
SLOT_BLOCKS = SLOTS // LANES
WAY_OF = (1, 0, 3, 2)

time_step = 0.04
half_gain = 0.2
source_scale = 0.004 * 12.566370614359172
exponent = 4.2
inv_ln2 = 1.0 / math.log(2.0)


def split(value):
    high = value.astype(bf16)
    return high, (value - high.astype(f32)).astype(bf16)


def wall_update(radius, shift, level, pressure):
    mach = (0.05 / time_step) * shift
    one_less = 1.0 - mach
    divisor = one_less * radius
    inverse = pl.reciprocal(divisor, approx=True)
    inverse = inverse * (2.0 - divisor * inverse)
    inv_radius = inverse * one_less
    wall = jnp.exp2(level - (exponent * inv_ln2) * jnp.log(radius))
    squared = time_step * time_step
    excess = (
        wall
        - (0.2 * squared + (0.08 * time_step) * shift) * inv_radius
        - (squared + squared * pressure)
    )
    driving = (1.0 + mach) * excess - (1.5 - 0.5 * mach) * (shift * shift)
    shift = shift + driving * inverse
    radius = radius + shift
    return radius, shift, (source_scale / time_step) * (radius * radius) * shift


def kernel(
    cells_h, slot_h, way_h, cells_b, press, vel, stretch, rest, speed0,
    PR, VX, VY, VZ, R, S, MSK, CAT, INFO,
    A, AR, SB, DB, OH, OHT, PHL, PG, VHL, SRC, XS, XR, YS, YR, VYS, VYR,
    MT, MR, AMSK, LT, LR, cells_s, slot_s, way_s, cells_v,
    in_sem, meta_s, meta_r, xs, xr, vs, vr, ds_, dr, fs, fr,
):
    _, cx, cy, nz = vel.shape
    nq = nz // LANES
    half = cx * cy
    ncol = 2 * half
    jbs = cy // 16
    part = min(256, ncol)
    planes = part // (2 * cy)
    groups = cx // planes
    shift = (planes * cy).bit_length() - 1
    zero_row = lax.axis_index("gx") // 4096
    gx, gy = lax.axis_index("gx"), lax.axis_index("gy")
    ngx, ngy = lax.axis_size("gx"), lax.axis_size("gy")
    has_lo, has_hi = gy > 0, gy < ngy - 1
    targets = (
        (lax.rem(gx + 1, ngx), gy),
        (lax.rem(gx + ngx - 1, ngx), gy),
        (gx, lax.rem(gy + 1, ngy)),
        (gx, lax.rem(gy + ngy - 1, ngy)),
    )
    sends = (None, None, has_hi, has_lo)
    takes = (None, None, has_lo, has_hi)

    def under(flag, action):
        if flag is None:
            action()
        else:
            pl.when(flag)(action)

    barrier = pltpu.get_barrier_semaphore()
    for d in range(4):
        under(
            sends[d],
            lambda d=d: pl.semaphore_signal(
                barrier, inc=1, device_id=targets[d], device_id_type=MESH
            ),
        )

    inputs = [(cells_h, cells_s), (slot_h, slot_s), (way_h, way_s), (cells_b, cells_v)]
    for q in range(nq):
        inputs.append((press.at[:, :, pl.ds(q * LANES, LANES)], PR.at[q, :, pl.ds(8, cy), :]))
    for q in range(nq):
        lanes = pl.ds(q * LANES, LANES)
        inputs.append((vel.at[1, :, :, lanes], VY.at[q, :, pl.ds(8, cy), :]))
    own = pl.ds(0, SLOTS)
    inputs.append((rest, A.at[own, :]))
    inputs.append((stretch, R.at[own, :]))
    inputs.append((speed0, S.at[own, :]))
    for q in range(nq):
        lanes = pl.ds(q * LANES, LANES)
        inputs.append((vel.at[0, :, :, lanes], VX.at[q, pl.ds(1, cx), :, :]))
        inputs.append((vel.at[2, :, :, lanes], VZ.at[q]))
    loads = [pltpu.make_async_copy(a, b, in_sem.at[k]) for k, (a, b) in enumerate(inputs)]
    for load in loads:
        load.start()
    small_loads, loads = loads[:4], loads[4:]

    @pl.when(jnp.logical_not(has_lo))
    def _():
        MR[2] = jnp.zeros((8, LANES), f32)
        YR[:, 0] = jnp.zeros(YR.shape[:1] + YR.shape[2:], f32)
        VYR[0] = jnp.zeros(VYR.shape[1:], f32)

    @pl.when(jnp.logical_not(has_hi))
    def _():
        MR[3] = jnp.zeros((8, LANES), f32)
        YR[:, 1] = jnp.zeros(YR.shape[:1] + YR.shape[2:], f32)
        VYR[1] = jnp.zeros(VYR.shape[1:], f32)

    edge_rows = jnp.zeros((nq, cx, 8, LANES), f32)
    PR[:, :, 0:8, :] = edge_rows
    PR[:, :, 8 + cy : 16 + cy, :] = edge_rows
    VY[:, :, 0:8, :] = edge_rows
    VY[:, :, 8 + cy : 16 + cy, :] = edge_rows
    empty = jnp.zeros((ARRIVE, BLOCK), f32)
    R[SLOTS:ROWS, :] = empty + 1.0
    S[SLOTS:ROWS, :] = empty
    A[SLOTS:ROWS, :] = empty
    MSK[SLOTS:ROWS, :] = jnp.full((ARRIVE, LANES), -1.0, f32)
    OHT[:, SLOTS:ROWS] = jnp.zeros((ncol, ARRIVE), bf16)
    VHL[ROWS - 32 : ROWS, :] = jnp.zeros((32, 2 * BLOCK), bf16)
    OH[SLOTS:ROWS, :] = jnp.zeros((ARRIVE, ncol), bf16)
    pl.semaphore_wait(barrier, 2 + has_lo.astype(jnp.int32) + has_hi.astype(jnp.int32))

    def remote(src, dst, send_sem, recv_sem, d):
        return pltpu.make_async_remote_copy(
            src_ref=src, dst_ref=dst, send_sem=send_sem, recv_sem=recv_sem,
            device_id=targets[d], device_id_type=MESH,
        )

    def meta_copy(d):
        return [remote(MT, MR.at[d], meta_s.at[d], meta_r.at[d], d)]

    def p_copy(t, d):
        if d < 2:
            src, dst = XS.at[t, 1 - d], XR.at[t, d]
        else:
            src, dst = YS.at[t, 3 - d], YR.at[t, d - 2]
        return [remote(src, dst, xs.at[t, d], xr.at[t, d], d)]

    def first_copies(d):
        side = (cx - 2, 0)[d]
        for q in range(nq):
            lanes = pl.ds(q * LANES, LANES)
            yield remote(
                press.at[pl.ds(side, 2), :, lanes], XR.at[0, d, q], fs.at[0, d, q], fr.at[0, d, q], d
            )
        for q in range(nq):
            lanes = pl.ds(q * LANES, LANES)
            yield remote(
                vel.at[0, pl.ds((cx - 1, 0)[d], 1), :, lanes],
                VX.at[q, pl.ds((0, cx + 1)[d], 1), :, :],
                fs.at[1, d, q],
                fr.at[1, d, q],
                d,
            )

    def v_copy(d):
        return [remote(VYS.at[3 - d], VYR.at[d - 2], vs.at[d], vr.at[d], d)]

    def dep_copy(t, d):
        to = AR.at[:, pl.ds(t * 32 + d * DEP, DEP), :]
        return [remote(SB.at[t], to, ds_.at[t, d], dr.at[t, d], d)]

    odd = lax.rem(gy, 2) == 1
    even = jnp.logical_not(odd)
    far_hi, near_hi = has_hi & odd, has_hi & even
    far_lo, near_lo = has_lo & even, has_lo & odd

    def start(make, ways=(0, 1, 2, 3)):
        order = ((far_hi, 2), (far_lo, 3), (None, 0), (None, 1), (near_hi, 2), (near_lo, 3))
        for flag, d in order:
            if d in ways:
                under(flag, lambda d=d: [copy.start() for copy in make(d)] and None)

    def wait_sent(make, ways=(0, 1, 2, 3)):
        for d in ways:
            under(sends[d], lambda d=d: [copy.wait_send() for copy in make(d)] and None)

    def wait_taken(make, ways=(0, 1, 2, 3)):
        for d in ways:
            under(takes[d], lambda d=d: [copy.wait_recv() for copy in make(d)] and None)

    for d in range(2):
        for copy in first_copies(d):
            copy.start()
    edges = ((0, 1), (cy - 2, cy - 1))

    def one(row):
        return pl.ds(row + zero_row, 1)

    pitch = cy + 16
    PR_rows = PR.reshape(nq * cx * pitch, LANES)
    VY_rows = VY.reshape(nq * cx * pitch, LANES)

    def across(q, row):
        return pl.ds(q * cx * pitch + 8 + row, cx, stride=pitch), slice(None)

    def pack_rows(t):
        for side in range(2):
            for r in range(2):
                for q in range(nq):
                    YS[t, side, r, q] = PR_rows[across(q, edges[side][r])]

    def unpack_rows(t):
        for side in range(2):
            for r in range(2):
                for q in range(nq):
                    PR_rows[across(q, edges[side][r])] = YS[t, side, r, q]

    def column_row(i, h, jb):
        return (i // planes) * part + (h * planes + i % planes) * cy + jb * 16

    def keep_parts(i, jb, q, value):
        high, low = split(value)
        row = column_row(i, q // 2, jb)
        col = (q % 2) * 2 * LANES
        PHL[row : row + 16, col : col + LANES] = high
        PHL[row : row + 16, col + LANES : col + 2 * LANES] = low

    def rows_of(jb):
        return slice(jb * 16, jb * 16 + 16), slice(8 + jb * 16, 24 + jb * 16)

    def split_all():
        for i in range(cx):
            for jb in range(jbs):
                for q in range(nq):
                    keep_parts(i, jb, q, PR[q, i, rows_of(jb)[1], :])

    for load in small_loads:
        load.wait()

    lane8 = lax.broadcasted_iota(jnp.int32, (8, LANES), 1)
    sub8 = lax.broadcasted_iota(jnp.int32, (8, LANES), 0)
    slot_id = sub8 * LANES + lane8
    label = cells_v[...] + 1
    leave_at = jnp.where(label > 0, STEPS, -1)
    entry_of = (lane8 // 32) * DEP + lane8 % DEP
    wanted = (lane8 // DEP) % 4
    wanted = jnp.where(wanted < 2, 1 - wanted, 5 - wanted)
    meta = jnp.zeros((8, LANES), jnp.int32)
    for e in range(STEPS * DEP):
        slot = slot_s[e // DEP, 0, 0, e % DEP]
        moved = jnp.where(slot >= 0, cells_s[jnp.maximum(slot, 0)] + 1, 0)
        meta = jnp.where((entry_of == e) & (wanted == way_s[e // DEP, 0, 0, e % DEP]), moved, meta)
        leave_at = jnp.where(slot_id == slot, e // DEP, leave_at)
    MT[...] = meta.astype(f32)

    start(meta_copy)

    lrow = lax.broadcasted_iota(jnp.int32, (LANES, LANES), 0)
    lcol = lax.broadcasted_iota(jnp.int32, (LANES, LANES), 1)
    wide = lax.broadcasted_iota(jnp.int32, (16, ncol), 1).astype(f32)

    def code_of(lab):
        cell = lab - 1
        place = cell >> 1
        row = (place >> shift) * part + (cell & 1) * (planes * cy)
        return jnp.where(lab > 0, row + (place & (planes * cy - 1)), -1).astype(f32)

    def turn(stack):
        stack = stack + [jnp.zeros((8, LANES), f32)] * (16 - len(stack))
        LT[...] = jnp.concatenate(stack, axis=0).T

    def hot_rows(r, at):
        def body(m, carry):
            rows = pl.ds(pl.multiple_of(m * 16, 16), 16)
            hot = jnp.where(LT[rows, at : at + 1] == wide, 1.0, 0.0).astype(bf16)
            OH[pl.ds(pl.multiple_of(r * LANES + m * 16, 16), 16), :] = hot
            return carry

        lax.fori_loop(0, LANES // 16, body, 0, unroll=4)

    def hot_columns(first, last):
        def body(m, carry):
            ident = (lrow + m * LANES).astype(f32)
            rows = pl.ds(pl.multiple_of(m * LANES, LANES), LANES)
            for r in range(first, last):
                hot = jnp.where(ident == LR[r : r + 1, :], 1.0, 0.0).astype(bf16)
                OHT[rows, r * LANES : (r + 1) * LANES] = hot
            return carry

        lax.fori_loop(0, ncol // LANES, body, 0)

    code = code_of(label)
    turn([code, leave_at.astype(f32)])
    LR[0:8, :] = code
    for r in range(SLOT_BLOCKS):
        hot_rows(r, r)
    for r in range(SLOT_BLOCKS):
        MSK[r * LANES : (r + 1) * LANES, :] = jnp.broadcast_to(
            LT[:, 8 + r : 9 + r], (LANES, LANES)
        )
    hot_columns(0, SLOT_BLOCKS)

    for k in range(nq):
        loads[k].wait()
    pack_rows(0)
    start(lambda d: p_copy(0, d), (2, 3))
    for q in range(nq):
        for r in range(2):
            XS[0, 0, q, r] = PR[q, r, 8 : 8 + cy, :]
            XS[0, 1, q, r] = PR[q, cx - 2 + r, 8 : 8 + cy, :]
    for k in range(nq, 2 * nq):
        loads[k].wait()
    for q in range(nq):
        VYS[0, q] = VY_rows[across(q, 0)]
        VYS[1, q] = VY_rows[across(q, cy - 1)]
    start(v_copy, (2, 3))

    for k in range(2 * nq, 2 * nq + 3):
        loads[k].wait()

    def first_state(n, carry):
        rows = pl.ds(pl.multiple_of(n * 16, 16), 16)
        rest_now = A[rows, :]
        R[rows, :] = R[rows, :] * rest_now
        S[rows, :] = time_step * S[rows, :]
        A[rows, :] = inv_ln2 * (
            jnp.log((time_step * time_step) * (1.0 + 0.2 / rest_now))
            + exponent * jnp.log(rest_now)
        )
        return carry

    lax.fori_loop(0, SLOTS // 16, first_state, 0, unroll=4)
    for k in range(2 * nq + 3, 4 * nq + 3):
        loads[k].wait()

    def plan():
        wait_taken(meta_copy)
        came = (lane8 // DEP) % 4
        alab = jnp.where(
            came == 0, MR[0], jnp.where(came == 1, MR[1], jnp.where(came == 2, MR[2], MR[3]))
        )
        acode = code_of(alab.astype(jnp.int32))
        turn([acode, alab])
        LR[8:16, :] = acode
        hot_rows(SLOT_BLOCKS, 0)
        hot_columns(SLOT_BLOCKS, SLOT_BLOCKS + 1)
        AMSK[...] = jnp.broadcast_to(LT[:, 8:9], (LANES, LANES))
        INFO[0] = label.astype(f32)
        INFO[1] = leave_at.astype(f32)
        INFO[2] = alab

    def slope_z(tiles):
        height = tiles[0].shape[0]
        lane = lax.broadcasted_iota(jnp.int32, (height, LANES), 1)
        zero = jnp.zeros((height, LANES), f32)
        ahead = [pltpu.roll(v, LANES - 1, 1) for v in tiles] + [zero]
        behind = [zero] + [pltpu.roll(v, 1, 1) for v in tiles]
        return [
            jnp.where(lane == LANES - 1, ahead[q + 1], ahead[q])
            - jnp.where(lane == 0, behind[q], behind[q + 1])
            for q in range(nq)
        ]

    low_gate = jnp.where(has_lo, 1.0, 0.0).astype(f32)
    high_gate = jnp.where(has_hi, 1.0, 0.0).astype(f32)

    def halves(w):
        return slice(w * LANES, (w + 1) * LANES), slice(2 * w * LANES, 2 * (w + 1) * LANES)

    def gather(w):
        narrow, pair = halves(w)
        both = jnp.dot(OH[...], PHL[:, pair], preferred_element_type=f32)
        PG[:, narrow] = both[:, :LANES] + both[:, LANES:]

    def scatter(w):
        narrow, pair = halves(w)
        both = jnp.dot(OHT[...], VHL[:, pair], preferred_element_type=f32)
        SRC[:, narrow] = both[:, :LANES] + both[:, LANES:]

    def leavers(t, to):
        for k in range(DEP):
            slot = jnp.maximum(slot_s[t, 0, 0, k], 0)
            cell = jnp.maximum(cells_s[slot], 0)
            place = cell >> 1
            row = pl.ds(slot, 1)
            DB[0, k : k + 1, :] = R[row, :]
            DB[1, k : k + 1, :] = S[row, :]
            DB[2, k : k + 1, :] = A[row, :]
            for w in range(2):
                DB[3, k : k + 1, halves(w)[0]] = PR[
                    2 * (cell & 1) + w,
                    place >> (cy.bit_length() - 1),
                    pl.ds(8 + (place & (cy - 1)), 1),
                    :,
                ]
        radius, speed, _ = wall_update(DB[0], DB[1], DB[2], DB[3])
        SB[to, 0] = radius
        SB[to, 1] = speed
        SB[to, 2] = DB[2]

    def take_arrivals(t):
        wait_taken(lambda d: dep_copy(t, d))
        rows = pl.ds(pl.multiple_of(t * 32, 32), 32)
        to = pl.ds(pl.multiple_of(SLOTS + t * 32, 32), 32)
        R[to, :] = AR[0, rows, :]
        S[to, :] = AR[1, rows, :]
        A[to, :] = AR[2, rows, :]
        MSK[to, :] = jnp.where(AMSK[rows, :] > 0.0, 2.0 * STEPS, -1.0)

    def step(t, carry):
        limit = t.astype(f32)

        def bubbles(first, w):
            rows = slice(first, first + 16)
            col = halves(w)[0]
            radius, speed, rate = wall_update(R[rows, col], S[rows, col], A[rows, col], PG[rows, col])
            R[rows, col] = radius
            S[rows, col] = speed
            high, low = split(jnp.where(MSK[rows, :] >= limit, rate, 0.0))
            VHL[rows, 2 * w * LANES : (2 * w + 1) * LANES] = high
            VHL[rows, (2 * w + 1) * LANES : (2 * w + 2) * LANES] = low

        @pl.when(t > 0)
        def _():
            take_arrivals(t - 1)

        split_all()
        last = t // (STEPS - 1)
        leavers(t, t + last)
        gather(0)

        @pl.when(last == 0)
        def _():
            start(lambda d: dep_copy(t, d))

        gather(1)
        for first in range(0, ROWS - 32, 16):
            bubbles(first, 0)
        scatter(0)
        for first in range(0, ROWS - 32, 16):
            bubbles(first, 1)
        scatter(1)

        def flow_x(i):
            for q in range(nq):
                for jb in range(jbs):
                    rows, at = rows_of(jb)
                    flow = VX[q, i + 1, rows, :]
                    if i == 0:
                        flow = flow - half_gain * PR[q, 1, at, :]
                    elif i == cx - 1:
                        flow = flow + half_gain * PR[q, cx - 2, at, :]
                    else:
                        flow = flow - half_gain * (PR[q, i + 1, at, :] - PR[q, i - 1, at, :])
                    VX[q, i + 1, rows, :] = flow

        def flow_z(i, jb):
            rows, at = rows_of(jb)
            slopes = slope_z([PR[q, i, at, :] for q in range(nq)])
            for q in range(nq):
                VZ[q, i, rows, :] = VZ[q, i, rows, :] - half_gain * slopes[q]

        def flow_y(i, jb):
            _, at = rows_of(jb)
            for q in range(nq):
                VY[q, i, at, :] = VY[q, i, at, :] - half_gain * (
                    PR[q, i, pl.ds(9 + jb * 16 + zero_row, 16), :]
                    - PR[q, i, pl.ds(7 + jb * 16 + zero_row, 16), :]
                )

        def pressure(i, jb):
            rows, at = rows_of(jb)
            slopes = slope_z([VZ[q, i, rows, :] for q in range(nq)])
            for q in range(nq):
                rise = slopes[q] + (
                    VY[q, i, pl.ds(9 + jb * 16 + zero_row, 16), :]
                    - VY[q, i, pl.ds(7 + jb * 16 + zero_row, 16), :]
                )
                if i + 1 < cx:
                    rise = rise + VX[q, i + 2, rows, :]
                if i > 0:
                    rise = rise - VX[q, i, rows, :]
                row = column_row(i, q // 2, jb)
                col = (q % 2) * LANES
                PR[q, i, at, :] = (
                    PR[q, i, at, :] - half_gain * rise + SRC[row : row + 16, col : col + LANES]
                )

        for i in range(cx):
            flow_x(i)
            for jb in range(jbs):
                flow_z(i, jb)
                flow_y(i, jb)
        for i in range(cx):
            for jb in range(jbs):
                pressure(i, jb)
        pack_rows(t + 1)

        pl.when(t == 0)(plan)
        wait_taken(lambda d: p_copy(t, d), (2, 3))

        @pl.when(t > 0)
        def _():
            wait_taken(lambda d: p_copy(t, d), (0, 1))

        @pl.when(t == 0)
        def _():
            for d in range(2):
                for copy in first_copies(d):
                    copy.wait_recv()
            wait_taken(v_copy, (2, 3))

        below, above = VYR[0], VYR[1]
        below = low_gate * (below - half_gain * (YS[t, 0, 0] - YR[t, 0, 0]))
        above = high_gate * (above - half_gain * (YR[t, 1, 1] - YS[t, 1, 1]))
        VYR[0] = below
        VYR[1] = above
        both_gains = half_gain * half_gain
        YS[t + 1, 0, 0] = YS[t + 1, 0, 0] + half_gain * below
        YS[t + 1, 0, 1] = YS[t + 1, 0, 1] + both_gains * YR[t, 0, 1]
        YS[t + 1, 1, 0] = YS[t + 1, 1, 0] + both_gains * YR[t, 1, 0]
        YS[t + 1, 1, 1] = YS[t + 1, 1, 1] - half_gain * above
        for q in range(nq):
            for jb in range(jbs):
                rows, at = rows_of(jb)
                far, near = XR[t, 0, q, 0, rows, :], XR[t, 0, q, 1, rows, :]
                beside = VX[q, 0, rows, :] - half_gain * (XS[t, 0, q, 0, rows, :] - far)
                VX[q, 0, rows, :] = beside
                VX[q, 1, rows, :] = VX[q, 1, rows, :] + half_gain * near
                first = PR[q, 0, at, :] + half_gain * beside
                second = PR[q, 1, at, :] + both_gains * near
                PR[q, 0, at, :] = first
                PR[q, 1, at, :] = second
                XS[t + 1, 0, q, 0, rows, :] = first
                XS[t + 1, 0, q, 1, rows, :] = second
                near, far = XR[t, 1, q, 0, rows, :], XR[t, 1, q, 1, rows, :]
                beside = VX[q, cx + 1, rows, :] - half_gain * (far - XS[t, 1, q, 1, rows, :])
                VX[q, cx + 1, rows, :] = beside
                VX[q, cx, rows, :] = VX[q, cx, rows, :] - half_gain * near
                first = PR[q, cx - 2, at, :] + both_gains * near
                second = PR[q, cx - 1, at, :] - half_gain * beside
                PR[q, cx - 2, at, :] = first
                PR[q, cx - 1, at, :] = second
                XS[t + 1, 1, q, 0, rows, :] = first
                XS[t + 1, 1, q, 1, rows, :] = second
        ends = ((0, 0, 0), (1, 0, 1), (cx - 2, 1, 0), (cx - 1, 1, 1))
        for i, x_side, x_row in ends:
            for side in range(2):
                for r in range(2):
                    for q in range(nq):
                        row = one(edges[side][r])
                        if i == 0:
                            part_x = half_gain * VX[q, 0, row, :]
                        elif i == 1:
                            part_x = both_gains * XR[t, 0, q, 1, row, :]
                        elif i == cx - 2:
                            part_x = both_gains * XR[t, 1, q, 0, row, :]
                        else:
                            part_x = -half_gain * VX[q, cx + 1, row, :]
                        value = YS[t + 1, side, r, q, one(i), :] + part_x
                        YS[t + 1, side, r, q, one(i), :] = value
                        XS[t + 1, x_side, q, x_row, row, :] = value

        @pl.when(t < STEPS - 1)
        def _():
            start(lambda d: p_copy(t + 1, d))

        unpack_rows(t + 1)
        for q in range(nq):
            low, high = across(q, 0), across(q, cy - 1)
            VY_rows[low] = VY_rows[low] + half_gain * YR[t, 0, 1, q]
            VY_rows[high] = VY_rows[high] - half_gain * YR[t, 1, 0, q]

        @pl.when(t == STEPS - 2)
        def _():
            leavers(t + 1, t + 1)
            start(lambda d: dep_copy(t + 1, d))

        wait_sent(lambda d: dep_copy(t, d))

        @pl.when(t > 0)
        def _():
            wait_sent(lambda d: p_copy(t, d), (0, 1))

        wait_sent(lambda d: p_copy(t, d), (2, 3))

        return carry

    lax.fori_loop(0, STEPS, step, 0)

    take_arrivals(STEPS - 1)
    keep = AMSK[...] > 0.0
    for k, state in enumerate((R, S)):
        for w in range(2):
            high, low = split(jnp.where(keep, state[SLOTS:ROWS, halves(w)[0]], 0.0))
            to = slice(k * BLOCK + w * LANES, k * BLOCK + (w + 1) * LANES)
            CAT[0:ARRIVE, to] = high
            CAT[ARRIVE : 2 * ARRIVE, to] = low

    wait_sent(meta_copy)
    wait_sent(v_copy, (2, 3))
    for d in range(2):
        for copy in first_copies(d):
            copy.wait_send()


def write_out(
    p, vx, vy, vz, r, s, mask, cat, info, p_out, v_out, r_out, s_out, c_out, r_end, s_end, c_end, lt, sems
):
    _, cx, cy, nz = v_out.shape
    pairs = []
    for q in range(nz // LANES):
        lanes = pl.ds(q * LANES, LANES)
        pairs.append((vx.at[q, pl.ds(1, cx), :, :], v_out.at[0, :, :, lanes]))
        pairs.append((vy.at[q, :, pl.ds(8, cy), :], v_out.at[1, :, :, lanes]))
        pairs.append((vz.at[q], v_out.at[2, :, :, lanes]))
        pairs.append((p.at[q, :, pl.ds(8, cy), :], p_out.at[:, :, lanes]))
    copies = [pltpu.make_async_copy(a, b, sems.at[k]) for k, (a, b) in enumerate(pairs)]
    for copy in copies:
        copy.start()

    lane8 = lax.broadcasted_iota(jnp.int32, (8, LANES), 1)
    sub8 = lax.broadcasted_iota(jnp.int32, (8, LANES), 0)
    lrow = lax.broadcasted_iota(jnp.int32, (LANES, LANES), 0)
    lcol = lax.broadcasted_iota(jnp.int32, (LANES, LANES), 1)
    label, leave_at, alab = info[0], info[1], info[2]
    present = alab > 0.0
    upper = jnp.where(lrow <= lcol, 1.0, 0.0)
    upper_block = jnp.where(lrow // 32 == lcol // 32, upper, 0.0).astype(bf16)
    upper = upper.astype(bf16)
    ones = jnp.ones((LANES, LANES), bf16)
    present_f = jnp.where(present, 1.0, 0.0)
    arank = jnp.dot(present_f.astype(bf16), upper_block, preferred_element_type=f32) - 1.0
    arank = jnp.where(present, arank, -5.0)
    vacant = label == 0.0
    ranks = []
    for t in range(STEPS):
        vacant = vacant | (leave_at == float(t))
        flag = jnp.where(vacant, 1.0, 0.0).astype(bf16)
        rank = jnp.dot(flag, upper, preferred_element_type=f32) - 1.0
        total = jnp.dot(flag, ones, preferred_element_type=f32)
        for k in range(SLOT_BLOCKS - 1):
            rank = rank + jnp.where(sub8 > k, total[k : k + 1, :], 0.0)
        ranks.append(jnp.where(vacant, rank, -1.0))
        count = jnp.sum(jnp.where(lane8 // 32 == t, present_f, 0.0), axis=1, keepdims=True)
        vacant = vacant & (rank >= count)
    lt[...] = jnp.concatenate(ranks + [jnp.zeros((LANES - 8 * STEPS, LANES), f32)], axis=0).T

    group = lcol // 32
    alab_high, alab_low = split(alab)
    final = jnp.where(leave_at == float(STEPS), label, 0.0)
    nt = (((1,), (1,)), ((), ()))
    for k in range(SLOT_BLOCKS):
        rows = slice(k * LANES, (k + 1) * LANES)
        mine = jnp.broadcast_to(lt[:, k : k + 1], (LANES, LANES))
        for t in range(1, STEPS):
            mine = jnp.where(group == t, lt[:, 8 * t + k : 8 * t + k + 1], mine)
        hot = jnp.where(mine == arank[0:1, :], 1.0, 0.0).astype(bf16)
        there = lax.dot_general(alab_high, hot, nt, preferred_element_type=f32)
        there = there + lax.dot_general(alab_low, hot, nt, preferred_element_type=f32)
        final = final + jnp.where(sub8 == k, there, 0.0)
        both = jnp.concatenate([hot, hot], axis=1)
        placed = jnp.dot(both, cat[...], preferred_element_type=f32)
        keep = mask[rows, :]
        keep = jnp.concatenate([keep, keep], axis=1) >= float(STEPS)
        r_end[rows, :] = jnp.where(keep, r[rows, :], 0.0) + placed[:, :BLOCK]
        s_end[rows, :] = (1.0 / time_step) * (jnp.where(keep, s[rows, :], 0.0) + placed[:, BLOCK:])
        if k % 4 == 3:
            rows_of = pl.ds((k - 3) * LANES, 4 * LANES)
            for a, b in ((r_end, r_out), (s_end, s_out)):
                copy = pltpu.make_async_copy(a.at[rows_of, :], b.at[rows_of, :], sems.at[len(copies)])
                copy.start()
                copies.append(copy)
    c_end[...] = final.astype(jnp.int32) - 1
    copy = pltpu.make_async_copy(c_end, c_out, sems.at[len(copies)])
    copy.start()
    copies.append(copy)
    for copy in copies:
        copy.wait()


def on_device(
    pressure, velocity, stretch, rest_radius, wall_speed, block_cells, depart_slot, depart_way
):
    cx, cy, nz = pressure.shape
    nq = nz // LANES
    ncol = 2 * cx * cy
    vmem = pl.BlockSpec(memory_space=pltpu.VMEM)
    hbm = pl.BlockSpec(memory_space=pl.ANY)
    dma = pltpu.SemaphoreType.DMA
    vmem_out = pltpu.VMEM
    parts = pl.pallas_call(
        kernel,
        out_shape=(
            vmem_out((nq, cx, cy + 16, LANES), f32),
            vmem_out((nq, cx + 2, cy, LANES), f32),
            vmem_out((nq, cx, cy + 16, LANES), f32),
            vmem_out((nq, cx, cy, LANES), f32),
            vmem_out((ROWS, BLOCK), f32),
            vmem_out((ROWS, BLOCK), f32),
            vmem_out((ROWS, LANES), f32),
            vmem_out((2 * ARRIVE, 2 * BLOCK), bf16),
            vmem_out((3, SLOT_BLOCKS, LANES), f32),
        ),
        in_specs=[pl.BlockSpec(memory_space=pltpu.HBM)] * 9,
        out_specs=(vmem,) * 9,
        scratch_shapes=[
            pltpu.VMEM((ROWS, BLOCK), f32),
            pltpu.VMEM((3, ARRIVE, BLOCK), f32),
            pltpu.VMEM((STEPS + 1, 3, DEP, BLOCK), f32),
            pltpu.VMEM((4, DEP, BLOCK), f32),
            pltpu.VMEM((ROWS, ncol), bf16),
            pltpu.VMEM((ncol, ROWS), bf16),
            pltpu.VMEM((ncol, 2 * BLOCK), bf16),
            pltpu.VMEM((ROWS, BLOCK), f32),
            pltpu.VMEM((ROWS, 2 * BLOCK), bf16),
            pltpu.VMEM((ncol, BLOCK), f32),
            pltpu.VMEM((STEPS + 1, 2, nq, 2, cy, LANES), f32),
            pltpu.VMEM((STEPS, 2, nq, 2, cy, LANES), f32),
            pltpu.VMEM((STEPS + 1, 2, 2, nq, cx, LANES), f32),
            pltpu.VMEM((STEPS, 2, 2, nq, cx, LANES), f32),
            pltpu.VMEM((2, nq, cx, LANES), f32),
            pltpu.VMEM((2, nq, cx, LANES), f32),
            pltpu.VMEM((8, LANES), f32),
            pltpu.VMEM((4, 8, LANES), f32),
            pltpu.VMEM((ARRIVE, LANES), f32),
            pltpu.VMEM((LANES, LANES), f32),
            pltpu.VMEM((16, LANES), f32),
            pltpu.SMEM((SLOTS,), jnp.int32),
            pltpu.SMEM((STEPS, 1, 1, DEP), jnp.int32),
            pltpu.SMEM((STEPS, 1, 1, DEP), jnp.int32),
            pltpu.VMEM((SLOT_BLOCKS, LANES), jnp.int32),
            dma((4 * nq + 7,)),
            dma((4,)),
            dma((4,)),
            dma((STEPS, 4)),
            dma((STEPS, 4)),
            dma((4,)),
            dma((4,)),
            dma((STEPS, 4)),
            dma((STEPS, 4)),
            dma((2, 2, nq)),
            dma((2, 2, nq)),
        ],
        compiler_params=pltpu.CompilerParams(
            collective_id=0, has_side_effects=True, vmem_limit_bytes=36 * 2**20
        ),
        cost_estimate=pl.CostEstimate(
            flops=10 * 2**30, bytes_accessed=13 * 2**20, transcendentals=2**22
        ),
    )(
        *(
            pltpu.with_memory_space_constraint(value, pltpu.HBM)
            for value in (
                block_cells,
                depart_slot,
                depart_way,
                block_cells.reshape(SLOT_BLOCKS, LANES),
                pressure,
                velocity,
                stretch,
                rest_radius,
                wall_speed,
            )
        )
    )
    parts = [pltpu.with_memory_space_constraint(part, pltpu.VMEM) for part in parts]
    p, v, r, s, c = pl.pallas_call(
        write_out,
        out_shape=(
            jax.ShapeDtypeStruct(pressure.shape, f32),
            jax.ShapeDtypeStruct(velocity.shape, f32),
            jax.ShapeDtypeStruct(stretch.shape, f32),
            jax.ShapeDtypeStruct(stretch.shape, f32),
            jax.ShapeDtypeStruct((SLOT_BLOCKS, LANES), jnp.int32),
        ),
        in_specs=[vmem] * 9,
        out_specs=(hbm,) * 5,
        scratch_shapes=[
            pltpu.VMEM((SLOTS, BLOCK), f32),
            pltpu.VMEM((SLOTS, BLOCK), f32),
            pltpu.VMEM((SLOT_BLOCKS, LANES), jnp.int32),
            pltpu.VMEM((LANES, LANES), f32),
            dma((4 * nq + 5,)),
        ],
        compiler_params=pltpu.CompilerParams(vmem_limit_bytes=8 * 2**20),
        cost_estimate=pl.CostEstimate(flops=0, bytes_accessed=13 * 2**20, transcendentals=0),
    )(*parts)
    return p, v, r, s, c.reshape(-1)


def solution(mesh):
    placed = (
        P("gx", "gy", None),
        P(None, "gx", "gy", None),
        P(("gx", "gy"), None),
        P(("gx", "gy"), None),
        P(("gx", "gy"), None),
        P(("gx", "gy")),
        P(None, "gx", "gy", None),
        P(None, "gx", "gy", None),
    )
    return jax.shard_map(
        on_device,
        mesh=mesh,
        in_specs=placed,
        out_specs=(
            P("gx", "gy", None),
            P(None, "gx", "gy", None),
            P(("gx", "gy"), None),
            P(("gx", "gy"), None),
            P(("gx", "gy")),
        ),
        check_vma=False,
    )
```

```python
import functools
import math

import jax
import jax.numpy as jnp
from jax import lax
from jax.experimental import pallas as pl
from jax.experimental.pallas import tpu as pltpu
from jax.sharding import PartitionSpec as P

MESH = pl.DeviceIdType.MESH
f32 = jnp.float32
bf16 = jnp.bfloat16

STEPS = 4
DEP = 8
SLOTS = 1024
BLOCK = 256
LANES = 128
ARRIVE = STEPS * 4 * DEP
ROWS = SLOTS + ARRIVE
SLOT_BLOCKS = SLOTS // LANES
WAY_OF = (1, 0, 3, 2)

time_step = 0.04
half_gain = 0.2
source_scale = 0.004 * 12.566370614359172
exponent = 4.2
inv_ln2 = 1.0 / math.log(2.0)


def split(value):
    high = value.astype(bf16)
    return high, (value - high.astype(f32)).astype(bf16)


def wall_update(radius, shift, level, pressure):
    mach = (0.05 / time_step) * shift
    one_less = 1.0 - mach
    divisor = one_less * radius
    inverse = pl.reciprocal(divisor, approx=True)
    inverse = inverse * (2.0 - divisor * inverse)
    inv_radius = inverse * one_less
    wall = jnp.exp2(level - (exponent * inv_ln2) * jnp.log(radius))
    squared = time_step * time_step
    excess = (
        wall
        - (0.2 * squared + (0.08 * time_step) * shift) * inv_radius
        - (squared + squared * pressure)
    )
    driving = (1.0 + mach) * excess - (1.5 - 0.5 * mach) * (shift * shift)
    shift = shift + driving * inverse
    radius = radius + shift
    return radius, shift, (source_scale / time_step) * (radius * radius) * shift


def kernel(
    cells_h, slot_h, way_h, cells_b, press, vel, stretch, rest, speed0,
    PR, VX, VY, VZ, R, S, MSK, CAT, INFO,
    A, AR, SB, DB, OH, OHT, PHL, PG, VHL, SRC, XS, XR, YS, YR, VYS, VYR,
    MT, MR, AMSK, LT, LR, cells_s, slot_s, way_s, cells_v,
    in_sem, meta_s, meta_r, xs, xr, vs, vr, ds_, dr, fs, fr,
):
    _, cx, cy, nz = vel.shape
    nq = nz // LANES
    half = cx * cy
    ncol = 2 * half
    jbs = cy // 16
    part = min(256, ncol)
    planes = part // (2 * cy)
    groups = cx // planes
    shift = (planes * cy).bit_length() - 1
    zero_row = lax.axis_index("gx") // 4096
    gx, gy = lax.axis_index("gx"), lax.axis_index("gy")
    ngx, ngy = lax.axis_size("gx"), lax.axis_size("gy")
    has_lo, has_hi = gy > 0, gy < ngy - 1
    targets = (
        (lax.rem(gx + 1, ngx), gy),
        (lax.rem(gx + ngx - 1, ngx), gy),
        (gx, lax.rem(gy + 1, ngy)),
        (gx, lax.rem(gy + ngy - 1, ngy)),
    )
    sends = (None, None, has_hi, has_lo)
    takes = (None, None, has_lo, has_hi)

    def under(flag, action):
        if flag is None:
            action()
        else:
            pl.when(flag)(action)

    barrier = pltpu.get_barrier_semaphore()
    for d in range(4):
        under(
            sends[d],
            lambda d=d: pl.semaphore_signal(
                barrier, inc=1, device_id=targets[d], device_id_type=MESH
            ),
        )

    inputs = [(cells_h, cells_s), (slot_h, slot_s), (way_h, way_s), (cells_b, cells_v)]
    for q in range(nq):
        inputs.append((press.at[:, :, pl.ds(q * LANES, LANES)], PR.at[q, :, pl.ds(8, cy), :]))
    for q in range(nq):
        lanes = pl.ds(q * LANES, LANES)
        inputs.append((vel.at[1, :, :, lanes], VY.at[q, :, pl.ds(8, cy), :]))
    own = pl.ds(0, SLOTS)
    inputs.append((rest, A.at[own, :]))
    inputs.append((stretch, R.at[own, :]))
    inputs.append((speed0, S.at[own, :]))
    for q in range(nq):
        lanes = pl.ds(q * LANES, LANES)
        inputs.append((vel.at[0, :, :, lanes], VX.at[q, pl.ds(1, cx), :, :]))
        inputs.append((vel.at[2, :, :, lanes], VZ.at[q]))
    loads = [pltpu.make_async_copy(a, b, in_sem.at[k]) for k, (a, b) in enumerate(inputs)]
    for load in loads:
        load.start()
    small_loads, loads = loads[:4], loads[4:]

    @pl.when(jnp.logical_not(has_lo))
    def _():
        MR[2] = jnp.zeros((8, LANES), f32)
        YR[:, 0] = jnp.zeros(YR.shape[:1] + YR.shape[2:], f32)
        VYR[0] = jnp.zeros(VYR.shape[1:], f32)

    @pl.when(jnp.logical_not(has_hi))
    def _():
        MR[3] = jnp.zeros((8, LANES), f32)
        YR[:, 1] = jnp.zeros(YR.shape[:1] + YR.shape[2:], f32)
        VYR[1] = jnp.zeros(VYR.shape[1:], f32)

    edge_rows = jnp.zeros((nq, cx, 8, LANES), f32)
    PR[:, :, 0:8, :] = edge_rows
    PR[:, :, 8 + cy : 16 + cy, :] = edge_rows
    VY[:, :, 0:8, :] = edge_rows
    VY[:, :, 8 + cy : 16 + cy, :] = edge_rows
    empty = jnp.zeros((ARRIVE, BLOCK), f32)
    R[SLOTS:ROWS, :] = empty + 1.0
    S[SLOTS:ROWS, :] = empty
    A[SLOTS:ROWS, :] = empty
    MSK[SLOTS:ROWS, :] = jnp.full((ARRIVE, LANES), -1.0, f32)
    OHT[:, SLOTS:ROWS] = jnp.zeros((ncol, ARRIVE), bf16)
    VHL[ROWS - 32 : ROWS, :] = jnp.zeros((32, 2 * BLOCK), bf16)
    OH[SLOTS:ROWS, :] = jnp.zeros((ARRIVE, ncol), bf16)
    pl.semaphore_wait(barrier, 2 + has_lo.astype(jnp.int32) + has_hi.astype(jnp.int32))

    def remote(src, dst, send_sem, recv_sem, d):
        return pltpu.make_async_remote_copy(
            src_ref=src, dst_ref=dst, send_sem=send_sem, recv_sem=recv_sem,
            device_id=targets[d], device_id_type=MESH,
        )

    def meta_copy(d):
        return [remote(MT, MR.at[d], meta_s.at[d], meta_r.at[d], d)]

    def p_copy(t, d):
        if d < 2:
            src, dst = XS.at[t, 1 - d], XR.at[t, d]
        else:
            src, dst = YS.at[t, 3 - d], YR.at[t, d - 2]
        return [remote(src, dst, xs.at[t, d], xr.at[t, d], d)]

    def first_copies(d):
        side = (cx - 2, 0)[d]
        for q in range(nq):
            lanes = pl.ds(q * LANES, LANES)
            yield remote(
                press.at[pl.ds(side, 2), :, lanes], XR.at[0, d, q], fs.at[0, d, q], fr.at[0, d, q], d
            )
        for q in range(nq):
            lanes = pl.ds(q * LANES, LANES)
            yield remote(
                vel.at[0, pl.ds((cx - 1, 0)[d], 1), :, lanes],
                VX.at[q, pl.ds((0, cx + 1)[d], 1), :, :],
                fs.at[1, d, q],
                fr.at[1, d, q],
                d,
            )

    def v_copy(d):
        return [remote(VYS.at[3 - d], VYR.at[d - 2], vs.at[d], vr.at[d], d)]

    def dep_copy(t, d):
        to = AR.at[:, pl.ds(t * 32 + d * DEP, DEP), :]
        return [remote(SB.at[t], to, ds_.at[t, d], dr.at[t, d], d)]

    odd = lax.rem(gy, 2) == 1
    even = jnp.logical_not(odd)
    far_hi, near_hi = has_hi & odd, has_hi & even
    far_lo, near_lo = has_lo & even, has_lo & odd

    def start(make, ways=(0, 1, 2, 3)):
        order = ((far_hi, 2), (far_lo, 3), (None, 0), (None, 1), (near_hi, 2), (near_lo, 3))
        for flag, d in order:
            if d in ways:
                under(flag, lambda d=d: [copy.start() for copy in make(d)] and None)

    def wait_sent(make, ways=(0, 1, 2, 3)):
        for d in ways:
            under(sends[d], lambda d=d: [copy.wait_send() for copy in make(d)] and None)

    def wait_taken(make, ways=(0, 1, 2, 3)):
        for d in ways:
            under(takes[d], lambda d=d: [copy.wait_recv() for copy in make(d)] and None)

    for d in range(2):
        for copy in first_copies(d):
            copy.start()
    edges = ((0, 1), (cy - 2, cy - 1))

    def one(row):
        return pl.ds(row + zero_row, 1)

    def pack_rows(t):
        for side in range(2):
            for r in range(2):
                for q in range(nq):
                    for i in range(cx):
                        YS[t, side, r, q, one(i), :] = PR[q, i, one(8 + edges[side][r]), :]

    def unpack_rows(t):
        for side in range(2):
            for r in range(2):
                for q in range(nq):
                    for i in range(cx):
                        PR[q, i, one(8 + edges[side][r]), :] = YS[t, side, r, q, one(i), :]

    def column_row(i, h, jb):
        return (i // planes) * part + (h * planes + i % planes) * cy + jb * 16

    def keep_parts(i, jb, q, value):
        high, low = split(value)
        row = column_row(i, q // 2, jb)
        col = (q % 2) * 2 * LANES
        PHL[row : row + 16, col : col + LANES] = high
        PHL[row : row + 16, col + LANES : col + 2 * LANES] = low

    def rows_of(jb):
        return slice(jb * 16, jb * 16 + 16), slice(8 + jb * 16, 24 + jb * 16)

    def split_all():
        for i in range(cx):
            for jb in range(jbs):
                for q in range(nq):
                    keep_parts(i, jb, q, PR[q, i, rows_of(jb)[1], :])

    for load in small_loads:
        load.wait()

    lane8 = lax.broadcasted_iota(jnp.int32, (8, LANES), 1)
    sub8 = lax.broadcasted_iota(jnp.int32, (8, LANES), 0)
    slot_id = sub8 * LANES + lane8
    label = cells_v[...] + 1
    leave_at = jnp.where(label > 0, STEPS, -1)
    entry_of = (lane8 // 32) * DEP + lane8 % DEP
    wanted = (lane8 // DEP) % 4
    wanted = jnp.where(wanted < 2, 1 - wanted, 5 - wanted)
    meta = jnp.zeros((8, LANES), jnp.int32)
    for e in range(STEPS * DEP):
        slot = slot_s[e // DEP, 0, 0, e % DEP]
        moved = jnp.where(slot >= 0, cells_s[jnp.maximum(slot, 0)] + 1, 0)
        meta = jnp.where((entry_of == e) & (wanted == way_s[e // DEP, 0, 0, e % DEP]), moved, meta)
        leave_at = jnp.where(slot_id == slot, e // DEP, leave_at)
    MT[...] = meta.astype(f32)

    start(meta_copy)

    lrow = lax.broadcasted_iota(jnp.int32, (LANES, LANES), 0)
    lcol = lax.broadcasted_iota(jnp.int32, (LANES, LANES), 1)
    wide = lax.broadcasted_iota(jnp.int32, (16, ncol), 1).astype(f32)

    def code_of(lab):
        cell = lab - 1
        place = cell >> 1
        row = (place >> shift) * part + (cell & 1) * (planes * cy)
        return jnp.where(lab > 0, row + (place & (planes * cy - 1)), -1).astype(f32)

    def turn(stack):
        stack = stack + [jnp.zeros((8, LANES), f32)] * (16 - len(stack))
        LT[...] = jnp.concatenate(stack, axis=0).T

    def hot_rows(r, at):
        def body(m, carry):
            rows = pl.ds(pl.multiple_of(m * 16, 16), 16)
            hot = jnp.where(LT[rows, at : at + 1] == wide, 1.0, 0.0).astype(bf16)
            OH[pl.ds(pl.multiple_of(r * LANES + m * 16, 16), 16), :] = hot
            return carry

        lax.fori_loop(0, LANES // 16, body, 0, unroll=4)

    def hot_columns(first, last):
        def body(m, carry):
            ident = (lrow + m * LANES).astype(f32)
            rows = pl.ds(pl.multiple_of(m * LANES, LANES), LANES)
            for r in range(first, last):
                hot = jnp.where(ident == LR[r : r + 1, :], 1.0, 0.0).astype(bf16)
                OHT[rows, r * LANES : (r + 1) * LANES] = hot
            return carry

        lax.fori_loop(0, ncol // LANES, body, 0)

    code = code_of(label)
    turn([code, leave_at.astype(f32)])
    LR[0:8, :] = code
    for r in range(SLOT_BLOCKS):
        hot_rows(r, r)
    for r in range(SLOT_BLOCKS):
        MSK[r * LANES : (r + 1) * LANES, :] = jnp.broadcast_to(
            LT[:, 8 + r : 9 + r], (LANES, LANES)
        )
    hot_columns(0, SLOT_BLOCKS)

    for k in range(nq):
        loads[k].wait()
    pack_rows(0)
    start(lambda d: p_copy(0, d), (2, 3))
    for q in range(nq):
        for r in range(2):
            XS[0, 0, q, r] = PR[q, r, 8 : 8 + cy, :]
            XS[0, 1, q, r] = PR[q, cx - 2 + r, 8 : 8 + cy, :]
    for k in range(nq, 2 * nq):
        loads[k].wait()
    for q in range(nq):
        for i in range(cx):
            VYS[0, q, one(i), :] = VY[q, i, one(8), :]
            VYS[1, q, one(i), :] = VY[q, i, one(7 + cy), :]
    start(v_copy, (2, 3))

    for k in range(2 * nq, 2 * nq + 3):
        loads[k].wait()

    def first_state(n, carry):
        rows = pl.ds(pl.multiple_of(n * 16, 16), 16)
        rest_now = A[rows, :]
        R[rows, :] = R[rows, :] * rest_now
        S[rows, :] = time_step * S[rows, :]
        A[rows, :] = inv_ln2 * (
            jnp.log((time_step * time_step) * (1.0 + 0.2 / rest_now))
            + exponent * jnp.log(rest_now)
        )
        return carry

    lax.fori_loop(0, SLOTS // 16, first_state, 0, unroll=4)
    for k in range(2 * nq + 3, 4 * nq + 3):
        loads[k].wait()

    def plan():
        wait_taken(meta_copy)
        came = (lane8 // DEP) % 4
        alab = jnp.where(
            came == 0, MR[0], jnp.where(came == 1, MR[1], jnp.where(came == 2, MR[2], MR[3]))
        )
        acode = code_of(alab.astype(jnp.int32))
        turn([acode, alab])
        LR[8:16, :] = acode
        hot_rows(SLOT_BLOCKS, 0)
        hot_columns(SLOT_BLOCKS, SLOT_BLOCKS + 1)
        AMSK[...] = jnp.broadcast_to(LT[:, 8:9], (LANES, LANES))
        INFO[0] = label.astype(f32)
        INFO[1] = leave_at.astype(f32)
        INFO[2] = alab

    lane = lax.broadcasted_iota(jnp.int32, (16, LANES), 1)
    zero = jnp.zeros((16, LANES), f32)

    def rise_before(tiles):
        turned = [pltpu.roll(v, 2, 1) for v in tiles]
        before = [jnp.where(lane < 2, turned[q - 1], turned[q]) for q in range(nq)]
        before[0] = jnp.where(lane == 1, zero, before[0])
        here = [jnp.where(lane == 0, zero, tiles[0])] + tiles[1:]
        return [a - b for a, b in zip(here, before)]

    def rise_after(tiles):
        turned = [pltpu.roll(v, LANES - 2, 1) for v in tiles]
        after = [jnp.where(lane >= LANES - 2, turned[(q + 1) % nq], turned[q]) for q in range(nq)]
        after[-1] = jnp.where(lane == LANES - 1, zero, after[-1])
        here = [jnp.where(lane == 0, zero, tiles[0])] + tiles[1:]
        return [a - b for a, b in zip(after, here)]

    def shift_z(i, carry):
        for jb in range(jbs):
            rows = rows_of(jb)[0]
            turned = [pltpu.roll(VZ[q, i, rows, :], 1, 1) for q in range(nq)]
            for q in range(nq):
                VZ[q, i, rows, :] = jnp.where(lane == 0, turned[q - 1], turned[q])
        return carry

    lax.fori_loop(0, cx, shift_z, 0, unroll=4)

    low_gate = jnp.where(has_lo, 1.0, 0.0).astype(f32)
    high_gate = jnp.where(has_hi, 1.0, 0.0).astype(f32)

    def halves(w):
        return slice(w * LANES, (w + 1) * LANES), slice(2 * w * LANES, 2 * (w + 1) * LANES)

    def gather(w):
        narrow, pair = halves(w)
        both = jnp.dot(OH[...], PHL[:, pair], preferred_element_type=f32)
        PG[:, narrow] = both[:, :LANES] + both[:, LANES:]

    def scatter(w):
        narrow, pair = halves(w)
        both = jnp.dot(OHT[...], VHL[:, pair], preferred_element_type=f32)
        SRC[:, narrow] = both[:, :LANES] + both[:, LANES:]

    def leavers(t, to):
        for k in range(DEP):
            slot = jnp.maximum(slot_s[t, 0, 0, k], 0)
            cell = jnp.maximum(cells_s[slot], 0)
            place = cell >> 1
            row = pl.ds(slot, 1)
            DB[0, k : k + 1, :] = R[row, :]
            DB[1, k : k + 1, :] = S[row, :]
            DB[2, k : k + 1, :] = A[row, :]
            for w in range(2):
                DB[3, k : k + 1, halves(w)[0]] = PR[
                    2 * (cell & 1) + w,
                    place >> (cy.bit_length() - 1),
                    pl.ds(8 + (place & (cy - 1)), 1),
                    :,
                ]
        radius, speed, _ = wall_update(DB[0], DB[1], DB[2], DB[3])
        SB[to, 0] = radius
        SB[to, 1] = speed
        SB[to, 2] = DB[2]

    def take_arrivals(t):
        wait_taken(lambda d: dep_copy(t, d))
        rows = pl.ds(pl.multiple_of(t * 32, 32), 32)
        to = pl.ds(pl.multiple_of(SLOTS + t * 32, 32), 32)
        R[to, :] = AR[0, rows, :]
        S[to, :] = AR[1, rows, :]
        A[to, :] = AR[2, rows, :]
        MSK[to, :] = jnp.where(AMSK[rows, :] > 0.0, 2.0 * STEPS, -1.0)

    def step(t, carry):
        limit = t.astype(f32)

        def bubbles(first, w):
            rows = slice(first, first + 16)
            col = halves(w)[0]
            radius, speed, rate = wall_update(R[rows, col], S[rows, col], A[rows, col], PG[rows, col])
            R[rows, col] = radius
            S[rows, col] = speed
            high, low = split(jnp.where(MSK[rows, :] >= limit, rate, 0.0))
            VHL[rows, 2 * w * LANES : (2 * w + 1) * LANES] = high
            VHL[rows, (2 * w + 1) * LANES : (2 * w + 2) * LANES] = low

        @pl.when(t > 0)
        def _():
            take_arrivals(t - 1)

        split_all()
        last = t // (STEPS - 1)
        leavers(t, t + last)
        gather(0)

        @pl.when(last == 0)
        def _():
            start(lambda d: dep_copy(t, d))

        gather(1)
        for first in range(0, ROWS - 32, 16):
            bubbles(first, 0)
        scatter(0)
        for first in range(0, ROWS - 32, 16):
            bubbles(first, 1)
        scatter(1)

        def flow_x(i):
            for q in range(nq):
                for jb in range(jbs):
                    rows, at = rows_of(jb)
                    flow = VX[q, i + 1, rows, :]
                    if i == 0:
                        flow = flow - half_gain * PR[q, 1, at, :]
                    elif i == cx - 1:
                        flow = flow + half_gain * PR[q, cx - 2, at, :]
                    else:
                        flow = flow - half_gain * (PR[q, i + 1, at, :] - PR[q, i - 1, at, :])
                    VX[q, i + 1, rows, :] = flow

        def flow_z(i, jb):
            rows, at = rows_of(jb)
            slopes = rise_before([PR[q, i, at, :] for q in range(nq)])
            for q in range(nq):
                VZ[q, i, rows, :] = VZ[q, i, rows, :] - half_gain * slopes[q]

        def flow_y(i, jb):
            _, at = rows_of(jb)
            for q in range(nq):
                VY[q, i, at, :] = VY[q, i, at, :] - half_gain * (
                    PR[q, i, pl.ds(9 + jb * 16 + zero_row, 16), :]
                    - PR[q, i, pl.ds(7 + jb * 16 + zero_row, 16), :]
                )

        def pressure(i, jb):
            rows, at = rows_of(jb)
            slopes = rise_after([VZ[q, i, rows, :] for q in range(nq)])
            for q in range(nq):
                rise = slopes[q] + (
                    VY[q, i, pl.ds(9 + jb * 16 + zero_row, 16), :]
                    - VY[q, i, pl.ds(7 + jb * 16 + zero_row, 16), :]
                )
                if i + 1 < cx:
                    rise = rise + VX[q, i + 2, rows, :]
                if i > 0:
                    rise = rise - VX[q, i, rows, :]
                row = column_row(i, q // 2, jb)
                col = (q % 2) * LANES
                PR[q, i, at, :] = (
                    PR[q, i, at, :] - half_gain * rise + SRC[row : row + 16, col : col + LANES]
                )

        for i in range(cx):
            flow_x(i)
            for jb in range(jbs):
                flow_z(i, jb)
                flow_y(i, jb)
        for i in range(cx):
            for jb in range(jbs):
                pressure(i, jb)
        pack_rows(t + 1)

        pl.when(t == 0)(plan)
        wait_sent(lambda d: p_copy(t, d), (2, 3))
        wait_taken(lambda d: p_copy(t, d), (2, 3))

        @pl.when(t > 0)
        def _():
            wait_sent(lambda d: dep_copy(t - 1, d))
            wait_sent(lambda d: p_copy(t, d), (0, 1))
            wait_taken(lambda d: p_copy(t, d), (0, 1))

        @pl.when(t == 0)
        def _():
            for d in range(2):
                for copy in first_copies(d):
                    copy.wait_recv()
            wait_taken(v_copy, (2, 3))

        below, above = VYR[0], VYR[1]
        below = low_gate * (below - half_gain * (YS[t, 0, 0] - YR[t, 0, 0]))
        above = high_gate * (above - half_gain * (YR[t, 1, 1] - YS[t, 1, 1]))
        VYR[0] = below
        VYR[1] = above
        both_gains = half_gain * half_gain
        YS[t + 1, 0, 0] = YS[t + 1, 0, 0] + half_gain * below
        YS[t + 1, 0, 1] = YS[t + 1, 0, 1] + both_gains * YR[t, 0, 1]
        YS[t + 1, 1, 0] = YS[t + 1, 1, 0] + both_gains * YR[t, 1, 0]
        YS[t + 1, 1, 1] = YS[t + 1, 1, 1] - half_gain * above
        for q in range(nq):
            for jb in range(jbs):
                rows, at = rows_of(jb)
                far, near = XR[t, 0, q, 0, rows, :], XR[t, 0, q, 1, rows, :]
                beside = VX[q, 0, rows, :] - half_gain * (XS[t, 0, q, 0, rows, :] - far)
                VX[q, 0, rows, :] = beside
                VX[q, 1, rows, :] = VX[q, 1, rows, :] + half_gain * near
                first = PR[q, 0, at, :] + half_gain * beside
                second = PR[q, 1, at, :] + both_gains * near
                PR[q, 0, at, :] = first
                PR[q, 1, at, :] = second
                XS[t + 1, 0, q, 0, rows, :] = first
                XS[t + 1, 0, q, 1, rows, :] = second
                near, far = XR[t, 1, q, 0, rows, :], XR[t, 1, q, 1, rows, :]
                beside = VX[q, cx + 1, rows, :] - half_gain * (far - XS[t, 1, q, 1, rows, :])
                VX[q, cx + 1, rows, :] = beside
                VX[q, cx, rows, :] = VX[q, cx, rows, :] - half_gain * near
                first = PR[q, cx - 2, at, :] + both_gains * near
                second = PR[q, cx - 1, at, :] - half_gain * beside
                PR[q, cx - 2, at, :] = first
                PR[q, cx - 1, at, :] = second
                XS[t + 1, 1, q, 0, rows, :] = first
                XS[t + 1, 1, q, 1, rows, :] = second
        ends = ((0, 0, 0), (1, 0, 1), (cx - 2, 1, 0), (cx - 1, 1, 1))
        for i, x_side, x_row in ends:
            for side in range(2):
                for r in range(2):
                    for q in range(nq):
                        row = one(edges[side][r])
                        if i == 0:
                            part_x = half_gain * VX[q, 0, row, :]
                        elif i == 1:
                            part_x = both_gains * XR[t, 0, q, 1, row, :]
                        elif i == cx - 2:
                            part_x = both_gains * XR[t, 1, q, 0, row, :]
                        else:
                            part_x = -half_gain * VX[q, cx + 1, row, :]
                        value = YS[t + 1, side, r, q, one(i), :] + part_x
                        YS[t + 1, side, r, q, one(i), :] = value
                        XS[t + 1, x_side, q, x_row, row, :] = value

        @pl.when(t < STEPS - 1)
        def _():
            start(lambda d: p_copy(t + 1, d))

        unpack_rows(t + 1)
        for q in range(nq):
            for i in range(cx):
                low, high = one(8), one(7 + cy)
                VY[q, i, low, :] = VY[q, i, low, :] + half_gain * YR[t, 0, 1, q, one(i), :]
                VY[q, i, high, :] = VY[q, i, high, :] - half_gain * YR[t, 1, 0, q, one(i), :]

        @pl.when(t == STEPS - 2)
        def _():
            leavers(t + 1, t + 1)
            start(lambda d: dep_copy(t + 1, d))

        return carry

    lax.fori_loop(0, STEPS, step, 0)

    take_arrivals(STEPS - 1)
    keep = AMSK[...] > 0.0
    for k, state in enumerate((R, S)):
        for w in range(2):
            high, low = split(jnp.where(keep, state[SLOTS:ROWS, halves(w)[0]], 0.0))
            to = slice(k * BLOCK + w * LANES, k * BLOCK + (w + 1) * LANES)
            CAT[0:ARRIVE, to] = high
            CAT[ARRIVE : 2 * ARRIVE, to] = low

    wait_sent(meta_copy)
    wait_sent(lambda d: dep_copy(STEPS - 1, d))
    wait_sent(v_copy, (2, 3))
    for d in range(2):
        for copy in first_copies(d):
            copy.wait_send()


def write_out(
    p, vx, vy, vz, r, s, mask, cat, info, p_out, v_out, r_out, s_out, c_out, r_end, s_end, z_end, c_end, lt, sems
):
    _, cx, cy, nz = v_out.shape
    pairs = []
    for q in range(nz // LANES):
        lanes = pl.ds(q * LANES, LANES)
        pairs.append((vx.at[q, pl.ds(1, cx), :, :], v_out.at[0, :, :, lanes]))
        pairs.append((vy.at[q, :, pl.ds(8, cy), :], v_out.at[1, :, :, lanes]))
        pairs.append((p.at[q, :, pl.ds(8, cy), :], p_out.at[:, :, lanes]))
    copies = [pltpu.make_async_copy(a, b, sems.at[k]) for k, (a, b) in enumerate(pairs)]
    for copy in copies:
        copy.start()

    nq = nz // LANES
    lane = lax.broadcasted_iota(jnp.int32, (cy, LANES), 1)

    def shift_z(i, carry):
        turned = [pltpu.roll(vz[q, i], LANES - 1, 1) for q in range(nq)]
        for q in range(nq):
            z_end[q, i] = jnp.where(lane == LANES - 1, turned[(q + 1) % nq], turned[q])
        return carry

    lax.fori_loop(0, cx, shift_z, 0, unroll=2)
    for q in range(nq):
        to = v_out.at[2, :, :, pl.ds(q * LANES, LANES)]
        copy = pltpu.make_async_copy(z_end.at[q], to, sems.at[len(copies)])
        copy.start()
        copies.append(copy)

    lane8 = lax.broadcasted_iota(jnp.int32, (8, LANES), 1)
    sub8 = lax.broadcasted_iota(jnp.int32, (8, LANES), 0)
    lrow = lax.broadcasted_iota(jnp.int32, (LANES, LANES), 0)
    lcol = lax.broadcasted_iota(jnp.int32, (LANES, LANES), 1)
    label, leave_at, alab = info[0], info[1], info[2]
    present = alab > 0.0
    upper = jnp.where(lrow <= lcol, 1.0, 0.0)
    upper_block = jnp.where(lrow // 32 == lcol // 32, upper, 0.0).astype(bf16)
    upper = upper.astype(bf16)
    ones = jnp.ones((LANES, LANES), bf16)
    present_f = jnp.where(present, 1.0, 0.0)
    arank = jnp.dot(present_f.astype(bf16), upper_block, preferred_element_type=f32) - 1.0
    arank = jnp.where(present, arank, -5.0)
    vacant = label == 0.0
    ranks = []
    for t in range(STEPS):
        vacant = vacant | (leave_at == float(t))
        flag = jnp.where(vacant, 1.0, 0.0).astype(bf16)
        rank = jnp.dot(flag, upper, preferred_element_type=f32) - 1.0
        total = jnp.dot(flag, ones, preferred_element_type=f32)
        for k in range(SLOT_BLOCKS - 1):
            rank = rank + jnp.where(sub8 > k, total[k : k + 1, :], 0.0)
        ranks.append(jnp.where(vacant, rank, -1.0))
        count = jnp.sum(jnp.where(lane8 // 32 == t, present_f, 0.0), axis=1, keepdims=True)
        vacant = vacant & (rank >= count)
    lt[...] = jnp.concatenate(ranks + [jnp.zeros((LANES - 8 * STEPS, LANES), f32)], axis=0).T

    group = lcol // 32
    alab_high, alab_low = split(alab)
    final = jnp.where(leave_at == float(STEPS), label, 0.0)
    nt = (((1,), (1,)), ((), ()))
    for k in range(SLOT_BLOCKS):
        rows = slice(k * LANES, (k + 1) * LANES)
        mine = jnp.broadcast_to(lt[:, k : k + 1], (LANES, LANES))
        for t in range(1, STEPS):
            mine = jnp.where(group == t, lt[:, 8 * t + k : 8 * t + k + 1], mine)
        hot = jnp.where(mine == arank[0:1, :], 1.0, 0.0).astype(bf16)
        there = lax.dot_general(alab_high, hot, nt, preferred_element_type=f32)
        there = there + lax.dot_general(alab_low, hot, nt, preferred_element_type=f32)
        final = final + jnp.where(sub8 == k, there, 0.0)
        both = jnp.concatenate([hot, hot], axis=1)
        placed = jnp.dot(both, cat[...], preferred_element_type=f32)
        keep = mask[rows, :]
        keep = jnp.concatenate([keep, keep], axis=1) >= float(STEPS)
        r_end[rows, :] = jnp.where(keep, r[rows, :], 0.0) + placed[:, :BLOCK]
        s_end[rows, :] = (1.0 / time_step) * (jnp.where(keep, s[rows, :], 0.0) + placed[:, BLOCK:])
        if k % 4 == 3:
            rows_of = pl.ds((k - 3) * LANES, 4 * LANES)
            for a, b in ((r_end, r_out), (s_end, s_out)):
                copy = pltpu.make_async_copy(a.at[rows_of, :], b.at[rows_of, :], sems.at[len(copies)])
                copy.start()
                copies.append(copy)
    c_end[...] = final.astype(jnp.int32) - 1
    copy = pltpu.make_async_copy(c_end, c_out, sems.at[len(copies)])
    copy.start()
    copies.append(copy)
    for copy in copies:
        copy.wait()


def on_device(
    pressure, velocity, stretch, rest_radius, wall_speed, block_cells, depart_slot, depart_way
):
    cx, cy, nz = pressure.shape
    nq = nz // LANES
    ncol = 2 * cx * cy
    vmem = pl.BlockSpec(memory_space=pltpu.VMEM)
    hbm = pl.BlockSpec(memory_space=pl.ANY)
    dma = pltpu.SemaphoreType.DMA
    vmem_out = pltpu.VMEM
    parts = pl.pallas_call(
        kernel,
        out_shape=(
            vmem_out((nq, cx, cy + 16, LANES), f32),
            vmem_out((nq, cx + 2, cy, LANES), f32),
            vmem_out((nq, cx, cy + 16, LANES), f32),
            vmem_out((nq, cx, cy, LANES), f32),
            vmem_out((ROWS, BLOCK), f32),
            vmem_out((ROWS, BLOCK), f32),
            vmem_out((ROWS, LANES), f32),
            vmem_out((2 * ARRIVE, 2 * BLOCK), bf16),
            vmem_out((3, SLOT_BLOCKS, LANES), f32),
        ),
        in_specs=[pl.BlockSpec(memory_space=pltpu.HBM)] * 9,
        out_specs=(vmem,) * 9,
        scratch_shapes=[
            pltpu.VMEM((ROWS, BLOCK), f32),
            pltpu.VMEM((3, ARRIVE, BLOCK), f32),
            pltpu.VMEM((STEPS + 1, 3, DEP, BLOCK), f32),
            pltpu.VMEM((4, DEP, BLOCK), f32),
            pltpu.VMEM((ROWS, ncol), bf16),
            pltpu.VMEM((ncol, ROWS), bf16),
            pltpu.VMEM((ncol, 2 * BLOCK), bf16),
            pltpu.VMEM((ROWS, BLOCK), f32),
            pltpu.VMEM((ROWS, 2 * BLOCK), bf16),
            pltpu.VMEM((ncol, BLOCK), f32),
            pltpu.VMEM((STEPS + 1, 2, nq, 2, cy, LANES), f32),
            pltpu.VMEM((STEPS, 2, nq, 2, cy, LANES), f32),
            pltpu.VMEM((STEPS + 1, 2, 2, nq, cx, LANES), f32),
            pltpu.VMEM((STEPS, 2, 2, nq, cx, LANES), f32),
            pltpu.VMEM((2, nq, cx, LANES), f32),
            pltpu.VMEM((2, nq, cx, LANES), f32),
            pltpu.VMEM((8, LANES), f32),
            pltpu.VMEM((4, 8, LANES), f32),
            pltpu.VMEM((ARRIVE, LANES), f32),
            pltpu.VMEM((LANES, LANES), f32),
            pltpu.VMEM((16, LANES), f32),
            pltpu.SMEM((SLOTS,), jnp.int32),
            pltpu.SMEM((STEPS, 1, 1, DEP), jnp.int32),
            pltpu.SMEM((STEPS, 1, 1, DEP), jnp.int32),
            pltpu.VMEM((SLOT_BLOCKS, LANES), jnp.int32),
            dma((4 * nq + 7,)),
            dma((4,)),
            dma((4,)),
            dma((STEPS, 4)),
            dma((STEPS, 4)),
            dma((4,)),
            dma((4,)),
            dma((STEPS, 4)),
            dma((STEPS, 4)),
            dma((2, 2, nq)),
            dma((2, 2, nq)),
        ],
        compiler_params=pltpu.CompilerParams(
            collective_id=0, has_side_effects=True, vmem_limit_bytes=36 * 2**20
        ),
        cost_estimate=pl.CostEstimate(
            flops=10 * 2**30, bytes_accessed=13 * 2**20, transcendentals=2**22
        ),
    )(
        *(
            pltpu.with_memory_space_constraint(value, pltpu.HBM)
            for value in (
                block_cells,
                depart_slot,
                depart_way,
                block_cells.reshape(SLOT_BLOCKS, LANES),
                pressure,
                velocity,
                stretch,
                rest_radius,
                wall_speed,
            )
        )
    )
    parts = [pltpu.with_memory_space_constraint(part, pltpu.VMEM) for part in parts]
    p, v, r, s, c = pl.pallas_call(
        write_out,
        out_shape=(
            jax.ShapeDtypeStruct(pressure.shape, f32),
            jax.ShapeDtypeStruct(velocity.shape, f32),
            jax.ShapeDtypeStruct(stretch.shape, f32),
            jax.ShapeDtypeStruct(stretch.shape, f32),
            jax.ShapeDtypeStruct((SLOT_BLOCKS, LANES), jnp.int32),
        ),
        in_specs=[vmem] * 9,
        out_specs=(hbm,) * 5,
        scratch_shapes=[
            pltpu.VMEM((SLOTS, BLOCK), f32),
            pltpu.VMEM((SLOTS, BLOCK), f32),
            pltpu.VMEM((nq, cx, cy, LANES), f32),
            pltpu.VMEM((SLOT_BLOCKS, LANES), jnp.int32),
            pltpu.VMEM((LANES, LANES), f32),
            dma((4 * nq + 5,)),
        ],
        compiler_params=pltpu.CompilerParams(vmem_limit_bytes=8 * 2**20),
        cost_estimate=pl.CostEstimate(flops=0, bytes_accessed=13 * 2**20, transcendentals=0),
    )(*parts)
    return p, v, r, s, c.reshape(-1)


def solution(mesh):
    placed = (
        P("gx", "gy", None),
        P(None, "gx", "gy", None),
        P(("gx", "gy"), None),
        P(("gx", "gy"), None),
        P(("gx", "gy"), None),
        P(("gx", "gy")),
        P(None, "gx", "gy", None),
        P(None, "gx", "gy", None),
    )
    return jax.shard_map(
        on_device,
        mesh=mesh,
        in_specs=placed,
        out_specs=(
            P("gx", "gy", None),
            P(None, "gx", "gy", None),
            P(("gx", "gy"), None),
            P(("gx", "gy"), None),
            P(("gx", "gy")),
        ),
        check_vma=False,
    )
```

```python
import functools
import math

import jax
import jax.numpy as jnp
from jax import lax
from jax.experimental import pallas as pl
from jax.experimental.pallas import tpu as pltpu
from jax.sharding import PartitionSpec as P

MESH = pl.DeviceIdType.MESH
f32 = jnp.float32
bf16 = jnp.bfloat16

STEPS = 4
DEP = 8
SLOTS = 1024
BLOCK = 256
LANES = 128
ARRIVE = STEPS * 4 * DEP
ROWS = SLOTS + ARRIVE
SLOT_BLOCKS = SLOTS // LANES
WAY_OF = (1, 0, 3, 2)

time_step = 0.04
half_gain = 0.2
source_scale = 0.004 * 12.566370614359172
exponent = 4.2
inv_ln2 = 1.0 / math.log(2.0)


def split(value):
    high = value.astype(bf16)
    return high, (value - high.astype(f32)).astype(bf16)


def wall_update(radius, shift, level, pressure):
    mach = (0.05 / time_step) * shift
    one_less = 1.0 - mach
    divisor = one_less * radius
    inverse = pl.reciprocal(divisor, approx=True)
    inverse = inverse * (2.0 - divisor * inverse)
    inv_radius = inverse * one_less
    wall = jnp.exp2(level - (exponent * inv_ln2) * jnp.log(radius))
    squared = time_step * time_step
    excess = (
        wall
        - (0.2 * squared + (0.08 * time_step) * shift) * inv_radius
        - (squared + squared * pressure)
    )
    driving = (1.0 + mach) * excess - (1.5 - 0.5 * mach) * (shift * shift)
    shift = shift + driving * inverse
    radius = radius + shift
    return radius, shift, (source_scale / time_step) * (radius * radius) * shift


def kernel(
    cells_h, slot_h, way_h, cells_b, press, vel, stretch, rest, speed0,
    PR, VX, VY, VZ, R, S, MSK, CAT, INFO,
    A, AR, SB, DB, OH, OHT, PHL, PG, VHL, SRC, XS, XR, YS, YR, VYS, VYR,
    MT, MR, AMSK, LT, LR, cells_s, slot_s, way_s, cells_v,
    in_sem, meta_s, meta_r, xs, xr, vs, vr, ds_, dr, fs, fr,
):
    _, cx, cy, nz = vel.shape
    nq = nz // LANES
    half = cx * cy
    ncol = 2 * half
    jbs = cy // 16
    part = min(256, ncol)
    planes = part // (2 * cy)
    groups = cx // planes
    shift = (planes * cy).bit_length() - 1
    zero_row = lax.axis_index("gx") // 4096
    gx, gy = lax.axis_index("gx"), lax.axis_index("gy")
    ngx, ngy = lax.axis_size("gx"), lax.axis_size("gy")
    has_lo, has_hi = gy > 0, gy < ngy - 1
    targets = (
        (lax.rem(gx + 1, ngx), gy),
        (lax.rem(gx + ngx - 1, ngx), gy),
        (gx, lax.rem(gy + 1, ngy)),
        (gx, lax.rem(gy + ngy - 1, ngy)),
    )
    sends = (None, None, has_hi, has_lo)
    takes = (None, None, has_lo, has_hi)

    def under(flag, action):
        if flag is None:
            action()
        else:
            pl.when(flag)(action)

    barrier = pltpu.get_barrier_semaphore()
    for d in range(4):
        under(
            sends[d],
            lambda d=d: pl.semaphore_signal(
                barrier, inc=1, device_id=targets[d], device_id_type=MESH
            ),
        )

    inputs = [(cells_h, cells_s), (slot_h, slot_s), (way_h, way_s), (cells_b, cells_v)]
    for q in range(nq):
        inputs.append((press.at[:, :, pl.ds(q * LANES, LANES)], PR.at[q, :, pl.ds(8, cy), :]))
    for q in range(nq):
        lanes = pl.ds(q * LANES, LANES)
        inputs.append((vel.at[1, :, :, lanes], VY.at[q, :, pl.ds(8, cy), :]))
    own = pl.ds(0, SLOTS)
    inputs.append((rest, A.at[own, :]))
    inputs.append((stretch, R.at[own, :]))
    inputs.append((speed0, S.at[own, :]))
    for q in range(nq):
        lanes = pl.ds(q * LANES, LANES)
        inputs.append((vel.at[0, :, :, lanes], VX.at[q, pl.ds(1, cx), :, :]))
        inputs.append((vel.at[2, :, :, lanes], VZ.at[q]))
    loads = [pltpu.make_async_copy(a, b, in_sem.at[k]) for k, (a, b) in enumerate(inputs)]
    for load in loads:
        load.start()
    small_loads, loads = loads[:4], loads[4:]

    @pl.when(jnp.logical_not(has_lo))
    def _():
        MR[2] = jnp.zeros((8, LANES), f32)
        YR[:, 0] = jnp.zeros(YR.shape[:1] + YR.shape[2:], f32)
        VYR[0] = jnp.zeros(VYR.shape[1:], f32)

    @pl.when(jnp.logical_not(has_hi))
    def _():
        MR[3] = jnp.zeros((8, LANES), f32)
        YR[:, 1] = jnp.zeros(YR.shape[:1] + YR.shape[2:], f32)
        VYR[1] = jnp.zeros(VYR.shape[1:], f32)

    edge_rows = jnp.zeros((nq, cx, 8, LANES), f32)
    PR[:, :, 0:8, :] = edge_rows
    PR[:, :, 8 + cy : 16 + cy, :] = edge_rows
    VY[:, :, 0:8, :] = edge_rows
    VY[:, :, 8 + cy : 16 + cy, :] = edge_rows
    empty = jnp.zeros((ARRIVE, BLOCK), f32)
    R[SLOTS:ROWS, :] = empty + 1.0
    S[SLOTS:ROWS, :] = empty
    A[SLOTS:ROWS, :] = empty
    MSK[SLOTS:ROWS, :] = jnp.full((ARRIVE, LANES), -1.0, f32)
    OHT[:, SLOTS:ROWS] = jnp.zeros((ncol, ARRIVE), bf16)
    VHL[ROWS - 32 : ROWS, :] = jnp.zeros((32, 2 * BLOCK), bf16)
    OH[SLOTS:ROWS, :] = jnp.zeros((ARRIVE, ncol), bf16)
    pl.semaphore_wait(barrier, 2 + has_lo.astype(jnp.int32) + has_hi.astype(jnp.int32))

    def remote(src, dst, send_sem, recv_sem, d):
        return pltpu.make_async_remote_copy(
            src_ref=src, dst_ref=dst, send_sem=send_sem, recv_sem=recv_sem,
            device_id=targets[d], device_id_type=MESH,
        )

    def meta_copy(d):
        return [remote(MT, MR.at[d], meta_s.at[d], meta_r.at[d], d)]

    def p_copy(t, d):
        if d < 2:
            src, dst = XS.at[t, 1 - d], XR.at[t, d]
        else:
            src, dst = YS.at[t, 3 - d], YR.at[t, d - 2]
        return [remote(src, dst, xs.at[t, d], xr.at[t, d], d)]

    def first_copies(d):
        side = (cx - 2, 0)[d]
        for q in range(nq):
            lanes = pl.ds(q * LANES, LANES)
            yield remote(
                press.at[pl.ds(side, 2), :, lanes], XR.at[0, d, q], fs.at[0, d, q], fr.at[0, d, q], d
            )
        for q in range(nq):
            lanes = pl.ds(q * LANES, LANES)
            yield remote(
                vel.at[0, pl.ds((cx - 1, 0)[d], 1), :, lanes],
                VX.at[q, pl.ds((0, cx + 1)[d], 1), :, :],
                fs.at[1, d, q],
                fr.at[1, d, q],
                d,
            )

    def v_copy(d):
        return [remote(VYS.at[3 - d], VYR.at[d - 2], vs.at[d], vr.at[d], d)]

    def dep_copy(t, d):
        to = AR.at[:, pl.ds(t * 32 + d * DEP, DEP), :]
        return [remote(SB.at[t], to, ds_.at[t, d], dr.at[t, d], d)]

    odd = lax.rem(gy, 2) == 1
    even = jnp.logical_not(odd)
    far_hi, near_hi = has_hi & odd, has_hi & even
    far_lo, near_lo = has_lo & even, has_lo & odd

    def start(make, ways=(0, 1, 2, 3)):
        order = ((far_hi, 2), (far_lo, 3), (None, 0), (None, 1), (near_hi, 2), (near_lo, 3))
        for flag, d in order:
            if d in ways:
                under(flag, lambda d=d: [copy.start() for copy in make(d)] and None)

    def wait_sent(make, ways=(0, 1, 2, 3)):
        for d in ways:
            under(sends[d], lambda d=d: [copy.wait_send() for copy in make(d)] and None)

    def wait_taken(make, ways=(0, 1, 2, 3)):
        for d in ways:
            under(takes[d], lambda d=d: [copy.wait_recv() for copy in make(d)] and None)

    for d in range(2):
        for copy in first_copies(d):
            copy.start()
    edges = ((0, 1), (cy - 2, cy - 1))

    def one(row):
        return pl.ds(row + zero_row, 1)

    pitch = cy + 16
    PR_rows = PR.reshape(nq * cx * pitch, LANES)
    VY_rows = VY.reshape(nq * cx * pitch, LANES)

    def across(q, row):
        return pl.ds(q * cx * pitch + 8 + row, cx, stride=pitch), slice(None)

    def pack_rows(t):
        for side in range(2):
            for r in range(2):
                for q in range(nq):
                    YS[t, side, r, q] = PR_rows[across(q, edges[side][r])]

    def unpack_rows(t):
        for side in range(2):
            for r in range(2):
                for q in range(nq):
                    PR_rows[across(q, edges[side][r])] = YS[t, side, r, q]

    def column_row(i, h, jb):
        return (i // planes) * part + (h * planes + i % planes) * cy + jb * 16

    def keep_parts(i, jb, q, value):
        high, low = split(value)
        row = column_row(i, q // 2, jb)
        col = (q % 2) * 2 * LANES
        PHL[row : row + 16, col : col + LANES] = high
        PHL[row : row + 16, col + LANES : col + 2 * LANES] = low

    def rows_of(jb):
        return slice(jb * 16, jb * 16 + 16), slice(8 + jb * 16, 24 + jb * 16)

    def split_all():
        for i in range(cx):
            for jb in range(jbs):
                for q in range(nq):
                    keep_parts(i, jb, q, PR[q, i, rows_of(jb)[1], :])

    for load in small_loads:
        load.wait()

    lane8 = lax.broadcasted_iota(jnp.int32, (8, LANES), 1)
    sub8 = lax.broadcasted_iota(jnp.int32, (8, LANES), 0)
    slot_id = sub8 * LANES + lane8
    label = cells_v[...] + 1
    leave_at = jnp.where(label > 0, STEPS, -1)
    entry_of = (lane8 // 32) * DEP + lane8 % DEP
    wanted = (lane8 // DEP) % 4
    wanted = jnp.where(wanted < 2, 1 - wanted, 5 - wanted)
    meta = jnp.zeros((8, LANES), jnp.int32)
    for e in range(STEPS * DEP):
        slot = slot_s[e // DEP, 0, 0, e % DEP]
        moved = jnp.where(slot >= 0, cells_s[jnp.maximum(slot, 0)] + 1, 0)
        meta = jnp.where((entry_of == e) & (wanted == way_s[e // DEP, 0, 0, e % DEP]), moved, meta)
        leave_at = jnp.where(slot_id == slot, e // DEP, leave_at)
    MT[...] = meta.astype(f32)

    start(meta_copy)

    lrow = lax.broadcasted_iota(jnp.int32, (LANES, LANES), 0)
    lcol = lax.broadcasted_iota(jnp.int32, (LANES, LANES), 1)
    wide = lax.broadcasted_iota(jnp.int32, (16, ncol), 1).astype(f32)

    def code_of(lab):
        cell = lab - 1
        place = cell >> 1
        row = (place >> shift) * part + (cell & 1) * (planes * cy)
        return jnp.where(lab > 0, row + (place & (planes * cy - 1)), -1).astype(f32)

    def turn(stack):
        stack = stack + [jnp.zeros((8, LANES), f32)] * (16 - len(stack))
        LT[...] = jnp.concatenate(stack, axis=0).T

    def hot_rows(r, at):
        def body(m, carry):
            rows = pl.ds(pl.multiple_of(m * 16, 16), 16)
            hot = jnp.where(LT[rows, at : at + 1] == wide, 1.0, 0.0).astype(bf16)
            OH[pl.ds(pl.multiple_of(r * LANES + m * 16, 16), 16), :] = hot
            return carry

        lax.fori_loop(0, LANES // 16, body, 0, unroll=4)

    def hot_columns(first, last):
        def body(m, carry):
            ident = (lrow + m * LANES).astype(f32)
            rows = pl.ds(pl.multiple_of(m * LANES, LANES), LANES)
            for r in range(first, last):
                hot = jnp.where(ident == LR[r : r + 1, :], 1.0, 0.0).astype(bf16)
                OHT[rows, r * LANES : (r + 1) * LANES] = hot
            return carry

        lax.fori_loop(0, ncol // LANES, body, 0)

    code = code_of(label)
    turn([code, leave_at.astype(f32)])
    LR[0:8, :] = code
    for r in range(SLOT_BLOCKS):
        hot_rows(r, r)
    for r in range(SLOT_BLOCKS):
        MSK[r * LANES : (r + 1) * LANES, :] = jnp.broadcast_to(
            LT[:, 8 + r : 9 + r], (LANES, LANES)
        )
    hot_columns(0, SLOT_BLOCKS)

    for k in range(nq):
        loads[k].wait()
    pack_rows(0)
    start(lambda d: p_copy(0, d), (2, 3))
    for q in range(nq):
        for r in range(2):
            XS[0, 0, q, r] = PR[q, r, 8 : 8 + cy, :]
            XS[0, 1, q, r] = PR[q, cx - 2 + r, 8 : 8 + cy, :]
    for k in range(nq, 2 * nq):
        loads[k].wait()
    for q in range(nq):
        VYS[0, q] = VY_rows[across(q, 0)]
        VYS[1, q] = VY_rows[across(q, cy - 1)]
    start(v_copy, (2, 3))

    for k in range(2 * nq, 2 * nq + 3):
        loads[k].wait()

    def first_state(n, carry):
        rows = pl.ds(pl.multiple_of(n * 16, 16), 16)
        rest_now = A[rows, :]
        R[rows, :] = R[rows, :] * rest_now
        S[rows, :] = time_step * S[rows, :]
        A[rows, :] = inv_ln2 * (
            jnp.log((time_step * time_step) * (1.0 + 0.2 / rest_now))
            + exponent * jnp.log(rest_now)
        )
        return carry

    lax.fori_loop(0, SLOTS // 16, first_state, 0, unroll=4)
    for k in range(2 * nq + 3, 4 * nq + 3):
        loads[k].wait()

    def plan():
        wait_taken(meta_copy)
        came = (lane8 // DEP) % 4
        alab = jnp.where(
            came == 0, MR[0], jnp.where(came == 1, MR[1], jnp.where(came == 2, MR[2], MR[3]))
        )
        acode = code_of(alab.astype(jnp.int32))
        turn([acode, alab])
        LR[8:16, :] = acode
        hot_rows(SLOT_BLOCKS, 0)
        hot_columns(SLOT_BLOCKS, SLOT_BLOCKS + 1)
        AMSK[...] = jnp.broadcast_to(LT[:, 8:9], (LANES, LANES))
        INFO[0] = label.astype(f32)
        INFO[1] = leave_at.astype(f32)
        INFO[2] = alab

    def slope_z(tiles):
        height = tiles[0].shape[0]
        lane = lax.broadcasted_iota(jnp.int32, (height, LANES), 1)
        zero = jnp.zeros((height, LANES), f32)
        ahead = [pltpu.roll(v, LANES - 1, 1) for v in tiles] + [zero]
        behind = [zero] + [pltpu.roll(v, 1, 1) for v in tiles]
        return [
            jnp.where(lane == LANES - 1, ahead[q + 1], ahead[q])
            - jnp.where(lane == 0, behind[q], behind[q + 1])
            for q in range(nq)
        ]

    low_gate = jnp.where(has_lo, 1.0, 0.0).astype(f32)
    high_gate = jnp.where(has_hi, 1.0, 0.0).astype(f32)

    def halves(w):
        return slice(w * LANES, (w + 1) * LANES), slice(2 * w * LANES, 2 * (w + 1) * LANES)

    def gather(w, rows=slice(0, ROWS)):
        narrow, pair = halves(w)
        both = jnp.dot(OH[rows, :], PHL[:, pair], preferred_element_type=f32)
        PG[rows, narrow] = both[:, :LANES] + both[:, LANES:]

    def scatter(w, rows):
        narrow, pair = halves(w)
        both = jnp.dot(OHT[rows, :], VHL[:, pair], preferred_element_type=f32)
        SRC[rows, narrow] = both[:, :LANES] + both[:, LANES:]

    def leavers(t, to):
        for k in range(DEP):
            slot = jnp.maximum(slot_s[t, 0, 0, k], 0)
            cell = jnp.maximum(cells_s[slot], 0)
            place = cell >> 1
            row = pl.ds(slot, 1)
            DB[0, k : k + 1, :] = R[row, :]
            DB[1, k : k + 1, :] = S[row, :]
            DB[2, k : k + 1, :] = A[row, :]
            for w in range(2):
                DB[3, k : k + 1, halves(w)[0]] = PR[
                    2 * (cell & 1) + w,
                    place >> (cy.bit_length() - 1),
                    pl.ds(8 + (place & (cy - 1)), 1),
                    :,
                ]
        radius, speed, _ = wall_update(DB[0], DB[1], DB[2], DB[3])
        SB[to, 0] = radius
        SB[to, 1] = speed
        SB[to, 2] = DB[2]

    def take_arrivals(t):
        wait_taken(lambda d: dep_copy(t, d))
        rows = pl.ds(pl.multiple_of(t * 32, 32), 32)
        to = pl.ds(pl.multiple_of(SLOTS + t * 32, 32), 32)
        R[to, :] = AR[0, rows, :]
        S[to, :] = AR[1, rows, :]
        A[to, :] = AR[2, rows, :]
        MSK[to, :] = jnp.where(AMSK[rows, :] > 0.0, 2.0 * STEPS, -1.0)

    def step(t, carry):
        limit = t.astype(f32)

        def bubbles(first, w):
            rows = slice(first, first + 16)
            col = halves(w)[0]
            radius, speed, rate = wall_update(R[rows, col], S[rows, col], A[rows, col], PG[rows, col])
            R[rows, col] = radius
            S[rows, col] = speed
            high, low = split(jnp.where(MSK[rows, :] >= limit, rate, 0.0))
            VHL[rows, 2 * w * LANES : (2 * w + 1) * LANES] = high
            VHL[rows, (2 * w + 1) * LANES : (2 * w + 2) * LANES] = low

        @pl.when(t > 0)
        def _():
            take_arrivals(t - 1)

        split_all()
        last = t // (STEPS - 1)
        leavers(t, t + last)
        gather(0)

        @pl.when(last == 0)
        def _():
            start(lambda d: dep_copy(t, d))

        def pieces(count, size):
            return [slice(k * size // count, (k + 1) * size // count) for k in range(count)]

        for rows in pieces(3, ROWS):
            gather(1, rows)
            for first in range(rows.start, min(rows.stop, ROWS - 32), 16):
                bubbles(first, 0)
        for rows, part_rows in zip(pieces(2, ncol), ((0, 560), (560, ROWS - 32))):
            scatter(0, rows)
            for first in range(*part_rows, 16):
                bubbles(first, 1)

        def flow_x(i):
            for q in range(nq):
                for jb in range(jbs):
                    rows, at = rows_of(jb)
                    flow = VX[q, i + 1, rows, :]
                    if i == 0:
                        flow = flow - half_gain * PR[q, 1, at, :]
                    elif i == cx - 1:
                        flow = flow + half_gain * PR[q, cx - 2, at, :]
                    else:
                        flow = flow - half_gain * (PR[q, i + 1, at, :] - PR[q, i - 1, at, :])
                    VX[q, i + 1, rows, :] = flow

        def flow_z(i, jb):
            rows, at = rows_of(jb)
            slopes = slope_z([PR[q, i, at, :] for q in range(nq)])
            for q in range(nq):
                VZ[q, i, rows, :] = VZ[q, i, rows, :] - half_gain * slopes[q]

        def flow_y(i, jb):
            _, at = rows_of(jb)
            for q in range(nq):
                VY[q, i, at, :] = VY[q, i, at, :] - half_gain * (
                    PR[q, i, pl.ds(9 + jb * 16 + zero_row, 16), :]
                    - PR[q, i, pl.ds(7 + jb * 16 + zero_row, 16), :]
                )

        def pressure(i, jb):
            rows, at = rows_of(jb)
            slopes = slope_z([VZ[q, i, rows, :] for q in range(nq)])
            for q in range(nq):
                rise = slopes[q] + (
                    VY[q, i, pl.ds(9 + jb * 16 + zero_row, 16), :]
                    - VY[q, i, pl.ds(7 + jb * 16 + zero_row, 16), :]
                )
                if i + 1 < cx:
                    rise = rise + VX[q, i + 2, rows, :]
                if i > 0:
                    rise = rise - VX[q, i, rows, :]
                row = column_row(i, q // 2, jb)
                col = (q % 2) * LANES
                PR[q, i, at, :] = (
                    PR[q, i, at, :] - half_gain * rise + SRC[row : row + 16, col : col + LANES]
                )

        for rows, part_planes in zip(pieces(2, ncol), pieces(2, cx)):
            scatter(1, rows)
            for i in range(part_planes.start, part_planes.stop):
                flow_x(i)
                for jb in range(jbs):
                    flow_z(i, jb)
                    flow_y(i, jb)
        for i in range(cx):
            for jb in range(jbs):
                pressure(i, jb)
        pack_rows(t + 1)

        pl.when(t == 0)(plan)
        wait_taken(lambda d: p_copy(t, d), (2, 3))

        @pl.when(t > 0)
        def _():
            wait_taken(lambda d: p_copy(t, d), (0, 1))

        @pl.when(t == 0)
        def _():
            for d in range(2):
                for copy in first_copies(d):
                    copy.wait_recv()
            wait_taken(v_copy, (2, 3))

        below, above = VYR[0], VYR[1]
        below = low_gate * (below - half_gain * (YS[t, 0, 0] - YR[t, 0, 0]))
        above = high_gate * (above - half_gain * (YR[t, 1, 1] - YS[t, 1, 1]))
        VYR[0] = below
        VYR[1] = above
        both_gains = half_gain * half_gain
        YS[t + 1, 0, 0] = YS[t + 1, 0, 0] + half_gain * below
        YS[t + 1, 0, 1] = YS[t + 1, 0, 1] + both_gains * YR[t, 0, 1]
        YS[t + 1, 1, 0] = YS[t + 1, 1, 0] + both_gains * YR[t, 1, 0]
        YS[t + 1, 1, 1] = YS[t + 1, 1, 1] - half_gain * above
        for q in range(nq):
            for jb in range(jbs):
                rows, at = rows_of(jb)
                far, near = XR[t, 0, q, 0, rows, :], XR[t, 0, q, 1, rows, :]
                beside = VX[q, 0, rows, :] - half_gain * (XS[t, 0, q, 0, rows, :] - far)
                VX[q, 0, rows, :] = beside
                VX[q, 1, rows, :] = VX[q, 1, rows, :] + half_gain * near
                first = PR[q, 0, at, :] + half_gain * beside
                second = PR[q, 1, at, :] + both_gains * near
                PR[q, 0, at, :] = first
                PR[q, 1, at, :] = second
                XS[t + 1, 0, q, 0, rows, :] = first
                XS[t + 1, 0, q, 1, rows, :] = second
                near, far = XR[t, 1, q, 0, rows, :], XR[t, 1, q, 1, rows, :]
                beside = VX[q, cx + 1, rows, :] - half_gain * (far - XS[t, 1, q, 1, rows, :])
                VX[q, cx + 1, rows, :] = beside
                VX[q, cx, rows, :] = VX[q, cx, rows, :] - half_gain * near
                first = PR[q, cx - 2, at, :] + both_gains * near
                second = PR[q, cx - 1, at, :] - half_gain * beside
                PR[q, cx - 2, at, :] = first
                PR[q, cx - 1, at, :] = second
                XS[t + 1, 1, q, 0, rows, :] = first
                XS[t + 1, 1, q, 1, rows, :] = second
        ends = ((0, 0, 0), (1, 0, 1), (cx - 2, 1, 0), (cx - 1, 1, 1))
        for i, x_side, x_row in ends:
            for side in range(2):
                for r in range(2):
                    for q in range(nq):
                        row = one(edges[side][r])
                        if i == 0:
                            part_x = half_gain * VX[q, 0, row, :]
                        elif i == 1:
                            part_x = both_gains * XR[t, 0, q, 1, row, :]
                        elif i == cx - 2:
                            part_x = both_gains * XR[t, 1, q, 0, row, :]
                        else:
                            part_x = -half_gain * VX[q, cx + 1, row, :]
                        value = YS[t + 1, side, r, q, one(i), :] + part_x
                        YS[t + 1, side, r, q, one(i), :] = value
                        XS[t + 1, x_side, q, x_row, row, :] = value

        @pl.when(t < STEPS - 1)
        def _():
            start(lambda d: p_copy(t + 1, d))

        unpack_rows(t + 1)
        for q in range(nq):
            low, high = across(q, 0), across(q, cy - 1)
            VY_rows[low] = VY_rows[low] + half_gain * YR[t, 0, 1, q]
            VY_rows[high] = VY_rows[high] - half_gain * YR[t, 1, 0, q]

        @pl.when(t == STEPS - 2)
        def _():
            leavers(t + 1, t + 1)
            start(lambda d: dep_copy(t + 1, d))

        wait_sent(lambda d: dep_copy(t, d))

        @pl.when(t > 0)
        def _():
            wait_sent(lambda d: p_copy(t, d), (0, 1))

        wait_sent(lambda d: p_copy(t, d), (2, 3))

        return carry

    lax.fori_loop(0, STEPS, step, 0)

    take_arrivals(STEPS - 1)
    keep = AMSK[...] > 0.0
    for k, state in enumerate((R, S)):
        for w in range(2):
            high, low = split(jnp.where(keep, state[SLOTS:ROWS, halves(w)[0]], 0.0))
            to = slice(k * BLOCK + w * LANES, k * BLOCK + (w + 1) * LANES)
            CAT[0:ARRIVE, to] = high
            CAT[ARRIVE : 2 * ARRIVE, to] = low

    wait_sent(meta_copy)
    wait_sent(v_copy, (2, 3))
    for d in range(2):
        for copy in first_copies(d):
            copy.wait_send()


def write_out(
    p, vx, vy, vz, r, s, mask, cat, info, p_out, v_out, r_out, s_out, c_out, r_end, s_end, c_end, lt, sems
):
    _, cx, cy, nz = v_out.shape
    pairs = []
    for q in range(nz // LANES):
        lanes = pl.ds(q * LANES, LANES)
        pairs.append((vx.at[q, pl.ds(1, cx), :, :], v_out.at[0, :, :, lanes]))
        pairs.append((vy.at[q, :, pl.ds(8, cy), :], v_out.at[1, :, :, lanes]))
        pairs.append((vz.at[q], v_out.at[2, :, :, lanes]))
        pairs.append((p.at[q, :, pl.ds(8, cy), :], p_out.at[:, :, lanes]))
    copies = [pltpu.make_async_copy(a, b, sems.at[k]) for k, (a, b) in enumerate(pairs)]
    for copy in copies:
        copy.start()

    lane8 = lax.broadcasted_iota(jnp.int32, (8, LANES), 1)
    sub8 = lax.broadcasted_iota(jnp.int32, (8, LANES), 0)
    lrow = lax.broadcasted_iota(jnp.int32, (LANES, LANES), 0)
    lcol = lax.broadcasted_iota(jnp.int32, (LANES, LANES), 1)
    label, leave_at, alab = info[0], info[1], info[2]
    present = alab > 0.0
    upper = jnp.where(lrow <= lcol, 1.0, 0.0)
    upper_block = jnp.where(lrow // 32 == lcol // 32, upper, 0.0).astype(bf16)
    upper = upper.astype(bf16)
    ones = jnp.ones((LANES, LANES), bf16)
    present_f = jnp.where(present, 1.0, 0.0)
    arank = jnp.dot(present_f.astype(bf16), upper_block, preferred_element_type=f32) - 1.0
    arank = jnp.where(present, arank, -5.0)
    vacant = label == 0.0
    ranks = []
    for t in range(STEPS):
        vacant = vacant | (leave_at == float(t))
        flag = jnp.where(vacant, 1.0, 0.0).astype(bf16)
        rank = jnp.dot(flag, upper, preferred_element_type=f32) - 1.0
        total = jnp.dot(flag, ones, preferred_element_type=f32)
        for k in range(SLOT_BLOCKS - 1):
            rank = rank + jnp.where(sub8 > k, total[k : k + 1, :], 0.0)
        ranks.append(jnp.where(vacant, rank, -1.0))
        count = jnp.sum(jnp.where(lane8 // 32 == t, present_f, 0.0), axis=1, keepdims=True)
        vacant = vacant & (rank >= count)
    lt[...] = jnp.concatenate(ranks + [jnp.zeros((LANES - 8 * STEPS, LANES), f32)], axis=0).T

    group = lcol // 32
    alab_high, alab_low = split(alab)
    final = jnp.where(leave_at == float(STEPS), label, 0.0)
    nt = (((1,), (1,)), ((), ()))
    for k in range(SLOT_BLOCKS):
        rows = slice(k * LANES, (k + 1) * LANES)
        mine = jnp.broadcast_to(lt[:, k : k + 1], (LANES, LANES))
        for t in range(1, STEPS):
            mine = jnp.where(group == t, lt[:, 8 * t + k : 8 * t + k + 1], mine)
        hot = jnp.where(mine == arank[0:1, :], 1.0, 0.0).astype(bf16)
        there = lax.dot_general(alab_high, hot, nt, preferred_element_type=f32)
        there = there + lax.dot_general(alab_low, hot, nt, preferred_element_type=f32)
        final = final + jnp.where(sub8 == k, there, 0.0)
        both = jnp.concatenate([hot, hot], axis=1)
        placed = jnp.dot(both, cat[...], preferred_element_type=f32)
        keep = mask[rows, :]
        keep = jnp.concatenate([keep, keep], axis=1) >= float(STEPS)
        r_end[rows, :] = jnp.where(keep, r[rows, :], 0.0) + placed[:, :BLOCK]
        s_end[rows, :] = (1.0 / time_step) * (jnp.where(keep, s[rows, :], 0.0) + placed[:, BLOCK:])
        if k % 4 == 3:
            rows_of = pl.ds((k - 3) * LANES, 4 * LANES)
            for a, b in ((r_end, r_out), (s_end, s_out)):
                copy = pltpu.make_async_copy(a.at[rows_of, :], b.at[rows_of, :], sems.at[len(copies)])
                copy.start()
                copies.append(copy)
    c_end[...] = final.astype(jnp.int32) - 1
    copy = pltpu.make_async_copy(c_end, c_out, sems.at[len(copies)])
    copy.start()
    copies.append(copy)
    for copy in copies:
        copy.wait()


def on_device(
    pressure, velocity, stretch, rest_radius, wall_speed, block_cells, depart_slot, depart_way
):
    cx, cy, nz = pressure.shape
    nq = nz // LANES
    ncol = 2 * cx * cy
    vmem = pl.BlockSpec(memory_space=pltpu.VMEM)
    hbm = pl.BlockSpec(memory_space=pl.ANY)
    dma = pltpu.SemaphoreType.DMA
    vmem_out = pltpu.VMEM
    parts = pl.pallas_call(
        kernel,
        out_shape=(
            vmem_out((nq, cx, cy + 16, LANES), f32),
            vmem_out((nq, cx + 2, cy, LANES), f32),
            vmem_out((nq, cx, cy + 16, LANES), f32),
            vmem_out((nq, cx, cy, LANES), f32),
            vmem_out((ROWS, BLOCK), f32),
            vmem_out((ROWS, BLOCK), f32),
            vmem_out((ROWS, LANES), f32),
            vmem_out((2 * ARRIVE, 2 * BLOCK), bf16),
            vmem_out((3, SLOT_BLOCKS, LANES), f32),
        ),
        in_specs=[pl.BlockSpec(memory_space=pltpu.HBM)] * 9,
        out_specs=(vmem,) * 9,
        scratch_shapes=[
            pltpu.VMEM((ROWS, BLOCK), f32),
            pltpu.VMEM((3, ARRIVE, BLOCK), f32),
            pltpu.VMEM((STEPS + 1, 3, DEP, BLOCK), f32),
            pltpu.VMEM((4, DEP, BLOCK), f32),
            pltpu.VMEM((ROWS, ncol), bf16),
            pltpu.VMEM((ncol, ROWS), bf16),
            pltpu.VMEM((ncol, 2 * BLOCK), bf16),
            pltpu.VMEM((ROWS, BLOCK), f32),
            pltpu.VMEM((ROWS, 2 * BLOCK), bf16),
            pltpu.VMEM((ncol, BLOCK), f32),
            pltpu.VMEM((STEPS + 1, 2, nq, 2, cy, LANES), f32),
            pltpu.VMEM((STEPS, 2, nq, 2, cy, LANES), f32),
            pltpu.VMEM((STEPS + 1, 2, 2, nq, cx, LANES), f32),
            pltpu.VMEM((STEPS, 2, 2, nq, cx, LANES), f32),
            pltpu.VMEM((2, nq, cx, LANES), f32),
            pltpu.VMEM((2, nq, cx, LANES), f32),
            pltpu.VMEM((8, LANES), f32),
            pltpu.VMEM((4, 8, LANES), f32),
            pltpu.VMEM((ARRIVE, LANES), f32),
            pltpu.VMEM((LANES, LANES), f32),
            pltpu.VMEM((16, LANES), f32),
            pltpu.SMEM((SLOTS,), jnp.int32),
            pltpu.SMEM((STEPS, 1, 1, DEP), jnp.int32),
            pltpu.SMEM((STEPS, 1, 1, DEP), jnp.int32),
            pltpu.VMEM((SLOT_BLOCKS, LANES), jnp.int32),
            dma((4 * nq + 7,)),
            dma((4,)),
            dma((4,)),
            dma((STEPS, 4)),
            dma((STEPS, 4)),
            dma((4,)),
            dma((4,)),
            dma((STEPS, 4)),
            dma((STEPS, 4)),
            dma((2, 2, nq)),
            dma((2, 2, nq)),
        ],
        compiler_params=pltpu.CompilerParams(
            collective_id=0, has_side_effects=True, vmem_limit_bytes=36 * 2**20
        ),
        cost_estimate=pl.CostEstimate(
            flops=10 * 2**30, bytes_accessed=13 * 2**20, transcendentals=2**22
        ),
    )(
        *(
            pltpu.with_memory_space_constraint(value, pltpu.HBM)
            for value in (
                block_cells,
                depart_slot,
                depart_way,
                block_cells.reshape(SLOT_BLOCKS, LANES),
                pressure,
                velocity,
                stretch,
                rest_radius,
                wall_speed,
            )
        )
    )
    parts = [pltpu.with_memory_space_constraint(part, pltpu.VMEM) for part in parts]
    p, v, r, s, c = pl.pallas_call(
        write_out,
        out_shape=(
            jax.ShapeDtypeStruct(pressure.shape, f32),
            jax.ShapeDtypeStruct(velocity.shape, f32),
            jax.ShapeDtypeStruct(stretch.shape, f32),
            jax.ShapeDtypeStruct(stretch.shape, f32),
            jax.ShapeDtypeStruct((SLOT_BLOCKS, LANES), jnp.int32),
        ),
        in_specs=[vmem] * 9,
        out_specs=(hbm,) * 5,
        scratch_shapes=[
            pltpu.VMEM((SLOTS, BLOCK), f32),
            pltpu.VMEM((SLOTS, BLOCK), f32),
            pltpu.VMEM((SLOT_BLOCKS, LANES), jnp.int32),
            pltpu.VMEM((LANES, LANES), f32),
            dma((4 * nq + 5,)),
        ],
        compiler_params=pltpu.CompilerParams(vmem_limit_bytes=8 * 2**20),
        cost_estimate=pl.CostEstimate(flops=0, bytes_accessed=13 * 2**20, transcendentals=0),
    )(*parts)
    return p, v, r, s, c.reshape(-1)


def solution(mesh):
    placed = (
        P("gx", "gy", None),
        P(None, "gx", "gy", None),
        P(("gx", "gy"), None),
        P(("gx", "gy"), None),
        P(("gx", "gy"), None),
        P(("gx", "gy")),
        P(None, "gx", "gy", None),
        P(None, "gx", "gy", None),
    )
    return jax.shard_map(
        on_device,
        mesh=mesh,
        in_specs=placed,
        out_specs=(
            P("gx", "gy", None),
            P(None, "gx", "gy", None),
            P(("gx", "gy"), None),
            P(("gx", "gy"), None),
            P(("gx", "gy")),
        ),
        check_vma=False,
    )
```

```python
import functools
import math

import jax
import jax.numpy as jnp
from jax import lax
from jax.experimental import pallas as pl
from jax.experimental.pallas import tpu as pltpu
from jax.sharding import PartitionSpec as P

MESH = pl.DeviceIdType.MESH
f32 = jnp.float32
bf16 = jnp.bfloat16

STEPS = 4
DEP = 8
SLOTS = 1024
BLOCK = 256
LANES = 128
ARRIVE = STEPS * 4 * DEP
ROWS = SLOTS + ARRIVE
SLOT_BLOCKS = SLOTS // LANES
WAY_OF = (1, 0, 3, 2)

time_step = 0.04
half_gain = 0.2
source_scale = 0.004 * 12.566370614359172
exponent = 4.2
inv_ln2 = 1.0 / math.log(2.0)


def split(value):
    high = value.astype(bf16)
    return high, (value - high.astype(f32)).astype(bf16)


def wall_update(radius, shift, level, pressure):
    mach = (0.05 / time_step) * shift
    one_less = 1.0 - mach
    divisor = one_less * radius
    inverse = pl.reciprocal(divisor, approx=True)
    inverse = inverse * (2.0 - divisor * inverse)
    inv_radius = inverse * one_less
    wall = jnp.exp2(level - (exponent * inv_ln2) * jnp.log(radius))
    squared = time_step * time_step
    excess = (
        wall
        - (0.2 * squared + (0.08 * time_step) * shift) * inv_radius
        - (squared + squared * pressure)
    )
    driving = (1.0 + mach) * excess - (1.5 - 0.5 * mach) * (shift * shift)
    shift = shift + driving * inverse
    radius = radius + shift
    return radius, shift, (source_scale / time_step) * (radius * radius) * shift


def kernel(
    cells_h, slot_h, way_h, cells_b, press, vel, stretch, rest, speed0,
    PR, VX, VY, VZ, R, S, MSK, CAT, INFO,
    A, AR, SB, DB, OH, OHT, PHL, PG, VHL, SRC, VXH, XS, XR, YS, YR, VYS, VYR,
    MT, MR, AMSK, LT, LR, cells_s, slot_s, way_s, cells_v,
    in_sem, meta_s, meta_r, xs, xr, vs, vr, ds_, dr, fs, fr,
):
    _, cx, cy, nz = vel.shape
    nq = nz // LANES
    half = cx * cy
    ncol = 2 * half
    jbs = cy // 16
    part = min(256, ncol)
    planes = part // (2 * cy)
    groups = cx // planes
    shift = (planes * cy).bit_length() - 1
    zero_row = lax.axis_index("gx") // 4096
    gx, gy = lax.axis_index("gx"), lax.axis_index("gy")
    ngx, ngy = lax.axis_size("gx"), lax.axis_size("gy")
    has_lo, has_hi = gy > 0, gy < ngy - 1
    targets = (
        (lax.rem(gx + 1, ngx), gy),
        (lax.rem(gx + ngx - 1, ngx), gy),
        (gx, lax.rem(gy + 1, ngy)),
        (gx, lax.rem(gy + ngy - 1, ngy)),
    )
    sends = (None, None, has_hi, has_lo)
    takes = (None, None, has_lo, has_hi)

    def under(flag, action):
        if flag is None:
            action()
        else:
            pl.when(flag)(action)

    barrier = pltpu.get_barrier_semaphore()
    for d in range(4):
        under(
            sends[d],
            lambda d=d: pl.semaphore_signal(
                barrier, inc=1, device_id=targets[d], device_id_type=MESH
            ),
        )

    inputs = [(cells_h, cells_s), (slot_h, slot_s), (way_h, way_s), (cells_b, cells_v)]
    for q in range(nq):
        inputs.append((press.at[:, :, pl.ds(q * LANES, LANES)], PR.at[q, pl.ds(1, cx), pl.ds(8, cy), :]))
    for q in range(nq):
        lanes = pl.ds(q * LANES, LANES)
        inputs.append((vel.at[1, :, :, lanes], VY.at[q, :, pl.ds(8, cy), :]))
    own = pl.ds(0, SLOTS)
    inputs.append((rest, A.at[own, :]))
    inputs.append((stretch, R.at[own, :]))
    inputs.append((speed0, S.at[own, :]))
    for q in range(nq):
        lanes = pl.ds(q * LANES, LANES)
        inputs.append((vel.at[0, :, :, lanes], VX.at[q, pl.ds(1, cx), :, :]))
        inputs.append((vel.at[2, :, :, lanes], VZ.at[q]))
    loads = [pltpu.make_async_copy(a, b, in_sem.at[k]) for k, (a, b) in enumerate(inputs)]
    for load in loads:
        load.start()
    small_loads, loads = loads[:4], loads[4:]

    @pl.when(jnp.logical_not(has_lo))
    def _():
        MR[2] = jnp.zeros((8, LANES), f32)
        YR[:, 0] = jnp.zeros(YR.shape[:1] + YR.shape[2:], f32)
        VYR[0] = jnp.zeros(VYR.shape[1:], f32)

    @pl.when(jnp.logical_not(has_hi))
    def _():
        MR[3] = jnp.zeros((8, LANES), f32)
        YR[:, 1] = jnp.zeros(YR.shape[:1] + YR.shape[2:], f32)
        VYR[1] = jnp.zeros(VYR.shape[1:], f32)

    edge_rows = jnp.zeros((nq, cx, 8, LANES), f32)
    for q in range(nq):
        for i in range(cx + 2):
            PR[q, i, 0:8, :] = edge_rows[0, 0]
            PR[q, i, 8 + cy : 16 + cy, :] = edge_rows[0, 0]
        for i in (0, cx + 1):
            PR[q, i, 8 : 8 + cy, :] = jnp.zeros((cy, LANES), f32)
            VX[q, i] = jnp.zeros((cy, LANES), f32)
    VY[:, :, 0:8, :] = edge_rows
    VY[:, :, 8 + cy : 16 + cy, :] = edge_rows
    empty = jnp.zeros((ARRIVE, BLOCK), f32)
    R[SLOTS:ROWS, :] = empty + 1.0
    S[SLOTS:ROWS, :] = empty
    A[SLOTS:ROWS, :] = empty
    MSK[SLOTS:ROWS, :] = jnp.full((ARRIVE, LANES), -1.0, f32)
    OHT[:, SLOTS:ROWS] = jnp.zeros((ncol, ARRIVE), bf16)
    VHL[ROWS - 32 : ROWS, :] = jnp.zeros((32, 2 * BLOCK), bf16)
    OH[SLOTS:ROWS, :] = jnp.zeros((ARRIVE, ncol), bf16)
    pl.semaphore_wait(barrier, 2 + has_lo.astype(jnp.int32) + has_hi.astype(jnp.int32))

    def remote(src, dst, send_sem, recv_sem, d):
        return pltpu.make_async_remote_copy(
            src_ref=src, dst_ref=dst, send_sem=send_sem, recv_sem=recv_sem,
            device_id=targets[d], device_id_type=MESH,
        )

    def meta_copy(d):
        return [remote(MT, MR.at[d], meta_s.at[d], meta_r.at[d], d)]

    def p_copy(t, d):
        if d < 2:
            src, dst = XS.at[t, 1 - d], XR.at[t, d]
        else:
            src, dst = YS.at[t, 3 - d], YR.at[t, d - 2]
        return [remote(src, dst, xs.at[t, d], xr.at[t, d], d)]

    def first_copies(d):
        side = (cx - 2, 0)[d]
        for q in range(nq):
            lanes = pl.ds(q * LANES, LANES)
            yield remote(
                press.at[pl.ds(side, 2), :, lanes], XR.at[0, d, q], fs.at[0, d, q], fr.at[0, d, q], d
            )
        for q in range(nq):
            lanes = pl.ds(q * LANES, LANES)
            yield remote(
                vel.at[0, pl.ds((cx - 1, 0)[d], 1), :, lanes],
                VXH.at[d, pl.ds(q, 1), :, :],
                fs.at[1, d, q],
                fr.at[1, d, q],
                d,
            )

    def v_copy(d):
        return [remote(VYS.at[3 - d], VYR.at[d - 2], vs.at[d], vr.at[d], d)]

    def dep_copy(t, d):
        to = AR.at[:, pl.ds(t * 32 + d * DEP, DEP), :]
        return [remote(SB.at[t], to, ds_.at[t, d], dr.at[t, d], d)]

    odd = lax.rem(gy, 2) == 1
    even = jnp.logical_not(odd)
    far_hi, near_hi = has_hi & odd, has_hi & even
    far_lo, near_lo = has_lo & even, has_lo & odd

    def start(make, ways=(0, 1, 2, 3)):
        order = ((far_hi, 2), (far_lo, 3), (None, 0), (None, 1), (near_hi, 2), (near_lo, 3))
        for flag, d in order:
            if d in ways:
                under(flag, lambda d=d: [copy.start() for copy in make(d)] and None)

    def wait_sent(make, ways=(0, 1, 2, 3)):
        for d in ways:
            under(sends[d], lambda d=d: [copy.wait_send() for copy in make(d)] and None)

    def wait_taken(make, ways=(0, 1, 2, 3)):
        for d in ways:
            under(takes[d], lambda d=d: [copy.wait_recv() for copy in make(d)] and None)

    for d in range(2):
        for copy in first_copies(d):
            copy.start()
    edges = ((0, 1), (cy - 2, cy - 1))

    def one(row):
        return pl.ds(row + zero_row, 1)

    pitch = cy + 16
    PR_rows = PR.reshape(nq * (cx + 2) * pitch, LANES)
    VY_rows = VY.reshape(nq * cx * pitch, LANES)

    def across(q, row):
        return pl.ds(q * cx * pitch + 8 + row, cx, stride=pitch), slice(None)

    def across_p(q, row):
        return pl.ds((q * (cx + 2) + 1) * pitch + 8 + row, cx, stride=pitch), slice(None)

    def pack_rows(t):
        for side in range(2):
            for r in range(2):
                for q in range(nq):
                    YS[t, side, r, q] = PR_rows[across_p(q, edges[side][r])]

    def unpack_rows(t):
        for side in range(2):
            for r in range(2):
                for q in range(nq):
                    PR_rows[across_p(q, edges[side][r])] = YS[t, side, r, q]

    def column_row(m, k, h, jb):
        return pl.multiple_of(m * part + (h * planes + k) * cy + jb * 16, 16)

    def rows_of(jb):
        return slice(jb * 16, jb * 16 + 16), slice(8 + jb * 16, 24 + jb * 16)

    def split_all():
        def body(m, carry):
            for k in range(planes):
                for jb in range(jbs):
                    for q in range(nq):
                        high, low = split(PR[q, m * planes + k + 1, rows_of(jb)[1], :])
                        rows = pl.ds(column_row(m, k, q // 2, jb), 16)
                        col = (q % 2) * 2 * LANES
                        PHL[rows, col : col + LANES] = high
                        PHL[rows, col + LANES : col + 2 * LANES] = low
            return carry

        lax.fori_loop(0, groups, body, 0)

    for load in small_loads:
        load.wait()

    lane8 = lax.broadcasted_iota(jnp.int32, (8, LANES), 1)
    sub8 = lax.broadcasted_iota(jnp.int32, (8, LANES), 0)
    slot_id = sub8 * LANES + lane8
    label = cells_v[...] + 1
    leave_at = jnp.where(label > 0, STEPS, -1)
    entry_of = (lane8 // 32) * DEP + lane8 % DEP
    wanted = (lane8 // DEP) % 4
    wanted = jnp.where(wanted < 2, 1 - wanted, 5 - wanted)
    meta = jnp.zeros((8, LANES), jnp.int32)
    for e in range(STEPS * DEP):
        slot = slot_s[e // DEP, 0, 0, e % DEP]
        moved = jnp.where(slot >= 0, cells_s[jnp.maximum(slot, 0)] + 1, 0)
        meta = jnp.where((entry_of == e) & (wanted == way_s[e // DEP, 0, 0, e % DEP]), moved, meta)
        leave_at = jnp.where(slot_id == slot, e // DEP, leave_at)
    MT[...] = meta.astype(f32)

    start(meta_copy)

    lrow = lax.broadcasted_iota(jnp.int32, (LANES, LANES), 0)
    lcol = lax.broadcasted_iota(jnp.int32, (LANES, LANES), 1)
    wide = lax.broadcasted_iota(jnp.int32, (16, ncol), 1).astype(f32)

    def code_of(lab):
        cell = lab - 1
        place = cell >> 1
        row = (place >> shift) * part + (cell & 1) * (planes * cy)
        return jnp.where(lab > 0, row + (place & (planes * cy - 1)), -1).astype(f32)

    def turn(stack):
        stack = stack + [jnp.zeros((8, LANES), f32)] * (16 - len(stack))
        LT[...] = jnp.concatenate(stack, axis=0).T

    def hot_rows(r, at):
        def body(m, carry):
            rows = pl.ds(pl.multiple_of(m * 16, 16), 16)
            hot = jnp.where(LT[rows, at : at + 1] == wide, 1.0, 0.0).astype(bf16)
            OH[pl.ds(pl.multiple_of(r * LANES + m * 16, 16), 16), :] = hot
            return carry

        lax.fori_loop(0, LANES // 16, body, 0, unroll=4)

    def hot_columns(first, last):
        def body(m, carry):
            ident = (lrow + m * LANES).astype(f32)
            rows = pl.ds(pl.multiple_of(m * LANES, LANES), LANES)
            for r in range(first, last):
                hot = jnp.where(ident == LR[r : r + 1, :], 1.0, 0.0).astype(bf16)
                OHT[rows, r * LANES : (r + 1) * LANES] = hot
            return carry

        lax.fori_loop(0, ncol // LANES, body, 0)

    code = code_of(label)
    turn([code, leave_at.astype(f32)])
    LR[0:8, :] = code
    for r in range(SLOT_BLOCKS):
        hot_rows(r, r)
    for r in range(SLOT_BLOCKS):
        MSK[r * LANES : (r + 1) * LANES, :] = jnp.broadcast_to(
            LT[:, 8 + r : 9 + r], (LANES, LANES)
        )
    hot_columns(0, SLOT_BLOCKS)

    for k in range(nq):
        loads[k].wait()
    pack_rows(0)
    start(lambda d: p_copy(0, d), (2, 3))
    for q in range(nq):
        for r in range(2):
            XS[0, 0, q, r] = PR[q, r + 1, 8 : 8 + cy, :]
            XS[0, 1, q, r] = PR[q, cx - 1 + r, 8 : 8 + cy, :]
    for k in range(nq, 2 * nq):
        loads[k].wait()
    for q in range(nq):
        VYS[0, q] = VY_rows[across(q, 0)]
        VYS[1, q] = VY_rows[across(q, cy - 1)]
    start(v_copy, (2, 3))

    for k in range(2 * nq, 2 * nq + 3):
        loads[k].wait()

    def first_state(n, carry):
        rows = pl.ds(pl.multiple_of(n * 16, 16), 16)
        rest_now = A[rows, :]
        R[rows, :] = R[rows, :] * rest_now
        S[rows, :] = time_step * S[rows, :]
        A[rows, :] = inv_ln2 * (
            jnp.log((time_step * time_step) * (1.0 + 0.2 / rest_now))
            + exponent * jnp.log(rest_now)
        )
        return carry

    lax.fori_loop(0, SLOTS // 16, first_state, 0, unroll=4)
    for k in range(2 * nq + 3, 4 * nq + 3):
        loads[k].wait()

    def plan():
        wait_taken(meta_copy)
        came = (lane8 // DEP) % 4
        alab = jnp.where(
            came == 0, MR[0], jnp.where(came == 1, MR[1], jnp.where(came == 2, MR[2], MR[3]))
        )
        acode = code_of(alab.astype(jnp.int32))
        turn([acode, alab])
        LR[8:16, :] = acode
        hot_rows(SLOT_BLOCKS, 0)
        hot_columns(SLOT_BLOCKS, SLOT_BLOCKS + 1)
        AMSK[...] = jnp.broadcast_to(LT[:, 8:9], (LANES, LANES))
        INFO[0] = label.astype(f32)
        INFO[1] = leave_at.astype(f32)
        INFO[2] = alab

    def slope_z(tiles):
        height = tiles[0].shape[0]
        lane = lax.broadcasted_iota(jnp.int32, (height, LANES), 1)
        zero = jnp.zeros((height, LANES), f32)
        ahead = [pltpu.roll(v, LANES - 1, 1) for v in tiles] + [zero]
        behind = [zero] + [pltpu.roll(v, 1, 1) for v in tiles]
        return [
            jnp.where(lane == LANES - 1, ahead[q + 1], ahead[q])
            - jnp.where(lane == 0, behind[q], behind[q + 1])
            for q in range(nq)
        ]

    low_gate = jnp.where(has_lo, 1.0, 0.0).astype(f32)
    high_gate = jnp.where(has_hi, 1.0, 0.0).astype(f32)

    def halves(w):
        return slice(w * LANES, (w + 1) * LANES), slice(2 * w * LANES, 2 * (w + 1) * LANES)

    def gather(w, rows=slice(0, ROWS)):
        narrow, pair = halves(w)
        both = jnp.dot(OH[rows, :], PHL[:, pair], preferred_element_type=f32)
        PG[rows, narrow] = both[:, :LANES] + both[:, LANES:]

    def scatter(w, rows):
        narrow, pair = halves(w)
        both = jnp.dot(OHT[rows, :], VHL[:, pair], preferred_element_type=f32)
        SRC[rows, narrow] = both[:, :LANES] + both[:, LANES:]

    def leavers(t, to):
        for k in range(DEP):
            slot = jnp.maximum(slot_s[t, 0, 0, k], 0)
            cell = jnp.maximum(cells_s[slot], 0)
            place = cell >> 1
            row = pl.ds(slot, 1)
            DB[0, k : k + 1, :] = R[row, :]
            DB[1, k : k + 1, :] = S[row, :]
            DB[2, k : k + 1, :] = A[row, :]
            for w in range(2):
                DB[3, k : k + 1, halves(w)[0]] = PR[
                    2 * (cell & 1) + w,
                    (place >> (cy.bit_length() - 1)) + 1,
                    pl.ds(8 + (place & (cy - 1)), 1),
                    :,
                ]
        radius, speed, _ = wall_update(DB[0], DB[1], DB[2], DB[3])
        SB[to, 0] = radius
        SB[to, 1] = speed
        SB[to, 2] = DB[2]

    def take_arrivals(t):
        wait_taken(lambda d: dep_copy(t, d))
        rows = pl.ds(pl.multiple_of(t * 32, 32), 32)
        to = pl.ds(pl.multiple_of(SLOTS + t * 32, 32), 32)
        R[to, :] = AR[0, rows, :]
        S[to, :] = AR[1, rows, :]
        A[to, :] = AR[2, rows, :]
        MSK[to, :] = jnp.where(AMSK[rows, :] > 0.0, 2.0 * STEPS, -1.0)

    def step(t, carry):
        limit = t.astype(f32)

        def bubbles(first, w):
            rows = pl.ds(pl.multiple_of(first, 16), 16)
            col = halves(w)[0]
            radius, speed, rate = wall_update(R[rows, col], S[rows, col], A[rows, col], PG[rows, col])
            R[rows, col] = radius
            S[rows, col] = speed
            high, low = split(jnp.where(MSK[rows, :] >= limit, rate, 0.0))
            VHL[rows, 2 * w * LANES : (2 * w + 1) * LANES] = high
            VHL[rows, (2 * w + 1) * LANES : (2 * w + 2) * LANES] = low

        @pl.when(t > 0)
        def _():
            take_arrivals(t - 1)

        split_all()
        last = t // (STEPS - 1)
        leavers(t, t + last)
        def first_half(n, carry):
            gather(0, pl.ds(pl.multiple_of(n * (ROWS // 2), 16), ROWS // 2))
            return carry

        lax.fori_loop(0, 2, first_half, 0)

        @pl.when(last == 0)
        def _():
            start(lambda d: dep_copy(t, d))

        turns = 4
        many, few = ROWS // turns, ncol // turns

        def second_half(n, carry):
            gather(1, pl.ds(pl.multiple_of(n * many, 16), many))
            for first in range(0, many, 16):
                bubbles(n * many + first, 0)
            return carry

        lax.fori_loop(0, turns, second_half, 0)

        def first_sum(n, carry):
            scatter(0, pl.ds(pl.multiple_of(n * few, 16), few))
            for first in range(0, many, 16):
                bubbles(n * many + first, 1)
            return carry

        lax.fori_loop(0, turns, first_sum, 0)

        def flow_x(i):
            for q in range(nq):
                for jb in range(jbs):
                    rows, at = rows_of(jb)
                    VX[q, i + 1, rows, :] = VX[q, i + 1, rows, :] - half_gain * (
                        PR[q, i + 2, at, :] - PR[q, i, at, :]
                    )

        def flow_z(i, jb):
            rows, at = rows_of(jb)
            slopes = slope_z([PR[q, i + 1, at, :] for q in range(nq)])
            for q in range(nq):
                VZ[q, i, rows, :] = VZ[q, i, rows, :] - half_gain * slopes[q]

        def flow_y(i, jb):
            _, at = rows_of(jb)
            for q in range(nq):
                VY[q, i, at, :] = VY[q, i, at, :] - half_gain * (
                    PR[q, i + 1, pl.ds(9 + jb * 16 + zero_row, 16), :]
                    - PR[q, i + 1, pl.ds(7 + jb * 16 + zero_row, 16), :]
                )

        def pressure(m, k, jb):
            i = m * planes + k
            rows, at = rows_of(jb)
            slopes = slope_z([VZ[q, i, rows, :] for q in range(nq)])
            for q in range(nq):
                rise = (
                    slopes[q]
                    + (
                        VY[q, i, pl.ds(9 + jb * 16 + zero_row, 16), :]
                        - VY[q, i, pl.ds(7 + jb * 16 + zero_row, 16), :]
                    )
                    + (VX[q, i + 2, rows, :] - VX[q, i, rows, :])
                )
                col = (q % 2) * LANES
                added = SRC[pl.ds(column_row(m, k, q // 2, jb), 16), col : col + LANES]
                PR[q, i + 1, at, :] = PR[q, i + 1, at, :] - half_gain * rise + added

        def flows(m, carry):
            scatter(1, pl.ds(pl.multiple_of(m * part, 16), part))
            for k in range(planes):
                i = m * planes + k
                flow_x(i)
                for jb in range(jbs):
                    flow_z(i, jb)
                    flow_y(i, jb)
            return carry

        lax.fori_loop(0, groups, flows, 0)

        def pressures(m, carry):
            for k in range(planes):
                for jb in range(jbs):
                    pressure(m, k, jb)
            return carry

        lax.fori_loop(0, groups, pressures, 0)
        pack_rows(t + 1)

        pl.when(t == 0)(plan)
        wait_taken(lambda d: p_copy(t, d), (2, 3))

        @pl.when(t > 0)
        def _():
            wait_taken(lambda d: p_copy(t, d), (0, 1))

        @pl.when(t == 0)
        def _():
            for d in range(2):
                for copy in first_copies(d):
                    copy.wait_recv()
            wait_taken(v_copy, (2, 3))

        below, above = VYR[0], VYR[1]
        below = low_gate * (below - half_gain * (YS[t, 0, 0] - YR[t, 0, 0]))
        above = high_gate * (above - half_gain * (YR[t, 1, 1] - YS[t, 1, 1]))
        VYR[0] = below
        VYR[1] = above
        both_gains = half_gain * half_gain
        YS[t + 1, 0, 0] = YS[t + 1, 0, 0] + half_gain * below
        YS[t + 1, 0, 1] = YS[t + 1, 0, 1] + both_gains * YR[t, 0, 1]
        YS[t + 1, 1, 0] = YS[t + 1, 1, 0] + both_gains * YR[t, 1, 0]
        YS[t + 1, 1, 1] = YS[t + 1, 1, 1] - half_gain * above
        for q in range(nq):
            for jb in range(jbs):
                rows, at = rows_of(jb)
                far, near = XR[t, 0, q, 0, rows, :], XR[t, 0, q, 1, rows, :]
                beside = VXH[0, q, rows, :] - half_gain * (XS[t, 0, q, 0, rows, :] - far)
                VXH[0, q, rows, :] = beside
                VX[q, 1, rows, :] = VX[q, 1, rows, :] + half_gain * near
                first = PR[q, 1, at, :] + half_gain * beside
                second = PR[q, 2, at, :] + both_gains * near
                PR[q, 1, at, :] = first
                PR[q, 2, at, :] = second
                XS[t + 1, 0, q, 0, rows, :] = first
                XS[t + 1, 0, q, 1, rows, :] = second
                near, far = XR[t, 1, q, 0, rows, :], XR[t, 1, q, 1, rows, :]
                beside = VXH[1, q, rows, :] - half_gain * (far - XS[t, 1, q, 1, rows, :])
                VXH[1, q, rows, :] = beside
                VX[q, cx, rows, :] = VX[q, cx, rows, :] - half_gain * near
                first = PR[q, cx - 1, at, :] + both_gains * near
                second = PR[q, cx, at, :] - half_gain * beside
                PR[q, cx - 1, at, :] = first
                PR[q, cx, at, :] = second
                XS[t + 1, 1, q, 0, rows, :] = first
                XS[t + 1, 1, q, 1, rows, :] = second
        ends = ((0, 0, 0), (1, 0, 1), (cx - 2, 1, 0), (cx - 1, 1, 1))
        for i, x_side, x_row in ends:
            for side in range(2):
                for r in range(2):
                    for q in range(nq):
                        row = one(edges[side][r])
                        if i == 0:
                            part_x = half_gain * VXH[0, q, row, :]
                        elif i == 1:
                            part_x = both_gains * XR[t, 0, q, 1, row, :]
                        elif i == cx - 2:
                            part_x = both_gains * XR[t, 1, q, 0, row, :]
                        else:
                            part_x = -half_gain * VXH[1, q, row, :]
                        value = YS[t + 1, side, r, q, one(i), :] + part_x
                        YS[t + 1, side, r, q, one(i), :] = value
                        XS[t + 1, x_side, q, x_row, row, :] = value

        @pl.when(t < STEPS - 1)
        def _():
            start(lambda d: p_copy(t + 1, d))

        unpack_rows(t + 1)
        for q in range(nq):
            low, high = across(q, 0), across(q, cy - 1)
            VY_rows[low] = VY_rows[low] + half_gain * YR[t, 0, 1, q]
            VY_rows[high] = VY_rows[high] - half_gain * YR[t, 1, 0, q]

        @pl.when(t == STEPS - 2)
        def _():
            leavers(t + 1, t + 1)
            start(lambda d: dep_copy(t + 1, d))

        wait_sent(lambda d: dep_copy(t, d))

        @pl.when(t > 0)
        def _():
            wait_sent(lambda d: p_copy(t, d), (0, 1))

        wait_sent(lambda d: p_copy(t, d), (2, 3))

        return carry

    lax.fori_loop(0, STEPS, step, 0)

    take_arrivals(STEPS - 1)
    keep = AMSK[...] > 0.0
    for k, state in enumerate((R, S)):
        for w in range(2):
            high, low = split(jnp.where(keep, state[SLOTS:ROWS, halves(w)[0]], 0.0))
            to = slice(k * BLOCK + w * LANES, k * BLOCK + (w + 1) * LANES)
            CAT[0:ARRIVE, to] = high
            CAT[ARRIVE : 2 * ARRIVE, to] = low

    wait_sent(meta_copy)
    wait_sent(v_copy, (2, 3))
    for d in range(2):
        for copy in first_copies(d):
            copy.wait_send()


def write_out(
    p, vx, vy, vz, r, s, mask, cat, info, p_out, v_out, r_out, s_out, c_out, r_end, s_end, c_end, lt, sems
):
    _, cx, cy, nz = v_out.shape
    pairs = []
    for q in range(nz // LANES):
        lanes = pl.ds(q * LANES, LANES)
        pairs.append((vx.at[q, pl.ds(1, cx), :, :], v_out.at[0, :, :, lanes]))
        pairs.append((vy.at[q, :, pl.ds(8, cy), :], v_out.at[1, :, :, lanes]))
        pairs.append((vz.at[q], v_out.at[2, :, :, lanes]))
        pairs.append((p.at[q, pl.ds(1, cx), pl.ds(8, cy), :], p_out.at[:, :, lanes]))
    copies = [pltpu.make_async_copy(a, b, sems.at[k]) for k, (a, b) in enumerate(pairs)]
    for copy in copies:
        copy.start()

    lane8 = lax.broadcasted_iota(jnp.int32, (8, LANES), 1)
    sub8 = lax.broadcasted_iota(jnp.int32, (8, LANES), 0)
    lrow = lax.broadcasted_iota(jnp.int32, (LANES, LANES), 0)
    lcol = lax.broadcasted_iota(jnp.int32, (LANES, LANES), 1)
    label, leave_at, alab = info[0], info[1], info[2]
    present = alab > 0.0
    upper = jnp.where(lrow <= lcol, 1.0, 0.0)
    upper_block = jnp.where(lrow // 32 == lcol // 32, upper, 0.0).astype(bf16)
    upper = upper.astype(bf16)
    ones = jnp.ones((LANES, LANES), bf16)
    present_f = jnp.where(present, 1.0, 0.0)
    arank = jnp.dot(present_f.astype(bf16), upper_block, preferred_element_type=f32) - 1.0
    arank = jnp.where(present, arank, -5.0)
    vacant = label == 0.0
    ranks = []
    for t in range(STEPS):
        vacant = vacant | (leave_at == float(t))
        flag = jnp.where(vacant, 1.0, 0.0).astype(bf16)
        rank = jnp.dot(flag, upper, preferred_element_type=f32) - 1.0
        total = jnp.dot(flag, ones, preferred_element_type=f32)
        for k in range(SLOT_BLOCKS - 1):
            rank = rank + jnp.where(sub8 > k, total[k : k + 1, :], 0.0)
        ranks.append(jnp.where(vacant, rank, -1.0))
        count = jnp.sum(jnp.where(lane8 // 32 == t, present_f, 0.0), axis=1, keepdims=True)
        vacant = vacant & (rank >= count)
    lt[...] = jnp.concatenate(ranks + [jnp.zeros((LANES - 8 * STEPS, LANES), f32)], axis=0).T

    group = lcol // 32
    alab_high, alab_low = split(alab)
    final = jnp.where(leave_at == float(STEPS), label, 0.0)
    nt = (((1,), (1,)), ((), ()))
    for k in range(SLOT_BLOCKS):
        rows = slice(k * LANES, (k + 1) * LANES)
        mine = jnp.broadcast_to(lt[:, k : k + 1], (LANES, LANES))
        for t in range(1, STEPS):
            mine = jnp.where(group == t, lt[:, 8 * t + k : 8 * t + k + 1], mine)
        hot = jnp.where(mine == arank[0:1, :], 1.0, 0.0).astype(bf16)
        there = lax.dot_general(alab_high, hot, nt, preferred_element_type=f32)
        there = there + lax.dot_general(alab_low, hot, nt, preferred_element_type=f32)
        final = final + jnp.where(sub8 == k, there, 0.0)
        both = jnp.concatenate([hot, hot], axis=1)
        placed = jnp.dot(both, cat[...], preferred_element_type=f32)
        keep = mask[rows, :]
        keep = jnp.concatenate([keep, keep], axis=1) >= float(STEPS)
        r_end[rows, :] = jnp.where(keep, r[rows, :], 0.0) + placed[:, :BLOCK]
        s_end[rows, :] = (1.0 / time_step) * (jnp.where(keep, s[rows, :], 0.0) + placed[:, BLOCK:])
        if k % 4 == 3:
            rows_of = pl.ds((k - 3) * LANES, 4 * LANES)
            for a, b in ((r_end, r_out), (s_end, s_out)):
                copy = pltpu.make_async_copy(a.at[rows_of, :], b.at[rows_of, :], sems.at[len(copies)])
                copy.start()
                copies.append(copy)
    c_end[...] = final.astype(jnp.int32) - 1
    copy = pltpu.make_async_copy(c_end, c_out, sems.at[len(copies)])
    copy.start()
    copies.append(copy)
    for copy in copies:
        copy.wait()


def on_device(
    pressure, velocity, stretch, rest_radius, wall_speed, block_cells, depart_slot, depart_way
):
    cx, cy, nz = pressure.shape
    nq = nz // LANES
    ncol = 2 * cx * cy
    vmem = pl.BlockSpec(memory_space=pltpu.VMEM)
    hbm = pl.BlockSpec(memory_space=pl.ANY)
    dma = pltpu.SemaphoreType.DMA
    vmem_out = pltpu.VMEM
    parts = pl.pallas_call(
        kernel,
        out_shape=(
            vmem_out((nq, cx + 2, cy + 16, LANES), f32),
            vmem_out((nq, cx + 2, cy, LANES), f32),
            vmem_out((nq, cx, cy + 16, LANES), f32),
            vmem_out((nq, cx, cy, LANES), f32),
            vmem_out((ROWS, BLOCK), f32),
            vmem_out((ROWS, BLOCK), f32),
            vmem_out((ROWS, LANES), f32),
            vmem_out((2 * ARRIVE, 2 * BLOCK), bf16),
            vmem_out((3, SLOT_BLOCKS, LANES), f32),
        ),
        in_specs=[pl.BlockSpec(memory_space=pltpu.HBM)] * 9,
        out_specs=(vmem,) * 9,
        scratch_shapes=[
            pltpu.VMEM((ROWS, BLOCK), f32),
            pltpu.VMEM((3, ARRIVE, BLOCK), f32),
            pltpu.VMEM((STEPS + 1, 3, DEP, BLOCK), f32),
            pltpu.VMEM((4, DEP, BLOCK), f32),
            pltpu.VMEM((ROWS, ncol), bf16),
            pltpu.VMEM((ncol, ROWS), bf16),
            pltpu.VMEM((ncol, 2 * BLOCK), bf16),
            pltpu.VMEM((ROWS, BLOCK), f32),
            pltpu.VMEM((ROWS, 2 * BLOCK), bf16),
            pltpu.VMEM((ncol, BLOCK), f32),
            pltpu.VMEM((2, nq, cy, LANES), f32),
            pltpu.VMEM((STEPS + 1, 2, nq, 2, cy, LANES), f32),
            pltpu.VMEM((STEPS, 2, nq, 2, cy, LANES), f32),
            pltpu.VMEM((STEPS + 1, 2, 2, nq, cx, LANES), f32),
            pltpu.VMEM((STEPS, 2, 2, nq, cx, LANES), f32),
            pltpu.VMEM((2, nq, cx, LANES), f32),
            pltpu.VMEM((2, nq, cx, LANES), f32),
            pltpu.VMEM((8, LANES), f32),
            pltpu.VMEM((4, 8, LANES), f32),
            pltpu.VMEM((ARRIVE, LANES), f32),
            pltpu.VMEM((LANES, LANES), f32),
            pltpu.VMEM((16, LANES), f32),
            pltpu.SMEM((SLOTS,), jnp.int32),
            pltpu.SMEM((STEPS, 1, 1, DEP), jnp.int32),
            pltpu.SMEM((STEPS, 1, 1, DEP), jnp.int32),
            pltpu.VMEM((SLOT_BLOCKS, LANES), jnp.int32),
            dma((4 * nq + 7,)),
            dma((4,)),
            dma((4,)),
            dma((STEPS, 4)),
            dma((STEPS, 4)),
            dma((4,)),
            dma((4,)),
            dma((STEPS, 4)),
            dma((STEPS, 4)),
            dma((2, 2, nq)),
            dma((2, 2, nq)),
        ],
        compiler_params=pltpu.CompilerParams(
            collective_id=0, has_side_effects=True, vmem_limit_bytes=36 * 2**20
        ),
        cost_estimate=pl.CostEstimate(
            flops=10 * 2**30, bytes_accessed=13 * 2**20, transcendentals=2**22
        ),
    )(
        *(
            pltpu.with_memory_space_constraint(value, pltpu.HBM)
            for value in (
                block_cells,
                depart_slot,
                depart_way,
                block_cells.reshape(SLOT_BLOCKS, LANES),
                pressure,
                velocity,
                stretch,
                rest_radius,
                wall_speed,
            )
        )
    )
    parts = [pltpu.with_memory_space_constraint(part, pltpu.VMEM) for part in parts]
    p, v, r, s, c = pl.pallas_call(
        write_out,
        out_shape=(
            jax.ShapeDtypeStruct(pressure.shape, f32),
            jax.ShapeDtypeStruct(velocity.shape, f32),
            jax.ShapeDtypeStruct(stretch.shape, f32),
            jax.ShapeDtypeStruct(stretch.shape, f32),
            jax.ShapeDtypeStruct((SLOT_BLOCKS, LANES), jnp.int32),
        ),
        in_specs=[vmem] * 9,
        out_specs=(hbm,) * 5,
        scratch_shapes=[
            pltpu.VMEM((SLOTS, BLOCK), f32),
            pltpu.VMEM((SLOTS, BLOCK), f32),
            pltpu.VMEM((SLOT_BLOCKS, LANES), jnp.int32),
            pltpu.VMEM((LANES, LANES), f32),
            dma((4 * nq + 5,)),
        ],
        compiler_params=pltpu.CompilerParams(vmem_limit_bytes=8 * 2**20),
        cost_estimate=pl.CostEstimate(flops=0, bytes_accessed=13 * 2**20, transcendentals=0),
    )(*parts)
    return p, v, r, s, c.reshape(-1)


def solution(mesh):
    placed = (
        P("gx", "gy", None),
        P(None, "gx", "gy", None),
        P(("gx", "gy"), None),
        P(("gx", "gy"), None),
        P(("gx", "gy"), None),
        P(("gx", "gy")),
        P(None, "gx", "gy", None),
        P(None, "gx", "gy", None),
    )
    return jax.shard_map(
        on_device,
        mesh=mesh,
        in_specs=placed,
        out_specs=(
            P("gx", "gy", None),
            P(None, "gx", "gy", None),
            P(("gx", "gy"), None),
            P(("gx", "gy"), None),
            P(("gx", "gy")),
        ),
        check_vma=False,
    )
```

```python
import functools
import math

import jax
import jax.numpy as jnp
from jax import lax
from jax.experimental import pallas as pl
from jax.experimental.pallas import tpu as pltpu
from jax.sharding import PartitionSpec as P

MESH = pl.DeviceIdType.MESH
f32 = jnp.float32
bf16 = jnp.bfloat16

STEPS = 4
DEP = 8
SLOTS = 1024
BLOCK = 256
LANES = 128
ARRIVE = STEPS * 4 * DEP
ROWS = SLOTS + ARRIVE
SLOT_BLOCKS = SLOTS // LANES
WAY_OF = (1, 0, 3, 2)

time_step = 0.04
half_gain = 0.2
source_scale = 0.004 * 12.566370614359172
exponent = 4.2
inv_ln2 = 1.0 / math.log(2.0)


def split(value):
    high = value.astype(bf16)
    return high, (value - high.astype(f32)).astype(bf16)


def wall_update(radius, shift, level, pressure):
    mach = (0.05 / time_step) * shift
    one_less = 1.0 - mach
    divisor = one_less * radius
    inverse = pl.reciprocal(divisor, approx=True)
    inverse = inverse * (2.0 - divisor * inverse)
    inv_radius = inverse * one_less
    wall = jnp.exp2(level - (exponent * inv_ln2) * jnp.log(radius))
    squared = time_step * time_step
    excess = (
        wall
        - (0.2 * squared + (0.08 * time_step) * shift) * inv_radius
        - (squared + squared * pressure)
    )
    driving = (1.0 + mach) * excess - (1.5 - 0.5 * mach) * (shift * shift)
    shift = shift + driving * inverse
    radius = radius + shift
    return radius, shift, (source_scale / time_step) * (radius * radius) * shift


def kernel(
    cells_h, slot_h, way_h, cells_b, press, vel, stretch, rest, speed0,
    PR, VX, VY, VZ, R, S, MSK, CAT, INFO,
    A, AR, SB, DB, OH, OHT, PHL, PG, VHL, SRC, XS, XR, YS, YR, VYS, VYR,
    MT, MR, AMSK, LT, LR, cells_s, slot_s, way_s, cells_v,
    in_sem, meta_s, meta_r, xs, xr, vs, vr, ds_, dr, fs, fr,
):
    _, cx, cy, nz = vel.shape
    nq = nz // LANES
    half = cx * cy
    ncol = 2 * half
    jbs = cy // 16
    part = min(256, ncol)
    planes = part // (2 * cy)
    groups = cx // planes
    shift = (planes * cy).bit_length() - 1
    zero_row = lax.axis_index("gx") // 4096
    gx, gy = lax.axis_index("gx"), lax.axis_index("gy")
    ngx, ngy = lax.axis_size("gx"), lax.axis_size("gy")
    has_lo, has_hi = gy > 0, gy < ngy - 1
    targets = (
        (lax.rem(gx + 1, ngx), gy),
        (lax.rem(gx + ngx - 1, ngx), gy),
        (gx, lax.rem(gy + 1, ngy)),
        (gx, lax.rem(gy + ngy - 1, ngy)),
    )
    sends = (None, None, has_hi, has_lo)
    takes = (None, None, has_lo, has_hi)

    def under(flag, action):
        if flag is None:
            action()
        else:
            pl.when(flag)(action)

    barrier = pltpu.get_barrier_semaphore()
    for d in range(4):
        under(
            sends[d],
            lambda d=d: pl.semaphore_signal(
                barrier, inc=1, device_id=targets[d], device_id_type=MESH
            ),
        )

    inputs = [(cells_h, cells_s), (slot_h, slot_s), (way_h, way_s), (cells_b, cells_v)]
    for q in range(nq):
        inputs.append((press.at[:, :, pl.ds(q * LANES, LANES)], PR.at[q, :, pl.ds(8, cy), :]))
    for q in range(nq):
        lanes = pl.ds(q * LANES, LANES)
        inputs.append((vel.at[1, :, :, lanes], VY.at[q, :, pl.ds(8, cy), :]))
    own = pl.ds(0, SLOTS)
    inputs.append((rest, A.at[own, :]))
    inputs.append((stretch, R.at[own, :]))
    inputs.append((speed0, S.at[own, :]))
    for q in range(nq):
        lanes = pl.ds(q * LANES, LANES)
        inputs.append((vel.at[0, :, :, lanes], VX.at[q, pl.ds(1, cx), :, :]))
        inputs.append((vel.at[2, :, :, lanes], VZ.at[q]))
    loads = [pltpu.make_async_copy(a, b, in_sem.at[k]) for k, (a, b) in enumerate(inputs)]
    for load in loads:
        load.start()
    small_loads, loads = loads[:4], loads[4:]

    @pl.when(jnp.logical_not(has_lo))
    def _():
        MR[2] = jnp.zeros((8, LANES), f32)
        YR[:, 0] = jnp.zeros(YR.shape[:1] + YR.shape[2:], f32)
        VYR[0] = jnp.zeros(VYR.shape[1:], f32)

    @pl.when(jnp.logical_not(has_hi))
    def _():
        MR[3] = jnp.zeros((8, LANES), f32)
        YR[:, 1] = jnp.zeros(YR.shape[:1] + YR.shape[2:], f32)
        VYR[1] = jnp.zeros(VYR.shape[1:], f32)

    edge_rows = jnp.zeros((nq, cx, 8, LANES), f32)
    PR[:, :, 0:8, :] = edge_rows
    PR[:, :, 8 + cy : 16 + cy, :] = edge_rows
    VY[:, :, 0:8, :] = edge_rows
    VY[:, :, 8 + cy : 16 + cy, :] = edge_rows
    empty = jnp.zeros((ARRIVE, BLOCK), f32)
    R[SLOTS:ROWS, :] = empty + 1.0
    S[SLOTS:ROWS, :] = empty
    A[SLOTS:ROWS, :] = empty
    MSK[SLOTS:ROWS, :] = jnp.full((ARRIVE, LANES), -1.0, f32)
    OHT[:, SLOTS:ROWS] = jnp.zeros((ncol, ARRIVE), bf16)
    VHL[SLOTS:ROWS, :] = jnp.zeros((ARRIVE, 2 * BLOCK), bf16)
    OH[SLOTS:ROWS, :] = jnp.zeros((ARRIVE, ncol), bf16)
    pl.semaphore_wait(barrier, 2 + has_lo.astype(jnp.int32) + has_hi.astype(jnp.int32))

    def remote(src, dst, send_sem, recv_sem, d):
        return pltpu.make_async_remote_copy(
            src_ref=src, dst_ref=dst, send_sem=send_sem, recv_sem=recv_sem,
            device_id=targets[d], device_id_type=MESH,
        )

    def meta_copy(d):
        return [remote(MT, MR.at[d], meta_s.at[d], meta_r.at[d], d)]

    def p_copy(t, d):
        if d < 2:
            src, dst = XS.at[t, 1 - d], XR.at[t, d]
        else:
            src, dst = YS.at[t, 3 - d], YR.at[t, d - 2]
        return [remote(src, dst, xs.at[t, d], xr.at[t, d], d)]

    def first_copies(d):
        side = (cx - 2, 0)[d]
        for q in range(nq):
            lanes = pl.ds(q * LANES, LANES)
            yield remote(
                press.at[pl.ds(side, 2), :, lanes], XR.at[0, d, q], fs.at[0, d, q], fr.at[0, d, q], d
            )
        for q in range(nq):
            lanes = pl.ds(q * LANES, LANES)
            yield remote(
                vel.at[0, pl.ds((cx - 1, 0)[d], 1), :, lanes],
                VX.at[q, pl.ds((0, cx + 1)[d], 1), :, :],
                fs.at[1, d, q],
                fr.at[1, d, q],
                d,
            )

    def v_copy(d):
        return [remote(VYS.at[3 - d], VYR.at[d - 2], vs.at[d], vr.at[d], d)]

    def dep_copy(t, d):
        to = AR.at[:, pl.ds(t * 32 + d * DEP, DEP), :]
        return [remote(SB.at[t], to, ds_.at[t, d], dr.at[t, d], d)]

    odd = lax.rem(gy, 2) == 1
    even = jnp.logical_not(odd)
    far_hi, near_hi = has_hi & odd, has_hi & even
    far_lo, near_lo = has_lo & even, has_lo & odd

    def start(make, ways=(0, 1, 2, 3)):
        order = ((far_hi, 2), (far_lo, 3), (None, 0), (None, 1), (near_hi, 2), (near_lo, 3))
        for flag, d in order:
            if d in ways:
                under(flag, lambda d=d: [copy.start() for copy in make(d)] and None)

    def wait_sent(make, ways=(0, 1, 2, 3)):
        for d in ways:
            under(sends[d], lambda d=d: [copy.wait_send() for copy in make(d)] and None)

    def wait_taken(make, ways=(0, 1, 2, 3)):
        for d in ways:
            under(takes[d], lambda d=d: [copy.wait_recv() for copy in make(d)] and None)

    for d in range(2):
        for copy in first_copies(d):
            copy.start()
    edges = ((0, 1), (cy - 2, cy - 1))

    def one(row):
        return pl.ds(row + zero_row, 1)

    pitch = cy + 16
    PR_rows = PR.reshape(nq * cx * pitch, LANES)
    VY_rows = VY.reshape(nq * cx * pitch, LANES)

    def across(q, row):
        return pl.ds(q * cx * pitch + 8 + row, cx, stride=pitch), slice(None)

    def pack_rows(t):
        for side in range(2):
            for r in range(2):
                for q in range(nq):
                    YS[t, side, r, q] = PR_rows[across(q, edges[side][r])]

    def unpack_rows(t):
        for side in range(2):
            for r in range(2):
                for q in range(nq):
                    PR_rows[across(q, edges[side][r])] = YS[t, side, r, q]

    def column_row(i, h, jb):
        return (i // planes) * part + (h * planes + i % planes) * cy + jb * 16

    def keep_parts(i, jb, q, value):
        high, low = split(value)
        row = column_row(i, q // 2, jb)
        col = (q % 2) * 2 * LANES
        PHL[row : row + 16, col : col + LANES] = high
        PHL[row : row + 16, col + LANES : col + 2 * LANES] = low

    def rows_of(jb):
        return slice(jb * 16, jb * 16 + 16), slice(8 + jb * 16, 24 + jb * 16)

    def split_all():
        for i in range(cx):
            for jb in range(jbs):
                for q in range(nq):
                    keep_parts(i, jb, q, PR[q, i, rows_of(jb)[1], :])

    for load in small_loads:
        load.wait()

    lane8 = lax.broadcasted_iota(jnp.int32, (8, LANES), 1)
    sub8 = lax.broadcasted_iota(jnp.int32, (8, LANES), 0)
    slot_id = sub8 * LANES + lane8
    label = cells_v[...] + 1
    leave_at = jnp.where(label > 0, STEPS, -1)
    entry_of = (lane8 // 32) * DEP + lane8 % DEP
    wanted = (lane8 // DEP) % 4
    wanted = jnp.where(wanted < 2, 1 - wanted, 5 - wanted)
    meta = jnp.zeros((8, LANES), jnp.int32)
    for e in range(STEPS * DEP):
        slot = slot_s[e // DEP, 0, 0, e % DEP]
        moved = jnp.where(slot >= 0, cells_s[jnp.maximum(slot, 0)] + 1, 0)
        meta = jnp.where((entry_of == e) & (wanted == way_s[e // DEP, 0, 0, e % DEP]), moved, meta)
        leave_at = jnp.where(slot_id == slot, e // DEP, leave_at)
    MT[...] = meta.astype(f32)

    start(meta_copy)

    lrow = lax.broadcasted_iota(jnp.int32, (LANES, LANES), 0)
    lcol = lax.broadcasted_iota(jnp.int32, (LANES, LANES), 1)
    wide = lax.broadcasted_iota(jnp.int32, (16, ncol), 1).astype(f32)

    def code_of(lab):
        cell = lab - 1
        place = cell >> 1
        row = (place >> shift) * part + (cell & 1) * (planes * cy)
        return jnp.where(lab > 0, row + (place & (planes * cy - 1)), -1).astype(f32)

    def turn(stack):
        stack = stack + [jnp.zeros((8, LANES), f32)] * (16 - len(stack))
        LT[...] = jnp.concatenate(stack, axis=0).T

    def hot_rows(r, at):
        def body(m, carry):
            rows = pl.ds(pl.multiple_of(m * 16, 16), 16)
            hot = jnp.where(LT[rows, at : at + 1] == wide, 1.0, 0.0).astype(bf16)
            OH[pl.ds(pl.multiple_of(r * LANES + m * 16, 16), 16), :] = hot
            return carry

        lax.fori_loop(0, LANES // 16, body, 0, unroll=4)

    def hot_columns(first, last):
        def body(m, carry):
            ident = (lrow + m * LANES).astype(f32)
            rows = pl.ds(pl.multiple_of(m * LANES, LANES), LANES)
            for r in range(first, last):
                hot = jnp.where(ident == LR[r : r + 1, :], 1.0, 0.0).astype(bf16)
                OHT[rows, r * LANES : (r + 1) * LANES] = hot
            return carry

        lax.fori_loop(0, ncol // LANES, body, 0)

    code = code_of(label)
    turn([code, leave_at.astype(f32)])
    LR[0:8, :] = code
    for r in range(SLOT_BLOCKS):
        hot_rows(r, r)
    for r in range(SLOT_BLOCKS):
        MSK[r * LANES : (r + 1) * LANES, :] = jnp.broadcast_to(
            LT[:, 8 + r : 9 + r], (LANES, LANES)
        )
    hot_columns(0, SLOT_BLOCKS)

    for k in range(nq):
        loads[k].wait()
    pack_rows(0)
    start(lambda d: p_copy(0, d), (2, 3))
    for q in range(nq):
        for r in range(2):
            XS[0, 0, q, r] = PR[q, r, 8 : 8 + cy, :]
            XS[0, 1, q, r] = PR[q, cx - 2 + r, 8 : 8 + cy, :]
    for k in range(nq, 2 * nq):
        loads[k].wait()
    for q in range(nq):
        VYS[0, q] = VY_rows[across(q, 0)]
        VYS[1, q] = VY_rows[across(q, cy - 1)]
    start(v_copy, (2, 3))

    for k in range(2 * nq, 2 * nq + 3):
        loads[k].wait()

    def first_state(n, carry):
        rows = pl.ds(pl.multiple_of(n * 16, 16), 16)
        rest_now = A[rows, :]
        R[rows, :] = R[rows, :] * rest_now
        S[rows, :] = time_step * S[rows, :]
        A[rows, :] = inv_ln2 * (
            jnp.log((time_step * time_step) * (1.0 + 0.2 / rest_now))
            + exponent * jnp.log(rest_now)
        )
        return carry

    lax.fori_loop(0, SLOTS // 16, first_state, 0, unroll=4)
    for k in range(2 * nq + 3, 4 * nq + 3):
        loads[k].wait()

    def plan():
        wait_taken(meta_copy)
        came = (lane8 // DEP) % 4
        alab = jnp.where(
            came == 0, MR[0], jnp.where(came == 1, MR[1], jnp.where(came == 2, MR[2], MR[3]))
        )
        acode = code_of(alab.astype(jnp.int32))
        turn([acode, alab])
        LR[8:16, :] = acode
        hot_rows(SLOT_BLOCKS, 0)
        hot_columns(SLOT_BLOCKS, SLOT_BLOCKS + 1)
        AMSK[...] = jnp.broadcast_to(LT[:, 8:9], (LANES, LANES))
        INFO[0] = label.astype(f32)
        INFO[1] = leave_at.astype(f32)
        INFO[2] = alab

    def slope_z(tiles):
        height = tiles[0].shape[0]
        lane = lax.broadcasted_iota(jnp.int32, (height, LANES), 1)
        zero = jnp.zeros((height, LANES), f32)
        ahead = [pltpu.roll(v, LANES - 1, 1) for v in tiles] + [zero]
        behind = [zero] + [pltpu.roll(v, 1, 1) for v in tiles]
        return [
            jnp.where(lane == LANES - 1, ahead[q + 1], ahead[q])
            - jnp.where(lane == 0, behind[q], behind[q + 1])
            for q in range(nq)
        ]

    low_gate = jnp.where(has_lo, 1.0, 0.0).astype(f32)
    high_gate = jnp.where(has_hi, 1.0, 0.0).astype(f32)

    def halves(w):
        return slice(w * LANES, (w + 1) * LANES), slice(2 * w * LANES, 2 * (w + 1) * LANES)

    def gather(w, rows=slice(0, ROWS)):
        narrow, pair = halves(w)
        both = jnp.dot(OH[rows, :], PHL[:, pair], preferred_element_type=f32)
        PG[rows, narrow] = both[:, :LANES] + both[:, LANES:]

    def scatter(w, rows, count):
        narrow, pair = halves(w)
        both = jnp.dot(OHT[rows, :count], VHL[:count, pair], preferred_element_type=f32)
        SRC[rows, narrow] = both[:, :LANES] + both[:, LANES:]

    def leavers(t, to):
        for k in range(DEP):
            slot = jnp.maximum(slot_s[t, 0, 0, k], 0)
            cell = jnp.maximum(cells_s[slot], 0)
            place = cell >> 1
            row = pl.ds(slot, 1)
            DB[0, k : k + 1, :] = R[row, :]
            DB[1, k : k + 1, :] = S[row, :]
            DB[2, k : k + 1, :] = A[row, :]
            for w in range(2):
                DB[3, k : k + 1, halves(w)[0]] = PR[
                    2 * (cell & 1) + w,
                    place >> (cy.bit_length() - 1),
                    pl.ds(8 + (place & (cy - 1)), 1),
                    :,
                ]
        radius, speed, _ = wall_update(DB[0], DB[1], DB[2], DB[3])
        SB[to, 0] = radius
        SB[to, 1] = speed
        SB[to, 2] = DB[2]

    def take_arrivals(t):
        wait_taken(lambda d: dep_copy(t, d))
        rows, to = slice(t * 32, t * 32 + 32), slice(SLOTS + t * 32, SLOTS + t * 32 + 32)
        R[to, :] = AR[0, rows, :]
        S[to, :] = AR[1, rows, :]
        A[to, :] = AR[2, rows, :]
        MSK[to, :] = jnp.where(AMSK[rows, :] > 0.0, 2.0 * STEPS, -1.0)

    def when(flag):
        return lambda action: action() if flag else None

    def step(t):
        limit = float(t)
        live = SLOTS + 32 * t
        final = t == STEPS - 1

        def bubbles(first, w):
            rows = slice(first, first + 16)
            col = halves(w)[0]
            radius, speed, rate = wall_update(R[rows, col], S[rows, col], A[rows, col], PG[rows, col])
            R[rows, col] = radius
            S[rows, col] = speed
            high, low = split(jnp.where(MSK[rows, :] >= limit, rate, 0.0))
            VHL[rows, 2 * w * LANES : (2 * w + 1) * LANES] = high
            VHL[rows, (2 * w + 1) * LANES : (2 * w + 2) * LANES] = low

        @when(t > 0)
        def _():
            take_arrivals(t - 1)

        split_all()
        last = t // (STEPS - 1)
        if not final:
            leavers(t, t)
        gather(0, slice(0, live))

        @when(last == 0)
        def _():
            start(lambda d: dep_copy(t, d))

        def pieces(count, size):
            ends = [k * size // count // 16 * 16 for k in range(count)] + [size]
            return [slice(ends[k], ends[k + 1]) for k in range(count)]

        for rows in pieces(2, live):
            gather(1, rows)
            for first in range(rows.start, rows.stop, 16):
                bubbles(first, 0)
        for rows, part_rows in zip(pieces(2, ncol), pieces(2, live)):
            scatter(0, rows, SLOTS if t == 0 else ROWS)
            for first in range(part_rows.start, part_rows.stop, 16):
                bubbles(first, 1)

        def flow_x(i):
            for q in range(nq):
                for jb in range(jbs):
                    rows, at = rows_of(jb)
                    flow = VX[q, i + 1, rows, :]
                    if i == 0:
                        flow = flow - half_gain * PR[q, 1, at, :]
                    elif i == cx - 1:
                        flow = flow + half_gain * PR[q, cx - 2, at, :]
                    else:
                        flow = flow - half_gain * (PR[q, i + 1, at, :] - PR[q, i - 1, at, :])
                    VX[q, i + 1, rows, :] = flow

        def flow_z(i, jb):
            rows, at = rows_of(jb)
            slopes = slope_z([PR[q, i, at, :] for q in range(nq)])
            for q in range(nq):
                VZ[q, i, rows, :] = VZ[q, i, rows, :] - half_gain * slopes[q]

        def flow_y(i, jb):
            _, at = rows_of(jb)
            for q in range(nq):
                VY[q, i, at, :] = VY[q, i, at, :] - half_gain * (
                    PR[q, i, pl.ds(9 + jb * 16 + zero_row, 16), :]
                    - PR[q, i, pl.ds(7 + jb * 16 + zero_row, 16), :]
                )

        def pressure(i, jb):
            rows, at = rows_of(jb)
            slopes = slope_z([VZ[q, i, rows, :] for q in range(nq)])
            for q in range(nq):
                rise = slopes[q] + (
                    VY[q, i, pl.ds(9 + jb * 16 + zero_row, 16), :]
                    - VY[q, i, pl.ds(7 + jb * 16 + zero_row, 16), :]
                )
                if i + 1 < cx:
                    rise = rise + VX[q, i + 2, rows, :]
                if i > 0:
                    rise = rise - VX[q, i, rows, :]
                row = column_row(i, q // 2, jb)
                col = (q % 2) * LANES
                PR[q, i, at, :] = (
                    PR[q, i, at, :] - half_gain * rise + SRC[row : row + 16, col : col + LANES]
                )

        for rows, part_planes in zip(pieces(2, ncol), pieces(2, cx)):
            scatter(1, rows, SLOTS if t == 0 else ROWS)
            for i in range(part_planes.start, part_planes.stop):
                flow_x(i)
                for jb in range(jbs):
                    flow_z(i, jb)
                    flow_y(i, jb)
        for i in range(cx):
            for jb in range(jbs):
                pressure(i, jb)
        pack_rows(t + 1)

        when(t == 0)(plan)
        wait_taken(lambda d: p_copy(t, d), (2, 3))

        @when(t > 0)
        def _():
            wait_taken(lambda d: p_copy(t, d), (0, 1))

        @when(t == 0)
        def _():
            for d in range(2):
                for copy in first_copies(d):
                    copy.wait_recv()
            wait_taken(v_copy, (2, 3))

        below, above = VYR[0], VYR[1]
        below = low_gate * (below - half_gain * (YS[t, 0, 0] - YR[t, 0, 0]))
        above = high_gate * (above - half_gain * (YR[t, 1, 1] - YS[t, 1, 1]))
        VYR[0] = below
        VYR[1] = above
        both_gains = half_gain * half_gain
        YS[t + 1, 0, 0] = YS[t + 1, 0, 0] + half_gain * below
        YS[t + 1, 0, 1] = YS[t + 1, 0, 1] + both_gains * YR[t, 0, 1]
        YS[t + 1, 1, 0] = YS[t + 1, 1, 0] + both_gains * YR[t, 1, 0]
        YS[t + 1, 1, 1] = YS[t + 1, 1, 1] - half_gain * above
        for q in range(nq):
            for jb in range(jbs):
                rows, at = rows_of(jb)
                far, near = XR[t, 0, q, 0, rows, :], XR[t, 0, q, 1, rows, :]
                beside = VX[q, 0, rows, :] - half_gain * (XS[t, 0, q, 0, rows, :] - far)
                VX[q, 0, rows, :] = beside
                VX[q, 1, rows, :] = VX[q, 1, rows, :] + half_gain * near
                first = PR[q, 0, at, :] + half_gain * beside
                second = PR[q, 1, at, :] + both_gains * near
                PR[q, 0, at, :] = first
                PR[q, 1, at, :] = second
                if not final:
                    XS[t + 1, 0, q, 0, rows, :] = first
                if not final:
                    XS[t + 1, 0, q, 1, rows, :] = second
                near, far = XR[t, 1, q, 0, rows, :], XR[t, 1, q, 1, rows, :]
                beside = VX[q, cx + 1, rows, :] - half_gain * (far - XS[t, 1, q, 1, rows, :])
                VX[q, cx + 1, rows, :] = beside
                VX[q, cx, rows, :] = VX[q, cx, rows, :] - half_gain * near
                first = PR[q, cx - 2, at, :] + both_gains * near
                second = PR[q, cx - 1, at, :] - half_gain * beside
                PR[q, cx - 2, at, :] = first
                PR[q, cx - 1, at, :] = second
                if not final:
                    XS[t + 1, 1, q, 0, rows, :] = first
                if not final:
                    XS[t + 1, 1, q, 1, rows, :] = second
        ends = ((0, 0, 0), (1, 0, 1), (cx - 2, 1, 0), (cx - 1, 1, 1))
        for i, x_side, x_row in ends:
            for side in range(2):
                for r in range(2):
                    for q in range(nq):
                        row = one(edges[side][r])
                        if i == 0:
                            part_x = half_gain * VX[q, 0, row, :]
                        elif i == 1:
                            part_x = both_gains * XR[t, 0, q, 1, row, :]
                        elif i == cx - 2:
                            part_x = both_gains * XR[t, 1, q, 0, row, :]
                        else:
                            part_x = -half_gain * VX[q, cx + 1, row, :]
                        value = YS[t + 1, side, r, q, one(i), :] + part_x
                        YS[t + 1, side, r, q, one(i), :] = value
                        if not final:
                            XS[t + 1, x_side, q, x_row, row, :] = value

        @when(t < STEPS - 1)
        def _():
            start(lambda d: p_copy(t + 1, d))

        unpack_rows(t + 1)
        for q in range(nq):
            low, high = across(q, 0), across(q, cy - 1)
            VY_rows[low] = VY_rows[low] + half_gain * YR[t, 0, 1, q]
            VY_rows[high] = VY_rows[high] - half_gain * YR[t, 1, 0, q]

        @when(t == STEPS - 2)
        def _():
            leavers(t + 1, t + 1)
            start(lambda d: dep_copy(t + 1, d))

        wait_sent(lambda d: dep_copy(t, d))

        @when(t > 0)
        def _():
            wait_sent(lambda d: p_copy(t, d), (0, 1))

        wait_sent(lambda d: p_copy(t, d), (2, 3))

    for t in range(STEPS):
        step(t)

    take_arrivals(STEPS - 1)
    keep = AMSK[...] > 0.0
    for k, state in enumerate((R, S)):
        for w in range(2):
            high, low = split(jnp.where(keep, state[SLOTS:ROWS, halves(w)[0]], 0.0))
            to = slice(k * BLOCK + w * LANES, k * BLOCK + (w + 1) * LANES)
            CAT[0:ARRIVE, to] = high
            CAT[ARRIVE : 2 * ARRIVE, to] = low

    wait_sent(meta_copy)
    wait_sent(v_copy, (2, 3))
    for d in range(2):
        for copy in first_copies(d):
            copy.wait_send()


def write_out(
    p, vx, vy, vz, r, s, mask, cat, info, p_out, v_out, r_out, s_out, c_out, r_end, s_end, c_end, lt, sems
):
    _, cx, cy, nz = v_out.shape
    pairs = []
    for q in range(nz // LANES):
        lanes = pl.ds(q * LANES, LANES)
        pairs.append((vx.at[q, pl.ds(1, cx), :, :], v_out.at[0, :, :, lanes]))
        pairs.append((vy.at[q, :, pl.ds(8, cy), :], v_out.at[1, :, :, lanes]))
        pairs.append((vz.at[q], v_out.at[2, :, :, lanes]))
        pairs.append((p.at[q, :, pl.ds(8, cy), :], p_out.at[:, :, lanes]))
    copies = [pltpu.make_async_copy(a, b, sems.at[k]) for k, (a, b) in enumerate(pairs)]
    for copy in copies:
        copy.start()

    lane8 = lax.broadcasted_iota(jnp.int32, (8, LANES), 1)
    sub8 = lax.broadcasted_iota(jnp.int32, (8, LANES), 0)
    lrow = lax.broadcasted_iota(jnp.int32, (LANES, LANES), 0)
    lcol = lax.broadcasted_iota(jnp.int32, (LANES, LANES), 1)
    label, leave_at, alab = info[0], info[1], info[2]
    present = alab > 0.0
    upper = jnp.where(lrow <= lcol, 1.0, 0.0)
    upper_block = jnp.where(lrow // 32 == lcol // 32, upper, 0.0).astype(bf16)
    upper = upper.astype(bf16)
    ones = jnp.ones((LANES, LANES), bf16)
    present_f = jnp.where(present, 1.0, 0.0)
    arank = jnp.dot(present_f.astype(bf16), upper_block, preferred_element_type=f32) - 1.0
    arank = jnp.where(present, arank, -5.0)
    vacant = label == 0.0
    ranks = []
    for t in range(STEPS):
        vacant = vacant | (leave_at == float(t))
        flag = jnp.where(vacant, 1.0, 0.0).astype(bf16)
        rank = jnp.dot(flag, upper, preferred_element_type=f32) - 1.0
        total = jnp.dot(flag, ones, preferred_element_type=f32)
        for k in range(SLOT_BLOCKS - 1):
            rank = rank + jnp.where(sub8 > k, total[k : k + 1, :], 0.0)
        ranks.append(jnp.where(vacant, rank, -1.0))
        count = jnp.sum(jnp.where(lane8 // 32 == t, present_f, 0.0), axis=1, keepdims=True)
        vacant = vacant & (rank >= count)
    lt[...] = jnp.concatenate(ranks + [jnp.zeros((LANES - 8 * STEPS, LANES), f32)], axis=0).T

    group = lcol // 32
    alab_high, alab_low = split(alab)
    final = jnp.where(leave_at == float(STEPS), label, 0.0)
    nt = (((1,), (1,)), ((), ()))
    for k in range(SLOT_BLOCKS):
        rows = slice(k * LANES, (k + 1) * LANES)
        mine = jnp.broadcast_to(lt[:, k : k + 1], (LANES, LANES))
        for t in range(1, STEPS):
            mine = jnp.where(group == t, lt[:, 8 * t + k : 8 * t + k + 1], mine)
        hot = jnp.where(mine == arank[0:1, :], 1.0, 0.0).astype(bf16)
        there = lax.dot_general(alab_high, hot, nt, preferred_element_type=f32)
        there = there + lax.dot_general(alab_low, hot, nt, preferred_element_type=f32)
        final = final + jnp.where(sub8 == k, there, 0.0)
        both = jnp.concatenate([hot, hot], axis=1)
        placed = jnp.dot(both, cat[...], preferred_element_type=f32)
        keep = mask[rows, :]
        keep = jnp.concatenate([keep, keep], axis=1) >= float(STEPS)
        r_end[rows, :] = jnp.where(keep, r[rows, :], 0.0) + placed[:, :BLOCK]
        s_end[rows, :] = (1.0 / time_step) * (jnp.where(keep, s[rows, :], 0.0) + placed[:, BLOCK:])
        if k % 4 == 3:
            rows_of = pl.ds((k - 3) * LANES, 4 * LANES)
            for a, b in ((r_end, r_out), (s_end, s_out)):
                copy = pltpu.make_async_copy(a.at[rows_of, :], b.at[rows_of, :], sems.at[len(copies)])
                copy.start()
                copies.append(copy)
    c_end[...] = final.astype(jnp.int32) - 1
    copy = pltpu.make_async_copy(c_end, c_out, sems.at[len(copies)])
    copy.start()
    copies.append(copy)
    for copy in copies:
        copy.wait()


def on_device(
    pressure, velocity, stretch, rest_radius, wall_speed, block_cells, depart_slot, depart_way
):
    cx, cy, nz = pressure.shape
    nq = nz // LANES
    ncol = 2 * cx * cy
    vmem = pl.BlockSpec(memory_space=pltpu.VMEM)
    hbm = pl.BlockSpec(memory_space=pl.ANY)
    dma = pltpu.SemaphoreType.DMA
    vmem_out = pltpu.VMEM
    parts = pl.pallas_call(
        kernel,
        out_shape=(
            vmem_out((nq, cx, cy + 16, LANES), f32),
            vmem_out((nq, cx + 2, cy, LANES), f32),
            vmem_out((nq, cx, cy + 16, LANES), f32),
            vmem_out((nq, cx, cy, LANES), f32),
            vmem_out((ROWS, BLOCK), f32),
            vmem_out((ROWS, BLOCK), f32),
            vmem_out((ROWS, LANES), f32),
            vmem_out((2 * ARRIVE, 2 * BLOCK), bf16),
            vmem_out((3, SLOT_BLOCKS, LANES), f32),
        ),
        in_specs=[pl.BlockSpec(memory_space=pltpu.HBM)] * 9,
        out_specs=(vmem,) * 9,
        scratch_shapes=[
            pltpu.VMEM((ROWS, BLOCK), f32),
            pltpu.VMEM((3, ARRIVE, BLOCK), f32),
            pltpu.VMEM((STEPS + 1, 3, DEP, BLOCK), f32),
            pltpu.VMEM((4, DEP, BLOCK), f32),
            pltpu.VMEM((ROWS, ncol), bf16),
            pltpu.VMEM((ncol, ROWS), bf16),
            pltpu.VMEM((ncol, 2 * BLOCK), bf16),
            pltpu.VMEM((ROWS, BLOCK), f32),
            pltpu.VMEM((ROWS, 2 * BLOCK), bf16),
            pltpu.VMEM((ncol, BLOCK), f32),
            pltpu.VMEM((STEPS + 1, 2, nq, 2, cy, LANES), f32),
            pltpu.VMEM((STEPS, 2, nq, 2, cy, LANES), f32),
            pltpu.VMEM((STEPS + 1, 2, 2, nq, cx, LANES), f32),
            pltpu.VMEM((STEPS, 2, 2, nq, cx, LANES), f32),
            pltpu.VMEM((2, nq, cx, LANES), f32),
            pltpu.VMEM((2, nq, cx, LANES), f32),
            pltpu.VMEM((8, LANES), f32),
            pltpu.VMEM((4, 8, LANES), f32),
            pltpu.VMEM((ARRIVE, LANES), f32),
            pltpu.VMEM((LANES, LANES), f32),
            pltpu.VMEM((16, LANES), f32),
            pltpu.SMEM((SLOTS,), jnp.int32),
            pltpu.SMEM((STEPS, 1, 1, DEP), jnp.int32),
            pltpu.SMEM((STEPS, 1, 1, DEP), jnp.int32),
            pltpu.VMEM((SLOT_BLOCKS, LANES), jnp.int32),
            dma((4 * nq + 7,)),
            dma((4,)),
            dma((4,)),
            dma((STEPS, 4)),
            dma((STEPS, 4)),
            dma((4,)),
            dma((4,)),
            dma((STEPS, 4)),
            dma((STEPS, 4)),
            dma((2, 2, nq)),
            dma((2, 2, nq)),
        ],
        compiler_params=pltpu.CompilerParams(
            collective_id=0, has_side_effects=True, vmem_limit_bytes=36 * 2**20
        ),
        cost_estimate=pl.CostEstimate(
            flops=10 * 2**30, bytes_accessed=13 * 2**20, transcendentals=2**22
        ),
    )(
        *(
            pltpu.with_memory_space_constraint(value, pltpu.HBM)
            for value in (
                block_cells,
                depart_slot,
                depart_way,
                block_cells.reshape(SLOT_BLOCKS, LANES),
                pressure,
                velocity,
                stretch,
                rest_radius,
                wall_speed,
            )
        )
    )
    parts = [pltpu.with_memory_space_constraint(part, pltpu.VMEM) for part in parts]
    p, v, r, s, c = pl.pallas_call(
        write_out,
        out_shape=(
            jax.ShapeDtypeStruct(pressure.shape, f32),
            jax.ShapeDtypeStruct(velocity.shape, f32),
            jax.ShapeDtypeStruct(stretch.shape, f32),
            jax.ShapeDtypeStruct(stretch.shape, f32),
            jax.ShapeDtypeStruct((SLOT_BLOCKS, LANES), jnp.int32),
        ),
        in_specs=[vmem] * 9,
        out_specs=(hbm,) * 5,
        scratch_shapes=[
            pltpu.VMEM((SLOTS, BLOCK), f32),
            pltpu.VMEM((SLOTS, BLOCK), f32),
            pltpu.VMEM((SLOT_BLOCKS, LANES), jnp.int32),
            pltpu.VMEM((LANES, LANES), f32),
            dma((4 * nq + 5,)),
        ],
        compiler_params=pltpu.CompilerParams(vmem_limit_bytes=8 * 2**20),
        cost_estimate=pl.CostEstimate(flops=0, bytes_accessed=13 * 2**20, transcendentals=0),
    )(*parts)
    return p, v, r, s, c.reshape(-1)


def solution(mesh):
    placed = (
        P("gx", "gy", None),
        P(None, "gx", "gy", None),
        P(("gx", "gy"), None),
        P(("gx", "gy"), None),
        P(("gx", "gy"), None),
        P(("gx", "gy")),
        P(None, "gx", "gy", None),
        P(None, "gx", "gy", None),
    )
    return jax.shard_map(
        on_device,
        mesh=mesh,
        in_specs=placed,
        out_specs=(
            P("gx", "gy", None),
            P(None, "gx", "gy", None),
            P(("gx", "gy"), None),
            P(("gx", "gy"), None),
            P(("gx", "gy")),
        ),
        check_vma=False,
    )
```

```python
import functools
import math

import jax
import jax.numpy as jnp
from jax import lax
from jax.experimental import pallas as pl
from jax.experimental.pallas import tpu as pltpu
from jax.sharding import PartitionSpec as P

MESH = pl.DeviceIdType.MESH
f32 = jnp.float32
bf16 = jnp.bfloat16

STEPS = 4
DEP = 8
SLOTS = 1024
BLOCK = 256
LANES = 128
ARRIVE = STEPS * 4 * DEP
ROWS = SLOTS + ARRIVE
SLOT_BLOCKS = SLOTS // LANES
WAY_OF = (1, 0, 3, 2)

time_step = 0.04
half_gain = 0.2
source_scale = 0.004 * 12.566370614359172
exponent = 4.2
inv_ln2 = 1.0 / math.log(2.0)


def split(value):
    high = value.astype(bf16)
    return high, (value - high.astype(f32)).astype(bf16)


def wall_update(radius, shift, level, pressure):
    mach = (0.05 / time_step) * shift
    one_less = 1.0 - mach
    divisor = one_less * radius
    inverse = pl.reciprocal(divisor, approx=True)
    inverse = inverse * (2.0 - divisor * inverse)
    inv_radius = inverse * one_less
    wall = jnp.exp2(level - (exponent * inv_ln2) * jnp.log(radius))
    squared = time_step * time_step
    excess = (
        wall
        - (0.2 * squared + (0.08 * time_step) * shift) * inv_radius
        - (squared + squared * pressure)
    )
    driving = (1.0 + mach) * excess - (1.5 - 0.5 * mach) * (shift * shift)
    shift = shift + driving * inverse
    radius = radius + shift
    return radius, shift, (source_scale / time_step) * (radius * radius) * shift


def kernel(
    cells_h, slot_h, way_h, cells_b, press, vel, stretch, rest, speed0,
    PR, VX, VY, VZ, R, S, MSK, CAT, INFO,
    A, AR, SB, DB, OH, OHT, PHL, PG, VHL, SRC, XS, XR, YS, YR, VYS, VYR,
    MT, MR, AMSK, LT, LR, cells_s, slot_s, way_s, cells_v,
    in_sem, meta_s, meta_r, xs, xr, vs, vr, ds_, dr, fs, fr,
):
    _, cx, cy, nz = vel.shape
    nq = nz // LANES
    half = cx * cy
    ncol = 2 * half
    jbs = cy // 16
    part = min(256, ncol)
    planes = part // (2 * cy)
    groups = cx // planes
    shift = (planes * cy).bit_length() - 1
    zero_row = lax.axis_index("gx") // 4096
    gx, gy = lax.axis_index("gx"), lax.axis_index("gy")
    ngx, ngy = lax.axis_size("gx"), lax.axis_size("gy")
    has_lo, has_hi = gy > 0, gy < ngy - 1
    targets = (
        (lax.rem(gx + 1, ngx), gy),
        (lax.rem(gx + ngx - 1, ngx), gy),
        (gx, lax.rem(gy + 1, ngy)),
        (gx, lax.rem(gy + ngy - 1, ngy)),
    )
    sends = (None, None, has_hi, has_lo)
    takes = (None, None, has_lo, has_hi)

    def under(flag, action):
        if flag is None:
            action()
        else:
            pl.when(flag)(action)

    barrier = pltpu.get_barrier_semaphore()
    for d in range(4):
        under(
            sends[d],
            lambda d=d: pl.semaphore_signal(
                barrier, inc=1, device_id=targets[d], device_id_type=MESH
            ),
        )

    inputs = [(cells_h, cells_s), (slot_h, slot_s), (way_h, way_s), (cells_b, cells_v)]
    for q in range(nq):
        inputs.append((press.at[:, :, pl.ds(q * LANES, LANES)], PR.at[q, :, pl.ds(8, cy), :]))
    for q in range(nq):
        lanes = pl.ds(q * LANES, LANES)
        inputs.append((vel.at[1, :, :, lanes], VY.at[q, :, pl.ds(8, cy), :]))
    own = pl.ds(0, SLOTS)
    inputs.append((rest, A.at[own, :]))
    inputs.append((stretch, R.at[own, :]))
    inputs.append((speed0, S.at[own, :]))
    for q in range(nq):
        lanes = pl.ds(q * LANES, LANES)
        inputs.append((vel.at[0, :, :, lanes], VX.at[q, pl.ds(1, cx), :, :]))
        inputs.append((vel.at[2, :, :, lanes], VZ.at[q]))
    loads = [pltpu.make_async_copy(a, b, in_sem.at[k]) for k, (a, b) in enumerate(inputs)]
    for load in loads:
        load.start()
    small_loads, loads = loads[:4], loads[4:]

    @pl.when(jnp.logical_not(has_lo))
    def _():
        MR[2] = jnp.zeros((8, LANES), f32)
        YR[:, 0] = jnp.zeros(YR.shape[:1] + YR.shape[2:], f32)
        VYR[0] = jnp.zeros(VYR.shape[1:], f32)

    @pl.when(jnp.logical_not(has_hi))
    def _():
        MR[3] = jnp.zeros((8, LANES), f32)
        YR[:, 1] = jnp.zeros(YR.shape[:1] + YR.shape[2:], f32)
        VYR[1] = jnp.zeros(VYR.shape[1:], f32)

    edge_rows = jnp.zeros((nq, cx, 8, LANES), f32)
    PR[:, :, 0:8, :] = edge_rows
    PR[:, :, 8 + cy : 16 + cy, :] = edge_rows
    VY[:, :, 0:8, :] = edge_rows
    VY[:, :, 8 + cy : 16 + cy, :] = edge_rows
    empty = jnp.zeros((ARRIVE, BLOCK), f32)
    R[SLOTS:ROWS, :] = empty + 1.0
    S[SLOTS:ROWS, :] = empty
    A[SLOTS:ROWS, :] = empty
    MSK[SLOTS:ROWS, :] = jnp.full((ARRIVE, LANES), -1.0, f32)
    OHT[:, SLOTS:ROWS] = jnp.zeros((ncol, ARRIVE), bf16)
    VHL[SLOTS:ROWS, :] = jnp.zeros((ARRIVE, 2 * BLOCK), bf16)
    OH[SLOTS:ROWS, :] = jnp.zeros((ARRIVE, ncol), bf16)
    pl.semaphore_wait(barrier, 2 + has_lo.astype(jnp.int32) + has_hi.astype(jnp.int32))

    def remote(src, dst, send_sem, recv_sem, d):
        return pltpu.make_async_remote_copy(
            src_ref=src, dst_ref=dst, send_sem=send_sem, recv_sem=recv_sem,
            device_id=targets[d], device_id_type=MESH,
        )

    def meta_copy(d):
        return [remote(MT, MR.at[d], meta_s.at[d], meta_r.at[d], d)]

    def p_copy(t, d):
        if d < 2:
            src, dst = XS.at[t, 1 - d], XR.at[t, d]
        else:
            src, dst = YS.at[t, 3 - d], YR.at[t, d - 2]
        return [remote(src, dst, xs.at[t, d], xr.at[t, d], d)]

    def first_copies(d):
        side = (cx - 2, 0)[d]
        for q in range(nq):
            lanes = pl.ds(q * LANES, LANES)
            yield remote(
                press.at[pl.ds(side, 2), :, lanes], XR.at[0, d, q], fs.at[0, d, q], fr.at[0, d, q], d
            )
        for q in range(nq):
            lanes = pl.ds(q * LANES, LANES)
            yield remote(
                vel.at[0, pl.ds((cx - 1, 0)[d], 1), :, lanes],
                VX.at[q, pl.ds((0, cx + 1)[d], 1), :, :],
                fs.at[1, d, q],
                fr.at[1, d, q],
                d,
            )

    def v_copy(d):
        return [remote(VYS.at[3 - d], VYR.at[d - 2], vs.at[d], vr.at[d], d)]

    def dep_copy(t, d):
        to = AR.at[:, pl.ds(t * 32 + d * DEP, DEP), :]
        return [remote(SB.at[t], to, ds_.at[t, d], dr.at[t, d], d)]

    odd = lax.rem(gy, 2) == 1
    even = jnp.logical_not(odd)
    far_hi, near_hi = has_hi & odd, has_hi & even
    far_lo, near_lo = has_lo & even, has_lo & odd

    def start(make, ways=(0, 1, 2, 3)):
        order = ((far_hi, 2), (far_lo, 3), (None, 0), (None, 1), (near_hi, 2), (near_lo, 3))
        for flag, d in order:
            if d in ways:
                under(flag, lambda d=d: [copy.start() for copy in make(d)] and None)

    def wait_sent(make, ways=(0, 1, 2, 3)):
        for d in ways:
            under(sends[d], lambda d=d: [copy.wait_send() for copy in make(d)] and None)

    def wait_taken(make, ways=(0, 1, 2, 3)):
        for d in ways:
            under(takes[d], lambda d=d: [copy.wait_recv() for copy in make(d)] and None)

    for d in range(2):
        for copy in first_copies(d):
            copy.start()
    edges = ((0, 1), (cy - 2, cy - 1))

    def one(row):
        return pl.ds(row + zero_row, 1)

    pitch = cy + 16
    PR_rows = PR.reshape(nq * cx * pitch, LANES)
    VY_rows = VY.reshape(nq * cx * pitch, LANES)

    def across(q, row):
        return pl.ds(q * cx * pitch + 8 + row, cx, stride=pitch), slice(None)

    def pack_rows(t):
        for side in range(2):
            for r in range(2):
                for q in range(nq):
                    YS[t, side, r, q] = PR_rows[across(q, edges[side][r])]

    def unpack_rows(t):
        for side in range(2):
            for r in range(2):
                for q in range(nq):
                    PR_rows[across(q, edges[side][r])] = YS[t, side, r, q]

    def column_row(i, h, jb):
        return (i // planes) * part + (h * planes + i % planes) * cy + jb * 16

    def keep_parts(i, jb, q, value):
        high, low = split(value)
        row = column_row(i, q // 2, jb)
        col = (q % 2) * 2 * LANES
        PHL[row : row + 16, col : col + LANES] = high
        PHL[row : row + 16, col + LANES : col + 2 * LANES] = low

    def rows_of(jb):
        return slice(jb * 16, jb * 16 + 16), slice(8 + jb * 16, 24 + jb * 16)

    def split_all():
        for i in range(cx):
            for jb in range(jbs):
                for q in range(nq):
                    keep_parts(i, jb, q, PR[q, i, rows_of(jb)[1], :])

    for k in range(nq):
        loads[k].wait()
    pack_rows(0)
    start(lambda d: p_copy(0, d), (2, 3))
    for q in range(nq):
        for r in range(2):
            XS[0, 0, q, r] = PR[q, r, 8 : 8 + cy, :]
            XS[0, 1, q, r] = PR[q, cx - 2 + r, 8 : 8 + cy, :]
    for k in range(nq, 2 * nq):
        loads[k].wait()
    for q in range(nq):
        VYS[0, q] = VY_rows[across(q, 0)]
        VYS[1, q] = VY_rows[across(q, cy - 1)]
    start(v_copy, (2, 3))

    for load in small_loads:
        load.wait()

    lane8 = lax.broadcasted_iota(jnp.int32, (8, LANES), 1)
    sub8 = lax.broadcasted_iota(jnp.int32, (8, LANES), 0)
    slot_id = sub8 * LANES + lane8
    label = cells_v[...] + 1
    leave_at = jnp.where(label > 0, STEPS, -1)
    entry_of = (lane8 // 32) * DEP + lane8 % DEP
    wanted = (lane8 // DEP) % 4
    wanted = jnp.where(wanted < 2, 1 - wanted, 5 - wanted)
    meta = jnp.zeros((8, LANES), jnp.int32)
    for e in range(STEPS * DEP):
        slot = slot_s[e // DEP, 0, 0, e % DEP]
        moved = jnp.where(slot >= 0, cells_s[jnp.maximum(slot, 0)] + 1, 0)
        meta = jnp.where((entry_of == e) & (wanted == way_s[e // DEP, 0, 0, e % DEP]), moved, meta)
        leave_at = jnp.where(slot_id == slot, e // DEP, leave_at)
    MT[...] = meta.astype(f32)

    start(meta_copy)

    lrow = lax.broadcasted_iota(jnp.int32, (LANES, LANES), 0)
    lcol = lax.broadcasted_iota(jnp.int32, (LANES, LANES), 1)
    wide = lax.broadcasted_iota(jnp.int32, (16, ncol), 1).astype(f32)

    def code_of(lab):
        cell = lab - 1
        place = cell >> 1
        row = (place >> shift) * part + (cell & 1) * (planes * cy)
        return jnp.where(lab > 0, row + (place & (planes * cy - 1)), -1).astype(f32)

    def turn(stack):
        stack = stack + [jnp.zeros((8, LANES), f32)] * (16 - len(stack))
        LT[...] = jnp.concatenate(stack, axis=0).T

    def hot_rows(r, at):
        def body(m, carry):
            rows = pl.ds(pl.multiple_of(m * 16, 16), 16)
            hot = jnp.where(LT[rows, at : at + 1] == wide, 1.0, 0.0).astype(bf16)
            OH[pl.ds(pl.multiple_of(r * LANES + m * 16, 16), 16), :] = hot
            return carry

        lax.fori_loop(0, LANES // 16, body, 0, unroll=4)

    def hot_columns(first, last):
        def body(m, carry):
            ident = (lrow + m * LANES).astype(f32)
            rows = pl.ds(pl.multiple_of(m * LANES, LANES), LANES)
            for r in range(first, last):
                hot = jnp.where(ident == LR[r : r + 1, :], 1.0, 0.0).astype(bf16)
                OHT[rows, r * LANES : (r + 1) * LANES] = hot
            return carry

        lax.fori_loop(0, ncol // LANES, body, 0)

    code = code_of(label)
    turn([code, leave_at.astype(f32)])
    LR[0:8, :] = code
    for r in range(SLOT_BLOCKS):
        hot_rows(r, r)
    for r in range(SLOT_BLOCKS):
        MSK[r * LANES : (r + 1) * LANES, :] = jnp.broadcast_to(
            LT[:, 8 + r : 9 + r], (LANES, LANES)
        )
    hot_columns(0, SLOT_BLOCKS)

    for k in range(2 * nq, 2 * nq + 3):
        loads[k].wait()

    def first_state(n, carry):
        rows = pl.ds(pl.multiple_of(n * 16, 16), 16)
        rest_now = A[rows, :]
        R[rows, :] = R[rows, :] * rest_now
        S[rows, :] = time_step * S[rows, :]
        A[rows, :] = inv_ln2 * (
            jnp.log((time_step * time_step) * (1.0 + 0.2 / rest_now))
            + exponent * jnp.log(rest_now)
        )
        return carry

    lax.fori_loop(0, SLOTS // 16, first_state, 0, unroll=4)
    for k in range(2 * nq + 3, 4 * nq + 3):
        loads[k].wait()

    def plan():
        wait_taken(meta_copy)
        came = (lane8 // DEP) % 4
        alab = jnp.where(
            came == 0, MR[0], jnp.where(came == 1, MR[1], jnp.where(came == 2, MR[2], MR[3]))
        )
        acode = code_of(alab.astype(jnp.int32))
        turn([acode, alab])
        LR[8:16, :] = acode
        hot_rows(SLOT_BLOCKS, 0)
        hot_columns(SLOT_BLOCKS, SLOT_BLOCKS + 1)
        AMSK[...] = jnp.broadcast_to(LT[:, 8:9], (LANES, LANES))
        INFO[0] = label.astype(f32)
        INFO[1] = leave_at.astype(f32)
        INFO[2] = alab

    def slope_z(tiles):
        height = tiles[0].shape[0]
        lane = lax.broadcasted_iota(jnp.int32, (height, LANES), 1)
        zero = jnp.zeros((height, LANES), f32)
        ahead = [pltpu.roll(v, LANES - 1, 1) for v in tiles] + [zero]
        behind = [zero] + [pltpu.roll(v, 1, 1) for v in tiles]
        return [
            jnp.where(lane == LANES - 1, ahead[q + 1], ahead[q])
            - jnp.where(lane == 0, behind[q], behind[q + 1])
            for q in range(nq)
        ]

    low_gate = jnp.where(has_lo, 1.0, 0.0).astype(f32)
    high_gate = jnp.where(has_hi, 1.0, 0.0).astype(f32)

    def halves(w):
        return slice(w * LANES, (w + 1) * LANES), slice(2 * w * LANES, 2 * (w + 1) * LANES)

    def gather(w, rows=slice(0, ROWS)):
        narrow, pair = halves(w)
        both = jnp.dot(OH[rows, :], PHL[:, pair], preferred_element_type=f32)
        PG[rows, narrow] = both[:, :LANES] + both[:, LANES:]

    def scatter(w, rows, count):
        narrow, pair = halves(w)
        both = jnp.dot(OHT[rows, :count], VHL[:count, pair], preferred_element_type=f32)
        SRC[rows, narrow] = both[:, :LANES] + both[:, LANES:]

    def leavers(t, to):
        for k in range(DEP):
            slot = jnp.maximum(slot_s[t, 0, 0, k], 0)
            cell = jnp.maximum(cells_s[slot], 0)
            place = cell >> 1
            row = pl.ds(slot, 1)
            DB[0, k : k + 1, :] = R[row, :]
            DB[1, k : k + 1, :] = S[row, :]
            DB[2, k : k + 1, :] = A[row, :]
            for w in range(2):
                DB[3, k : k + 1, halves(w)[0]] = PR[
                    2 * (cell & 1) + w,
                    place >> (cy.bit_length() - 1),
                    pl.ds(8 + (place & (cy - 1)), 1),
                    :,
                ]
        radius, speed, _ = wall_update(DB[0], DB[1], DB[2], DB[3])
        SB[to, 0] = radius
        SB[to, 1] = speed
        SB[to, 2] = DB[2]

    def take_arrivals(t):
        wait_taken(lambda d: dep_copy(t, d))
        rows, to = slice(t * 32, t * 32 + 32), slice(SLOTS + t * 32, SLOTS + t * 32 + 32)
        R[to, :] = AR[0, rows, :]
        S[to, :] = AR[1, rows, :]
        A[to, :] = AR[2, rows, :]
        MSK[to, :] = jnp.where(AMSK[rows, :] > 0.0, 2.0 * STEPS, -1.0)

    def when(flag):
        return lambda action: action() if flag else None

    def step(t):
        limit = float(t)
        live = SLOTS + 32 * t
        final = t == STEPS - 1

        def bubbles(first, w):
            rows = slice(first, first + 16)
            col = halves(w)[0]
            radius, speed, rate = wall_update(R[rows, col], S[rows, col], A[rows, col], PG[rows, col])
            R[rows, col] = radius
            S[rows, col] = speed
            high, low = split(jnp.where(MSK[rows, :] >= limit, rate, 0.0))
            VHL[rows, 2 * w * LANES : (2 * w + 1) * LANES] = high
            VHL[rows, (2 * w + 1) * LANES : (2 * w + 2) * LANES] = low

        @when(t > 0)
        def _():
            take_arrivals(t - 1)

        split_all()
        last = t // (STEPS - 1)
        if not final:
            leavers(t, t)
        gather(0, slice(0, live))

        @when(last == 0)
        def _():
            start(lambda d: dep_copy(t, d))

        def pieces(count, size):
            ends = [k * size // count // 16 * 16 for k in range(count)] + [size]
            return [slice(ends[k], ends[k + 1]) for k in range(count)]

        for rows in pieces(2, live):
            gather(1, rows)
            for first in range(rows.start, rows.stop, 16):
                bubbles(first, 0)
        for rows, part_rows in zip(pieces(2, ncol), pieces(2, live)):
            scatter(0, rows, SLOTS if t == 0 else ROWS)
            for first in range(part_rows.start, part_rows.stop, 16):
                bubbles(first, 1)

        def flow_x(i):
            for q in range(nq):
                for jb in range(jbs):
                    rows, at = rows_of(jb)
                    flow = VX[q, i + 1, rows, :]
                    if i == 0:
                        flow = flow - half_gain * PR[q, 1, at, :]
                    elif i == cx - 1:
                        flow = flow + half_gain * PR[q, cx - 2, at, :]
                    else:
                        flow = flow - half_gain * (PR[q, i + 1, at, :] - PR[q, i - 1, at, :])
                    VX[q, i + 1, rows, :] = flow

        def flow_z(i, jb):
            rows, at = rows_of(jb)
            slopes = slope_z([PR[q, i, at, :] for q in range(nq)])
            for q in range(nq):
                VZ[q, i, rows, :] = VZ[q, i, rows, :] - half_gain * slopes[q]

        def flow_y(i, jb):
            _, at = rows_of(jb)
            for q in range(nq):
                VY[q, i, at, :] = VY[q, i, at, :] - half_gain * (
                    PR[q, i, pl.ds(9 + jb * 16 + zero_row, 16), :]
                    - PR[q, i, pl.ds(7 + jb * 16 + zero_row, 16), :]
                )

        def pressure(i, jb):
            rows, at = rows_of(jb)
            slopes = slope_z([VZ[q, i, rows, :] for q in range(nq)])
            for q in range(nq):
                rise = slopes[q] + (
                    VY[q, i, pl.ds(9 + jb * 16 + zero_row, 16), :]
                    - VY[q, i, pl.ds(7 + jb * 16 + zero_row, 16), :]
                )
                if i + 1 < cx:
                    rise = rise + VX[q, i + 2, rows, :]
                if i > 0:
                    rise = rise - VX[q, i, rows, :]
                row = column_row(i, q // 2, jb)
                col = (q % 2) * LANES
                PR[q, i, at, :] = (
                    PR[q, i, at, :] - half_gain * rise + SRC[row : row + 16, col : col + LANES]
                )

        for rows, part_planes in zip(pieces(2, ncol), pieces(2, cx)):
            scatter(1, rows, SLOTS if t == 0 else ROWS)
            for i in range(part_planes.start, part_planes.stop):
                flow_x(i)
                for jb in range(jbs):
                    flow_z(i, jb)
                    flow_y(i, jb)
        for i in range(cx):
            for jb in range(jbs):
                pressure(i, jb)
        pack_rows(t + 1)

        when(t == 0)(plan)
        wait_taken(lambda d: p_copy(t, d), (2, 3))

        @when(t > 0)
        def _():
            wait_taken(lambda d: p_copy(t, d), (0, 1))

        @when(t == 0)
        def _():
            for d in range(2):
                for copy in first_copies(d):
                    copy.wait_recv()
            wait_taken(v_copy, (2, 3))

        below, above = VYR[0], VYR[1]
        below = low_gate * (below - half_gain * (YS[t, 0, 0] - YR[t, 0, 0]))
        above = high_gate * (above - half_gain * (YR[t, 1, 1] - YS[t, 1, 1]))
        VYR[0] = below
        VYR[1] = above
        both_gains = half_gain * half_gain
        YS[t + 1, 0, 0] = YS[t + 1, 0, 0] + half_gain * below
        YS[t + 1, 0, 1] = YS[t + 1, 0, 1] + both_gains * YR[t, 0, 1]
        YS[t + 1, 1, 0] = YS[t + 1, 1, 0] + both_gains * YR[t, 1, 0]
        YS[t + 1, 1, 1] = YS[t + 1, 1, 1] - half_gain * above
        for q in range(nq):
            for jb in range(jbs):
                rows, at = rows_of(jb)
                far, near = XR[t, 0, q, 0, rows, :], XR[t, 0, q, 1, rows, :]
                beside = VX[q, 0, rows, :] - half_gain * (XS[t, 0, q, 0, rows, :] - far)
                VX[q, 0, rows, :] = beside
                VX[q, 1, rows, :] = VX[q, 1, rows, :] + half_gain * near
                first = PR[q, 0, at, :] + half_gain * beside
                second = PR[q, 1, at, :] + both_gains * near
                PR[q, 0, at, :] = first
                PR[q, 1, at, :] = second
                if not final:
                    XS[t + 1, 0, q, 0, rows, :] = first
                if not final:
                    XS[t + 1, 0, q, 1, rows, :] = second
                near, far = XR[t, 1, q, 0, rows, :], XR[t, 1, q, 1, rows, :]
                beside = VX[q, cx + 1, rows, :] - half_gain * (far - XS[t, 1, q, 1, rows, :])
                VX[q, cx + 1, rows, :] = beside
                VX[q, cx, rows, :] = VX[q, cx, rows, :] - half_gain * near
                first = PR[q, cx - 2, at, :] + both_gains * near
                second = PR[q, cx - 1, at, :] - half_gain * beside
                PR[q, cx - 2, at, :] = first
                PR[q, cx - 1, at, :] = second
                if not final:
                    XS[t + 1, 1, q, 0, rows, :] = first
                if not final:
                    XS[t + 1, 1, q, 1, rows, :] = second
        ends = ((0, 0, 0), (1, 0, 1), (cx - 2, 1, 0), (cx - 1, 1, 1))
        for i, x_side, x_row in ends:
            for side in range(2):
                for r in range(2):
                    for q in range(nq):
                        row = one(edges[side][r])
                        if i == 0:
                            part_x = half_gain * VX[q, 0, row, :]
                        elif i == 1:
                            part_x = both_gains * XR[t, 0, q, 1, row, :]
                        elif i == cx - 2:
                            part_x = both_gains * XR[t, 1, q, 0, row, :]
                        else:
                            part_x = -half_gain * VX[q, cx + 1, row, :]
                        value = YS[t + 1, side, r, q, one(i), :] + part_x
                        YS[t + 1, side, r, q, one(i), :] = value
                        if not final:
                            XS[t + 1, x_side, q, x_row, row, :] = value

        @when(t < STEPS - 1)
        def _():
            start(lambda d: p_copy(t + 1, d))

        unpack_rows(t + 1)

        @when(t == STEPS - 2)
        def _():
            leavers(t + 1, t + 1)
            start(lambda d: dep_copy(t + 1, d))

        for q in range(nq):
            low, high = across(q, 0), across(q, cy - 1)
            VY_rows[low] = VY_rows[low] + half_gain * YR[t, 0, 1, q]
            VY_rows[high] = VY_rows[high] - half_gain * YR[t, 1, 0, q]

        wait_sent(lambda d: dep_copy(t, d))

        @when(t > 0)
        def _():
            wait_sent(lambda d: p_copy(t, d), (0, 1))

        wait_sent(lambda d: p_copy(t, d), (2, 3))

    for t in range(STEPS):
        step(t)

    take_arrivals(STEPS - 1)
    keep = AMSK[...] > 0.0
    for k, state in enumerate((R, S)):
        for w in range(2):
            high, low = split(jnp.where(keep, state[SLOTS:ROWS, halves(w)[0]], 0.0))
            to = slice(k * BLOCK + w * LANES, k * BLOCK + (w + 1) * LANES)
            CAT[0:ARRIVE, to] = high
            CAT[ARRIVE : 2 * ARRIVE, to] = low

    wait_sent(meta_copy)
    wait_sent(v_copy, (2, 3))
    for d in range(2):
        for copy in first_copies(d):
            copy.wait_send()


def write_out(
    p, vx, vy, vz, r, s, mask, cat, info, p_out, v_out, r_out, s_out, c_out, r_end, s_end, c_end, lt, sems
):
    _, cx, cy, nz = v_out.shape
    pairs = []
    for q in range(nz // LANES):
        lanes = pl.ds(q * LANES, LANES)
        pairs.append((vx.at[q, pl.ds(1, cx), :, :], v_out.at[0, :, :, lanes]))
        pairs.append((vy.at[q, :, pl.ds(8, cy), :], v_out.at[1, :, :, lanes]))
        pairs.append((vz.at[q], v_out.at[2, :, :, lanes]))
        pairs.append((p.at[q, :, pl.ds(8, cy), :], p_out.at[:, :, lanes]))
    copies = [pltpu.make_async_copy(a, b, sems.at[k]) for k, (a, b) in enumerate(pairs)]
    for copy in copies:
        copy.start()

    lane8 = lax.broadcasted_iota(jnp.int32, (8, LANES), 1)
    sub8 = lax.broadcasted_iota(jnp.int32, (8, LANES), 0)
    lrow = lax.broadcasted_iota(jnp.int32, (LANES, LANES), 0)
    lcol = lax.broadcasted_iota(jnp.int32, (LANES, LANES), 1)
    label, leave_at, alab = info[0], info[1], info[2]
    present = alab > 0.0
    upper = jnp.where(lrow <= lcol, 1.0, 0.0)
    upper_block = jnp.where(lrow // 32 == lcol // 32, upper, 0.0).astype(bf16)
    upper = upper.astype(bf16)
    ones = jnp.ones((LANES, LANES), bf16)
    present_f = jnp.where(present, 1.0, 0.0)
    arank = jnp.dot(present_f.astype(bf16), upper_block, preferred_element_type=f32) - 1.0
    arank = jnp.where(present, arank, -5.0)
    vacant = label == 0.0
    ranks = []
    for t in range(STEPS):
        vacant = vacant | (leave_at == float(t))
        flag = jnp.where(vacant, 1.0, 0.0).astype(bf16)
        rank = jnp.dot(flag, upper, preferred_element_type=f32) - 1.0
        total = jnp.dot(flag, ones, preferred_element_type=f32)
        for k in range(SLOT_BLOCKS - 1):
            rank = rank + jnp.where(sub8 > k, total[k : k + 1, :], 0.0)
        ranks.append(jnp.where(vacant, rank, -1.0))
        count = jnp.sum(jnp.where(lane8 // 32 == t, present_f, 0.0), axis=1, keepdims=True)
        vacant = vacant & (rank >= count)
    lt[...] = jnp.concatenate(ranks + [jnp.zeros((LANES - 8 * STEPS, LANES), f32)], axis=0).T

    group = lcol // 32
    alab_high, alab_low = split(alab)
    final = jnp.where(leave_at == float(STEPS), label, 0.0)
    nt = (((1,), (1,)), ((), ()))
    for k in range(SLOT_BLOCKS):
        rows = slice(k * LANES, (k + 1) * LANES)
        mine = jnp.broadcast_to(lt[:, k : k + 1], (LANES, LANES))
        for t in range(1, STEPS):
            mine = jnp.where(group == t, lt[:, 8 * t + k : 8 * t + k + 1], mine)
        hot = jnp.where(mine == arank[0:1, :], 1.0, 0.0).astype(bf16)
        there = lax.dot_general(alab_high, hot, nt, preferred_element_type=f32)
        there = there + lax.dot_general(alab_low, hot, nt, preferred_element_type=f32)
        final = final + jnp.where(sub8 == k, there, 0.0)
        both = jnp.concatenate([hot, hot], axis=1)
        placed = jnp.dot(both, cat[...], preferred_element_type=f32)
        keep = mask[rows, :]
        keep = jnp.concatenate([keep, keep], axis=1) >= float(STEPS)
        r_end[rows, :] = jnp.where(keep, r[rows, :], 0.0) + placed[:, :BLOCK]
        s_end[rows, :] = (1.0 / time_step) * (jnp.where(keep, s[rows, :], 0.0) + placed[:, BLOCK:])
        if k % 4 == 3:
            rows_of = pl.ds((k - 3) * LANES, 4 * LANES)
            for a, b in ((r_end, r_out), (s_end, s_out)):
                copy = pltpu.make_async_copy(a.at[rows_of, :], b.at[rows_of, :], sems.at[len(copies)])
                copy.start()
                copies.append(copy)
    c_end[...] = final.astype(jnp.int32) - 1
    copy = pltpu.make_async_copy(c_end, c_out, sems.at[len(copies)])
    copy.start()
    copies.append(copy)
    for copy in copies:
        copy.wait()


def on_device(
    pressure, velocity, stretch, rest_radius, wall_speed, block_cells, depart_slot, depart_way
):
    cx, cy, nz = pressure.shape
    nq = nz // LANES
    ncol = 2 * cx * cy
    vmem = pl.BlockSpec(memory_space=pltpu.VMEM)
    hbm = pl.BlockSpec(memory_space=pl.ANY)
    dma = pltpu.SemaphoreType.DMA
    vmem_out = pltpu.VMEM
    parts = pl.pallas_call(
        kernel,
        out_shape=(
            vmem_out((nq, cx, cy + 16, LANES), f32),
            vmem_out((nq, cx + 2, cy, LANES), f32),
            vmem_out((nq, cx, cy + 16, LANES), f32),
            vmem_out((nq, cx, cy, LANES), f32),
            vmem_out((ROWS, BLOCK), f32),
            vmem_out((ROWS, BLOCK), f32),
            vmem_out((ROWS, LANES), f32),
            vmem_out((2 * ARRIVE, 2 * BLOCK), bf16),
            vmem_out((3, SLOT_BLOCKS, LANES), f32),
        ),
        in_specs=[pl.BlockSpec(memory_space=pltpu.HBM)] * 9,
        out_specs=(vmem,) * 9,
        scratch_shapes=[
            pltpu.VMEM((ROWS, BLOCK), f32),
            pltpu.VMEM((3, ARRIVE, BLOCK), f32),
            pltpu.VMEM((STEPS + 1, 3, DEP, BLOCK), f32),
            pltpu.VMEM((4, DEP, BLOCK), f32),
            pltpu.VMEM((ROWS, ncol), bf16),
            pltpu.VMEM((ncol, ROWS), bf16),
            pltpu.VMEM((ncol, 2 * BLOCK), bf16),
            pltpu.VMEM((ROWS, BLOCK), f32),
            pltpu.VMEM((ROWS, 2 * BLOCK), bf16),
            pltpu.VMEM((ncol, BLOCK), f32),
            pltpu.VMEM((STEPS + 1, 2, nq, 2, cy, LANES), f32),
            pltpu.VMEM((STEPS, 2, nq, 2, cy, LANES), f32),
            pltpu.VMEM((STEPS + 1, 2, 2, nq, cx, LANES), f32),
            pltpu.VMEM((STEPS, 2, 2, nq, cx, LANES), f32),
            pltpu.VMEM((2, nq, cx, LANES), f32),
            pltpu.VMEM((2, nq, cx, LANES), f32),
            pltpu.VMEM((8, LANES), f32),
            pltpu.VMEM((4, 8, LANES), f32),
            pltpu.VMEM((ARRIVE, LANES), f32),
            pltpu.VMEM((LANES, LANES), f32),
            pltpu.VMEM((16, LANES), f32),
            pltpu.SMEM((SLOTS,), jnp.int32),
            pltpu.SMEM((STEPS, 1, 1, DEP), jnp.int32),
            pltpu.SMEM((STEPS, 1, 1, DEP), jnp.int32),
            pltpu.VMEM((SLOT_BLOCKS, LANES), jnp.int32),
            dma((4 * nq + 7,)),
            dma((4,)),
            dma((4,)),
            dma((STEPS, 4)),
            dma((STEPS, 4)),
            dma((4,)),
            dma((4,)),
            dma((STEPS, 4)),
            dma((STEPS, 4)),
            dma((2, 2, nq)),
            dma((2, 2, nq)),
        ],
        compiler_params=pltpu.CompilerParams(
            collective_id=0, has_side_effects=True, vmem_limit_bytes=36 * 2**20
        ),
        cost_estimate=pl.CostEstimate(
            flops=10 * 2**30, bytes_accessed=13 * 2**20, transcendentals=2**22
        ),
    )(
        *(
            pltpu.with_memory_space_constraint(value, pltpu.HBM)
            for value in (
                block_cells,
                depart_slot,
                depart_way,
                block_cells.reshape(SLOT_BLOCKS, LANES),
                pressure,
                velocity,
                stretch,
                rest_radius,
                wall_speed,
            )
        )
    )
    parts = [pltpu.with_memory_space_constraint(part, pltpu.VMEM) for part in parts]
    p, v, r, s, c = pl.pallas_call(
        write_out,
        out_shape=(
            jax.ShapeDtypeStruct(pressure.shape, f32),
            jax.ShapeDtypeStruct(velocity.shape, f32),
            jax.ShapeDtypeStruct(stretch.shape, f32),
            jax.ShapeDtypeStruct(stretch.shape, f32),
            jax.ShapeDtypeStruct((SLOT_BLOCKS, LANES), jnp.int32),
        ),
        in_specs=[vmem] * 9,
        out_specs=(hbm,) * 5,
        scratch_shapes=[
            pltpu.VMEM((SLOTS, BLOCK), f32),
            pltpu.VMEM((SLOTS, BLOCK), f32),
            pltpu.VMEM((SLOT_BLOCKS, LANES), jnp.int32),
            pltpu.VMEM((LANES, LANES), f32),
            dma((4 * nq + 5,)),
        ],
        compiler_params=pltpu.CompilerParams(vmem_limit_bytes=8 * 2**20),
        cost_estimate=pl.CostEstimate(flops=0, bytes_accessed=13 * 2**20, transcendentals=0),
    )(*parts)
    return p, v, r, s, c.reshape(-1)


def solution(mesh):
    placed = (
        P("gx", "gy", None),
        P(None, "gx", "gy", None),
        P(("gx", "gy"), None),
        P(("gx", "gy"), None),
        P(("gx", "gy"), None),
        P(("gx", "gy")),
        P(None, "gx", "gy", None),
        P(None, "gx", "gy", None),
    )
    return jax.shard_map(
        on_device,
        mesh=mesh,
        in_specs=placed,
        out_specs=(
            P("gx", "gy", None),
            P(None, "gx", "gy", None),
            P(("gx", "gy"), None),
            P(("gx", "gy"), None),
            P(("gx", "gy")),
        ),
        check_vma=False,
    )
```

```python
import functools
import math

import jax
import jax.numpy as jnp
from jax import lax
from jax.experimental import pallas as pl
from jax.experimental.pallas import tpu as pltpu
from jax.sharding import PartitionSpec as P

MESH = pl.DeviceIdType.MESH
f32 = jnp.float32
bf16 = jnp.bfloat16

STEPS = 4
DEP = 8
SLOTS = 1024
BLOCK = 256
LANES = 128
ARRIVE = STEPS * 4 * DEP
ROWS = SLOTS + ARRIVE
SLOT_BLOCKS = SLOTS // LANES
WAY_OF = (1, 0, 3, 2)

time_step = 0.04
half_gain = 0.2
source_scale = 0.004 * 12.566370614359172
exponent = 4.2
inv_ln2 = 1.0 / math.log(2.0)


def split(value):
    high = value.astype(bf16)
    return high, (value - high.astype(f32)).astype(bf16)


def wall_update(radius, shift, level, pressure):
    mach = (0.05 / time_step) * shift
    one_less = 1.0 - mach
    divisor = one_less * radius
    inverse = pl.reciprocal(divisor, approx=True)
    inverse = inverse * (2.0 - divisor * inverse)
    inv_radius = inverse * one_less
    wall = jnp.exp2(level - (exponent * inv_ln2) * jnp.log(radius))
    squared = time_step * time_step
    excess = (
        wall
        - (0.2 * squared + (0.08 * time_step) * shift) * inv_radius
        - (squared + squared * pressure)
    )
    driving = (1.0 + mach) * excess - (1.5 - 0.5 * mach) * (shift * shift)
    shift = shift + driving * inverse
    radius = radius + shift
    return radius, shift, (source_scale / time_step) * (radius * radius) * shift


def kernel(
    cells_h, slot_h, way_h, cells_b, press, vel, stretch, rest, speed0,
    PR, VX, VY, VZ, R, S, MSK, CAT, INFO,
    A, AR, SB, DB, OH, OHT, PHL, PG, VHL, SRC, XS, XR, YS, YR, VYS, VYR,
    MT, MR, AMSK, LT, LR, cells_s, slot_s, way_s, cells_v,
    in_sem, meta_s, meta_r, xs, xr, vs, vr, ds_, dr, fs, fr,
):
    _, cx, cy, nz = vel.shape
    nq = nz // LANES
    half = cx * cy
    ncol = 2 * half
    jbs = cy // 16
    part = min(256, ncol)
    planes = part // (2 * cy)
    groups = cx // planes
    shift = (planes * cy).bit_length() - 1
    zero_row = lax.axis_index("gx") // 4096
    gx, gy = lax.axis_index("gx"), lax.axis_index("gy")
    ngx, ngy = lax.axis_size("gx"), lax.axis_size("gy")
    has_lo, has_hi = gy > 0, gy < ngy - 1
    targets = (
        (lax.rem(gx + 1, ngx), gy),
        (lax.rem(gx + ngx - 1, ngx), gy),
        (gx, lax.rem(gy + 1, ngy)),
        (gx, lax.rem(gy + ngy - 1, ngy)),
    )
    sends = (None, None, has_hi, has_lo)
    takes = (None, None, has_lo, has_hi)

    def under(flag, action):
        if flag is None:
            action()
        else:
            pl.when(flag)(action)

    barrier = pltpu.get_barrier_semaphore()
    for d in range(4):
        under(
            sends[d],
            lambda d=d: pl.semaphore_signal(
                barrier, inc=1, device_id=targets[d], device_id_type=MESH
            ),
        )

    inputs = [(cells_h, cells_s), (slot_h, slot_s), (way_h, way_s), (cells_b, cells_v)]
    for q in range(nq):
        inputs.append((press.at[:, :, pl.ds(q * LANES, LANES)], PR.at[q, :, pl.ds(8, cy), :]))
    for q in range(nq):
        lanes = pl.ds(q * LANES, LANES)
        inputs.append((vel.at[1, :, :, lanes], VY.at[q, :, pl.ds(8, cy), :]))
    own = pl.ds(0, SLOTS)
    inputs.append((rest, A.at[own, :]))
    inputs.append((stretch, R.at[own, :]))
    inputs.append((speed0, S.at[own, :]))
    for q in range(nq):
        lanes = pl.ds(q * LANES, LANES)
        inputs.append((vel.at[0, :, :, lanes], VX.at[q, pl.ds(1, cx), :, :]))
        inputs.append((vel.at[2, :, :, lanes], VZ.at[q]))
    loads = [pltpu.make_async_copy(a, b, in_sem.at[k]) for k, (a, b) in enumerate(inputs)]
    for load in loads:
        load.start()
    small_loads, loads = loads[:4], loads[4:]

    @pl.when(jnp.logical_not(has_lo))
    def _():
        MR[2] = jnp.zeros((8, LANES), f32)
        YR[:, 0] = jnp.zeros(YR.shape[:1] + YR.shape[2:], f32)
        VYR[0] = jnp.zeros(VYR.shape[1:], f32)

    @pl.when(jnp.logical_not(has_hi))
    def _():
        MR[3] = jnp.zeros((8, LANES), f32)
        YR[:, 1] = jnp.zeros(YR.shape[:1] + YR.shape[2:], f32)
        VYR[1] = jnp.zeros(VYR.shape[1:], f32)

    edge_rows = jnp.zeros((nq, cx, 8, LANES), f32)
    PR[:, :, 0:8, :] = edge_rows
    PR[:, :, 8 + cy : 16 + cy, :] = edge_rows
    VY[:, :, 0:8, :] = edge_rows
    VY[:, :, 8 + cy : 16 + cy, :] = edge_rows
    empty = jnp.zeros((ARRIVE, BLOCK), f32)
    R[SLOTS:ROWS, :] = empty + 1.0
    S[SLOTS:ROWS, :] = empty
    A[SLOTS:ROWS, :] = empty
    MSK[SLOTS:ROWS, :] = jnp.full((ARRIVE, LANES), -1.0, f32)
    OHT[:, SLOTS:ROWS] = jnp.zeros((ncol, ARRIVE), bf16)
    VHL[SLOTS:ROWS, :] = jnp.zeros((ARRIVE, 2 * BLOCK), bf16)
    OH[SLOTS:ROWS, :] = jnp.zeros((ARRIVE, ncol), bf16)
    pl.semaphore_wait(barrier, 2 + has_lo.astype(jnp.int32) + has_hi.astype(jnp.int32))

    def remote(src, dst, send_sem, recv_sem, d):
        return pltpu.make_async_remote_copy(
            src_ref=src, dst_ref=dst, send_sem=send_sem, recv_sem=recv_sem,
            device_id=targets[d], device_id_type=MESH,
        )

    def meta_copy(d):
        return [remote(MT, MR.at[d], meta_s.at[d], meta_r.at[d], d)]

    def p_copy(t, d):
        if d < 2:
            src, dst = XS.at[t, 1 - d], XR.at[t, d]
        else:
            src, dst = YS.at[t, 3 - d], YR.at[t, d - 2]
        return [remote(src, dst, xs.at[t, d], xr.at[t, d], d)]

    def first_copies(d):
        side = (cx - 2, 0)[d]
        for q in range(nq):
            lanes = pl.ds(q * LANES, LANES)
            yield remote(
                press.at[pl.ds(side, 2), :, lanes], XR.at[0, d, q], fs.at[0, d, q], fr.at[0, d, q], d
            )
        for q in range(nq):
            lanes = pl.ds(q * LANES, LANES)
            yield remote(
                vel.at[0, pl.ds((cx - 1, 0)[d], 1), :, lanes],
                VX.at[q, pl.ds((0, cx + 1)[d], 1), :, :],
                fs.at[1, d, q],
                fr.at[1, d, q],
                d,
            )

    def v_copy(d):
        return [remote(VYS.at[3 - d], VYR.at[d - 2], vs.at[d], vr.at[d], d)]

    def dep_copy(t, d):
        to = AR.at[:, pl.ds(t * 32 + d * DEP, DEP), :]
        return [remote(SB.at[t], to, ds_.at[t, d], dr.at[t, d], d)]

    odd = lax.rem(gy, 2) == 1
    even = jnp.logical_not(odd)
    far_hi, near_hi = has_hi & odd, has_hi & even
    far_lo, near_lo = has_lo & even, has_lo & odd

    def start(make, ways=(0, 1, 2, 3)):
        order = ((far_hi, 2), (far_lo, 3), (None, 0), (None, 1), (near_hi, 2), (near_lo, 3))
        for flag, d in order:
            if d in ways:
                under(flag, lambda d=d: [copy.start() for copy in make(d)] and None)

    def wait_sent(make, ways=(0, 1, 2, 3)):
        for d in ways:
            under(sends[d], lambda d=d: [copy.wait_send() for copy in make(d)] and None)

    def wait_taken(make, ways=(0, 1, 2, 3)):
        for d in ways:
            under(takes[d], lambda d=d: [copy.wait_recv() for copy in make(d)] and None)

    for d in range(2):
        for copy in first_copies(d):
            copy.start()
    edges = ((0, 1), (cy - 2, cy - 1))

    def one(row):
        return pl.ds(row + zero_row, 1)

    pitch = cy + 16
    PR_rows = PR.reshape(nq * cx * pitch, LANES)
    VY_rows = VY.reshape(nq * cx * pitch, LANES)

    def across(q, row):
        return pl.ds(q * cx * pitch + 8 + row, cx, stride=pitch), slice(None)

    def pack_rows(t):
        for side in range(2):
            for r in range(2):
                for q in range(nq):
                    YS[t, side, r, q] = PR_rows[across(q, edges[side][r])]

    def unpack_rows(t):
        for side in range(2):
            for r in range(2):
                for q in range(nq):
                    PR_rows[across(q, edges[side][r])] = YS[t, side, r, q]

    def column_row(i, h, jb):
        return (i // planes) * part + (h * planes + i % planes) * cy + jb * 16

    def keep_parts(i, jb, q, value):
        high, low = split(value)
        row = column_row(i, q // 2, jb)
        col = (q % 2) * 2 * LANES
        PHL[row : row + 16, col : col + LANES] = high
        PHL[row : row + 16, col + LANES : col + 2 * LANES] = low

    def rows_of(jb):
        return slice(jb * 16, jb * 16 + 16), slice(8 + jb * 16, 24 + jb * 16)

    def split_all():
        for i in range(cx):
            for jb in range(jbs):
                for q in range(nq):
                    keep_parts(i, jb, q, PR[q, i, rows_of(jb)[1], :])

    for k in range(nq):
        loads[k].wait()
    pack_rows(0)
    start(lambda d: p_copy(0, d), (2, 3))
    for q in range(nq):
        for r in range(2):
            XS[0, 0, q, r] = PR[q, r, 8 : 8 + cy, :]
            XS[0, 1, q, r] = PR[q, cx - 2 + r, 8 : 8 + cy, :]
    for k in range(nq, 2 * nq):
        loads[k].wait()
    for q in range(nq):
        VYS[0, q] = VY_rows[across(q, 0)]
        VYS[1, q] = VY_rows[across(q, cy - 1)]
    start(v_copy, (2, 3))

    for load in small_loads:
        load.wait()

    lane8 = lax.broadcasted_iota(jnp.int32, (8, LANES), 1)
    sub8 = lax.broadcasted_iota(jnp.int32, (8, LANES), 0)
    slot_id = sub8 * LANES + lane8
    label = cells_v[...] + 1
    leave_at = jnp.where(label > 0, STEPS, -1)
    entry_of = (lane8 // 32) * DEP + lane8 % DEP
    wanted = (lane8 // DEP) % 4
    wanted = jnp.where(wanted < 2, 1 - wanted, 5 - wanted)
    meta = jnp.zeros((8, LANES), jnp.int32)
    for e in range(STEPS * DEP):
        slot = slot_s[e // DEP, 0, 0, e % DEP]
        moved = jnp.where(slot >= 0, cells_s[jnp.maximum(slot, 0)] + 1, 0)
        meta = jnp.where((entry_of == e) & (wanted == way_s[e // DEP, 0, 0, e % DEP]), moved, meta)
        leave_at = jnp.where(slot_id == slot, e // DEP, leave_at)
    MT[...] = meta.astype(f32)

    start(meta_copy)

    lrow = lax.broadcasted_iota(jnp.int32, (LANES, LANES), 0)
    lcol = lax.broadcasted_iota(jnp.int32, (LANES, LANES), 1)
    wide = lax.broadcasted_iota(jnp.int32, (16, ncol), 1).astype(f32)

    def code_of(lab):
        cell = lab - 1
        place = cell >> 1
        row = (place >> shift) * part + (cell & 1) * (planes * cy)
        return jnp.where(lab > 0, row + (place & (planes * cy - 1)), -1).astype(f32)

    def turn(stack):
        stack = stack + [jnp.zeros((8, LANES), f32)] * (16 - len(stack))
        LT[...] = jnp.concatenate(stack, axis=0).T

    def hot_rows(r, at):
        def body(m, carry):
            rows = pl.ds(pl.multiple_of(m * 16, 16), 16)
            hot = jnp.where(LT[rows, at : at + 1] == wide, 1.0, 0.0).astype(bf16)
            OH[pl.ds(pl.multiple_of(r * LANES + m * 16, 16), 16), :] = hot
            return carry

        lax.fori_loop(0, LANES // 16, body, 0, unroll=4)

    def hot_columns(first, last):
        def body(m, carry):
            ident = (lrow + m * LANES).astype(f32)
            rows = pl.ds(pl.multiple_of(m * LANES, LANES), LANES)
            for r in range(first, last):
                hot = jnp.where(ident == LR[r : r + 1, :], 1.0, 0.0).astype(bf16)
                OHT[rows, r * LANES : (r + 1) * LANES] = hot
            return carry

        lax.fori_loop(0, ncol // LANES, body, 0)

    code = code_of(label)
    turn([code, leave_at.astype(f32)])
    LR[0:8, :] = code
    for r in range(SLOT_BLOCKS):
        hot_rows(r, r)
    for r in range(SLOT_BLOCKS):
        MSK[r * LANES : (r + 1) * LANES, :] = jnp.broadcast_to(
            LT[:, 8 + r : 9 + r], (LANES, LANES)
        )
    hot_columns(0, SLOT_BLOCKS)

    for k in range(2 * nq, 2 * nq + 3):
        loads[k].wait()

    def first_state(n, carry):
        rows = pl.ds(pl.multiple_of(n * 16, 16), 16)
        rest_now = A[rows, :]
        R[rows, :] = R[rows, :] * rest_now
        S[rows, :] = time_step * S[rows, :]
        A[rows, :] = inv_ln2 * (
            jnp.log((time_step * time_step) * (1.0 + 0.2 / rest_now))
            + exponent * jnp.log(rest_now)
        )
        return carry

    lax.fori_loop(0, SLOTS // 16, first_state, 0, unroll=4)
    for k in range(2 * nq + 3, 4 * nq + 3):
        loads[k].wait()

    def plan():
        wait_taken(meta_copy)
        came = (lane8 // DEP) % 4
        alab = jnp.where(
            came == 0, MR[0], jnp.where(came == 1, MR[1], jnp.where(came == 2, MR[2], MR[3]))
        )
        acode = code_of(alab.astype(jnp.int32))
        turn([acode, alab])
        LR[8:16, :] = acode
        hot_rows(SLOT_BLOCKS, 0)
        hot_columns(SLOT_BLOCKS, SLOT_BLOCKS + 1)
        AMSK[...] = jnp.broadcast_to(LT[:, 8:9], (LANES, LANES))
        INFO[0] = label.astype(f32)
        INFO[1] = leave_at.astype(f32)
        INFO[2] = alab

    def slope_z(tiles):
        height = tiles[0].shape[0]
        lane = lax.broadcasted_iota(jnp.int32, (height, LANES), 1)
        zero = jnp.zeros((height, LANES), f32)
        ahead = [pltpu.roll(v, LANES - 1, 1) for v in tiles] + [zero]
        behind = [zero] + [pltpu.roll(v, 1, 1) for v in tiles]
        return [
            jnp.where(lane == LANES - 1, ahead[q + 1], ahead[q])
            - jnp.where(lane == 0, behind[q], behind[q + 1])
            for q in range(nq)
        ]

    low_gate = jnp.where(has_lo, 1.0, 0.0).astype(f32)
    high_gate = jnp.where(has_hi, 1.0, 0.0).astype(f32)

    def halves(w):
        return slice(w * LANES, (w + 1) * LANES), slice(2 * w * LANES, 2 * (w + 1) * LANES)

    def gather(w, rows=slice(0, ROWS)):
        narrow, pair = halves(w)
        both = jnp.dot(OH[rows, :], PHL[:, pair], preferred_element_type=f32)
        PG[rows, narrow] = both[:, :LANES] + both[:, LANES:]

    def scatter(w, rows, count):
        narrow, pair = halves(w)
        both = jnp.dot(OHT[rows, :count], VHL[:count, pair], preferred_element_type=f32)
        SRC[rows, narrow] = both[:, :LANES] + both[:, LANES:]

    def leavers(t, to):
        for k in range(DEP):
            slot = jnp.maximum(slot_s[t, 0, 0, k], 0)
            cell = jnp.maximum(cells_s[slot], 0)
            place = cell >> 1
            row = pl.ds(slot, 1)
            DB[0, k : k + 1, :] = R[row, :]
            DB[1, k : k + 1, :] = S[row, :]
            DB[2, k : k + 1, :] = A[row, :]
            for w in range(2):
                DB[3, k : k + 1, halves(w)[0]] = PR[
                    2 * (cell & 1) + w,
                    place >> (cy.bit_length() - 1),
                    pl.ds(8 + (place & (cy - 1)), 1),
                    :,
                ]
        radius, speed, _ = wall_update(DB[0], DB[1], DB[2], DB[3])
        SB[to, 0] = radius
        SB[to, 1] = speed
        SB[to, 2] = DB[2]

    def take_arrivals(t):
        wait_taken(lambda d: dep_copy(t, d))
        rows, to = slice(t * 32, t * 32 + 32), slice(SLOTS + t * 32, SLOTS + t * 32 + 32)
        R[to, :] = AR[0, rows, :]
        S[to, :] = AR[1, rows, :]
        A[to, :] = AR[2, rows, :]
        MSK[to, :] = jnp.where(AMSK[rows, :] > 0.0, 2.0 * STEPS, -1.0)

    def when(flag):
        return lambda action: action() if flag else None

    def settle(t):
        wait_sent(lambda d: dep_copy(t, d))
        wait_sent(lambda d: p_copy(t, d), (2, 3) if t == 0 else (0, 1, 2, 3))

    def step(t):
        limit = float(t)
        live = SLOTS + 32 * t
        final = t == STEPS - 1

        def bubbles(first, w):
            rows = slice(first, first + 16)
            col = halves(w)[0]
            radius, speed, rate = wall_update(R[rows, col], S[rows, col], A[rows, col], PG[rows, col])
            R[rows, col] = radius
            S[rows, col] = speed
            high, low = split(jnp.where(MSK[rows, :] >= limit, rate, 0.0))
            VHL[rows, 2 * w * LANES : (2 * w + 1) * LANES] = high
            VHL[rows, (2 * w + 1) * LANES : (2 * w + 2) * LANES] = low

        @when(t > 0)
        def _():
            take_arrivals(t - 1)

        split_all()
        last = t // (STEPS - 1)
        if not final:
            leavers(t, t)
        gather(0, slice(0, live))

        @when(last == 0)
        def _():
            start(lambda d: dep_copy(t, d))

        def pieces(count, size):
            ends = [k * size // count // 16 * 16 for k in range(count)] + [size]
            return [slice(ends[k], ends[k + 1]) for k in range(count)]

        for rows in pieces(2, live):
            gather(1, rows)
            for first in range(rows.start, rows.stop, 16):
                bubbles(first, 0)
        for rows, part_rows in zip(pieces(2, ncol), pieces(2, live)):
            scatter(0, rows, SLOTS if t == 0 else ROWS)
            for first in range(part_rows.start, part_rows.stop, 16):
                bubbles(first, 1)

        def flow_x(i):
            for q in range(nq):
                for jb in range(jbs):
                    rows, at = rows_of(jb)
                    flow = VX[q, i + 1, rows, :]
                    if i == 0:
                        flow = flow - half_gain * PR[q, 1, at, :]
                    elif i == cx - 1:
                        flow = flow + half_gain * PR[q, cx - 2, at, :]
                    else:
                        flow = flow - half_gain * (PR[q, i + 1, at, :] - PR[q, i - 1, at, :])
                    VX[q, i + 1, rows, :] = flow

        def flow_z(i, jb):
            rows, at = rows_of(jb)
            slopes = slope_z([PR[q, i, at, :] for q in range(nq)])
            for q in range(nq):
                VZ[q, i, rows, :] = VZ[q, i, rows, :] - half_gain * slopes[q]

        def flow_y(i, jb):
            _, at = rows_of(jb)
            for q in range(nq):
                VY[q, i, at, :] = VY[q, i, at, :] - half_gain * (
                    PR[q, i, pl.ds(9 + jb * 16 + zero_row, 16), :]
                    - PR[q, i, pl.ds(7 + jb * 16 + zero_row, 16), :]
                )

        def pressure(i, jb):
            rows, at = rows_of(jb)
            slopes = slope_z([VZ[q, i, rows, :] for q in range(nq)])
            for q in range(nq):
                rise = slopes[q] + (
                    VY[q, i, pl.ds(9 + jb * 16 + zero_row, 16), :]
                    - VY[q, i, pl.ds(7 + jb * 16 + zero_row, 16), :]
                )
                if i + 1 < cx:
                    rise = rise + VX[q, i + 2, rows, :]
                if i > 0:
                    rise = rise - VX[q, i, rows, :]
                row = column_row(i, q // 2, jb)
                col = (q % 2) * LANES
                PR[q, i, at, :] = (
                    PR[q, i, at, :] - half_gain * rise + SRC[row : row + 16, col : col + LANES]
                )

        for rows, part_planes in zip(pieces(2, ncol), pieces(2, cx)):
            scatter(1, rows, SLOTS if t == 0 else ROWS)
            for i in range(part_planes.start, part_planes.stop):
                flow_x(i)
                for jb in range(jbs):
                    flow_z(i, jb)
                    flow_y(i, jb)
        for i in range(cx):
            for jb in range(jbs):
                pressure(i, jb)
        pack_rows(t + 1)

        when(t == 0)(plan)
        wait_taken(lambda d: p_copy(t, d), (2, 3))

        @when(t > 0)
        def _():
            wait_taken(lambda d: p_copy(t, d), (0, 1))

        @when(t == 0)
        def _():
            for d in range(2):
                for copy in first_copies(d):
                    copy.wait_recv()
            wait_taken(v_copy, (2, 3))

        below, above = VYR[0], VYR[1]
        below = low_gate * (below - half_gain * (YS[t, 0, 0] - YR[t, 0, 0]))
        above = high_gate * (above - half_gain * (YR[t, 1, 1] - YS[t, 1, 1]))
        VYR[0] = below
        VYR[1] = above
        both_gains = half_gain * half_gain
        YS[t + 1, 0, 0] = YS[t + 1, 0, 0] + half_gain * below
        YS[t + 1, 0, 1] = YS[t + 1, 0, 1] + both_gains * YR[t, 0, 1]
        YS[t + 1, 1, 0] = YS[t + 1, 1, 0] + both_gains * YR[t, 1, 0]
        YS[t + 1, 1, 1] = YS[t + 1, 1, 1] - half_gain * above
        for q in range(nq):
            for jb in range(jbs):
                rows, at = rows_of(jb)
                far, near = XR[t, 0, q, 0, rows, :], XR[t, 0, q, 1, rows, :]
                beside = VX[q, 0, rows, :] - half_gain * (XS[t, 0, q, 0, rows, :] - far)
                VX[q, 0, rows, :] = beside
                VX[q, 1, rows, :] = VX[q, 1, rows, :] + half_gain * near
                first = PR[q, 0, at, :] + half_gain * beside
                second = PR[q, 1, at, :] + both_gains * near
                PR[q, 0, at, :] = first
                PR[q, 1, at, :] = second
                if not final:
                    XS[t + 1, 0, q, 0, rows, :] = first
                if not final:
                    XS[t + 1, 0, q, 1, rows, :] = second
                near, far = XR[t, 1, q, 0, rows, :], XR[t, 1, q, 1, rows, :]
                beside = VX[q, cx + 1, rows, :] - half_gain * (far - XS[t, 1, q, 1, rows, :])
                VX[q, cx + 1, rows, :] = beside
                VX[q, cx, rows, :] = VX[q, cx, rows, :] - half_gain * near
                first = PR[q, cx - 2, at, :] + both_gains * near
                second = PR[q, cx - 1, at, :] - half_gain * beside
                PR[q, cx - 2, at, :] = first
                PR[q, cx - 1, at, :] = second
                if not final:
                    XS[t + 1, 1, q, 0, rows, :] = first
                if not final:
                    XS[t + 1, 1, q, 1, rows, :] = second
        ends = ((0, 0, 0), (1, 0, 1), (cx - 2, 1, 0), (cx - 1, 1, 1))
        for i, x_side, x_row in ends:
            for side in range(2):
                for r in range(2):
                    for q in range(nq):
                        row = one(edges[side][r])
                        if i == 0:
                            part_x = half_gain * VX[q, 0, row, :]
                        elif i == 1:
                            part_x = both_gains * XR[t, 0, q, 1, row, :]
                        elif i == cx - 2:
                            part_x = both_gains * XR[t, 1, q, 0, row, :]
                        else:
                            part_x = -half_gain * VX[q, cx + 1, row, :]
                        value = YS[t + 1, side, r, q, one(i), :] + part_x
                        YS[t + 1, side, r, q, one(i), :] = value
                        if not final:
                            XS[t + 1, x_side, q, x_row, row, :] = value

        @when(t < STEPS - 1)
        def _():
            start(lambda d: p_copy(t + 1, d))

        unpack_rows(t + 1)

        @when(t == STEPS - 2)
        def _():
            leavers(t + 1, t + 1)
            start(lambda d: dep_copy(t + 1, d))

        for q in range(nq):
            low, high = across(q, 0), across(q, cy - 1)
            VY_rows[low] = VY_rows[low] + half_gain * YR[t, 0, 1, q]
            VY_rows[high] = VY_rows[high] - half_gain * YR[t, 1, 0, q]

        if t > 0:
            settle(t - 1)

    for t in range(STEPS):
        step(t)

    take_arrivals(STEPS - 1)
    keep = AMSK[...] > 0.0
    for k, state in enumerate((R, S)):
        for w in range(2):
            high, low = split(jnp.where(keep, state[SLOTS:ROWS, halves(w)[0]], 0.0))
            to = slice(k * BLOCK + w * LANES, k * BLOCK + (w + 1) * LANES)
            CAT[0:ARRIVE, to] = high
            CAT[ARRIVE : 2 * ARRIVE, to] = low

    settle(STEPS - 1)
    wait_sent(meta_copy)
    wait_sent(v_copy, (2, 3))
    for d in range(2):
        for copy in first_copies(d):
            copy.wait_send()


def write_out(
    p, vx, vy, vz, r, s, mask, cat, info, p_out, v_out, r_out, s_out, c_out, r_end, s_end, c_end, lt, sems
):
    _, cx, cy, nz = v_out.shape
    pairs = []
    for q in range(nz // LANES):
        lanes = pl.ds(q * LANES, LANES)
        pairs.append((vx.at[q, pl.ds(1, cx), :, :], v_out.at[0, :, :, lanes]))
        pairs.append((vy.at[q, :, pl.ds(8, cy), :], v_out.at[1, :, :, lanes]))
        pairs.append((vz.at[q], v_out.at[2, :, :, lanes]))
        pairs.append((p.at[q, :, pl.ds(8, cy), :], p_out.at[:, :, lanes]))
    copies = [pltpu.make_async_copy(a, b, sems.at[k]) for k, (a, b) in enumerate(pairs)]
    for copy in copies:
        copy.start()

    lane8 = lax.broadcasted_iota(jnp.int32, (8, LANES), 1)
    sub8 = lax.broadcasted_iota(jnp.int32, (8, LANES), 0)
    lrow = lax.broadcasted_iota(jnp.int32, (LANES, LANES), 0)
    lcol = lax.broadcasted_iota(jnp.int32, (LANES, LANES), 1)
    label, leave_at, alab = info[0], info[1], info[2]
    present = alab > 0.0
    upper = jnp.where(lrow <= lcol, 1.0, 0.0)
    upper_block = jnp.where(lrow // 32 == lcol // 32, upper, 0.0).astype(bf16)
    upper = upper.astype(bf16)
    ones = jnp.ones((LANES, LANES), bf16)
    present_f = jnp.where(present, 1.0, 0.0)
    arank = jnp.dot(present_f.astype(bf16), upper_block, preferred_element_type=f32) - 1.0
    arank = jnp.where(present, arank, -5.0)
    vacant = label == 0.0
    ranks = []
    for t in range(STEPS):
        vacant = vacant | (leave_at == float(t))
        flag = jnp.where(vacant, 1.0, 0.0).astype(bf16)
        rank = jnp.dot(flag, upper, preferred_element_type=f32) - 1.0
        total = jnp.dot(flag, ones, preferred_element_type=f32)
        for k in range(SLOT_BLOCKS - 1):
            rank = rank + jnp.where(sub8 > k, total[k : k + 1, :], 0.0)
        ranks.append(jnp.where(vacant, rank, -1.0))
        count = jnp.sum(jnp.where(lane8 // 32 == t, present_f, 0.0), axis=1, keepdims=True)
        vacant = vacant & (rank >= count)
    lt[...] = jnp.concatenate(ranks + [jnp.zeros((LANES - 8 * STEPS, LANES), f32)], axis=0).T

    group = lcol // 32
    alab_high, alab_low = split(alab)
    final = jnp.where(leave_at == float(STEPS), label, 0.0)
    nt = (((1,), (1,)), ((), ()))
    for k in range(SLOT_BLOCKS):
        rows = slice(k * LANES, (k + 1) * LANES)
        mine = jnp.broadcast_to(lt[:, k : k + 1], (LANES, LANES))
        for t in range(1, STEPS):
            mine = jnp.where(group == t, lt[:, 8 * t + k : 8 * t + k + 1], mine)
        hot = jnp.where(mine == arank[0:1, :], 1.0, 0.0).astype(bf16)
        there = lax.dot_general(alab_high, hot, nt, preferred_element_type=f32)
        there = there + lax.dot_general(alab_low, hot, nt, preferred_element_type=f32)
        final = final + jnp.where(sub8 == k, there, 0.0)
        both = jnp.concatenate([hot, hot], axis=1)
        placed = jnp.dot(both, cat[...], preferred_element_type=f32)
        keep = mask[rows, :]
        keep = jnp.concatenate([keep, keep], axis=1) >= float(STEPS)
        r_end[rows, :] = jnp.where(keep, r[rows, :], 0.0) + placed[:, :BLOCK]
        s_end[rows, :] = (1.0 / time_step) * (jnp.where(keep, s[rows, :], 0.0) + placed[:, BLOCK:])
        if k % 4 == 3:
            rows_of = pl.ds((k - 3) * LANES, 4 * LANES)
            for a, b in ((r_end, r_out), (s_end, s_out)):
                copy = pltpu.make_async_copy(a.at[rows_of, :], b.at[rows_of, :], sems.at[len(copies)])
                copy.start()
                copies.append(copy)
    c_end[...] = final.astype(jnp.int32) - 1
    copy = pltpu.make_async_copy(c_end, c_out, sems.at[len(copies)])
    copy.start()
    copies.append(copy)
    for copy in copies:
        copy.wait()


def on_device(
    pressure, velocity, stretch, rest_radius, wall_speed, block_cells, depart_slot, depart_way
):
    cx, cy, nz = pressure.shape
    nq = nz // LANES
    ncol = 2 * cx * cy
    vmem = pl.BlockSpec(memory_space=pltpu.VMEM)
    hbm = pl.BlockSpec(memory_space=pl.ANY)
    dma = pltpu.SemaphoreType.DMA
    vmem_out = pltpu.VMEM
    parts = pl.pallas_call(
        kernel,
        out_shape=(
            vmem_out((nq, cx, cy + 16, LANES), f32),
            vmem_out((nq, cx + 2, cy, LANES), f32),
            vmem_out((nq, cx, cy + 16, LANES), f32),
            vmem_out((nq, cx, cy, LANES), f32),
            vmem_out((ROWS, BLOCK), f32),
            vmem_out((ROWS, BLOCK), f32),
            vmem_out((ROWS, LANES), f32),
            vmem_out((2 * ARRIVE, 2 * BLOCK), bf16),
            vmem_out((3, SLOT_BLOCKS, LANES), f32),
        ),
        in_specs=[pl.BlockSpec(memory_space=pltpu.HBM)] * 9,
        out_specs=(vmem,) * 9,
        scratch_shapes=[
            pltpu.VMEM((ROWS, BLOCK), f32),
            pltpu.VMEM((3, ARRIVE, BLOCK), f32),
            pltpu.VMEM((STEPS + 1, 3, DEP, BLOCK), f32),
            pltpu.VMEM((4, DEP, BLOCK), f32),
            pltpu.VMEM((ROWS, ncol), bf16),
            pltpu.VMEM((ncol, ROWS), bf16),
            pltpu.VMEM((ncol, 2 * BLOCK), bf16),
            pltpu.VMEM((ROWS, BLOCK), f32),
            pltpu.VMEM((ROWS, 2 * BLOCK), bf16),
            pltpu.VMEM((ncol, BLOCK), f32),
            pltpu.VMEM((STEPS + 1, 2, nq, 2, cy, LANES), f32),
            pltpu.VMEM((STEPS, 2, nq, 2, cy, LANES), f32),
            pltpu.VMEM((STEPS + 1, 2, 2, nq, cx, LANES), f32),
            pltpu.VMEM((STEPS, 2, 2, nq, cx, LANES), f32),
            pltpu.VMEM((2, nq, cx, LANES), f32),
            pltpu.VMEM((2, nq, cx, LANES), f32),
            pltpu.VMEM((8, LANES), f32),
            pltpu.VMEM((4, 8, LANES), f32),
            pltpu.VMEM((ARRIVE, LANES), f32),
            pltpu.VMEM((LANES, LANES), f32),
            pltpu.VMEM((16, LANES), f32),
            pltpu.SMEM((SLOTS,), jnp.int32),
            pltpu.SMEM((STEPS, 1, 1, DEP), jnp.int32),
            pltpu.SMEM((STEPS, 1, 1, DEP), jnp.int32),
            pltpu.VMEM((SLOT_BLOCKS, LANES), jnp.int32),
            dma((4 * nq + 7,)),
            dma((4,)),
            dma((4,)),
            dma((STEPS, 4)),
            dma((STEPS, 4)),
            dma((4,)),
            dma((4,)),
            dma((STEPS, 4)),
            dma((STEPS, 4)),
            dma((2, 2, nq)),
            dma((2, 2, nq)),
        ],
        compiler_params=pltpu.CompilerParams(
            collective_id=0, has_side_effects=True, vmem_limit_bytes=36 * 2**20
        ),
        cost_estimate=pl.CostEstimate(
            flops=10 * 2**30, bytes_accessed=13 * 2**20, transcendentals=2**22
        ),
    )(
        *(
            pltpu.with_memory_space_constraint(value, pltpu.HBM)
            for value in (
                block_cells,
                depart_slot,
                depart_way,
                block_cells.reshape(SLOT_BLOCKS, LANES),
                pressure,
                velocity,
                stretch,
                rest_radius,
                wall_speed,
            )
        )
    )
    parts = [pltpu.with_memory_space_constraint(part, pltpu.VMEM) for part in parts]
    p, v, r, s, c = pl.pallas_call(
        write_out,
        out_shape=(
            jax.ShapeDtypeStruct(pressure.shape, f32),
            jax.ShapeDtypeStruct(velocity.shape, f32),
            jax.ShapeDtypeStruct(stretch.shape, f32),
            jax.ShapeDtypeStruct(stretch.shape, f32),
            jax.ShapeDtypeStruct((SLOT_BLOCKS, LANES), jnp.int32),
        ),
        in_specs=[vmem] * 9,
        out_specs=(hbm,) * 5,
        scratch_shapes=[
            pltpu.VMEM((SLOTS, BLOCK), f32),
            pltpu.VMEM((SLOTS, BLOCK), f32),
            pltpu.VMEM((SLOT_BLOCKS, LANES), jnp.int32),
            pltpu.VMEM((LANES, LANES), f32),
            dma((4 * nq + 5,)),
        ],
        compiler_params=pltpu.CompilerParams(vmem_limit_bytes=8 * 2**20),
        cost_estimate=pl.CostEstimate(flops=0, bytes_accessed=13 * 2**20, transcendentals=0),
    )(*parts)
    return p, v, r, s, c.reshape(-1)


def solution(mesh):
    placed = (
        P("gx", "gy", None),
        P(None, "gx", "gy", None),
        P(("gx", "gy"), None),
        P(("gx", "gy"), None),
        P(("gx", "gy"), None),
        P(("gx", "gy")),
        P(None, "gx", "gy", None),
        P(None, "gx", "gy", None),
    )
    return jax.shard_map(
        on_device,
        mesh=mesh,
        in_specs=placed,
        out_specs=(
            P("gx", "gy", None),
            P(None, "gx", "gy", None),
            P(("gx", "gy"), None),
            P(("gx", "gy"), None),
            P(("gx", "gy")),
        ),
        check_vma=False,
    )
```
